32 devices in a mesh: dp: 4 (over y, x), expert: 8 (over z, core).
Axes of the slice: x: 2, y: 2, z: 4, core: 2. Of those that a mesh axis runs over, the one named last changes fastest.
Arguments:
- tokens: bfloat16 [25216, 768], P(('dp', 'expert')), may hold values from -6 to 6
- image_count: int32 [32], P(('dp', 'expert')), may hold values from 1 to 4, as said below
- routes: int32 [25216, 2], P(('dp', 'expert')), may hold values from 0 to 7, all different within a row; in each aligned block of 788 rows (0 to 787, 788 to 1575, ...) at most 246 rows name the same one
- capacity: int32 [8], replicated, may hold values from 123 to 246, as said below
- ln1_gain: bfloat16 [768], P(('dp', 'expert')), may hold values from 0.5 to 1.5
- ln1_bias: bfloat16 [768], P(('dp', 'expert')), may hold values from -0.625 to 0.625
- qkv_weight: bfloat16 [768, 2304], P(('dp', 'expert')), may hold values from -0.21875 to 0.21875
- qv_bias: bfloat16 [2, 768], P(None, ('dp', 'expert')), may hold values from -0.625 to 0.625
- out_weight: bfloat16 [768, 768], P(('dp', 'expert')), may hold values from -0.875 to 0.875
- out_bias: bfloat16 [768], P(('dp', 'expert')), may hold values from -0.625 to 0.625
- ln2_gain: bfloat16 [768], P(('dp', 'expert')), may hold values from 0.5 to 1.5
- ln2_bias: bfloat16 [768], P(('dp', 'expert')), may hold values from -0.625 to 0.625
- router_weight: bfloat16 [768, 8], P(('dp', 'expert')), may hold values from -0.15625 to 0.15625
- expert_in: bfloat16 [8, 768, 3072], P('expert', None, 'dp'), may hold values from -0.21875 to 0.21875
- expert_in_bias: bfloat16 [8, 3072], P('expert', 'dp'), may hold values from -0.625 to 0.625
- expert_out: bfloat16 [8, 3072, 768], P('expert', 'dp'), may hold values from -0.4375 to 0.4375
- expert_out_bias: bfloat16 [8, 768], P('expert', 'dp'), may hold values from -1.5 to 1.5
- cotangent: bfloat16 [25216, 768], P(('dp', 'expert')), may hold values from -6 to 6
Outputs:
- block_out: bfloat16 [25216, 768], P(('dp', 'expert'))
- tokens_grad: float32 [25216, 768], P(('dp', 'expert'))
- ln1_gain_grad: float32 [768], P(('dp', 'expert'))
- ln1_bias_grad: float32 [768], P(('dp', 'expert'))
- qkv_weight_grad: float32 [768, 2304], P(('dp', 'expert'))
- qv_bias_grad: float32 [2, 768], P(None, ('dp', 'expert'))
- out_weight_grad: float32 [768, 768], P(('dp', 'expert'))
- out_bias_grad: float32 [768], P(('dp', 'expert'))
- ln2_gain_grad: float32 [768], P(('dp', 'expert'))
- ln2_bias_grad: float32 [768], P(('dp', 'expert'))
- router_weight_grad: float32 [768, 8], P(('dp', 'expert'))
- expert_in_grad: float32 [8, 768, 3072], P('expert', None, 'dp')
- expert_in_bias_grad: float32 [8, 3072], P('expert', 'dp')
- expert_out_grad: float32 [8, 3072, 768], P('expert', 'dp')
- expert_out_bias_grad: float32 [8, 768], P('expert', 'dp')
The draws below stay inside these ranges and needn't reach their ends.
Inputs may be any that keep to these rules, and one draw needn't show every extreme that they name: `routes`: within the rows of one device, each expert is named by at most 246 rows, and one expert by exactly 246 rows in some devices. Some expert's capacity is exactly 246. A device holds images in its first image_count slots; the rows of the other slots take no expert slot. Some device holds 4 images.
All inputs are finite; a program needn't handle non-finite values.
Results may differ from the reference program's by a relative error of at most 0.014.
Values may be sent and summed in bfloat16 or wider, within the bound.
No kernel may reach another device: no remote copies, remote signals or barrier semaphores. Data moves between devices by JAX's collectives and lax.ppermute only.
A program may use at most 256 MiB of HBM per device.

```python
import math
import jax
import jax.numpy as jnp
import numpy as np
from jax import lax

D = 768
HEADS = 12
HEAD_DIM = 64
FF = 3072
SEQ = 197
IMG_DEV = 4
TOK_DEV = 788
EXPERTS = 8
CAP = 246
DEVICE_COUNT = 32
TOKENS = 25216


def draw_image_count(key, part):
    key = jax.random.fold_in(key, 11)
    count_key, pick_key = jax.random.split(key)
    counts = jax.random.randint(count_key, (DEVICE_COUNT,), 1, IMG_DEV + 1)
    full_index = jax.random.randint(pick_key, (), 0, DEVICE_COUNT)
    return jnp.where(jnp.arange(DEVICE_COUNT) == full_index, IMG_DEV, counts).astype(jnp.int32)


def draw_capacity(key, part):
    key = jax.random.fold_in(key, 23)
    count_key, pick_key = jax.random.split(key)
    limits = jax.random.randint(count_key, (EXPERTS,), (CAP + 1) // 2, CAP + 1)
    full_index = jax.random.randint(pick_key, (), 0, EXPERTS)
    return jnp.where(jnp.arange(EXPERTS) == full_index, CAP, limits).astype(jnp.int32)


def level_of(key, extent, pieces, least, high):
    loudness, own = 1.0, jax.random.fold_in(key, 6)
    for position, blocks in pieces:
        draws = jnp.exp(jax.random.uniform(jax.random.fold_in(own, position), (blocks,), jnp.float32, least / len(pieces), high / len(pieces)))
        loudness = loudness * jnp.repeat(draws, extent[position] // blocks).reshape([-1 if axis == position else 1 for axis in range(len(extent))])
    return loudness


def shared_out(key, own, number, rows, count, top, most, slope):
    ranking = jax.random.permutation(key, count)
    heavy_load, common = load_shares(count, rows * top, most, slope, True), load_shares(count, rows * top, most, slope, False)
    places = jnp.arange(count)

    def named(sizes, turn):
        used = int((sizes > 0).sum())
        fixed = max(1, used // 4)
        moved = fixed + (places - fixed + turn * (used - fixed)) % max(1, count - fixed)
        return jnp.zeros((count,), jnp.int32).at[ranking[jnp.where(places < fixed, places, moved)]].set(jnp.asarray(sizes, jnp.int32))

    sizes = jnp.where(number % 4 == 0, named(heavy_load, number // 4), named(common, number - number // 4 - 1))
    mixed = jax.random.permutation(jax.random.fold_in(own, 3), count)
    source_of, receiver = mixed[0:count // 2 * 2:2], mixed[1:count // 2 * 2:2]
    margin = jnp.minimum(sizes[source_of] - 1, most - sizes[receiver]) // 2
    margin = jnp.where((source_of == ranking[0]) | (receiver == ranking[0]) | (sizes[receiver] == 0), 0, jnp.maximum(margin, 0))
    moved = jax.random.randint(jax.random.fold_in(own, 4), (count // 2,), 0, 1 << 20) % (margin + 1)
    sizes = sizes.at[source_of].add(-moved).at[receiver].add(moved)
    members = jnp.searchsorted(jnp.cumsum(sizes), jnp.arange(rows * top), side="right").astype(jnp.int32)
    table = members.reshape(top, rows).T
    table = table[jax.random.permutation(jax.random.fold_in(own, 1), rows)]
    turn = jax.random.randint(jax.random.fold_in(own, 2), (rows, 1), 0, top)
    return jnp.take_along_axis(table, (jnp.arange(top)[None, :] + turn) % top, axis=1)


def load_shares(number_of, total, limit, slope, full):
    loads = [(1 << 20) // math.isqrt(standing ** slope) + 1 for standing in range(1, number_of + 1)]
    largest = limit if full else min(limit, max(-(-total // number_of), total * loads[0] // sum(loads)))
    least = 1 if total - largest >= number_of - 1 else 0
    given, rest = [largest] + [least] * (number_of - 1), total - largest - least * (number_of - 1)
    while rest > 0:
        candidates = [i for i in range(1, number_of) if given[i] < largest] or [i for i in range(1, number_of) if given[i] < limit]
        whole, budget = sum([loads[i] for i in candidates]), rest
        for i in candidates:
            addition = min(limit - given[i], max(1, budget * loads[i] // whole), rest)
            given[i] = given[i] + addition
            rest = rest - addition
    return np.array(given)


def bell_draw(own_key, dims, spread, reach, cuts=(), kind=jnp.bfloat16):
    values = spread * jax.random.normal(own_key, dims, jnp.float32)
    if cuts:
        values = values * level_of(own_key, dims, cuts, -0.22, 0.18)
    return jnp.clip(values, -reach, reach).astype(kind)


def setup_inputs(seed: int = 0) -> dict:
    arg_keys = jax.random.split(jax.random.key(seed), 19)
    tokens = bell_draw(arg_keys[0], (TOKENS, D), 1.0, 6.0, ((0, 32),))
    image_count = draw_image_count(jax.random.fold_in(arg_keys[18], 71), 0)
    routes_keys = jax.random.split(jax.random.fold_in(arg_keys[2], 1), TOKENS // TOK_DEV)
    routes_turns = jax.random.permutation(jax.random.fold_in(arg_keys[2], 3), TOKENS // TOK_DEV)
    routes = jax.vmap(lambda own, number: shared_out(jax.random.fold_in(arg_keys[2], 2), own, number, TOK_DEV, EXPERTS, 2, CAP, 2))(routes_keys, routes_turns).reshape((TOKENS, 2))
    capacity = draw_capacity(jax.random.fold_in(arg_keys[18], 71), 0)
    ln1_gain = jnp.clip(1.0 + 0.1 * jax.random.normal(arg_keys[4], (D,), jnp.float32), 0.5, 1.5).astype(jnp.bfloat16)
    ln1_bias = bell_draw(arg_keys[5], (D,), 0.1, 0.625, ((0, 32),))
    qkv_weight = bell_draw(arg_keys[6], (D, 3 * D), D ** -0.5, 0.21875, ((0, 32),))
    qv_bias = bell_draw(arg_keys[7], (2, D), 0.1, 0.625, ((1, 32),))
    out_weight = bell_draw(arg_keys[8], (D, D), (D // 16) ** -0.5, 0.875, ((0, 32),))
    out_bias = bell_draw(arg_keys[9], (D,), 0.1, 0.625, ((0, 32),))
    ln2_gain = jnp.clip(1.0 + 0.1 * jax.random.normal(arg_keys[10], (D,), jnp.float32), 0.5, 1.5).astype(jnp.bfloat16)
    ln2_bias = bell_draw(arg_keys[11], (D,), 0.1, 0.625, ((0, 32),))
    router_weight = bell_draw(arg_keys[12], (D, EXPERTS), (2 * D) ** -0.5, 0.15625, ((0, 32),))
    expert_in = bell_draw(arg_keys[13], (EXPERTS, D, FF), D ** -0.5, 0.21875, ((0, 8), (2, 4)))
    expert_in_bias = bell_draw(arg_keys[14], (EXPERTS, FF), 0.1, 0.625, ((0, 8), (1, 4)))
    expert_out = bell_draw(arg_keys[15], (EXPERTS, FF, D), (max(1, (4 * FF) // (EXPERTS * EXPERTS))) ** -0.5, 0.4375, ((0, 8), (1, 4)))
    expert_out_bias = bell_draw(arg_keys[16], (EXPERTS, D), (0.03 * EXPERTS), 1.5, ((0, 8), (1, 4)))
    cotangent = bell_draw(arg_keys[17], (TOKENS, D), 1.0, 6.0, ((0, 32),))
    return dict(tokens=tokens, image_count=image_count, routes=routes, capacity=capacity, ln1_gain=ln1_gain, ln1_bias=ln1_bias, qkv_weight=qkv_weight, qv_bias=qv_bias, out_weight=out_weight, out_bias=out_bias, ln2_gain=ln2_gain, ln2_bias=ln2_bias, router_weight=router_weight, expert_in=expert_in, expert_in_bias=expert_in_bias, expert_out=expert_out, expert_out_bias=expert_out_bias, cotangent=cotangent)


@jax.custom_vjp
def low(v):
    return lax.optimization_barrier(v.astype(jnp.bfloat16)).astype(jnp.float32)

@jax.custom_vjp
def low_back(v):
    return v

def low_keep(v):
    return (low(v), None)

def low_pass(kept, grad):
    return (grad,)

def back_keep(v):
    return (v, None)

def back_low(kept, grad):
    return (low(grad),)
low.defvjp(low_keep, low_pass)
low_back.defvjp(back_keep, back_low)
EPS_NORM = 1e-06
NEG_FILL = -1e+30

def norm_layer(values, norm_gain, norm_bias):
    centered = values - lax.optimization_barrier(jnp.mean(values, axis=-1, keepdims=True))
    variance = lax.optimization_barrier(jnp.mean(centered * centered, axis=-1, keepdims=True))
    return centered * lax.rsqrt(variance + EPS_NORM) * norm_gain + norm_bias

def matmul_high(left, right):
    return jnp.dot(left, right, precision=lax.Precision.HIGHEST, preferred_element_type=jnp.float32)

def route_slots(routes_block, alive_block, capacity, slot_cap):
    expert_count = capacity.shape[0]
    expert_ids = jnp.arange(expert_count, dtype=jnp.int32)
    first_hit = ((routes_block[:, 0:1] == expert_ids[None, :]) & alive_block[:, None]).astype(jnp.int32)
    second_hit = ((routes_block[:, 1:2] == expert_ids[None, :]) & alive_block[:, None]).astype(jnp.int32)
    ahead_first = jnp.cumsum(first_hit, axis=0) - first_hit
    ahead_second = jnp.cumsum(second_hit, axis=0) - second_hit + lax.optimization_barrier(jnp.sum(first_hit, axis=0, keepdims=True))
    place_first = lax.optimization_barrier(jnp.sum(first_hit * ahead_first, axis=1))
    place_second = lax.optimization_barrier(jnp.sum(second_hit * ahead_second, axis=1))
    limit_first = lax.optimization_barrier(jnp.sum(first_hit * capacity[None, :], axis=1))
    limit_second = lax.optimization_barrier(jnp.sum(second_hit * capacity[None, :], axis=1))
    keep_first = place_first < limit_first
    keep_second = place_second < limit_second
    dump_slot = expert_count * slot_cap
    slot_first = jnp.where(keep_first, routes_block[:, 0] * slot_cap + place_first, dump_slot).astype(jnp.int32)
    slot_second = jnp.where(keep_second, routes_block[:, 1] * slot_cap + place_second, dump_slot).astype(jnp.int32)
    return (slot_first, slot_second, keep_first, keep_second)

def attend_block(qkv_block):
    query = qkv_block[:, :D].reshape(TOK_DEV, HEADS, HEAD_DIM)
    keyed = qkv_block[:, D:2 * D].reshape(TOK_DEV, HEADS, HEAD_DIM)
    valued = qkv_block[:, 2 * D:].reshape(TOK_DEV, HEADS, HEAD_DIM)
    image_ids = jnp.arange(TOK_DEV, dtype=jnp.int32) // SEQ
    same_image = image_ids[:, None] == image_ids[None, :]
    scores = low_back(jnp.einsum('qhd,khd->hqk', query, keyed, precision=lax.Precision.HIGHEST) * (1.0 / math.sqrt(HEAD_DIM)))
    scores = jnp.where(same_image[None], scores, NEG_FILL)
    probabilities = jax.nn.softmax(scores, axis=-1)
    attended = jnp.einsum('hqk,khd->qhd', low(probabilities), valued, precision=lax.Precision.HIGHEST)
    return low_back(low(attended.reshape(TOK_DEV, D)))

def expert_apply(packed):
    slot_rows, w_in, b_in, w_out, b_out = packed
    pre_act = low_back(matmul_high(slot_rows, w_in) + b_in)
    activated = low(jax.nn.gelu(pre_act, approximate=True))
    return low_back(low(matmul_high(activated, w_out) + b_out))

def fill_buffer(block_rows, slot_first, slot_second):
    buffer = jnp.zeros((EXPERTS * CAP + 1, D), block_rows.dtype)
    buffer = buffer.at[slot_first].add(block_rows).at[slot_second].add(block_rows)
    return buffer[:-1]

def pick_rows(returned_block, slot_index):
    padded = jnp.concatenate([returned_block, jnp.zeros((1, D), returned_block.dtype)], axis=0)
    return padded[slot_index]

def reference(tokens, image_count, routes, capacity, ln1_gain, ln1_bias, qkv_weight, qv_bias, out_weight, out_bias, ln2_gain, ln2_bias, router_weight, expert_in, expert_in_bias, expert_out, expert_out_bias, cotangent):
    row_ids = jnp.arange(TOKENS, dtype=jnp.int32)
    owner = row_ids // TOK_DEV
    alive_rows = row_ids % TOK_DEV // SEQ < image_count[owner]
    alive_f = alive_rows.astype(jnp.float32)

    def slots_for(routes_block, alive_block):
        return route_slots(routes_block, alive_block, capacity, CAP)
    slot_first, slot_second, keep_first, keep_second = jax.vmap(slots_for)(routes.reshape(DEVICE_COUNT, TOK_DEV, 2), alive_rows.reshape(DEVICE_COUNT, TOK_DEV))
    keep_pair = jnp.stack([keep_first.reshape(TOKENS), keep_second.reshape(TOKENS)], axis=1).astype(jnp.float32)

    def forward(tokens_f, g_one, b_one, w_qkv, b_qv, w_attn, b_attn, g_two, b_two, w_router, w_in, b_in, w_out, b_out):
        normed_one = low(norm_layer(tokens_f, g_one, b_one))
        bias_full = jnp.concatenate([b_qv[0], jnp.zeros((D,), jnp.float32), b_qv[1]])
        qkv_all = low_back(low(matmul_high(normed_one, w_qkv) + bias_full))
        attended = lax.map(jax.checkpoint(attend_block), qkv_all.reshape(DEVICE_COUNT, TOK_DEV, 3 * D)).reshape(TOKENS, D)
        attn_out = low_back(matmul_high(attended, w_attn) + b_attn)
        after_attn = tokens_f + alive_f[:, None] * attn_out
        normed_two = low(norm_layer(after_attn, g_two, b_two))
        logits = low_back(matmul_high(normed_two, w_router))
        gate_probs = jax.nn.softmax(logits, axis=-1)
        buffers = jax.vmap(fill_buffer)(normed_two.reshape(DEVICE_COUNT, TOK_DEV, D), slot_first, slot_second)
        by_expert = low_back(buffers.reshape(DEVICE_COUNT, EXPERTS, CAP, D).transpose(1, 0, 2, 3).reshape(EXPERTS, DEVICE_COUNT * CAP, D))
        outputs = lax.map(jax.checkpoint(expert_apply), (by_expert, w_in, b_in, w_out, b_out))
        returned = outputs.reshape(EXPERTS, DEVICE_COUNT, CAP, D).transpose(1, 0, 2, 3).reshape(DEVICE_COUNT, EXPERTS * CAP, D)
        picked_first = jax.vmap(pick_rows)(returned, slot_first).reshape(TOKENS, D)
        picked_second = jax.vmap(pick_rows)(returned, slot_second).reshape(TOKENS, D)
        gate_pair = jnp.take_along_axis(gate_probs, routes, axis=1) * keep_pair
        moe_out = gate_pair[:, 0:1] * picked_first + gate_pair[:, 1:2] * picked_second
        return after_attn + alive_f[:, None] * moe_out
    floats = [array.astype(jnp.float32) for array in (tokens, ln1_gain, ln1_bias, qkv_weight, qv_bias, out_weight, out_bias, ln2_gain, ln2_bias, router_weight, expert_in, expert_in_bias, expert_out, expert_out_bias)]
    block_value, pullback = jax.vjp(forward, *floats)
    grads = pullback(cotangent.astype(jnp.float32))
    return (block_value.astype(jnp.bfloat16), grads[0], grads[1], grads[2], grads[3], grads[4], grads[5], grads[6], grads[7], grads[8], grads[9], grads[10], grads[11], grads[12], grads[13])
```

```python
import functools

import jax
import jax.numpy as jnp
from jax import lax
from jax.experimental import pallas as pl
from jax.experimental.pallas import tpu as pltpu
from jax.sharding import PartitionSpec as P

HEADS = 12
SEQ = 197
EPS_NORM = 1e-06
NEG_FILL = -1e30
BF = jnp.bfloat16
F32 = jnp.float32
LANES = 128
GELU_A = 0.7978845608028654
GELU_B = 0.044715
BOTH = ("dp", "expert")


def up16(n):
    return -(-n // 16) * 16


def dot(left, right):
    return jnp.dot(left, right, preferred_element_type=F32)


def dot_t(left, right):
    return lax.dot_general(left, right, (((1,), (1,)), ((), ())), preferred_element_type=F32)


def t_dot(left, right):
    return lax.dot_general(left, right, (((0,), (0,)), ((), ())), preferred_element_type=F32)


def iota(shape, dim):
    return lax.broadcasted_iota(jnp.int32, shape, dim)


def params(mib=60):
    return pltpu.CompilerParams(vmem_limit_bytes=mib << 20)


def whole(shape):
    zeros = (0,) * len(shape)
    return pl.BlockSpec(shape, lambda *_: zeros, pipeline_mode=pl.Buffered(1))


SMALL = pl.CostEstimate(flops=1 << 20, bytes_accessed=1 << 16, transcendentals=0)
SMEM = pl.BlockSpec(memory_space=pltpu.SMEM)
ANY = pl.BlockSpec(memory_space=pl.ANY)


def norm_stats(values):
    centered = values - jnp.mean(values, axis=-1, keepdims=True)
    inverse = lax.rsqrt(jnp.mean(centered * centered, axis=-1, keepdims=True) + EPS_NORM)
    return centered * inverse, inverse


def norm_back(unit, inverse, gain, grad):
    scaled = grad * gain
    mean_one = jnp.mean(scaled, axis=-1, keepdims=True)
    mean_two = jnp.mean(scaled * unit, axis=-1, keepdims=True)
    return inverse * (scaled - mean_one - unit * mean_two)


def col_sum(values):
    return jnp.sum(values, axis=0, keepdims=True)


def pack_kernel(experts, core, qkv, out, router, vectors, mine, other):
    rows = qkv.shape[0]
    eye = (iota((rows, rows), 0) == iota((rows, rows), 1)).astype(BF)
    turned = dot_t(eye, vectors[...]).astype(BF)
    fill = jnp.zeros((rows, 2 * LANES - experts - turned.shape[1]), BF)
    value = jnp.concatenate([qkv[...], out[...], router[...], turned, fill], axis=1)
    half = value.shape[1] // 2

    @pl.when(core[0] == 0)
    def _():
        mine[...] = value[:, :half]
        other[...] = value[:, half:]

    @pl.when(core[0] != 0)
    def _():
        mine[...] = value[:, half:]
        other[...] = value[:, :half]


def pack_dense(core, qkv, out, router, vectors):
    rows = qkv.shape[0]
    half = (qkv.shape[1] + out.shape[1] + 2 * LANES) // 2
    vmem = pl.BlockSpec(memory_space=pltpu.VMEM)
    return pl.pallas_call(
        functools.partial(pack_kernel, router.shape[1]),
        in_specs=[SMEM] + [vmem] * 4,
        out_specs=[vmem] * 2,
        out_shape=[jax.ShapeDtypeStruct((rows, half), BF)] * 2,
        compiler_params=params(),
        cost_estimate=SMALL,
        name="pack_dense",
    )(core, qkv, out, router, vectors)


def forward_kernel(experts, subs, off, count, tok, *refs):
    n_pieces = len(refs) - 9
    pieces = refs[:n_pieces]
    w, small, qkv_o, n1_o, att_o, aa_o, n2_o, prob_o, sems = refs[n_pieces:]
    img = pl.program_id(0)
    width = tok.shape[-1]

    @pl.when(img == 0)
    def _():
        copies = []
        for i, piece in enumerate(pieces):
            rows, cols = piece.shape[0] // subs, piece.shape[1]
            col = pl.multiple_of(off[n_pieces * subs + i], LANES)
            for j in range(subs):
                row = pl.multiple_of(off[i * subs + j], 16)
                copies.append(
                    pltpu.make_async_copy(
                        piece.at[pl.ds(j * rows, rows), :],
                        w.at[pl.ds(row, rows), pl.ds(col, cols)],
                        sems.at[i * subs + j],
                    )
                )
        for c in copies:
            c.start()
        for c in copies:
            c.wait()
        small[...] = jnp.transpose(w[:, 4 * width : 4 * width + LANES].astype(F32))

    def vec(k):
        return small[experts + k : experts + k + 1, :]

    x = tok[0].astype(F32)
    rows = x.shape[0]
    unit, _ = norm_stats(x)
    n1 = (unit * vec(0) + vec(1)).astype(BF)
    n1_o[0] = n1
    biases = (vec(5), None, vec(6))
    for part in range(3):
        cols = slice(part * width, (part + 1) * width)
        block = dot(n1, w[:, cols])
        if biases[part] is not None:
            block = block + biases[part]
        qkv_o[0, :, cols] = block.astype(BF)
    low = iota((rows, LANES), 1) < LANES // 2
    seen = iota((rows, rows), 1) < SEQ
    scale = (width // HEADS) ** -0.5
    for pair in range(HEADS // 2):
        c = pair * LANES
        q2 = qkv_o[0, :, c : c + LANES]
        k2 = qkv_o[0, :, width + c : width + c + LANES]
        v2 = qkv_o[0, :, 2 * width + c : 2 * width + c + LANES]
        got = []
        for side, mask in enumerate((low, ~low)):
            scores = dot_t(jnp.where(mask, q2, jnp.zeros_like(q2)), k2) * scale
            scores = jnp.where(seen, scores, NEG_FILL)
            exps = jnp.exp(scores - jnp.max(scores, axis=-1, keepdims=True))
            prob = exps * (1.0 / jnp.sum(exps, axis=-1, keepdims=True))
            prob_o[0, 2 * pair + side] = prob
            got.append(dot(prob.astype(BF), v2))
        att_o[0, :, c : c + LANES] = jnp.where(low, got[0], got[1]).astype(BF)
    alive = (img < count[0]).astype(F32)
    after = x + alive * (dot(att_o[0], w[:, 3 * width : 4 * width]) + vec(2))
    aa_o[0] = after
    unit, _ = norm_stats(after)
    n2_o[0] = (unit * vec(3) + vec(4)).astype(BF)


def forward(off, subs, pieces, count, tok, experts, width_all):
    images, rows, width = tok.shape
    block = lambda cols: pl.BlockSpec((1, rows, cols), lambda i: (i, 0, 0))
    shape = lambda cols, t: jax.ShapeDtypeStruct((images, rows, cols), t)
    return pl.pallas_call(
        functools.partial(forward_kernel, experts, subs),
        grid=(images,),
        in_specs=[SMEM, SMEM, block(width)] + [ANY] * len(pieces),
        out_specs=[
            whole((width, width_all)),
            whole((LANES, width)),
            block(3 * width),
            block(width),
            block(width),
            block(width),
            block(width),
            pl.BlockSpec((1, HEADS, rows, rows), lambda i: (i, 0, 0, 0)),
        ],
        out_shape=[
            jax.ShapeDtypeStruct((width, width_all), BF),
            jax.ShapeDtypeStruct((LANES, width), F32),
            shape(3 * width, BF),
            shape(width, BF),
            shape(width, BF),
            shape(width, F32),
            shape(width, BF),
            jax.ShapeDtypeStruct((images, HEADS, rows, rows), F32),
        ],
        scratch_shapes=[pltpu.SemaphoreType.DMA((len(pieces) * subs,))],
        compiler_params=params(),
        cost_estimate=SMALL,
        name="tokens_forward",
    )(off, count, tok, *pieces)


def dispatch_kernel(experts, half, gated, slots, x, *refs):
    out = refs[-1]
    value = x[...]
    halves, block_rows = out.shape[1:3]
    first, second = slots[0:1, :], slots[1:2, :]
    if gated:
        router = refs[0][...].astype(BF)
        logits = dot_t(router, value)
        logits = jnp.where(iota(logits.shape, 0) < experts, logits, NEG_FILL)
        exps = jnp.exp(logits - jnp.max(logits, axis=0, keepdims=True))
        probs = exps / jnp.sum(exps, axis=0, keepdims=True)
    total = experts * block_rows
    for h in range(halves):
        place = iota((total, value.shape[0]), 0) + (half + h) * total
        hot = ((place == first) | (place == second)).astype(BF)
        out[:, h] = dot(hot, value).astype(BF).reshape(experts, block_rows, value.shape[1])
        if gated:
            row = iota((16, value.shape[0]), 0)
            for e in range(experts):
                gate = probs[e : e + 1, :]
                high = gate.astype(BF).astype(F32)
                pair = jnp.where(row == 14, high, jnp.where(row == 15, gate - high, 0.0))
                placed = dot_t(pair.astype(BF), hot[e * block_rows : (e + 1) * block_rows])
                tail = out[e, h, block_rows - 16 :, :block_rows].astype(F32)
                out[e, h, block_rows - 16 :, :block_rows] = jnp.where(
                    iota(tail.shape, 0) < 14, tail, placed
                ).astype(BF)


def dispatch(slots, x, small, experts, block_rows, half, halves, tag):
    rows, width = x.shape
    gated = small is not None
    more = [small] if gated else []
    vmem = pl.BlockSpec(memory_space=pltpu.VMEM)
    return pl.pallas_call(
        functools.partial(dispatch_kernel, experts, half, gated),
        in_specs=[vmem] * (2 + len(more)),
        out_specs=vmem,
        out_shape=jax.ShapeDtypeStruct((experts, halves, block_rows, width), BF),
        compiler_params=params(),
        cost_estimate=SMALL,
        name="dispatch_" + tag,
    )(slots, x, *more)


def expert_kernel(parts, n_before, *refs):
    x_ref, c_ref, b_in, b_out = refs[:4]
    pieces_in, pieces_out = refs[4 : 4 + parts], refs[4 + parts : 4 + 2 * parts]
    rest = refs[4 + 2 * parts + n_before :]
    act_o, pre_o, x_o, sg_o, r_o, d_o, db_in, db_out, win, wout, sems = rest
    step = pl.program_id(0)
    n, _, size, width = x_ref.shape
    piece = pieces_in[0].shape[1]

    def copies(q):
        cols = pl.ds(q * piece, piece)
        return (
            pltpu.make_async_copy(pieces_in[q], win.at[:, cols], sems.at[q]),
            pltpu.make_async_copy(pieces_out[q], wout.at[cols, :], sems.at[parts + q]),
        )

    @pl.when(step == 0)
    def _():
        for q in range(parts):
            for c in copies(q):
                c.start()
        db_in[...] = jnp.zeros_like(db_in)
        db_out[...] = jnp.zeros_like(db_out)

    eye = (iota((size, size), 0) == iota((size, size), 1)).astype(BF)
    for s in range(n):
        rows = slice(s * size, (s + 1) * size)
        x_o[rows, :] = x_ref[s, 0]
        turned = dot_t(eye, x_ref[s, 0, size - 16 :, :size])
        gate = jnp.sum(jnp.where(iota(turned.shape, 1) >= 14, turned, 0.0), axis=1, keepdims=True)
        sg_o[rows, :] = (gate * c_ref[s, 0].astype(F32)).astype(BF)
    x = x_o[...]
    slot_grad = sg_o[...]
    db_out[0:1, :] += col_sum(slot_grad.astype(F32))

    @pl.when(step == 0)
    def _():
        for q in range(parts):
            for c in copies(q):
                c.wait()

    for q in range(parts):
        cols = slice(q * piece, (q + 1) * piece)
        pre = dot(x, win[:, cols]) + b_in[q, 0:1, :]
        square = pre * pre
        turn = jnp.tanh(pre * (GELU_A + GELU_A * GELU_B * square))
        half_turn = 0.5 * turn + 0.5
        act_o[:, cols] = (pre * half_turn).astype(BF)
        slope = half_turn + (0.5 * pre) * (1.0 - turn * turn) * (GELU_A + 3 * GELU_A * GELU_B * square)
        pre_grad = dot_t(slot_grad, wout[cols, :]) * slope
        pre_o[:, cols] = pre_grad.astype(BF)
        db_in[q, 0:1, :] += col_sum(pre_grad)
    out = (dot(act_o[...], wout[...]) + b_out[0:1, :]).astype(BF)
    back = dot_t(pre_o[...], win[...])
    ones = jnp.ones((16, width), BF)
    for s in range(n):
        rows = slice(s * size, (s + 1) * size)
        r_o[s, 0] = out[rows]
        d_o[s] = back[rows].astype(BF)
        prod = c_ref[s, 0].astype(F32) * out[rows].astype(F32)
        high = prod.astype(BF)
        low = (prod - high.astype(F32)).astype(BF)
        gate_grad = dot_t(ones, high) + dot_t(ones, low)
        grad_high = gate_grad.astype(BF).astype(F32)
        row = iota(gate_grad.shape, 0)
        tail = back[(s + 1) * size - 16 : (s + 1) * size, :size]
        both = jnp.where(row == 14, grad_high, gate_grad - grad_high)
        d_o[s, size - 16 :, :size] = jnp.where(row < 14, tail, both).astype(BF)


def expert_call(x, c, w_in, w_out, b_in, b_out, half, halves, before):
    experts, _, size, width = x.shape
    parts, piece = len(w_in), w_in[0].shape[1]
    n = max(1, 256 // size)
    steps = experts // n
    rows, hidden = n * size, parts * piece
    before = list(before)
    tall = lambda cols: pl.BlockSpec((rows, cols), lambda i: (half * steps + i, 0))
    of_half = pl.BlockSpec((n, 1, size, width), lambda i: (i, half, 0, 0))
    total = halves * experts * size
    return pl.pallas_call(
        functools.partial(expert_kernel, parts, len(before)),
        grid=(steps,),
        in_specs=[
            pl.BlockSpec((n, 1, size, width), lambda i: (i, 0, 0, 0)),
            of_half,
            whole((parts, 8, piece)),
            whole((8, width)),
        ]
        + [ANY] * (2 * parts + len(before)),
        out_specs=[
            tall(hidden),
            tall(hidden),
            tall(width),
            tall(width),
            of_half,
            pl.BlockSpec((n, size, width), lambda i: (i, 0, 0)),
            whole((parts, 8, piece)),
            whole((8, width)),
        ],
        out_shape=[
            jax.ShapeDtypeStruct((total, hidden), BF),
            jax.ShapeDtypeStruct((total, hidden), BF),
            jax.ShapeDtypeStruct((total, width), BF),
            jax.ShapeDtypeStruct((total, width), BF),
            jax.ShapeDtypeStruct((experts, halves, size, width), BF),
            jax.ShapeDtypeStruct((experts, size, width), BF),
            jax.ShapeDtypeStruct((parts, 8, piece), F32),
            jax.ShapeDtypeStruct((8, width), F32),
        ],
        scratch_shapes=[
            pltpu.VMEM((width, hidden), BF),
            pltpu.VMEM((hidden, width), BF),
            pltpu.SemaphoreType.DMA((2 * parts,)),
        ],
        input_output_aliases={4 + 2 * parts + i: i for i in range(len(before))},
        compiler_params=params(),
        cost_estimate=SMALL,
        name="expert_" + "ab"[half],
    )(x, c, b_in, b_out, *w_in, *w_out, *before)


def backward_kernel(experts, n, split, off, count, slots, cot, n1, qkv, att, aa, n2, probs_in, w, small, *refs):
    backs = refs[:n]
    ag_o, gp_o, dq_o = refs[n : n + 3]
    grads = refs[n + 3 : n + 3 + split]
    dw, ds, marks = refs[n + 3 + split :]
    img = pl.program_id(0)
    width = n1.shape[-1]
    size = backs[0].shape[1]
    total = experts * size

    @pl.when(img == 0)
    def _():
        dw[...] = jnp.zeros_like(dw)
        ds[...] = jnp.zeros_like(ds)
        line = iota((LANES, size), 0)
        for h in range(n):
            for e in range(experts):
                ends = backs[h][e, size - 16 :, :size].astype(F32)
                for k in range(2):
                    marks[2 * h + k, :, e * size : (e + 1) * size] = jnp.where(
                        line == e, ends[14 + k : 15 + k, :], 0.0
                    ).astype(BF)

    def vec(k):
        return small[experts + k : experts + k + 1, :]

    def add_vec(k, value):
        ds[experts + k : experts + k + 1, :] += value

    alive = (img < count[0]).astype(F32)
    up = cot[0].astype(F32)
    rows = up.shape[0]
    normed = n2[0]
    lane = iota((rows, LANES), 1)
    router = jnp.where(iota(small.shape, 0) < experts, small[...], 0.0).astype(BF)
    logits = jnp.where(lane < experts, dot_t(normed, router), NEG_FILL)
    exps = jnp.exp(logits - jnp.max(logits, axis=-1, keepdims=True))
    probs = exps / jnp.sum(exps, axis=-1, keepdims=True)
    gp_o[0] = probs
    first, second = slots[0, :, 0:1], slots[0, :, 1:2]
    normed_grad = jnp.zeros((rows, width), F32)
    placed = jnp.zeros((rows, LANES), F32)
    for h in range(n):
        place = iota((rows, total), 1) + h * total
        hot = ((place == first) | (place == second)).astype(BF)
        normed_grad = normed_grad + dot(hot, backs[h][...].reshape(total, width))
        placed = placed + dot_t(hot, marks[2 * h]) + dot_t(hot, marks[2 * h + 1])
    logit_grad = (
        probs * (placed - jnp.sum(probs * placed, axis=-1, keepdims=True))
    ).astype(BF)
    normed_grad = normed_grad + dot(logit_grad, router)
    ds[...] += jnp.where(iota(ds.shape, 0) < experts, t_dot(logit_grad, normed), 0.0)
    unit, inverse = norm_stats(aa[0])
    add_vec(3, col_sum(normed_grad * unit))
    add_vec(4, col_sum(normed_grad))
    after_grad = up + norm_back(unit, inverse, vec(3), normed_grad)
    attn_grad = (alive * after_grad).astype(BF)
    add_vec(2, col_sum(attn_grad.astype(F32)))
    dw[:, 3 * width : 4 * width] += t_dot(att[0], attn_grad)
    att_grad = dot_t(attn_grad, w[:, 3 * width : 4 * width]).astype(BF)
    low = lane < LANES // 2
    scale = (width // HEADS) ** -0.5
    for pair in range(HEADS // 2):
        c = pair * LANES
        q2 = qkv[0, :, c : c + LANES]
        k2 = qkv[0, :, width + c : width + c + LANES]
        v2 = qkv[0, :, 2 * width + c : 2 * width + c + LANES]
        o2 = att_grad[:, c : c + LANES]
        got = []
        for side, mask in enumerate((low, ~low)):
            prob = probs_in[0, 2 * pair + side]
            prob_grad = dot_t(jnp.where(mask, o2, jnp.zeros_like(o2)), v2)
            inner = jnp.sum(prob * prob_grad, axis=-1, keepdims=True)
            score_grad = (prob * (prob_grad - inner)).astype(BF)
            got.append(
                (
                    dot(score_grad, k2) * scale,
                    t_dot(score_grad, q2) * scale,
                    t_dot(prob.astype(BF), o2),
                )
            )
        for k in range(3):
            dq_o[0, :, k * width + c : k * width + c + LANES] = jnp.where(
                low, got[0][k], got[1][k]
            ).astype(BF)
    grad = dq_o[0]
    dw[:, : 3 * width] += t_dot(n1[0], grad)
    for k in range(3):
        ds[experts + 5 + k : experts + 6 + k, :] += col_sum(grad[:, k * width : (k + 1) * width].astype(F32))
    ag_o[0] = after_grad

    @pl.when(img == pl.num_programs(0) - 1)
    def _():
        dw[:, 4 * width : 4 * width + LANES] = jnp.transpose(ds[...])
        with_weight = jnp.zeros((width, LANES), F32)
        with_sums = jnp.zeros((width, LANES), F32)
        for k in range(3 * width // LANES):
            cols = slice(k * LANES, (k + 1) * LANES)
            part, at = divmod(k * LANES, width)
            value = w[:, cols].astype(F32)
            sums = ds[experts + 5 + part : experts + 6 + part, at : at + LANES]
            with_weight = with_weight + value * dw[:, cols]
            with_sums = with_sums + value * sums
        sums = jnp.sum(with_sums, axis=1, keepdims=True)
        at = 4 * width
        sides = w[:, at : at + LANES].astype(F32)
        gain, shift = sides[:, experts : experts + 1], sides[:, experts + 1 : experts + 2]
        gains = (jnp.sum(with_weight, axis=1, keepdims=True) - shift * sums) / gain
        spot = iota((width, LANES), 1)
        cols = slice(at, at + LANES)
        dw[:, cols] = jnp.where(
            spot == experts, gains, jnp.where(spot == experts + 1, sums, dw[:, cols])
        )
        if split == 1:
            grads[0][...] = dw[...].astype(BF)
        else:
            cols = grads[0].shape[1]
            step = width // 16
            for h in range(2):
                col = pl.multiple_of(off[16 + h], LANES)
                for r in range(16):
                    row = pl.multiple_of(off[r], 16)
                    grads[h][r * step : (r + 1) * step, :] = dw[
                        pl.ds(row, step), pl.ds(col, cols)
                    ].astype(BF)


def backward(off, count, slots, cot, n1, qkv, att, aa, n2, prob, w, small, backs, experts, split):
    images, rows, width = cot.shape
    width_all = w.shape[1]
    n = len(backs)
    block = lambda cols: pl.BlockSpec((1, rows, cols), lambda i: (i, 0, 0))
    got = pl.pallas_call(
        functools.partial(backward_kernel, experts, n, split),
        grid=(images,),
        in_specs=[SMEM, SMEM, block(2), block(width), block(width), block(3 * width), block(width), block(width), block(width)]
        + [pl.BlockSpec((1, HEADS, rows, rows), lambda i: (i, 0, 0, 0))]
        + [whole(w.shape), whole(small.shape)]
        + [whole(backs[0].shape)] * n,
        out_specs=[block(width), block(LANES), block(3 * width)] + [whole((width, width_all // split))] * split,
        out_shape=[
            jax.ShapeDtypeStruct((images, rows, width), F32),
            jax.ShapeDtypeStruct((images, rows, LANES), F32),
            jax.ShapeDtypeStruct((images, rows, 3 * width), BF),
        ]
        + [jax.ShapeDtypeStruct((width, width_all // split), BF)] * split,
        scratch_shapes=[
            pltpu.VMEM((width, width_all), F32),
            pltpu.VMEM((LANES, width), F32),
            pltpu.VMEM((2 * n, LANES, backs[0].shape[0] * backs[0].shape[1]), BF),
        ],
        compiler_params=params(),
        cost_estimate=SMALL,
        name="tokens_backward",
    )(off, count, slots, cot, n1, qkv, att, aa, n2, prob, w, small, *backs)
    return got[0], got[1], got[2], got[3:]


def finish_kernel(experts, after_grad, grad, tok, w, small, out):
    width = tok.shape[-1]
    normed_grad = dot_t(grad[0], w[...])
    unit, inverse = norm_stats(tok[0].astype(F32))
    out[0] = after_grad[0] + norm_back(unit, inverse, small[experts : experts + 1, :], normed_grad)


def finish(after_grad, grad, tok, w, small, experts):
    images, rows, width = tok.shape
    block = lambda cols: pl.BlockSpec((1, rows, cols), lambda i: (i, 0, 0))
    return pl.pallas_call(
        functools.partial(finish_kernel, experts),
        grid=(images,),
        in_specs=[block(width), block(3 * width), block(width), whole((width, 3 * width)), whole(small.shape)],
        out_specs=block(width),
        out_shape=jax.ShapeDtypeStruct((images, rows, width), F32),
        compiler_params=params(),
        cost_estimate=SMALL,
        name="tokens_finish",
    )(after_grad, grad, tok, w, small)


def output_kernel(count, slots, aa, probs, outs, out):
    rows = aa.shape[1]
    experts, n, size, width = outs.shape
    total = experts * size
    alive = (pl.program_id(0) < count[0]).astype(F32)
    first, second = slots[0, :, 0:1], slots[0, :, 1:2]
    gates = jnp.concatenate(
        [jnp.broadcast_to(probs[0, :, e : e + 1], (rows, size)) for e in range(experts)], axis=1
    )
    moe = jnp.zeros(aa.shape[1:], F32)
    for h in range(n):
        place = iota((rows, total), 1) + h * total
        gate = jnp.where((place == first) | (place == second), gates, 0.0)
        high = gate.astype(BF)
        low = (gate - high.astype(F32)).astype(BF)
        value = outs[:, h].reshape(total, width)
        moe = moe + dot(high, value) + dot(low, value)
    out[0] = (aa[0] + alive * moe).astype(BF)


def block_output(count, slots, aa, probs, outs):
    images, rows, width = aa.shape
    block = lambda cols: pl.BlockSpec((1, rows, cols), lambda i: (i, 0, 0))
    return pl.pallas_call(
        output_kernel,
        grid=(images,),
        in_specs=[SMEM, block(2), block(width), block(LANES), whole(outs.shape)],
        out_specs=block(width),
        out_shape=jax.ShapeDtypeStruct((images, rows, width), BF),
        compiler_params=params(),
        cost_estimate=SMALL,
        name="block_output",
    )(count, slots, aa, probs, outs)


def slot_tables(routes, alive, capacity, half_cap, block_rows):
    expert_ids = jnp.arange(capacity.shape[0], dtype=jnp.int32)
    count = routes.shape[0]
    hit_one = ((routes[:, 0:1] == expert_ids) & alive[:, None]).astype(F32)
    hit_two = ((routes[:, 1:2] == expert_ids) & alive[:, None]).astype(F32)
    earlier = (iota((count, count), 1) < iota((count, count), 0)).astype(BF)
    ahead = dot(earlier, jnp.concatenate([hit_one, hit_two], axis=1).astype(BF))
    ahead_one = ahead[:, : capacity.shape[0]]
    ahead_two = ahead[:, capacity.shape[0] :] + jnp.sum(hit_one, axis=0, keepdims=True)
    limits = capacity.astype(F32)[None, :]
    slots = []
    for hit, before, choice in ((hit_one, ahead_one, 0), (hit_two, ahead_two, 1)):
        place = jnp.sum(hit * before, axis=1)
        keep = place < jnp.sum(hit * limits, axis=1)
        place = place.astype(jnp.int32)
        half = (place >= half_cap).astype(jnp.int32)
        spot = (half * capacity.shape[0] + routes[:, choice]) * block_rows + place - half * half_cap
        slots.append(jnp.where(keep, spot, -1))
    return jnp.stack(slots, axis=1), jnp.stack(slots, axis=0)


def local(sizes, *args):
    (tokens, image_count, routes, capacity, ln1_gain, ln1_bias, qkv_weight, qv_bias, out_weight, out_bias,
     ln2_gain, ln2_bias, router_weight, expert_in, expert_in_bias, expert_out, expert_out_bias, cotangent) = args
    dp, experts = sizes
    grouped = sizes == (4, 8)
    devices = dp * experts
    me_d = lax.axis_index("dp")
    me_e = lax.axis_index("expert")
    core = me_e % 2
    token_count, width = tokens.shape
    images = token_count // SEQ
    rows = up16(SEQ)
    cap = max(2, 5 * token_count // (2 * experts))
    halves = 2 if grouped else 1
    half_cap = -(-cap // halves)
    block_rows = up16(half_cap + 2)

    def hop(value, mask):
        return lax.ppermute(value, BOTH, [(i, i ^ mask) for i in range(devices)])

    def by_image(value):
        value = value.reshape(images, SEQ, value.shape[-1])
        fill = -1 if value.dtype == jnp.int32 else 0
        return jnp.pad(value, ((0, 0), (0, rows - SEQ), (0, 0)), constant_values=fill)

    def from_image(value):
        return value[:, :SEQ].reshape(token_count, value.shape[-1])

    def after(values, *done):
        return lax.optimization_barrier((values, done))[0]

    tok = by_image(tokens)

    vectors = [ln1_gain, ln1_bias, out_bias, ln2_gain, ln2_bias, qv_bias.reshape(-1)]
    vectors = jnp.concatenate(vectors).reshape(7, -1)
    width_all = 4 * width + 2 * LANES
    wide = expert_in.shape[2]
    spot = me_d * expert_out_bias.shape[1]
    if grouped:
        half = width_all // 2
        mine, other = pack_dense(
            core.reshape(1).astype(jnp.int32), qkv_weight, out_weight, router_weight, vectors
        )
        got = hop(other, 1)
        chip = jnp.where(
            core == 0, jnp.concatenate([mine, got], axis=0), jnp.concatenate([got, mine], axis=0)
        )
        in_x, out_y = hop(expert_in[0], 8), hop(expert_out[0], 16)
        line = jnp.concatenate([chip] + [hop(chip, 2 * dz) for dz in (1, 2, 3)], axis=0)
        held, in_x, out_y, tok = after((line, in_x, out_y, tok))
        own = [line] + [hop(held, 8 * dxy) for dxy in (3, 1, 2)]
        own = [own[0], own[2], own[3], own[1]]
        pieces = own + [hop(piece, 1) for piece in own]
        step = width // 16
        at_rows = jnp.stack([((me_d ^ a) * 4 + ((me_e // 2) ^ b)) * step for a in range(4) for b in range(4)])
        at_cols = jnp.stack([core * half, (1 - core) * half])
        off_back = jnp.concatenate([at_rows, at_cols]).astype(jnp.int32)
        off = jnp.concatenate([at_rows, at_rows, jnp.repeat(at_cols, 4)]).astype(jnp.int32)
        subs = 4
        bias_out = lax.dynamic_update_slice(jnp.zeros((1, width), BF), expert_out_bias, (0, spot))
        bias = jnp.concatenate([expert_in_bias, bias_out, jnp.zeros((6, wide), BF)], axis=0)
        own_in, own_out, relay_in, relay_out, bias = after(
            (expert_in[0], expert_out[0], in_x, out_y, bias), *own
        )
        near = [hop(own_in, 16), hop(own_out, 8)]
        far = [hop(relay_in, 16), hop(relay_out, 8)]
        w_in = [expert_in[0], in_x, near[0], far[0]]
        w_out = [expert_out[0], near[1], out_y, far[1]]
        bias_got = [hop(bias, 8 * q) for q in (1, 2, 3)]
        b_in = jnp.stack([bias] + bias_got).astype(F32)
        far += bias_got
        b_out = jnp.broadcast_to(jnp.sum(b_in[:, 1], axis=0), (8, width))
        after_line = held
    else:
        fill = width_all - 4 * width - experts - 7
        pack = jnp.concatenate(
            [qkv_weight, out_weight, router_weight, vectors.T, jnp.zeros((vectors.shape[1], fill), BF)], axis=1
        )
        pieces = [lax.all_gather(pack, BOTH, axis=0, tiled=True)]
        off = jnp.zeros((2,), jnp.int32)
        off_back = off
        subs = 1
        after_line, near, far = pieces[0], [], []
        w_in = lax.all_gather(expert_in[0], "dp", axis=0, tiled=False)
        w_out = lax.all_gather(expert_out[0], "dp", axis=0, tiled=False)
        w_in, w_out = [w_in[q] for q in range(dp)], [w_out[q] for q in range(dp)]
        b_in = lax.all_gather(jnp.broadcast_to(expert_in_bias, (8, wide)), "dp", axis=0, tiled=False).astype(F32)
        b_out = jnp.broadcast_to(
            lax.all_gather(expert_out_bias, "dp", axis=1, tiled=True).astype(F32), (8, width)
        )

    alive = (jnp.arange(images * rows, dtype=jnp.int32) // rows) < image_count[0]
    slots_col, slots_row = slot_tables(
        by_image(routes).reshape(-1, 2), alive, capacity, half_cap, block_rows
    )
    slots_col = slots_col.reshape(images, rows, 2)

    def exchange(blocks):
        return lax.all_to_all(blocks, "expert", 0, 0, tiled=True)

    cot = by_image(cotangent)
    cot_blocks = dispatch(slots_row, cot.reshape(-1, width), None, experts, block_rows, 0, halves, "plain")
    cot_sent = exchange(after(cot_blocks, after_line))

    w, small, qkv, n1, att, aa, n2, prob = forward(off, subs, pieces, image_count, tok, experts, width_all)
    row_sent = []
    flat = after(n2.reshape(-1, width), *near)
    for h in range(halves):
        sent = dispatch(slots_row, flat, small, experts, block_rows, h, 1, "ab"[h])
        waits = (*row_sent, *far) if h else ()
        sent, cot_sent = after((sent, cot_sent), *waits)
        row_sent.append(exchange(sent))

    back, db_ins, db_outs, tall = [], [], [], ()
    for h in range(halves):
        *tall, d, db_in, db_out = expert_call(
            row_sent[h], cot_sent, w_in, w_out, b_in, b_out, h, halves, tall
        )
        back.append(exchange(after(d, *back)))
        db_ins.append(db_in)
        db_outs.append(db_out)
    *tall, outs_back = tall
    act, pre, rows_in, slot_grad = after(tall, *back[:-1])
    db_in, db_out = sum(db_ins), sum(db_outs)

    def grad_in(q):
        return t_dot(rows_in, pre[:, q * wide : (q + 1) * wide])

    def grad_out(q):
        return t_dot(act[:, q * wide : (q + 1) * wide], slot_grad)

    if grouped:
        far_in, far_out = hop(grad_in(3).astype(BF), 8), hop(grad_out(3).astype(BF), 16)
        near_in, near_out = grad_in(1).astype(BF), grad_out(2).astype(BF)
        own_in, own_out = grad_in(0), grad_out(0)
        last_in = (grad_in(2) + far_in.astype(F32)).astype(BF)
        last_out = (grad_out(1) + far_out.astype(F32)).astype(BF)
        ready = (near_in, near_out, own_in, own_out, last_in, last_out)
        near_in, near_out = hop(near_in, 8), hop(near_out, 16)
        last_in, last_out = hop(last_in, 16), hop(last_out, 8)
        arrived = (near_in, near_out, last_in, last_out)
        g_in = (own_in + near_in.astype(F32) + last_in.astype(F32))[None]
        g_out = (own_out + near_out.astype(F32) + last_out.astype(F32))[None]
        g_bias = [
            jnp.concatenate([db_in[q, 0:1], db_out[0:1], jnp.zeros((6, wide), F32)], axis=0).astype(BF)
            for q in range(4)
        ]
        g_bias = sum([hop(g_bias[q], 8 * q).astype(F32) for q in (1, 2, 3)], g_bias[0].astype(F32))
        g_b_in = g_bias[0:1]
        g_b_out = lax.dynamic_slice(g_bias[1:2], (0, spot), expert_out_bias.shape)
    else:
        ready = arrived = ()
        every = range(dp)
        scatter = lambda v: lax.psum_scatter(v, "dp", scatter_dimension=0, tiled=True).astype(F32)
        g_in = scatter(jnp.stack([grad_in(q).astype(BF) for q in every]))
        g_out = scatter(jnp.stack([grad_out(q).astype(BF) for q in every]))
        g_b_in = lax.psum_scatter(
            db_in[:, 0].reshape(1, -1).astype(BF), "dp", scatter_dimension=1, tiled=True
        ).astype(F32)
        g_b_out = lax.psum_scatter(db_out[0:1].astype(BF), "dp", scatter_dimension=1, tiled=True).astype(F32)

    r_sent = exchange(after(outs_back, *back))
    back = after(back, *ready)
    after_grad, probs, grad, grads = backward(
        off_back, image_count, slots_col, cot, n1, qkv, att, aa, n2, prob, w, small, back, experts,
        2 if grouped else 1,
    )
    grads = after(grads, *arrived)
    block_out = from_image(block_output(image_count, slots_col, aa, probs, r_sent))
    tokens_grad = from_image(finish(after_grad, grad, tok, w, small, experts))

    def add(*values):
        return functools.reduce(lambda a, b: a + b, [v.astype(F32) for v in values])

    if grouped:
        chips = add(grads[0], hop(grads[1], 1)).astype(BF)
        quarter = width // 4
        ways = [chips[a * quarter : (a + 1) * quarter] for a in range(4)]
        line = add(ways[0], *[hop(ways[a], 8 * a) for a in (1, 2, 3)]).astype(BF)
        line, tokens_grad, r_sent, g_in, g_out = after((line, tokens_grad, r_sent, g_in, g_out))
        step = width // 16
        cuts = [line[b * step : (b + 1) * step] for b in range(4)]
        chip = add(cuts[0], *[hop(cuts[b], 2 * b) for b in (1, 2, 3)])
        n_rows = step // 2
        keep = lax.dynamic_slice_in_dim(chip, core * n_rows, n_rows, 0)
        chip, block_out = after((chip, block_out))
        give = lax.dynamic_slice_in_dim(chip, (1 - core) * n_rows, n_rows, 0)
        got = hop(give.astype(BF), 1).astype(F32)
        dense = jnp.where(
            core == 0, jnp.concatenate([keep, got], axis=1), jnp.concatenate([got, keep], axis=1)
        )
    else:
        dense = lax.psum_scatter(grads[0], BOTH, scatter_dimension=0, tiled=True).astype(F32)
    side = dense[:, 4 * width :]
    vecs = [side[:, experts + k] for k in range(8)]
    return (
        block_out,
        tokens_grad,
        vecs[0],
        vecs[1],
        dense[:, : 3 * width],
        jnp.stack([vecs[5], vecs[7]], axis=0),
        dense[:, 3 * width : 4 * width],
        vecs[2],
        vecs[3],
        vecs[4],
        side[:, :experts],
        g_in,
        g_b_in,
        g_out,
        g_b_out,
    )


def solution(mesh):
    rows, line, cols = P(BOTH, None), P(BOTH), P(None, BOTH)
    experts = (P("expert", None, "dp"), P("expert", "dp"), P("expert", "dp", None), P("expert", "dp"))
    dense = (line, line, rows, cols, rows, line, line, line, rows)
    return jax.shard_map(
        functools.partial(local, (mesh.shape["dp"], mesh.shape["expert"])),
        mesh=mesh,
        in_specs=(rows, line, rows, P(), *dense, *experts, rows),
        out_specs=(rows, rows, *dense, *experts),
        check_vma=False,
    )
```

```python
import functools

import jax
import jax.numpy as jnp
from jax import lax
from jax.experimental import pallas as pl
from jax.experimental.pallas import tpu as pltpu
from jax.sharding import PartitionSpec as P

HEADS = 12
SEQ = 197
EPS_NORM = 1e-06
NEG_FILL = -1e30
BF = jnp.bfloat16
F32 = jnp.float32
LANES = 128
GELU_A = 0.7978845608028654
GELU_B = 0.044715
BOTH = ("dp", "expert")


def up16(n):
    return -(-n // 16) * 16


def dot(left, right):
    return jnp.dot(left, right, preferred_element_type=F32)


def dot_t(left, right):
    return lax.dot_general(left, right, (((1,), (1,)), ((), ())), preferred_element_type=F32)


def t_dot(left, right):
    return lax.dot_general(left, right, (((0,), (0,)), ((), ())), preferred_element_type=F32)


def iota(shape, dim):
    return lax.broadcasted_iota(jnp.int32, shape, dim)


def params(mib=60):
    return pltpu.CompilerParams(vmem_limit_bytes=mib << 20)


def whole(shape):
    zeros = (0,) * len(shape)
    return pl.BlockSpec(shape, lambda *_: zeros, pipeline_mode=pl.Buffered(1))


SMALL = pl.CostEstimate(flops=1 << 20, bytes_accessed=1 << 16, transcendentals=0)
LARGE = pl.CostEstimate(flops=1 << 34, bytes_accessed=1 << 16, transcendentals=0)
SMEM = pl.BlockSpec(memory_space=pltpu.SMEM)
ANY = pl.BlockSpec(memory_space=pl.ANY)


def norm_stats(values):
    centered = values - jnp.mean(values, axis=-1, keepdims=True)
    inverse = lax.rsqrt(jnp.mean(centered * centered, axis=-1, keepdims=True) + EPS_NORM)
    return centered * inverse, inverse


def norm_back(unit, inverse, gain, grad):
    scaled = grad * gain
    mean_one = jnp.mean(scaled, axis=-1, keepdims=True)
    mean_two = jnp.mean(scaled * unit, axis=-1, keepdims=True)
    return inverse * (scaled - mean_one - unit * mean_two)


def col_sum(values):
    return jnp.sum(values, axis=0, keepdims=True)


def pack_kernel(core, qkv, out, router, vectors, pair, mine, other):
    rows = qkv.shape[0]
    eye = (iota((rows, rows), 0) == iota((rows, rows), 1)).astype(BF)
    turned = [dot_t(eye, router[...]), dot_t(eye, vectors[...].astype(BF))[:, :5], dot_t(eye, pair[...])]
    used = sum(t.shape[1] for t in turned)
    turned = jnp.concatenate([*turned, jnp.zeros((rows, 2 * LANES - used), F32)], axis=1)
    value = jnp.concatenate([qkv[...], out[...], turned.astype(BF)], axis=1)
    half = value.shape[1] // 2

    @pl.when(core[0] == 0)
    def _():
        mine[...] = value[:, :half]
        other[...] = value[:, half:]

    @pl.when(core[0] != 0)
    def _():
        mine[...] = value[:, half:]
        other[...] = value[:, :half]


def pack_dense(core, qkv, out, router, vectors, pair):
    rows = qkv.shape[0]
    half = (qkv.shape[1] + out.shape[1] + 2 * LANES) // 2
    vmem = pl.BlockSpec(memory_space=pltpu.VMEM)
    return pl.pallas_call(
        pack_kernel,
        in_specs=[SMEM] + [vmem] * 5,
        out_specs=[vmem] * 2,
        out_shape=[jax.ShapeDtypeStruct((rows, half), BF)] * 2,
        compiler_params=params(60),
        cost_estimate=LARGE,
        name="pack_dense",
    )(core, qkv, out, router, vectors, pair)


def forward_kernel(experts, subs, off, count, tok, *refs):
    n_pieces = len(refs) - 10
    pieces = refs[:n_pieces]
    w_o, small, qkv_o, n1_o, att_o, aa_o, n2_o, prob_o, w, sems = refs[n_pieces:]
    img = pl.program_id(0)
    width = tok.shape[-1]

    @pl.when(img == 0)
    def _():
        copies = []
        for i, piece in enumerate(pieces):
            rows, cols = piece.shape[0] // subs, piece.shape[1]
            col = pl.multiple_of(off[n_pieces * subs + i], LANES)
            for j in range(subs):
                row = pl.multiple_of(off[i * subs + j], 16)
                copies.append(
                    pltpu.make_async_copy(
                        piece.at[pl.ds(j * rows, rows), :],
                        w.at[pl.ds(row, rows), pl.ds(col, cols)],
                        sems.at[i * subs + j],
                    )
                )
        for c in copies:
            c.start()
        for c in copies:
            c.wait()
        small[...] = jnp.transpose(w[:, 4 * width : 4 * width + LANES].astype(F32))
        pltpu.make_async_copy(w, w_o, sems.at[0]).start()

    def vec(k):
        return small[experts + k : experts + k + 1, :]

    x = tok[0].astype(F32)
    rows = x.shape[0]
    unit, _ = norm_stats(x)
    n1 = (unit * vec(0) + vec(1)).astype(BF)
    n1_o[0] = n1
    biases = (vec(5), None, vec(6))
    for part in range(3):
        cols = slice(part * width, (part + 1) * width)
        block = dot(n1, w[:, cols])
        if biases[part] is not None:
            block = block + biases[part]
        qkv_o[0, :, cols] = block.astype(BF)
    low = iota((rows, LANES), 1) < LANES // 2
    seen = iota((rows, rows), 0) < SEQ
    scale = (width // HEADS) ** -0.5
    for pair in range(HEADS // 2):
        c = pair * LANES
        q2 = qkv_o[0, :, c : c + LANES]
        k2 = qkv_o[0, :, width + c : width + c + LANES]
        v2 = qkv_o[0, :, 2 * width + c : 2 * width + c + LANES]
        got = []
        for side, mask in enumerate((low, ~low)):
            scores = dot_t(k2, jnp.where(mask, q2, jnp.zeros_like(q2))) * scale
            scores = jnp.where(seen, scores, NEG_FILL)
            exps = jnp.exp(scores - jnp.max(scores, axis=0, keepdims=True))
            prob = exps * (1.0 / col_sum(exps))
            prob_o[0, 2 * pair + side] = prob
            got.append(t_dot(prob.astype(BF), v2))
        att_o[0, :, c : c + LANES] = jnp.where(low, got[0], got[1]).astype(BF)
    alive = (img < count[0]).astype(F32)
    after = x + alive * (dot(att_o[0], w[:, 3 * width : 4 * width]) + vec(2))
    aa_o[0] = after
    unit, _ = norm_stats(after)
    n2_o[0] = (unit * vec(3) + vec(4)).astype(BF)

    @pl.when(img == pl.num_programs(0) - 1)
    def _():
        pltpu.make_async_copy(w, w_o, sems.at[0]).wait()


def forward(off, subs, pieces, count, tok, experts, width_all):
    images, rows, width = tok.shape
    block = lambda cols: pl.BlockSpec((1, rows, cols), lambda i: (i, 0, 0))
    shape = lambda cols, t: jax.ShapeDtypeStruct((images, rows, cols), t)
    return pl.pallas_call(
        functools.partial(forward_kernel, experts, subs),
        grid=(images,),
        in_specs=[SMEM, SMEM, block(width)] + [ANY] * len(pieces),
        out_specs=[
            ANY,
            whole((LANES, width)),
            block(3 * width),
            block(width),
            block(width),
            block(width),
            block(width),
            pl.BlockSpec((1, HEADS, rows, rows), lambda i: (i, 0, 0, 0)),
        ],
        out_shape=[
            jax.ShapeDtypeStruct((width, width_all), BF),
            jax.ShapeDtypeStruct((LANES, width), F32),
            shape(3 * width, BF),
            shape(width, BF),
            shape(width, BF),
            shape(width, F32),
            shape(width, BF),
            jax.ShapeDtypeStruct((images, HEADS, rows, rows), F32),
        ],
        scratch_shapes=[
            pltpu.VMEM((width, width_all), BF),
            pltpu.SemaphoreType.DMA((len(pieces) * subs,)),
        ],
        compiler_params=params(60),
        cost_estimate=SMALL,
        name="tokens_forward",
    )(off, count, tok, *pieces)


def dispatch_kernel(experts, half, gated, slots, x, *refs):
    out = refs[-1]
    value = x[...]
    halves, block_rows = out.shape[1:3]
    first, second = slots[0:1, :], slots[1:2, :]
    if gated:
        router = refs[0][...].astype(BF)
        logits = dot_t(router, value)
        logits = jnp.where(iota(logits.shape, 0) < experts, logits, NEG_FILL)
        exps = jnp.exp(logits - jnp.max(logits, axis=0, keepdims=True))
        probs = exps / jnp.sum(exps, axis=0, keepdims=True)
    total = experts * block_rows
    for h in range(halves):
        place = iota((total, value.shape[0]), 0) + (half + h) * total
        hot = ((place == first) | (place == second)).astype(BF)
        out[:, h] = dot(hot, value).astype(BF).reshape(experts, block_rows, value.shape[1])
        if gated:
            row = iota((16, value.shape[0]), 0)
            for e in range(experts):
                gate = probs[e : e + 1, :]
                high = gate.astype(BF).astype(F32)
                pair = jnp.where(row == 14, high, jnp.where(row == 15, gate - high, 0.0))
                placed = dot_t(pair.astype(BF), hot[e * block_rows : (e + 1) * block_rows])
                tail = out[e, h, block_rows - 16 :, :block_rows].astype(F32)
                out[e, h, block_rows - 16 :, :block_rows] = jnp.where(
                    iota(tail.shape, 0) < 14, tail, placed
                ).astype(BF)


def dispatch(slots, x, small, experts, block_rows, half, halves, tag):
    rows, width = x.shape
    gated = small is not None
    more = [small] if gated else []
    vmem = pl.BlockSpec(memory_space=pltpu.VMEM)
    return pl.pallas_call(
        functools.partial(dispatch_kernel, experts, half, gated),
        in_specs=[vmem] * (2 + len(more)),
        out_specs=vmem,
        out_shape=jax.ShapeDtypeStruct((experts, halves, block_rows, width), BF),
        compiler_params=params(24),
        cost_estimate=SMALL,
        name="dispatch_" + tag,
    )(slots, x, *more)


def first_kernel(experts, half_cap, count, capacity, routes, x, out, slots):
    rows = routes.shape[1]
    halves, block_rows = out.shape[1:3]
    alive = iota((1, rows), 1) < count[0] * SEQ
    name = iota((up16(experts), rows), 0)
    earlier = (iota((rows, rows), 0) < iota((rows, rows), 1)).astype(BF)
    limits = jnp.zeros((up16(experts), 1), F32)
    for e in range(experts):
        limits = jnp.where(name[:, 0:1] == e, capacity[e].astype(F32), limits)
    base = 0.0
    for k in range(2):
        hit = jnp.where((routes[k : k + 1, :] == name) & alive, 1.0, 0.0)
        place = col_sum(hit * (dot(hit.astype(BF), earlier) + base))
        keep = place < col_sum(hit * limits)
        base = jnp.sum(hit, axis=1, keepdims=True)
        place = place.astype(jnp.int32)
        half = (place >= half_cap).astype(jnp.int32)
        spot = (half * experts + routes[k : k + 1, :]) * block_rows + place - half * half_cap
        slots[k : k + 1, :] = jnp.where(keep, spot, -1)
    dispatch_kernel(experts, 0, False, slots, x, out)


def first_dispatch(count, capacity, routes, x, half_cap, block_rows, halves):
    rows, width = x.shape
    experts = capacity.shape[0]
    vmem = pl.BlockSpec(memory_space=pltpu.VMEM)
    return pl.pallas_call(
        functools.partial(first_kernel, experts, half_cap),
        in_specs=[SMEM, SMEM, vmem, vmem],
        out_specs=[vmem, vmem],
        out_shape=[
            jax.ShapeDtypeStruct((experts, halves, block_rows, width), BF),
            jax.ShapeDtypeStruct((2, rows), jnp.int32),
        ],
        compiler_params=params(24),
        cost_estimate=SMALL,
        name="dispatch_first",
    )(count, capacity, routes, x)


def expert_kernel(places, n_arrays, n_before, *refs):
    x_ref, c_ref, b_in, b_out = refs[:4]
    arrays, parts = refs[4 : 4 + n_arrays], len(places) // 2
    rest = refs[4 + n_arrays + n_before :]
    act_o, pre_o, x_o, sg_o, r_o, d_o, db_in, db_out, win, wout, sems = rest
    step = pl.program_id(0)
    n, _, size, width = x_ref.shape
    piece = win.shape[1] // parts

    def copies(q):
        cols = pl.ds(q * piece, piece)
        (one, at_one), (two, at_two) = places[q], places[parts + q]
        return (
            pltpu.make_async_copy(
                arrays[one].at[pl.ds(at_one, width), :], win.at[:, cols], sems.at[q]
            ),
            pltpu.make_async_copy(
                arrays[two].at[pl.ds(at_two, piece), :], wout.at[cols, :], sems.at[parts + q]
            ),
        )

    @pl.when(step == 0)
    def _():
        for q in range(parts):
            for c in copies(q):
                c.start()
        db_in[...] = jnp.zeros_like(db_in)
        db_out[...] = jnp.zeros_like(db_out)

    eye = (iota((size, size), 0) == iota((size, size), 1)).astype(BF)
    for s in range(n):
        rows = slice(s * size, (s + 1) * size)
        x_o[rows, :] = x_ref[s, 0]
        turned = dot_t(eye, x_ref[s, 0, size - 16 :, :size])
        gate = jnp.sum(jnp.where(iota(turned.shape, 1) >= 14, turned, 0.0), axis=1, keepdims=True)
        sg_o[rows, :] = (gate * c_ref[s, 0].astype(F32)).astype(BF)
    x = x_o[...]
    slot_grad = sg_o[...]
    db_out[0:1, :] += col_sum(slot_grad.astype(F32))

    @pl.when(step == 0)
    def _():
        for q in range(parts):
            for c in copies(q):
                c.wait()

    for q in range(parts):
        cols = slice(q * piece, (q + 1) * piece)
        pre = dot(x, win[:, cols]) + b_in[q, 0:1, :]
        square = pre * pre
        turn = jnp.tanh(pre * (GELU_A + GELU_A * GELU_B * square))
        half_turn = 0.5 * turn + 0.5
        act_o[:, cols] = (pre * half_turn).astype(BF)
        slope = half_turn + (0.5 * pre) * (1.0 - turn * turn) * (GELU_A + 3 * GELU_A * GELU_B * square)
        pre_grad = dot_t(slot_grad, wout[cols, :]) * slope
        pre_o[:, cols] = pre_grad.astype(BF)
        db_in[q, 0:1, :] += col_sum(pre_grad)
    out = (dot(act_o[...], wout[...]) + b_out[0:1, :]).astype(BF)
    back = dot_t(pre_o[...], win[...])
    ones = jnp.ones((16, width), BF)
    for s in range(n):
        rows = slice(s * size, (s + 1) * size)
        r_o[s, 0] = out[rows]
        d_o[s] = back[rows].astype(BF)
        prod = c_ref[s, 0].astype(F32) * out[rows].astype(F32)
        high = prod.astype(BF)
        low = (prod - high.astype(F32)).astype(BF)
        gate_grad = dot_t(ones, high) + dot_t(ones, low)
        grad_high = gate_grad.astype(BF).astype(F32)
        row = iota(gate_grad.shape, 0)
        tail = back[(s + 1) * size - 16 : (s + 1) * size, :size]
        both = jnp.where(row == 14, grad_high, gate_grad - grad_high)
        d_o[s, size - 16 :, :size] = jnp.where(row < 14, tail, both).astype(BF)


def expert_call(x, c, arrays, places, b_in, b_out, half, halves, before):
    experts, _, size, width = x.shape
    parts, _, piece = b_in.shape
    n = max(1, 256 // size)
    steps = experts // n
    rows, hidden = n * size, parts * piece
    before = list(before)
    tall = lambda cols: pl.BlockSpec((rows, cols), lambda i: (half * steps + i, 0))
    of_half = pl.BlockSpec((n, 1, size, width), lambda i: (i, half, 0, 0))
    total = halves * experts * size
    return pl.pallas_call(
        functools.partial(expert_kernel, places, len(arrays), len(before)),
        grid=(steps,),
        in_specs=[
            pl.BlockSpec((n, 1, size, width), lambda i: (i, 0, 0, 0)),
            of_half,
            whole((parts, 8, piece)),
            whole((8, width)),
        ]
        + [ANY] * (len(arrays) + len(before)),
        out_specs=[
            tall(hidden),
            tall(hidden),
            tall(width),
            tall(width),
            of_half,
            pl.BlockSpec((n, size, width), lambda i: (i, 0, 0)),
            whole((parts, 8, piece)),
            whole((8, width)),
        ],
        out_shape=[
            jax.ShapeDtypeStruct((total, hidden), BF),
            jax.ShapeDtypeStruct((total, hidden), BF),
            jax.ShapeDtypeStruct((total, width), BF),
            jax.ShapeDtypeStruct((total, width), BF),
            jax.ShapeDtypeStruct((experts, halves, size, width), BF),
            jax.ShapeDtypeStruct((experts, size, width), BF),
            jax.ShapeDtypeStruct((parts, 8, piece), F32),
            jax.ShapeDtypeStruct((8, width), F32),
        ],
        scratch_shapes=[
            pltpu.VMEM((width, hidden), BF),
            pltpu.VMEM((hidden, width), BF),
            pltpu.SemaphoreType.DMA((2 * parts,)),
        ],
        input_output_aliases={4 + len(arrays) + i: i for i in range(len(before))},
        compiler_params=params(44),
        cost_estimate=SMALL,
        name="expert_" + "ab"[half],
    )(x, c, b_in, b_out, *arrays, *before)


def weight_kernel(more, x, pre, act, grad, bias, *refs):
    far, (in_o, out_o, in_acc, out_acc) = refs[:more], refs[more:]
    step = pl.program_id(0)
    width = x.shape[1]
    first, second = t_dot(x[...], pre[...]), t_dot(act[...], grad[...])

    @pl.when(step == 0)
    def _():
        in_acc[...] = first + far[0][:width, :].astype(F32) if more else first
        out_acc[...] = second + far[1][...].astype(F32) if more else second

    @pl.when(step > 0)
    def _():
        in_acc[...] += first
        out_acc[...] += second

    @pl.when(step == pl.num_programs(0) - 1)
    def _():
        in_o[:width, :] = in_acc[...].astype(in_o.dtype)
        sums = bias[0] + far[0][width:, :].astype(F32) if more else bias[0]
        in_o[width:, :] = sums.astype(in_o.dtype)
        out_o[...] = out_acc[...].astype(out_o.dtype)


def weight_grads(x, pre, act, grad, bias, piece, q_in, q_out, kind, far=()):
    total, width = x.shape
    rows = total // 2
    plain = pl.BlockSpec((rows, width), lambda k: (k, 0))
    return pl.pallas_call(
        functools.partial(weight_kernel, len(far)),
        grid=(total // rows,),
        in_specs=[
            plain,
            pl.BlockSpec((rows, piece), lambda k: (k, q_in)),
            pl.BlockSpec((rows, piece), lambda k: (k, q_out)),
            plain,
            pl.BlockSpec((1, 16, piece), lambda k: (q_in, 0, 0)),
        ]
        + [whole(f.shape) for f in far],
        out_specs=[whole((width + 16, piece)), whole((piece, width))],
        out_shape=[
            jax.ShapeDtypeStruct((width + 16, piece), kind),
            jax.ShapeDtypeStruct((piece, width), kind),
        ],
        scratch_shapes=[pltpu.VMEM((width, piece), F32), pltpu.VMEM((piece, width), F32)],
        compiler_params=params(60),
        cost_estimate=SMALL,
        name="weight_grads",
    )(x, pre, act, grad, bias, *far)


def backward_kernel(experts, n, split, off, count, slots, cot, n1, qkv, att, aa, n2, probs_in, w, small, *refs):
    backs = refs[:n]
    ag_o, gp_o, dq_o = refs[n : n + 3]
    grads = refs[n + 3 : n + 3 + split]
    dw, ds, marks, ag_all, dq_all = refs[n + 3 + split :]
    img = pl.program_id(0)
    width = n1.shape[-1]
    size = backs[0].shape[1]
    total = experts * size

    @pl.when(img == 0)
    def _():
        ds[...] = jnp.zeros_like(ds)
        line = iota((LANES, size), 0)
        for h in range(n):
            for e in range(experts):
                ends = backs[h][e, size - 16 :, :size].astype(F32)
                for k in range(2):
                    marks[2 * h + k, :, e * size : (e + 1) * size] = jnp.where(
                        line == e, ends[14 + k : 15 + k, :], 0.0
                    ).astype(BF)

    def vec(k):
        return small[experts + k : experts + k + 1, :]

    def add_vec(k, value):
        ds[experts + k : experts + k + 1, :] += value

    alive = (img < count[0]).astype(F32)
    up = cot[0].astype(F32)
    rows = up.shape[0]
    normed = n2[0]
    lane = iota((rows, LANES), 1)
    router = jnp.where(iota(small.shape, 0) < experts, small[...], 0.0).astype(BF)
    logits = jnp.where(lane < experts, dot_t(normed, router), NEG_FILL)
    exps = jnp.exp(logits - jnp.max(logits, axis=-1, keepdims=True))
    probs = exps / jnp.sum(exps, axis=-1, keepdims=True)
    gp_o[0] = probs
    first, second = slots[0, :, 0:1], slots[0, :, 1:2]
    normed_grad = jnp.zeros((rows, width), F32)
    placed = jnp.zeros((rows, LANES), F32)
    for h in range(n):
        place = iota((rows, total), 1) + h * total
        hot = ((place == first) | (place == second)).astype(BF)
        normed_grad = normed_grad + dot(hot, backs[h][...].reshape(total, width))
        placed = placed + dot_t(hot, marks[2 * h]) + dot_t(hot, marks[2 * h + 1])
    logit_grad = (
        probs * (placed - jnp.sum(probs * placed, axis=-1, keepdims=True))
    ).astype(BF)
    normed_grad = normed_grad + dot(logit_grad, router)
    ds[...] += jnp.where(iota(ds.shape, 0) < experts, t_dot(logit_grad, normed), 0.0)
    unit, inverse = norm_stats(aa[0])
    add_vec(3, col_sum(normed_grad * unit))
    add_vec(4, col_sum(normed_grad))
    after_grad = up + norm_back(unit, inverse, vec(3), normed_grad)
    attn_grad = (alive * after_grad).astype(BF)
    add_vec(2, col_sum(attn_grad.astype(F32)))
    ag_all[img] = attn_grad
    att_grad = dot_t(attn_grad, w[:, 3 * width : 4 * width]).astype(BF)
    low = lane < LANES // 2
    scale = (width // HEADS) ** -0.5
    for pair in range(HEADS // 2):
        c = pair * LANES
        q2 = qkv[0, :, c : c + LANES]
        k2 = qkv[0, :, width + c : width + c + LANES]
        v2 = qkv[0, :, 2 * width + c : 2 * width + c + LANES]
        o2 = att_grad[:, c : c + LANES]
        got = []
        for side, mask in enumerate((low, ~low)):
            prob = probs_in[0, 2 * pair + side]
            prob_grad = dot_t(v2, jnp.where(mask, o2, jnp.zeros_like(o2)))
            score_grad = (prob * (prob_grad - col_sum(prob * prob_grad))).astype(BF)
            got.append(
                (
                    t_dot(score_grad, k2) * scale,
                    dot(score_grad, q2) * scale,
                    dot(prob.astype(BF), o2),
                )
            )
        for k in range(3):
            dq_o[0, :, k * width + c : k * width + c + LANES] = jnp.where(
                low, got[0][k], got[1][k]
            ).astype(BF)
    grad = dq_o[0]
    dq_all[img] = grad
    for k in range(3):
        ds[experts + 5 + k : experts + 6 + k, :] += col_sum(grad[:, k * width : (k + 1) * width].astype(F32))
    ag_o[0] = after_grad

    @pl.when(img == pl.num_programs(0) - 1)
    def _():
        dw[:, 4 * width : 4 * width + LANES] = jnp.transpose(ds[...])
        left = n1[...].reshape(-1, width)
        for k in range(3):
            cols = slice(k * width, (k + 1) * width)
            dw[:, cols] = t_dot(left, dq_all[:, :, cols].reshape(-1, width))
        dw[:, 3 * width : 4 * width] = t_dot(
            att[...].reshape(-1, width), ag_all[...].reshape(-1, width)
        )
        with_weight = jnp.zeros((width, LANES), F32)
        with_sums = jnp.zeros((width, LANES), F32)
        for k in range(3 * width // LANES):
            cols = slice(k * LANES, (k + 1) * LANES)
            part, at = divmod(k * LANES, width)
            value = w[:, cols].astype(F32)
            sums = ds[experts + 5 + part : experts + 6 + part, at : at + LANES]
            with_weight = with_weight + value * dw[:, cols]
            with_sums = with_sums + value * sums
        sums = jnp.sum(with_sums, axis=1, keepdims=True)
        at = 4 * width
        sides = w[:, at : at + LANES].astype(F32)
        gain, shift = sides[:, experts : experts + 1], sides[:, experts + 1 : experts + 2]
        gains = (jnp.sum(with_weight, axis=1, keepdims=True) - shift * sums) / gain
        spot = iota((width, LANES), 1)
        cols = slice(at, at + LANES)
        dw[:, cols] = jnp.where(
            spot == experts, gains, jnp.where(spot == experts + 1, sums, dw[:, cols])
        )
        if split == 1:
            grads[0][...] = dw[...].astype(BF)
        else:
            cols = grads[0].shape[1]
            step = width // 16
            for h in range(2):
                col = pl.multiple_of(off[16 + h], LANES)
                for r in range(16):
                    row = pl.multiple_of(off[r], 16)
                    grads[h][r * step : (r + 1) * step, :] = dw[
                        pl.ds(row, step), pl.ds(col, cols)
                    ].astype(BF)


def backward(off, count, slots, cot, n1, qkv, att, aa, n2, prob, w, small, backs, experts, split):
    images, rows, width = cot.shape
    width_all = w.shape[1]
    n = len(backs)
    block = lambda cols: pl.BlockSpec((1, rows, cols), lambda i: (i, 0, 0))
    got = pl.pallas_call(
        functools.partial(backward_kernel, experts, n, split),
        grid=(images,),
        in_specs=[SMEM, SMEM, block(2), block(width), whole(n1.shape), block(3 * width), whole(att.shape), block(width), block(width)]
        + [pl.BlockSpec((1, HEADS, rows, rows), lambda i: (i, 0, 0, 0))]
        + [whole(w.shape), whole(small.shape)]
        + [whole(backs[0].shape)] * n,
        out_specs=[block(width), block(LANES), block(3 * width)] + [whole((width, width_all // split))] * split,
        out_shape=[
            jax.ShapeDtypeStruct((images, rows, width), F32),
            jax.ShapeDtypeStruct((images, rows, LANES), F32),
            jax.ShapeDtypeStruct((images, rows, 3 * width), BF),
        ]
        + [jax.ShapeDtypeStruct((width, width_all // split), BF)] * split,
        scratch_shapes=[
            pltpu.VMEM((width, width_all), F32),
            pltpu.VMEM((LANES, width), F32),
            pltpu.VMEM((2 * n, LANES, backs[0].shape[0] * backs[0].shape[1]), BF),
            pltpu.VMEM((images, rows, width), BF),
            pltpu.VMEM((images, rows, 3 * width), BF),
        ],
        compiler_params=params(),
        cost_estimate=SMALL,
        name="tokens_backward",
    )(off, count, slots, cot, n1, qkv, att, aa, n2, prob, w, small, *backs)
    return got[0], got[1], got[2], got[3:]


def finish_kernel(experts, after_grad, grad, tok, w, small, out):
    width = tok.shape[-1]
    normed_grad = dot_t(grad[0], w[...])
    unit, inverse = norm_stats(tok[0].astype(F32))
    out[0] = after_grad[0] + norm_back(unit, inverse, small[experts : experts + 1, :], normed_grad)


def finish(after_grad, grad, tok, w, small, experts):
    images, rows, width = tok.shape
    block = lambda cols: pl.BlockSpec((1, rows, cols), lambda i: (i, 0, 0))
    return pl.pallas_call(
        functools.partial(finish_kernel, experts),
        grid=(images,),
        in_specs=[block(width), block(3 * width), block(width), whole((width, 3 * width)), whole(small.shape)],
        out_specs=block(width),
        out_shape=jax.ShapeDtypeStruct((images, rows, width), F32),
        compiler_params=params(32),
        cost_estimate=SMALL,
        name="tokens_finish",
    )(after_grad, grad, tok, w, small)


def output_kernel(count, slots, aa, probs, outs, out):
    rows = aa.shape[1]
    experts, n, size, width = outs.shape
    total = experts * size
    alive = (pl.program_id(0) < count[0]).astype(F32)
    first, second = slots[0, :, 0:1], slots[0, :, 1:2]
    gates = jnp.concatenate(
        [jnp.broadcast_to(probs[0, :, e : e + 1], (rows, size)) for e in range(experts)], axis=1
    )
    moe = jnp.zeros(aa.shape[1:], F32)
    for h in range(n):
        place = iota((rows, total), 1) + h * total
        gate = jnp.where((place == first) | (place == second), gates, 0.0)
        high = gate.astype(BF)
        low = (gate - high.astype(F32)).astype(BF)
        value = outs[:, h].reshape(total, width)
        moe = moe + dot(high, value) + dot(low, value)
    out[0] = (aa[0] + alive * moe).astype(BF)


def block_output(count, slots, aa, probs, outs):
    images, rows, width = aa.shape
    block = lambda cols: pl.BlockSpec((1, rows, cols), lambda i: (i, 0, 0))
    return pl.pallas_call(
        output_kernel,
        grid=(images,),
        in_specs=[SMEM, block(2), block(width), block(LANES), whole(outs.shape)],
        out_specs=block(width),
        out_shape=jax.ShapeDtypeStruct((images, rows, width), BF),
        compiler_params=params(32),
        cost_estimate=SMALL,
        name="block_output",
    )(count, slots, aa, probs, outs)


def local(sizes, *args):
    (tokens, image_count, routes, capacity, ln1_gain, ln1_bias, qkv_weight, qv_bias, out_weight, out_bias,
     ln2_gain, ln2_bias, router_weight, expert_in, expert_in_bias, expert_out, expert_out_bias, cotangent) = args
    dp, experts = sizes
    grouped = sizes == (4, 8)
    devices = dp * experts
    me_d = lax.axis_index("dp")
    me_e = lax.axis_index("expert")
    core = me_e % 2
    token_count, width = tokens.shape
    images = token_count // SEQ
    rows = up16(SEQ)
    cap = max(2, 5 * token_count // (2 * experts))
    halves = 2 if grouped else 1
    half_cap = -(-cap // halves)
    block_rows = up16(half_cap + 2)

    def hop(value, mask):
        return lax.ppermute(value, BOTH, [(i, i ^ mask) for i in range(devices)])

    def by_image(value):
        value = value.reshape(images, SEQ, value.shape[-1])
        fill = -1 if value.dtype == jnp.int32 else 0
        return jnp.pad(value, ((0, 0), (0, rows - SEQ), (0, 0)), constant_values=fill)

    def from_image(value):
        return value[:, :SEQ].reshape(token_count, value.shape[-1])

    def side_rows(values):
        return functools.reduce(
            lambda a, b: a + b,
            [jnp.pad(v.astype(F32)[None], ((k, 7 - k), (0, 0))) for k, v in enumerate(values)],
        )

    def slots_and_blocks(value):
        return first_dispatch(image_count, capacity, routes.T, value, half_cap, block_rows, halves)

    def slot_forms(slots):
        slots = slots.reshape(2, images, SEQ)
        slots = jnp.pad(slots, ((0, 0), (0, 0), (0, rows - SEQ)), constant_values=-1)
        return slots.transpose(1, 2, 0), slots.reshape(2, -1)

    def after(values, *done):
        return lax.optimization_barrier((values, done))[0]

    tok = by_image(tokens)

    vectors = [ln1_gain, ln1_bias, out_bias, ln2_gain, ln2_bias]
    width_all = 4 * width + 2 * LANES
    wide = expert_in.shape[2]
    spot = me_d * expert_out_bias.shape[1]
    if grouped:
        half = width_all // 2
        mine, other = pack_dense(
            core.reshape(1).astype(jnp.int32), qkv_weight, out_weight, router_weight.T, side_rows(vectors), qv_bias
        )
        got = hop(other, 1)
        chip = jnp.where(
            core == 0, jnp.concatenate([mine, got], axis=0), jnp.concatenate([got, mine], axis=0)
        )
        bias_out = lax.dynamic_update_slice(jnp.zeros((1, width), BF), expert_out_bias, (0, spot))
        one = jnp.concatenate([expert_in[0], expert_in_bias, bias_out, jnp.zeros((14, wide), BF)], axis=0)
        two = expert_out[0]
        from_x, from_y = hop(one, 8), hop(two, 16)
        cot_blocks, slots = slots_and_blocks(after(cotangent, chip))
        slots_col, slots_row = slot_forms(slots)
        line = jnp.concatenate([chip] + [hop(chip, 2 * dz) for dz in (1, 2, 3)], axis=0)
        held, from_x, from_y = after((line, from_x, from_y))
        own = [line] + [hop(held, 8 * dxy) for dxy in (3, 1, 2)]
        own = [own[0], own[2], own[3], own[1]]
        step = width // 16
        at_rows = jnp.stack([((me_d ^ a) * 4 + ((me_e // 2) ^ b)) * step for a in range(4) for b in range(4)])
        at_cols = jnp.stack([core * half, (1 - core) * half])
        off_back = jnp.concatenate([at_rows, at_cols]).astype(jnp.int32)
        off = jnp.concatenate([at_rows, at_rows, jnp.repeat(at_cols, 4)]).astype(jnp.int32)
        own, tok, slots_row, off = after((own, tok, slots_row, off))
        pieces = own + [hop(piece, 1) for piece in own]
        subs = 4
        later_one, later_two, relay_x, relay_y = after((one, two, from_x, from_y), *own)
        near = hop(later_one, 16), hop(later_two, 8)
        relays = hop(relay_x, 16), hop(relay_y, 8)
        arrays = [one, from_x, near[0], relays[0]]
        b_in = jnp.stack([v[width : width + 8] for v in arrays]).astype(F32)
        arrays += [two, near[1], from_y, relays[1]]
        places = tuple((q, 0) for q in range(8))
        b_out = jnp.broadcast_to(jnp.sum(b_in[:, 1], axis=0), (8, width))
        after_line = held
    else:
        fill = width_all - 4 * width - experts - 7
        pack = jnp.concatenate(
            [qkv_weight, out_weight, router_weight, jnp.stack(vectors, axis=1), qv_bias.T, jnp.zeros((ln1_gain.shape[0], fill), BF)], axis=1
        )
        pieces = [lax.all_gather(pack, BOTH, axis=0, tiled=True)]
        cot_blocks, slots = slots_and_blocks(cotangent)
        slots_col, slots_row = slot_forms(slots)
        off = jnp.zeros((2,), jnp.int32)
        off_back = off
        subs = 1
        after_line = pieces[0]
        w_in = lax.all_gather(expert_in[0], "dp", axis=0, tiled=False)
        w_out = lax.all_gather(expert_out[0], "dp", axis=0, tiled=False)
        arrays = [w[q] for w in (w_in, w_out) for q in range(dp)]
        places = tuple((q, 0) for q in range(2 * dp))
        b_in = lax.all_gather(jnp.broadcast_to(expert_in_bias, (8, wide)), "dp", axis=0, tiled=False).astype(F32)
        b_out = jnp.broadcast_to(
            lax.all_gather(expert_out_bias, "dp", axis=1, tiled=True).astype(F32), (8, width)
        )

    def exchange(blocks):
        return lax.all_to_all(blocks, "expert", 0, 0, tiled=True)

    cot_sent = exchange(after(cot_blocks, after_line))
    cot = by_image(cotangent)

    w, small, qkv, n1, att, aa, n2, prob = forward(off, subs, pieces, image_count, tok, experts, width_all)
    row_sent = []
    flat = n2.reshape(-1, width)
    for h in range(halves):
        sent = dispatch(slots_row, flat, small, experts, block_rows, h, 1, "ab"[h])
        waits = (near, relays)[h] if grouped else ()
        sent, cot_sent = after((sent, cot_sent), *row_sent, *waits)
        if h:
            sent, cot, slots_col = after((sent, cot, slots_col))
        row_sent.append(exchange(sent))

    back, grads_out, db_ins, db_outs, tall = [], [], [], [], ()
    for h in range(halves):
        *tall, d, db_in, db_out = expert_call(
            row_sent[h], cot_sent, arrays, places, b_in, b_out, h, halves, tall
        )
        grads_out.append(d)
        if h + 1 < halves:
            back.append(exchange(d))
        db_ins.append(db_in)
        db_outs.append(db_out)
    *tall, outs_back = tall
    db_in, db_out = sum(db_ins), sum(db_outs)

    both = [db_in[:, 0:1]]
    if grouped:
        both.append(jnp.broadcast_to(db_out[0:1], db_in[:, 0:1].shape))
    bias_sums = jnp.concatenate(
        [*both, jnp.zeros((dp, 16 - len(both), wide), F32)], axis=1
    )

    def weights_of(q_in, q_out, kind, far=()):
        act, pre, rows_in, slot_grad = tall
        return weight_grads(rows_in, pre, act, slot_grad, bias_sums, wide, q_in, q_out, kind, far)

    if grouped:
        far_in, far_out = weights_of(3, 3, BF)
        tall = after(tall, far_in, far_out, *back)
        back.append(exchange(after(grads_out[-1], far_in, far_out, *back)))
        far_in, far_out = hop(far_in, 8), hop(far_out, 16)
        near_in, near_out = weights_of(1, 2, BF)
        own_in, own_out = weights_of(0, 0, F32)
        far = after((far_in, far_out), own_in, own_out, near_in, near_out)
        last_in, last_out = weights_of(2, 1, BF, far)
        ready = (near_in, near_out, own_in, own_out, last_in, last_out)
        near_in, near_out = hop(near_in, 8), hop(near_out, 16)
        last_in, last_out = hop(last_in, 16), hop(last_out, 8)
        arrived = (near_in, near_out, last_in, last_out)
        g_in = own_in + near_in.astype(F32) + last_in.astype(F32)
        g_in, g_bias = g_in[None, :width], g_in[width:]
        g_out = (own_out + near_out.astype(F32) + last_out.astype(F32))[None]
        g_b_in = g_bias[0:1]
        g_b_out = lax.dynamic_slice(g_bias[1:2], (0, spot), expert_out_bias.shape)
    else:
        ready = arrived = ()
        scatter = lambda v: lax.psum_scatter(v, "dp", scatter_dimension=0, tiled=True).astype(F32)
        back.append(exchange(grads_out[-1]))
        every = [weights_of(q, q, BF) for q in range(dp)]
        g_in = scatter(jnp.stack([e[0][:width] for e in every]))
        g_out = scatter(jnp.stack([e[1] for e in every]))
        g_b_in = lax.psum_scatter(
            db_in[:, 0].reshape(1, -1).astype(BF), "dp", scatter_dimension=1, tiled=True
        ).astype(F32)
        g_b_out = lax.psum_scatter(db_out[0:1].astype(BF), "dp", scatter_dimension=1, tiled=True).astype(F32)

    r_sent = exchange(after(outs_back, *back))
    back = after(back, *ready)
    after_grad, probs, grad, grads = backward(
        off_back, image_count, slots_col, cot, n1, qkv, att, aa, n2, prob, w, small, back, experts,
        2 if grouped else 1,
    )
    grads = after(grads, *arrived)
    block_out = from_image(block_output(image_count, slots_col, aa, probs, r_sent))
    tokens_grad = from_image(finish(after_grad, grad, tok, w, small, experts))

    def add(*values):
        return functools.reduce(lambda a, b: a + b, [v.astype(F32) for v in values])

    if grouped:
        sibling = hop(grads[1], 1)
        quarter = width // 4
        ways = [slice(a * quarter, (a + 1) * quarter) for a in range(4)]
        ways = [add(grads[0][a], sibling[a]).astype(BF) for a in ways]
        line = add(ways[0], *[hop(ways[a], 8 * a) for a in (1, 2, 3)]).astype(BF)
        line, tokens_grad, r_sent, g_in, g_out = after((line, tokens_grad, r_sent, g_in, g_out))
        step = width // 16
        cuts = [line[b * step : (b + 1) * step] for b in range(4)]
        chip = add(cuts[0], *[hop(cuts[b], 2 * b) for b in (1, 2, 3)])
        n_rows = step // 2
        keep = lax.dynamic_slice_in_dim(chip, core * n_rows, n_rows, 0)
        chip, block_out = after((chip, block_out))
        give = lax.dynamic_slice_in_dim(chip, (1 - core) * n_rows, n_rows, 0)
        got = hop(give.astype(BF), 1).astype(F32)
        dense = jnp.where(
            core == 0, jnp.concatenate([keep, got], axis=1), jnp.concatenate([got, keep], axis=1)
        )
    else:
        dense = lax.psum_scatter(grads[0], BOTH, scatter_dimension=0, tiled=True).astype(F32)
    side = dense[:, 4 * width :]
    vecs = [side[:, experts + k] for k in range(8)]
    return (
        block_out,
        tokens_grad,
        vecs[0],
        vecs[1],
        dense[:, : 3 * width],
        jnp.stack([vecs[5], vecs[7]], axis=0),
        dense[:, 3 * width : 4 * width],
        vecs[2],
        vecs[3],
        vecs[4],
        side[:, :experts],
        g_in,
        g_b_in,
        g_out,
        g_b_out,
    )


def solution(mesh):
    rows, line, cols = P(BOTH, None), P(BOTH), P(None, BOTH)
    experts = (P("expert", None, "dp"), P("expert", "dp"), P("expert", "dp", None), P("expert", "dp"))
    dense = (line, line, rows, cols, rows, line, line, line, rows)
    return jax.shard_map(
        functools.partial(local, (mesh.shape["dp"], mesh.shape["expert"])),
        mesh=mesh,
        in_specs=(rows, line, rows, P(), *dense, *experts, rows),
        out_specs=(rows, rows, *dense, *experts),
        check_vma=False,
    )
```

```python
import functools

import jax
import jax.numpy as jnp
from jax import lax
from jax.experimental import pallas as pl
from jax.experimental.pallas import tpu as pltpu
from jax.sharding import PartitionSpec as P

HEADS = 12
SEQ = 197
EPS_NORM = 1e-06
NEG_FILL = -1e30
BF = jnp.bfloat16
F32 = jnp.float32
LANES = 128
GELU_A = 0.7978845608028654
GELU_B = 0.044715
BOTH = ("dp", "expert")


def up16(n):
    return -(-n // 16) * 16


def dot(left, right):
    return jnp.dot(left, right, preferred_element_type=F32)


def dot_t(left, right):
    return lax.dot_general(left, right, (((1,), (1,)), ((), ())), preferred_element_type=F32)


def t_dot(left, right):
    return lax.dot_general(left, right, (((0,), (0,)), ((), ())), preferred_element_type=F32)


def iota(shape, dim):
    return lax.broadcasted_iota(jnp.int32, shape, dim)


def params(mib=60):
    return pltpu.CompilerParams(vmem_limit_bytes=mib << 20)


def whole(shape):
    zeros = (0,) * len(shape)
    return pl.BlockSpec(shape, lambda *_: zeros, pipeline_mode=pl.Buffered(1))


SMALL = pl.CostEstimate(flops=1 << 20, bytes_accessed=1 << 16, transcendentals=0)
LARGE = pl.CostEstimate(flops=1 << 34, bytes_accessed=1 << 16, transcendentals=0)
SMEM = pl.BlockSpec(memory_space=pltpu.SMEM)
ANY = pl.BlockSpec(memory_space=pl.ANY)


def norm_stats(values):
    centered = values - jnp.mean(values, axis=-1, keepdims=True)
    inverse = lax.rsqrt(jnp.mean(centered * centered, axis=-1, keepdims=True) + EPS_NORM)
    return centered * inverse, inverse


def norm_back(unit, inverse, gain, grad):
    scaled = grad * gain
    mean_one = jnp.mean(scaled, axis=-1, keepdims=True)
    mean_two = jnp.mean(scaled * unit, axis=-1, keepdims=True)
    return inverse * (scaled - mean_one - unit * mean_two)


def col_sum(values):
    return jnp.sum(values, axis=0, keepdims=True)


def pack_kernel(core, qkv, out, router, vectors, pair, mine, other):
    rows = qkv.shape[0]
    eye = (iota((rows, rows), 0) == iota((rows, rows), 1)).astype(BF)
    turned = [dot_t(eye, router[...]), dot_t(eye, vectors[...].astype(BF))[:, :5], dot_t(eye, pair[...])]
    used = sum(t.shape[1] for t in turned)
    turned = jnp.concatenate([*turned, jnp.zeros((rows, 2 * LANES - used), F32)], axis=1)
    value = jnp.concatenate([qkv[...], out[...], turned.astype(BF)], axis=1)
    half = value.shape[1] // 2

    @pl.when(core[0] == 0)
    def _():
        mine[...] = value[:, :half]
        other[...] = value[:, half:]

    @pl.when(core[0] != 0)
    def _():
        mine[...] = value[:, half:]
        other[...] = value[:, :half]


def pack_dense(core, qkv, out, router, vectors, pair):
    rows = qkv.shape[0]
    half = (qkv.shape[1] + out.shape[1] + 2 * LANES) // 2
    vmem = pl.BlockSpec(memory_space=pltpu.VMEM)
    return pl.pallas_call(
        pack_kernel,
        in_specs=[SMEM] + [vmem] * 5,
        out_specs=[vmem] * 2,
        out_shape=[jax.ShapeDtypeStruct((rows, half), BF)] * 2,
        compiler_params=params(60),
        cost_estimate=LARGE,
        name="pack_dense",
    )(core, qkv, out, router, vectors, pair)


def forward_kernel(experts, subs, off, count, tok, *refs):
    n_pieces = len(refs) - 10
    pieces = refs[:n_pieces]
    w_o, small, qkv_o, n1_o, att_o, aa_o, n2_o, prob_o, w, sems = refs[n_pieces:]
    img = pl.program_id(0)
    width = tok.shape[-1]

    @pl.when(img == 0)
    def _():
        copies = []
        for i, piece in enumerate(pieces):
            rows, cols = piece.shape[0] // subs, piece.shape[1]
            col = pl.multiple_of(off[n_pieces * subs + i], LANES)
            for j in range(subs):
                row = pl.multiple_of(off[i * subs + j], 16)
                copies.append(
                    pltpu.make_async_copy(
                        piece.at[pl.ds(j * rows, rows), :],
                        w.at[pl.ds(row, rows), pl.ds(col, cols)],
                        sems.at[i * subs + j],
                    )
                )
        for c in copies:
            c.start()
        for c in copies:
            c.wait()
        small[...] = jnp.transpose(w[:, 4 * width : 4 * width + LANES].astype(F32))
        pltpu.make_async_copy(w, w_o, sems.at[0]).start()

    def vec(k):
        return small[experts + k : experts + k + 1, :]

    x = tok[0].astype(F32)
    rows = x.shape[0]
    unit, _ = norm_stats(x)
    n1 = (unit * vec(0) + vec(1)).astype(BF)
    n1_o[0] = n1
    biases = (vec(5), None, vec(6))
    for part in range(3):
        cols = slice(part * width, (part + 1) * width)
        block = dot(n1, w[:, cols])
        if biases[part] is not None:
            block = block + biases[part]
        qkv_o[0, :, cols] = block.astype(BF)
    low = iota((rows, LANES), 1) < LANES // 2
    seen = iota((rows, rows), 0) < SEQ
    scale = (width // HEADS) ** -0.5
    for pair in range(HEADS // 2):
        c = pair * LANES
        q2 = qkv_o[0, :, c : c + LANES]
        k2 = qkv_o[0, :, width + c : width + c + LANES]
        v2 = qkv_o[0, :, 2 * width + c : 2 * width + c + LANES]
        got = []
        for side, mask in enumerate((low, ~low)):
            scores = dot_t(k2, jnp.where(mask, q2, jnp.zeros_like(q2))) * scale
            scores = jnp.where(seen, scores, NEG_FILL)
            exps = jnp.exp(scores - jnp.max(scores, axis=0, keepdims=True))
            prob = exps * (1.0 / col_sum(exps))
            prob_o[0, 2 * pair + side] = prob
            got.append(t_dot(prob.astype(BF), v2))
        att_o[0, :, c : c + LANES] = jnp.where(low, got[0], got[1]).astype(BF)
    alive = (img < count[0]).astype(F32)
    after = x + alive * (dot(att_o[0], w[:, 3 * width : 4 * width]) + vec(2))
    aa_o[0] = after
    unit, _ = norm_stats(after)
    n2_o[0] = (unit * vec(3) + vec(4)).astype(BF)

    @pl.when(img == pl.num_programs(0) - 1)
    def _():
        pltpu.make_async_copy(w, w_o, sems.at[0]).wait()


def forward(off, subs, pieces, count, tok, experts, width_all):
    images, rows, width = tok.shape
    block = lambda cols: pl.BlockSpec((1, rows, cols), lambda i: (i, 0, 0))
    shape = lambda cols, t: jax.ShapeDtypeStruct((images, rows, cols), t)
    return pl.pallas_call(
        functools.partial(forward_kernel, experts, subs),
        grid=(images,),
        in_specs=[SMEM, SMEM, block(width)] + [ANY] * len(pieces),
        out_specs=[
            ANY,
            whole((LANES, width)),
            block(3 * width),
            block(width),
            block(width),
            block(width),
            block(width),
            pl.BlockSpec((1, HEADS, rows, rows), lambda i: (i, 0, 0, 0)),
        ],
        out_shape=[
            jax.ShapeDtypeStruct((width, width_all), BF),
            jax.ShapeDtypeStruct((LANES, width), F32),
            shape(3 * width, BF),
            shape(width, BF),
            shape(width, BF),
            shape(width, F32),
            shape(width, BF),
            jax.ShapeDtypeStruct((images, HEADS, rows, rows), F32),
        ],
        scratch_shapes=[
            pltpu.VMEM((width, width_all), BF),
            pltpu.SemaphoreType.DMA((len(pieces) * subs,)),
        ],
        compiler_params=params(60),
        cost_estimate=SMALL,
        name="tokens_forward",
    )(off, count, tok, *pieces)


def dispatch_kernel(experts, half, gated, slots, x, *refs):
    out = refs[-1]
    value = x[...]
    halves, block_rows = out.shape[1:3]
    first, second = slots[0:1, :], slots[1:2, :]
    if gated:
        router = refs[0][...].astype(BF)
        logits = dot_t(router, value)
        logits = jnp.where(iota(logits.shape, 0) < experts, logits, NEG_FILL)
        exps = jnp.exp(logits - jnp.max(logits, axis=0, keepdims=True))
        probs = exps / jnp.sum(exps, axis=0, keepdims=True)
    total = experts * block_rows
    for h in range(halves):
        place = iota((total, value.shape[0]), 0) + (half + h) * total
        hot = ((place == first) | (place == second)).astype(BF)
        out[:, h] = dot(hot, value).astype(BF).reshape(experts, block_rows, value.shape[1])
        if gated:
            row = iota((16, value.shape[0]), 0)
            for e in range(experts):
                gate = probs[e : e + 1, :]
                high = gate.astype(BF).astype(F32)
                pair = jnp.where(row == 14, high, jnp.where(row == 15, gate - high, 0.0))
                placed = dot_t(pair.astype(BF), hot[e * block_rows : (e + 1) * block_rows])
                tail = out[e, h, block_rows - 16 :, :block_rows].astype(F32)
                out[e, h, block_rows - 16 :, :block_rows] = jnp.where(
                    iota(tail.shape, 0) < 14, tail, placed
                ).astype(BF)


def dispatch(slots, x, small, experts, block_rows, half, halves, tag):
    rows, width = x.shape
    gated = small is not None
    more = [small] if gated else []
    vmem = pl.BlockSpec(memory_space=pltpu.VMEM)
    return pl.pallas_call(
        functools.partial(dispatch_kernel, experts, half, gated),
        in_specs=[vmem] * (2 + len(more)),
        out_specs=vmem,
        out_shape=jax.ShapeDtypeStruct((experts, halves, block_rows, width), BF),
        compiler_params=params(24),
        cost_estimate=SMALL,
        name="dispatch_" + tag,
    )(slots, x, *more)


def first_kernel(experts, half_cap, count, capacity, routes, x, out, slots):
    rows = routes.shape[1]
    halves, block_rows = out.shape[1:3]
    alive = iota((1, rows), 1) < count[0] * SEQ
    name = iota((up16(experts), rows), 0)
    earlier = (iota((rows, rows), 0) < iota((rows, rows), 1)).astype(BF)
    limits = jnp.zeros((up16(experts), 1), F32)
    for e in range(experts):
        limits = jnp.where(name[:, 0:1] == e, capacity[e].astype(F32), limits)
    base = 0.0
    for k in range(2):
        hit = jnp.where((routes[k : k + 1, :] == name) & alive, 1.0, 0.0)
        place = col_sum(hit * (dot(hit.astype(BF), earlier) + base))
        keep = place < col_sum(hit * limits)
        base = jnp.sum(hit, axis=1, keepdims=True)
        place = place.astype(jnp.int32)
        half = (place >= half_cap).astype(jnp.int32)
        spot = (half * experts + routes[k : k + 1, :]) * block_rows + place - half * half_cap
        slots[k : k + 1, :] = jnp.where(keep, spot, -1)
    dispatch_kernel(experts, 0, False, slots, x, out)


def first_dispatch(count, capacity, routes, x, half_cap, block_rows, halves):
    rows, width = x.shape
    experts = capacity.shape[0]
    vmem = pl.BlockSpec(memory_space=pltpu.VMEM)
    return pl.pallas_call(
        functools.partial(first_kernel, experts, half_cap),
        in_specs=[SMEM, SMEM, vmem, vmem],
        out_specs=[vmem, vmem],
        out_shape=[
            jax.ShapeDtypeStruct((experts, halves, block_rows, width), BF),
            jax.ShapeDtypeStruct((2, rows), jnp.int32),
        ],
        compiler_params=params(24),
        cost_estimate=SMALL,
        name="dispatch_first",
    )(count, capacity, routes, x)


def expert_kernel(places, n_arrays, n_before, *refs):
    x_ref, c_ref, b_in, b_out = refs[:4]
    arrays, parts = refs[4 : 4 + n_arrays], len(places) // 2
    rest = refs[4 + n_arrays + n_before :]
    act_o, pre_o, x_o, sg_o, r_o, d_o, db_in, db_out, win, wout, sems = rest
    step = pl.program_id(0)
    n, _, size, width = x_ref.shape
    piece = win.shape[1] // parts

    def copies(q):
        cols = pl.ds(q * piece, piece)
        (one, at_one), (two, at_two) = places[q], places[parts + q]
        return (
            pltpu.make_async_copy(
                arrays[one].at[pl.ds(at_one, width), :], win.at[:, cols], sems.at[q]
            ),
            pltpu.make_async_copy(
                arrays[two].at[pl.ds(at_two, piece), :], wout.at[cols, :], sems.at[parts + q]
            ),
        )

    @pl.when(step == 0)
    def _():
        for q in range(parts):
            for c in copies(q):
                c.start()
        db_in[...] = jnp.zeros_like(db_in)
        db_out[...] = jnp.zeros_like(db_out)

    eye = (iota((size, size), 0) == iota((size, size), 1)).astype(BF)
    for s in range(n):
        rows = slice(s * size, (s + 1) * size)
        x_o[rows, :] = x_ref[s, 0]
        turned = dot_t(eye, x_ref[s, 0, size - 16 :, :size])
        gate = jnp.sum(jnp.where(iota(turned.shape, 1) >= 14, turned, 0.0), axis=1, keepdims=True)
        sg_o[rows, :] = (gate * c_ref[s, 0].astype(F32)).astype(BF)
    x = x_o[...]
    slot_grad = sg_o[...]
    db_out[0:1, :] += col_sum(slot_grad.astype(F32))

    @pl.when(step == 0)
    def _():
        for q in range(parts):
            for c in copies(q):
                c.wait()

    for q in range(parts):
        cols = slice(q * piece, (q + 1) * piece)
        pre = dot(x, win[:, cols]) + b_in[q, 0:1, :]
        square = pre * pre
        turn = jnp.tanh(pre * (GELU_A + GELU_A * GELU_B * square))
        half_turn = 0.5 * turn + 0.5
        act_o[:, cols] = (pre * half_turn).astype(BF)
        slope = half_turn + (0.5 * pre) * (1.0 - turn * turn) * (GELU_A + 3 * GELU_A * GELU_B * square)
        pre_grad = dot_t(slot_grad, wout[cols, :]) * slope
        pre_o[:, cols] = pre_grad.astype(BF)
        db_in[q, 0:1, :] += col_sum(pre_grad)
    out = (dot(act_o[...], wout[...]) + b_out[0:1, :]).astype(BF)
    back = dot_t(pre_o[...], win[...])
    ones = jnp.ones((16, width), BF)
    for s in range(n):
        rows = slice(s * size, (s + 1) * size)
        r_o[s, 0] = out[rows]
        d_o[s] = back[rows].astype(BF)
        prod = c_ref[s, 0].astype(F32) * out[rows].astype(F32)
        high = prod.astype(BF)
        low = (prod - high.astype(F32)).astype(BF)
        gate_grad = dot_t(ones, high) + dot_t(ones, low)
        grad_high = gate_grad.astype(BF).astype(F32)
        row = iota(gate_grad.shape, 0)
        tail = back[(s + 1) * size - 16 : (s + 1) * size, :size]
        both = jnp.where(row == 14, grad_high, gate_grad - grad_high)
        d_o[s, size - 16 :, :size] = jnp.where(row < 14, tail, both).astype(BF)


def expert_call(x, c, arrays, places, b_in, b_out, half, halves, before):
    experts, _, size, width = x.shape
    parts, _, piece = b_in.shape
    n = max(1, 256 // size)
    steps = experts // n
    rows, hidden = n * size, parts * piece
    before = list(before)
    tall = lambda cols: pl.BlockSpec((rows, cols), lambda i: (half * steps + i, 0))
    of_half = pl.BlockSpec((n, 1, size, width), lambda i: (i, half, 0, 0))
    total = halves * experts * size
    return pl.pallas_call(
        functools.partial(expert_kernel, places, len(arrays), len(before)),
        grid=(steps,),
        in_specs=[
            pl.BlockSpec((n, 1, size, width), lambda i: (i, 0, 0, 0)),
            of_half,
            whole((parts, 8, piece)),
            whole((8, width)),
        ]
        + [ANY] * (len(arrays) + len(before)),
        out_specs=[
            tall(hidden),
            tall(hidden),
            tall(width),
            tall(width),
            of_half,
            pl.BlockSpec((n, size, width), lambda i: (i, 0, 0)),
            whole((parts, 8, piece)),
            whole((8, width)),
        ],
        out_shape=[
            jax.ShapeDtypeStruct((total, hidden), BF),
            jax.ShapeDtypeStruct((total, hidden), BF),
            jax.ShapeDtypeStruct((total, width), BF),
            jax.ShapeDtypeStruct((total, width), BF),
            jax.ShapeDtypeStruct((experts, halves, size, width), BF),
            jax.ShapeDtypeStruct((experts, size, width), BF),
            jax.ShapeDtypeStruct((parts, 8, piece), F32),
            jax.ShapeDtypeStruct((8, width), F32),
        ],
        scratch_shapes=[
            pltpu.VMEM((width, hidden), BF),
            pltpu.VMEM((hidden, width), BF),
            pltpu.SemaphoreType.DMA((2 * parts,)),
        ],
        input_output_aliases={4 + len(arrays) + i: i for i in range(len(before))},
        compiler_params=params(44),
        cost_estimate=SMALL,
        name="expert_" + "ab"[half],
    )(x, c, b_in, b_out, *arrays, *before)


def weight_kernel(x, pre, act, grad, bias, in_o, out_o, in_acc, out_acc):
    step = pl.program_id(0)
    width = x.shape[1]
    first, second = t_dot(x[...], pre[...]), t_dot(act[...], grad[...])

    @pl.when(step == 0)
    def _():
        in_acc[...] = first
        out_acc[...] = second

    @pl.when(step > 0)
    def _():
        in_acc[...] += first
        out_acc[...] += second

    @pl.when(step == pl.num_programs(0) - 1)
    def _():
        in_o[:width, :] = in_acc[...].astype(in_o.dtype)
        in_o[width:, :] = bias[0].astype(in_o.dtype)
        out_o[...] = out_acc[...].astype(out_o.dtype)


def weight_grads(x, pre, act, grad, bias, piece, q_in, q_out, kind):
    total, width = x.shape
    rows = total // 2
    plain = pl.BlockSpec((rows, width), lambda k: (k, 0))
    return pl.pallas_call(
        weight_kernel,
        grid=(total // rows,),
        in_specs=[
            plain,
            pl.BlockSpec((rows, piece), lambda k: (k, q_in)),
            pl.BlockSpec((rows, piece), lambda k: (k, q_out)),
            plain,
            pl.BlockSpec((1, 16, piece), lambda k: (q_in, 0, 0)),
        ],
        out_specs=[whole((width + 16, piece)), whole((piece, width))],
        out_shape=[
            jax.ShapeDtypeStruct((width + 16, piece), kind),
            jax.ShapeDtypeStruct((piece, width), kind),
        ],
        scratch_shapes=[pltpu.VMEM((width, piece), F32), pltpu.VMEM((piece, width), F32)],
        compiler_params=params(60),
        cost_estimate=SMALL,
        name="weight_grads",
    )(x, pre, act, grad, bias)


def backward_kernel(experts, n, split, off, count, slots, cot, n1_far, qkv, att_far, aa, n2, probs_in, w_far, w_out, small, *refs):
    backs = refs[:n]
    ag_o, gp_o, dq_o = refs[n : n + 3]
    grads = refs[n + 3 : n + 3 + split]
    dw, ds, marks, ag_all, dq_all, n1, att, w, sems = refs[n + 3 + split :]
    img = pl.program_id(0)
    width = n1.shape[-1]
    late = [
        pltpu.make_async_copy(far, here, sems.at[k])
        for k, (far, here) in enumerate(((n1_far, n1), (att_far, att), (w_far, w)))
    ]
    size = backs[0].shape[1]
    total = experts * size

    @pl.when(img == 0)
    def _():
        for c in late:
            c.start()
        ds[...] = jnp.zeros_like(ds)
        line = iota((LANES, size), 0)
        for h in range(n):
            for e in range(experts):
                ends = backs[h][e, size - 16 :, :size].astype(F32)
                for k in range(2):
                    marks[2 * h + k, :, e * size : (e + 1) * size] = jnp.where(
                        line == e, ends[14 + k : 15 + k, :], 0.0
                    ).astype(BF)

    def vec(k):
        return small[experts + k : experts + k + 1, :]

    def add_vec(k, value):
        ds[experts + k : experts + k + 1, :] += value

    alive = (img < count[0]).astype(F32)
    up = cot[0].astype(F32)
    rows = up.shape[0]
    normed = n2[0]
    lane = iota((rows, LANES), 1)
    router = jnp.where(iota(small.shape, 0) < experts, small[...], 0.0).astype(BF)
    logits = jnp.where(lane < experts, dot_t(normed, router), NEG_FILL)
    exps = jnp.exp(logits - jnp.max(logits, axis=-1, keepdims=True))
    probs = exps / jnp.sum(exps, axis=-1, keepdims=True)
    gp_o[0] = probs
    first, second = slots[0, :, 0:1], slots[0, :, 1:2]
    normed_grad = jnp.zeros((rows, width), F32)
    placed = jnp.zeros((rows, LANES), F32)
    for h in range(n):
        place = iota((rows, total), 1) + h * total
        hot = ((place == first) | (place == second)).astype(BF)
        normed_grad = normed_grad + dot(hot, backs[h][...].reshape(total, width))
        placed = placed + dot_t(hot, marks[2 * h]) + dot_t(hot, marks[2 * h + 1])
    logit_grad = (
        probs * (placed - jnp.sum(probs * placed, axis=-1, keepdims=True))
    ).astype(BF)
    normed_grad = normed_grad + dot(logit_grad, router)
    ds[...] += jnp.where(iota(ds.shape, 0) < experts, t_dot(logit_grad, normed), 0.0)
    unit, inverse = norm_stats(aa[0])
    add_vec(3, col_sum(normed_grad * unit))
    add_vec(4, col_sum(normed_grad))
    after_grad = up + norm_back(unit, inverse, vec(3), normed_grad)
    attn_grad = (alive * after_grad).astype(BF)
    add_vec(2, col_sum(attn_grad.astype(F32)))
    ag_all[img] = attn_grad
    att_grad = dot_t(attn_grad, w_out[...]).astype(BF)
    low = lane < LANES // 2
    scale = (width // HEADS) ** -0.5
    for pair in range(HEADS // 2):
        c = pair * LANES
        q2 = qkv[0, :, c : c + LANES]
        k2 = qkv[0, :, width + c : width + c + LANES]
        v2 = qkv[0, :, 2 * width + c : 2 * width + c + LANES]
        o2 = att_grad[:, c : c + LANES]
        got = []
        for side, mask in enumerate((low, ~low)):
            prob = probs_in[0, 2 * pair + side]
            prob_grad = dot_t(v2, jnp.where(mask, o2, jnp.zeros_like(o2)))
            score_grad = (prob * (prob_grad - col_sum(prob * prob_grad))).astype(BF)
            got.append(
                (
                    t_dot(score_grad, k2) * scale,
                    dot(score_grad, q2) * scale,
                    dot(prob.astype(BF), o2),
                )
            )
        for k in range(3):
            dq_o[0, :, k * width + c : k * width + c + LANES] = jnp.where(
                low, got[0][k], got[1][k]
            ).astype(BF)
    grad = dq_o[0]
    dq_all[img] = grad
    for k in range(3):
        ds[experts + 5 + k : experts + 6 + k, :] += col_sum(grad[:, k * width : (k + 1) * width].astype(F32))
    ag_o[0] = after_grad

    @pl.when(img == pl.num_programs(0) - 1)
    def _():
        dw[:, 4 * width : 4 * width + LANES] = jnp.transpose(ds[...])
        for c in late:
            c.wait()
        left = n1[...].reshape(-1, width)
        for k in range(3):
            cols = slice(k * width, (k + 1) * width)
            dw[:, cols] = t_dot(left, dq_all[:, :, cols].reshape(-1, width))
        dw[:, 3 * width : 4 * width] = t_dot(
            att[...].reshape(-1, width), ag_all[...].reshape(-1, width)
        )
        with_weight = jnp.zeros((width, LANES), F32)
        with_sums = jnp.zeros((width, LANES), F32)
        for k in range(3 * width // LANES):
            cols = slice(k * LANES, (k + 1) * LANES)
            part, at = divmod(k * LANES, width)
            value = w[:, cols].astype(F32)
            sums = ds[experts + 5 + part : experts + 6 + part, at : at + LANES]
            with_weight = with_weight + value * dw[:, cols]
            with_sums = with_sums + value * sums
        sums = jnp.sum(with_sums, axis=1, keepdims=True)
        at = 4 * width
        sides = w[:, at : at + LANES].astype(F32)
        gain, shift = sides[:, experts : experts + 1], sides[:, experts + 1 : experts + 2]
        gains = (jnp.sum(with_weight, axis=1, keepdims=True) - shift * sums) / gain
        spot = iota((width, LANES), 1)
        cols = slice(at, at + LANES)
        dw[:, cols] = jnp.where(
            spot == experts, gains, jnp.where(spot == experts + 1, sums, dw[:, cols])
        )
        if split == 1:
            grads[0][...] = dw[...].astype(BF)
        else:
            cols = grads[0].shape[1]
            step = width // 16
            for h in range(2):
                col = pl.multiple_of(off[16 + h], LANES)
                for r in range(16):
                    row = pl.multiple_of(off[r], 16)
                    grads[h][r * step : (r + 1) * step, :] = dw[
                        pl.ds(row, step), pl.ds(col, cols)
                    ].astype(BF)


def backward(off, count, slots, cot, n1, qkv, att, aa, n2, prob, w, small, backs, experts, split):
    images, rows, width = cot.shape
    width_all = w.shape[1]
    n = len(backs)
    block = lambda cols: pl.BlockSpec((1, rows, cols), lambda i: (i, 0, 0))
    got = pl.pallas_call(
        functools.partial(backward_kernel, experts, n, split),
        grid=(images,),
        in_specs=[SMEM, SMEM, block(2), block(width), ANY, block(3 * width), ANY, block(width), block(width)]
        + [pl.BlockSpec((1, HEADS, rows, rows), lambda i: (i, 0, 0, 0))]
        + [ANY, pl.BlockSpec((width, width), lambda i: (0, 3), pipeline_mode=pl.Buffered(1)), whole(small.shape)]
        + [whole(backs[0].shape)] * n,
        out_specs=[block(width), block(LANES), block(3 * width)] + [whole((width, width_all // split))] * split,
        out_shape=[
            jax.ShapeDtypeStruct((images, rows, width), F32),
            jax.ShapeDtypeStruct((images, rows, LANES), F32),
            jax.ShapeDtypeStruct((images, rows, 3 * width), BF),
        ]
        + [jax.ShapeDtypeStruct((width, width_all // split), BF)] * split,
        scratch_shapes=[
            pltpu.VMEM((width, width_all), F32),
            pltpu.VMEM((LANES, width), F32),
            pltpu.VMEM((2 * n, LANES, backs[0].shape[0] * backs[0].shape[1]), BF),
            pltpu.VMEM((images, rows, width), BF),
            pltpu.VMEM((images, rows, 3 * width), BF),
            pltpu.VMEM((images, rows, width), BF),
            pltpu.VMEM((images, rows, width), BF),
            pltpu.VMEM(w.shape, BF),
            pltpu.SemaphoreType.DMA((3,)),
        ],
        compiler_params=params(),
        cost_estimate=SMALL,
        name="tokens_backward",
    )(off, count, slots, cot, n1, qkv, att, aa, n2, prob, w, w, small, *backs)
    return got[0], got[1], got[2], got[3:]


def finish_kernel(experts, after_grad, grad, tok, w, small, out):
    width = tok.shape[-1]
    normed_grad = dot_t(grad[0], w[...])
    unit, inverse = norm_stats(tok[0].astype(F32))
    out[0] = after_grad[0] + norm_back(unit, inverse, small[experts : experts + 1, :], normed_grad)


def finish(after_grad, grad, tok, w, small, experts):
    images, rows, width = tok.shape
    block = lambda cols: pl.BlockSpec((1, rows, cols), lambda i: (i, 0, 0))
    return pl.pallas_call(
        functools.partial(finish_kernel, experts),
        grid=(images,),
        in_specs=[block(width), block(3 * width), block(width), whole((width, 3 * width)), whole(small.shape)],
        out_specs=block(width),
        out_shape=jax.ShapeDtypeStruct((images, rows, width), F32),
        compiler_params=params(60),
        cost_estimate=SMALL,
        name="tokens_finish",
    )(after_grad, grad, tok, w, small)


def output_kernel(count, slots, aa, probs, outs, out):
    rows = aa.shape[1]
    experts, n, size, width = outs.shape
    total = experts * size
    alive = (pl.program_id(0) < count[0]).astype(F32)
    first, second = slots[0, :, 0:1], slots[0, :, 1:2]
    gates = jnp.concatenate(
        [jnp.broadcast_to(probs[0, :, e : e + 1], (rows, size)) for e in range(experts)], axis=1
    )
    moe = jnp.zeros(aa.shape[1:], F32)
    for h in range(n):
        place = iota((rows, total), 1) + h * total
        gate = jnp.where((place == first) | (place == second), gates, 0.0)
        high = gate.astype(BF)
        low = (gate - high.astype(F32)).astype(BF)
        value = outs[:, h].reshape(total, width)
        moe = moe + dot(high, value) + dot(low, value)
    out[0] = (aa[0] + alive * moe).astype(BF)


def block_output(count, slots, aa, probs, outs):
    images, rows, width = aa.shape
    block = lambda cols: pl.BlockSpec((1, rows, cols), lambda i: (i, 0, 0))
    return pl.pallas_call(
        output_kernel,
        grid=(images,),
        in_specs=[SMEM, block(2), block(width), block(LANES), whole(outs.shape)],
        out_specs=block(width),
        out_shape=jax.ShapeDtypeStruct((images, rows, width), BF),
        compiler_params=params(60),
        cost_estimate=SMALL,
        name="block_output",
    )(count, slots, aa, probs, outs)


def local(sizes, *args):
    (tokens, image_count, routes, capacity, ln1_gain, ln1_bias, qkv_weight, qv_bias, out_weight, out_bias,
     ln2_gain, ln2_bias, router_weight, expert_in, expert_in_bias, expert_out, expert_out_bias, cotangent) = args
    dp, experts = sizes
    grouped = sizes == (4, 8)
    devices = dp * experts
    me_d = lax.axis_index("dp")
    me_e = lax.axis_index("expert")
    core = me_e % 2
    token_count, width = tokens.shape
    images = token_count // SEQ
    rows = up16(SEQ)
    cap = max(2, 5 * token_count // (2 * experts))
    halves = 2 if grouped else 1
    half_cap = -(-cap // halves)
    block_rows = up16(half_cap + 2)

    def hop(value, mask):
        return lax.ppermute(value, BOTH, [(i, i ^ mask) for i in range(devices)])

    def by_image(value):
        value = value.reshape(images, SEQ, value.shape[-1])
        fill = -1 if value.dtype == jnp.int32 else 0
        return jnp.pad(value, ((0, 0), (0, rows - SEQ), (0, 0)), constant_values=fill)

    def from_image(value):
        return value[:, :SEQ].reshape(token_count, value.shape[-1])

    def side_rows(values):
        return functools.reduce(
            lambda a, b: a + b,
            [jnp.pad(v.astype(F32)[None], ((k, 7 - k), (0, 0))) for k, v in enumerate(values)],
        )

    def slots_and_blocks(value):
        return first_dispatch(image_count, capacity, routes.T, value, half_cap, block_rows, halves)

    def slot_forms(slots):
        slots = slots.reshape(2, images, SEQ)
        slots = jnp.pad(slots, ((0, 0), (0, 0), (0, rows - SEQ)), constant_values=-1)
        return slots.transpose(1, 2, 0), slots.reshape(2, -1)

    def after(values, *done):
        return lax.optimization_barrier((values, done))[0]

    tok = by_image(tokens)

    vectors = [ln1_gain, ln1_bias, out_bias, ln2_gain, ln2_bias]
    width_all = 4 * width + 2 * LANES
    wide = expert_in.shape[2]
    spot = me_d * expert_out_bias.shape[1]
    if grouped:
        half = width_all // 2
        mine, other = pack_dense(
            core.reshape(1).astype(jnp.int32), qkv_weight, out_weight, router_weight.T, side_rows(vectors), qv_bias
        )
        got = hop(other, 1)
        chip = jnp.where(
            core == 0, jnp.concatenate([mine, got], axis=0), jnp.concatenate([got, mine], axis=0)
        )
        bias_out = lax.dynamic_update_slice(jnp.zeros((1, width), BF), expert_out_bias, (0, spot))
        bias = jnp.concatenate([expert_in_bias, bias_out, jnp.zeros((14, wide), BF)], axis=0)
        one = jnp.concatenate([expert_in[0], bias], axis=0)
        two = jnp.concatenate([expert_out[0], bias], axis=0)
        from_x, from_y = hop(expert_in[0], 8), hop(expert_out[0], 16)
        cot_blocks, slots = slots_and_blocks(after(cotangent, chip))
        slots_col, slots_row = slot_forms(slots)
        line = jnp.concatenate([chip] + [hop(chip, 2 * dz) for dz in (1, 2, 3)], axis=0)
        held, from_x, from_y = after((line, from_x, from_y))
        own = [line] + [hop(held, 8 * dxy) for dxy in (3, 1, 2)]
        own = [own[0], own[2], own[3], own[1]]
        step = width // 16
        at_rows = jnp.stack([((me_d ^ a) * 4 + ((me_e // 2) ^ b)) * step for a in range(4) for b in range(4)])
        at_cols = jnp.stack([core * half, (1 - core) * half])
        off_back = jnp.concatenate([at_rows, at_cols]).astype(jnp.int32)
        off = jnp.concatenate([at_rows, at_rows, jnp.repeat(at_cols, 4)]).astype(jnp.int32)
        own, tok, slots_row, off, one, two = after((own, tok, slots_row, off, one, two))
        pieces = own + [hop(piece, 1) for piece in own]
        subs = 4
        later_one, later_two, relay_x, relay_y = after((one, two, from_x, from_y), *own)
        near = hop(later_one, 16), hop(later_two, 8)
        relays = hop(relay_x, 16), hop(relay_y, 8), hop(near[0][width:], 8)
        arrays = [one, from_x, near[0], relays[0]]
        biases = [bias, near[1][width:], near[0][width:], relays[2]]
        b_in = jnp.stack([v[:8] for v in biases]).astype(F32)
        arrays += [two, near[1], from_y, relays[1]]
        places = tuple((q, 0) for q in range(8))
        b_out = jnp.broadcast_to(jnp.sum(b_in[:, 1], axis=0), (8, width))
        after_line = held
    else:
        fill = width_all - 4 * width - experts - 7
        pack = jnp.concatenate(
            [qkv_weight, out_weight, router_weight, jnp.stack(vectors, axis=1), qv_bias.T, jnp.zeros((ln1_gain.shape[0], fill), BF)], axis=1
        )
        pieces = [lax.all_gather(pack, BOTH, axis=0, tiled=True)]
        cot_blocks, slots = slots_and_blocks(cotangent)
        slots_col, slots_row = slot_forms(slots)
        off = jnp.zeros((2,), jnp.int32)
        off_back = off
        subs = 1
        after_line = pieces[0]
        w_in = lax.all_gather(expert_in[0], "dp", axis=0, tiled=False)
        w_out = lax.all_gather(expert_out[0], "dp", axis=0, tiled=False)
        arrays = [w[q] for w in (w_in, w_out) for q in range(dp)]
        places = tuple((q, 0) for q in range(2 * dp))
        b_in = lax.all_gather(jnp.broadcast_to(expert_in_bias, (8, wide)), "dp", axis=0, tiled=False).astype(F32)
        b_out = jnp.broadcast_to(
            lax.all_gather(expert_out_bias, "dp", axis=1, tiled=True).astype(F32), (8, width)
        )

    def exchange(blocks):
        return lax.all_to_all(blocks, "expert", 0, 0, tiled=True)

    cot_sent = exchange(after(cot_blocks, after_line))
    cot = by_image(cotangent)

    w, small, qkv, n1, att, aa, n2, prob = forward(off, subs, pieces, image_count, tok, experts, width_all)
    row_sent = []
    flat = n2.reshape(-1, width)
    for h in range(halves):
        sent = dispatch(slots_row, flat, small, experts, block_rows, h, 1, "ab"[h])
        waits = (near, relays)[h] if grouped else ()
        sent, cot_sent = after((sent, cot_sent), *row_sent, *waits)
        if h:
            sent, cot, slots_col = after((sent, cot, slots_col))
        row_sent.append(exchange(sent))

    back, grads_out, db_ins, db_outs, tall = [], [], [], [], ()
    for h in range(halves):
        *tall, d, db_in, db_out = expert_call(
            row_sent[h], cot_sent, arrays, places, b_in, b_out, h, halves, tall
        )
        grads_out.append(d)
        if h + 1 < halves:
            back.append(exchange(d))
        db_ins.append(db_in)
        db_outs.append(db_out)
    *tall, outs_back = tall
    db_in, db_out = sum(db_ins), sum(db_outs)

    both = [db_in[:, 0:1]]
    if grouped:
        both.append(jnp.broadcast_to(db_out[0:1], db_in[:, 0:1].shape))
    bias_sums = jnp.concatenate(
        [*both, jnp.zeros((dp, 16 - len(both), wide), F32)], axis=1
    )

    def weights_of(q_in, q_out, kind):
        act, pre, rows_in, slot_grad = tall
        return weight_grads(rows_in, pre, act, slot_grad, bias_sums, wide, q_in, q_out, kind)

    if grouped:
        far_in, far_out = weights_of(3, 3, BF)
        tall = after(tall, far_in, far_out, *back)
        back.append(exchange(after(grads_out[-1], far_in, far_out, *back)))
        far_in, far_out = hop(far_in, 8), hop(far_out, 16)
        near_in, near_out = weights_of(1, 2, BF)
        last_in, last_out = weights_of(2, 1, F32)
        last_in = (last_in + far_in.astype(F32)).astype(BF)
        last_out = (last_out + far_out.astype(F32)).astype(BF)
        ready = (near_in, near_out, last_in, last_out)
        near_in, near_out = hop(near_in, 8), hop(near_out, 16)
        last_in, last_out = hop(last_in, 16), hop(last_out, 8)
        arrived = (near_in, near_out, last_in, last_out)
    else:
        ready = arrived = ()
        scatter = lambda v: lax.psum_scatter(v, "dp", scatter_dimension=0, tiled=True).astype(F32)
        back.append(exchange(grads_out[-1]))
        every = [weights_of(q, q, BF) for q in range(dp)]
        g_in = scatter(jnp.stack([e[0][:width] for e in every]))
        g_out = scatter(jnp.stack([e[1] for e in every]))
        g_b_in = lax.psum_scatter(
            db_in[:, 0].reshape(1, -1).astype(BF), "dp", scatter_dimension=1, tiled=True
        ).astype(F32)
        g_b_out = lax.psum_scatter(db_out[0:1].astype(BF), "dp", scatter_dimension=1, tiled=True).astype(F32)

    r_sent = exchange(after(outs_back, *back))
    back = after(back, *ready)
    after_grad, probs, grad, grads = backward(
        off_back, image_count, slots_col, cot, n1, qkv, att, aa, n2, prob, w, small, back, experts,
        2 if grouped else 1,
    )
    grads = after(grads, *arrived)
    block_out = from_image(block_output(image_count, slots_col, aa, probs, r_sent))
    def add(*values):
        return functools.reduce(lambda a, b: a + b, [v.astype(F32) for v in values])

    if grouped:
        sibling = hop(grads[1], 1)
        quarter = width // 4
        ways = [slice(a * quarter, (a + 1) * quarter) for a in range(4)]
        ways = [add(grads[0][a], sibling[a]).astype(BF) for a in ways]
        tall, bias_sums = after((tall, bias_sums), *ways)
        own_in, own_out = weights_of(0, 0, F32)
        g_in = own_in + near_in.astype(F32) + last_in.astype(F32)
        g_in, g_bias = g_in[None, :width], g_in[width:]
        g_out = (own_out + near_out.astype(F32) + last_out.astype(F32))[None]
        g_b_in = g_bias[0:1]
        g_b_out = lax.dynamic_slice(g_bias[1:2], (0, spot), expert_out_bias.shape)
        after_grad, grad = after((after_grad, grad), own_in, own_out)
    tokens_grad = from_image(finish(after_grad, grad, tok, w, small, experts))

    if grouped:
        ways[0], tokens_grad, g_in, g_out = after((ways[0], tokens_grad, g_in, g_out))
        line = add(ways[0], *[hop(ways[a], 8 * a) for a in (1, 2, 3)]).astype(BF)
        line, r_sent = after((line, r_sent))
        step = width // 16
        cuts = [line[b * step : (b + 1) * step] for b in range(4)]
        chip = add(cuts[0], *[hop(cuts[b], 2 * b) for b in (1, 2, 3)])
        n_rows = step // 2
        keep = lax.dynamic_slice_in_dim(chip, core * n_rows, n_rows, 0)
        chip, block_out = after((chip, block_out))
        give = lax.dynamic_slice_in_dim(chip, (1 - core) * n_rows, n_rows, 0)
        got = hop(give.astype(BF), 1).astype(F32)
        dense = jnp.where(
            core == 0, jnp.concatenate([keep, got], axis=1), jnp.concatenate([got, keep], axis=1)
        )
    else:
        dense = lax.psum_scatter(grads[0], BOTH, scatter_dimension=0, tiled=True).astype(F32)
    side = dense[:, 4 * width :]
    vecs = [side[:, experts + k] for k in range(8)]
    return (
        block_out,
        tokens_grad,
        vecs[0],
        vecs[1],
        dense[:, : 3 * width],
        jnp.stack([vecs[5], vecs[7]], axis=0),
        dense[:, 3 * width : 4 * width],
        vecs[2],
        vecs[3],
        vecs[4],
        side[:, :experts],
        g_in,
        g_b_in,
        g_out,
        g_b_out,
    )


def solution(mesh):
    rows, line, cols = P(BOTH, None), P(BOTH), P(None, BOTH)
    experts = (P("expert", None, "dp"), P("expert", "dp"), P("expert", "dp", None), P("expert", "dp"))
    dense = (line, line, rows, cols, rows, line, line, line, rows)
    return jax.shard_map(
        functools.partial(local, (mesh.shape["dp"], mesh.shape["expert"])),
        mesh=mesh,
        in_specs=(rows, line, rows, P(), *dense, *experts, rows),
        out_specs=(rows, rows, *dense, *experts),
        check_vma=False,
    )
```

```python
import functools

import jax
import jax.numpy as jnp
from jax import lax
from jax.experimental import pallas as pl
from jax.experimental.pallas import tpu as pltpu
from jax.sharding import PartitionSpec as P

HEADS = 12
SEQ = 197
EPS_NORM = 1e-06
NEG_FILL = -1e30
BF = jnp.bfloat16
F32 = jnp.float32
LANES = 128
GELU_A = 0.7978845608028654
GELU_B = 0.044715
BOTH = ("dp", "expert")


def up16(n):
    return -(-n // 16) * 16


def dot(left, right):
    return jnp.dot(left, right, preferred_element_type=F32)


def dot_t(left, right):
    return lax.dot_general(left, right, (((1,), (1,)), ((), ())), preferred_element_type=F32)


def t_dot(left, right):
    return lax.dot_general(left, right, (((0,), (0,)), ((), ())), preferred_element_type=F32)


def iota(shape, dim):
    return lax.broadcasted_iota(jnp.int32, shape, dim)


def params(mib=60):
    return pltpu.CompilerParams(vmem_limit_bytes=mib << 20)


def whole(shape):
    zeros = (0,) * len(shape)
    return pl.BlockSpec(shape, lambda *_: zeros, pipeline_mode=pl.Buffered(1))


SMALL = pl.CostEstimate(flops=1 << 20, bytes_accessed=1 << 16, transcendentals=0)
LARGE = pl.CostEstimate(flops=1 << 34, bytes_accessed=1 << 16, transcendentals=0)
SMEM = pl.BlockSpec(memory_space=pltpu.SMEM)
ANY = pl.BlockSpec(memory_space=pl.ANY)


def norm_stats(values):
    centered = values - jnp.mean(values, axis=-1, keepdims=True)
    inverse = lax.rsqrt(jnp.mean(centered * centered, axis=-1, keepdims=True) + EPS_NORM)
    return centered * inverse, inverse


def norm_back(unit, inverse, gain, grad):
    scaled = grad * gain
    mean_one = jnp.mean(scaled, axis=-1, keepdims=True)
    mean_two = jnp.mean(scaled * unit, axis=-1, keepdims=True)
    return inverse * (scaled - mean_one - unit * mean_two)


def col_sum(values):
    return jnp.sum(values, axis=0, keepdims=True)


def pack_kernel(core, qkv, out, router, vectors, pair, mine, other):
    rows = qkv.shape[0]
    eye = (iota((rows, rows), 0) == iota((rows, rows), 1)).astype(BF)
    turned = [dot_t(eye, router[...]), dot_t(eye, vectors[...].astype(BF))[:, :5], dot_t(eye, pair[...])]
    used = sum(t.shape[1] for t in turned)
    turned = jnp.concatenate([*turned, jnp.zeros((rows, 2 * LANES - used), F32)], axis=1)
    value = jnp.concatenate([qkv[...], out[...], turned.astype(BF)], axis=1)
    half = value.shape[1] // 2

    @pl.when(core[0] == 0)
    def _():
        mine[...] = value[:, :half]
        other[...] = value[:, half:]

    @pl.when(core[0] != 0)
    def _():
        mine[...] = value[:, half:]
        other[...] = value[:, :half]


def pack_dense(core, qkv, out, router, vectors, pair):
    rows = qkv.shape[0]
    half = (qkv.shape[1] + out.shape[1] + 2 * LANES) // 2
    vmem = pl.BlockSpec(memory_space=pltpu.VMEM)
    return pl.pallas_call(
        pack_kernel,
        in_specs=[SMEM] + [vmem] * 5,
        out_specs=[vmem] * 2,
        out_shape=[jax.ShapeDtypeStruct((rows, half), BF)] * 2,
        compiler_params=params(60),
        cost_estimate=LARGE,
        name="pack_dense",
    )(core, qkv, out, router, vectors, pair)


def forward_kernel(experts, subs, off, count, tok, *refs):
    n_pieces = len(refs) - 10
    pieces = refs[:n_pieces]
    w_o, small, qkv_o, n1_o, att_o, aa_o, n2_o, prob_o, w, sems = refs[n_pieces:]
    img = pl.program_id(0)
    width = tok.shape[-1]

    @pl.when(img == 0)
    def _():
        copies = []
        for i, piece in enumerate(pieces):
            rows, cols = piece.shape[0] // subs, piece.shape[1]
            col = pl.multiple_of(off[n_pieces * subs + i], LANES)
            for j in range(subs):
                row = pl.multiple_of(off[i * subs + j], 16)
                copies.append(
                    pltpu.make_async_copy(
                        piece.at[pl.ds(j * rows, rows), :],
                        w.at[pl.ds(row, rows), pl.ds(col, cols)],
                        sems.at[i * subs + j],
                    )
                )
        for c in copies:
            c.start()
        for c in copies:
            c.wait()
        small[...] = jnp.transpose(w[:, 4 * width : 4 * width + LANES].astype(F32))
        pltpu.make_async_copy(w, w_o, sems.at[0]).start()

    def vec(k):
        return small[experts + k : experts + k + 1, :]

    x = tok[0].astype(F32)
    rows = x.shape[0]
    unit, _ = norm_stats(x)
    n1 = (unit * vec(0) + vec(1)).astype(BF)
    n1_o[0] = n1
    biases = (vec(5), None, vec(6))
    for part in range(3):
        cols = slice(part * width, (part + 1) * width)
        block = dot(n1, w[:, cols])
        if biases[part] is not None:
            block = block + biases[part]
        qkv_o[0, :, cols] = block.astype(BF)
    low = iota((rows, LANES), 1) < LANES // 2
    seen = iota((rows, rows), 0) < SEQ
    scale = (width // HEADS) ** -0.5
    for pair in range(HEADS // 2):
        c = pair * LANES
        q2 = qkv_o[0, :, c : c + LANES]
        k2 = qkv_o[0, :, width + c : width + c + LANES]
        v2 = qkv_o[0, :, 2 * width + c : 2 * width + c + LANES]
        got = []
        for side, mask in enumerate((low, ~low)):
            scores = dot_t(k2, jnp.where(mask, q2, jnp.zeros_like(q2))) * scale
            scores = jnp.where(seen, scores, NEG_FILL)
            exps = jnp.exp(scores - jnp.max(scores, axis=0, keepdims=True))
            prob = exps * (1.0 / col_sum(exps))
            prob_o[0, 2 * pair + side] = prob
            got.append(t_dot(prob.astype(BF), v2))
        att_o[0, :, c : c + LANES] = jnp.where(low, got[0], got[1]).astype(BF)
    alive = (img < count[0]).astype(F32)
    after = x + alive * (dot(att_o[0], w[:, 3 * width : 4 * width]) + vec(2))
    aa_o[0] = after
    unit, _ = norm_stats(after)
    n2_o[0] = (unit * vec(3) + vec(4)).astype(BF)

    @pl.when(img == pl.num_programs(0) - 1)
    def _():
        pltpu.make_async_copy(w, w_o, sems.at[0]).wait()


def forward(off, subs, pieces, count, tok, experts, width_all):
    images, rows, width = tok.shape
    block = lambda cols: pl.BlockSpec((1, rows, cols), lambda i: (i, 0, 0))
    shape = lambda cols, t: jax.ShapeDtypeStruct((images, rows, cols), t)
    return pl.pallas_call(
        functools.partial(forward_kernel, experts, subs),
        grid=(images,),
        in_specs=[SMEM, SMEM, block(width)] + [ANY] * len(pieces),
        out_specs=[
            ANY,
            whole((LANES, width)),
            block(3 * width),
            block(width),
            block(width),
            block(width),
            block(width),
            pl.BlockSpec((1, HEADS, rows, rows), lambda i: (i, 0, 0, 0)),
        ],
        out_shape=[
            jax.ShapeDtypeStruct((width, width_all), BF),
            jax.ShapeDtypeStruct((LANES, width), F32),
            shape(3 * width, BF),
            shape(width, BF),
            shape(width, BF),
            shape(width, F32),
            shape(width, BF),
            jax.ShapeDtypeStruct((images, HEADS, rows, rows), F32),
        ],
        scratch_shapes=[
            pltpu.VMEM((width, width_all), BF),
            pltpu.SemaphoreType.DMA((len(pieces) * subs,)),
        ],
        compiler_params=params(60),
        cost_estimate=SMALL,
        name="tokens_forward",
    )(off, count, tok, *pieces)


def dispatch_kernel(experts, half, gated, slots, x, *refs):
    out = refs[-1]
    value = x[...]
    halves, block_rows = out.shape[1:3]
    first, second = slots[0:1, :], slots[1:2, :]
    if gated:
        router = refs[0][...].astype(BF)
        logits = dot_t(router, value)
        logits = jnp.where(iota(logits.shape, 0) < experts, logits, NEG_FILL)
        exps = jnp.exp(logits - jnp.max(logits, axis=0, keepdims=True))
        probs = exps / jnp.sum(exps, axis=0, keepdims=True)
    total = experts * block_rows
    for h in range(halves):
        place = iota((total, value.shape[0]), 0) + (half + h) * total
        hot = ((place == first) | (place == second)).astype(BF)
        out[:, h] = dot(hot, value).astype(BF).reshape(experts, block_rows, value.shape[1])
        if gated:
            row = iota((16, value.shape[0]), 0)
            for e in range(experts):
                gate = probs[e : e + 1, :]
                high = gate.astype(BF).astype(F32)
                pair = jnp.where(row == 14, high, jnp.where(row == 15, gate - high, 0.0))
                placed = dot_t(pair.astype(BF), hot[e * block_rows : (e + 1) * block_rows])
                tail = out[e, h, block_rows - 16 :, :block_rows].astype(F32)
                out[e, h, block_rows - 16 :, :block_rows] = jnp.where(
                    iota(tail.shape, 0) < 14, tail, placed
                ).astype(BF)


def dispatch(slots, x, small, experts, block_rows, half, halves, tag):
    rows, width = x.shape
    gated = small is not None
    more = [small] if gated else []
    vmem = pl.BlockSpec(memory_space=pltpu.VMEM)
    return pl.pallas_call(
        functools.partial(dispatch_kernel, experts, half, gated),
        in_specs=[vmem] * (2 + len(more)),
        out_specs=vmem,
        out_shape=jax.ShapeDtypeStruct((experts, halves, block_rows, width), BF),
        compiler_params=params(24),
        cost_estimate=SMALL,
        name="dispatch_" + tag,
    )(slots, x, *more)


def first_kernel(experts, half_cap, count, capacity, routes, x, out, slots):
    rows = routes.shape[1]
    halves, block_rows = out.shape[1:3]
    alive = iota((1, rows), 1) < count[0] * SEQ
    name = iota((up16(experts), rows), 0)
    earlier = (iota((rows, rows), 0) < iota((rows, rows), 1)).astype(BF)
    limits = jnp.zeros((up16(experts), 1), F32)
    for e in range(experts):
        limits = jnp.where(name[:, 0:1] == e, capacity[e].astype(F32), limits)
    base = 0.0
    for k in range(2):
        hit = jnp.where((routes[k : k + 1, :] == name) & alive, 1.0, 0.0)
        place = col_sum(hit * (dot(hit.astype(BF), earlier) + base))
        keep = place < col_sum(hit * limits)
        base = jnp.sum(hit, axis=1, keepdims=True)
        place = place.astype(jnp.int32)
        half = (place >= half_cap).astype(jnp.int32)
        spot = (half * experts + routes[k : k + 1, :]) * block_rows + place - half * half_cap
        slots[k : k + 1, :] = jnp.where(keep, spot, -1)
    dispatch_kernel(experts, 0, False, slots, x, out)


def first_dispatch(count, capacity, routes, x, half_cap, block_rows, halves):
    rows, width = x.shape
    experts = capacity.shape[0]
    vmem = pl.BlockSpec(memory_space=pltpu.VMEM)
    return pl.pallas_call(
        functools.partial(first_kernel, experts, half_cap),
        in_specs=[SMEM, SMEM, vmem, vmem],
        out_specs=[vmem, vmem],
        out_shape=[
            jax.ShapeDtypeStruct((experts, halves, block_rows, width), BF),
            jax.ShapeDtypeStruct((2, rows), jnp.int32),
        ],
        compiler_params=params(24),
        cost_estimate=SMALL,
        name="dispatch_first",
    )(count, capacity, routes, x)


def expert_kernel(places, n_arrays, n_before, *refs):
    x_ref, c_ref, b_in, b_out = refs[:4]
    arrays, parts = refs[4 : 4 + n_arrays], len(places) // 2
    rest = refs[4 + n_arrays + n_before :]
    act_o, pre_o, x_o, sg_o, r_o, d_o, db_in, db_out, win, wout, sems = rest
    step = pl.program_id(0)
    n, _, size, width = x_ref.shape
    piece = win.shape[1] // parts

    def copies(q):
        cols = pl.ds(q * piece, piece)
        (one, at_one), (two, at_two) = places[q], places[parts + q]
        return (
            pltpu.make_async_copy(
                arrays[one].at[pl.ds(at_one, width), :], win.at[:, cols], sems.at[q]
            ),
            pltpu.make_async_copy(
                arrays[two].at[pl.ds(at_two, piece), :], wout.at[cols, :], sems.at[parts + q]
            ),
        )

    @pl.when(step == 0)
    def _():
        for q in range(parts):
            for c in copies(q):
                c.start()
        db_in[...] = jnp.zeros_like(db_in)
        db_out[...] = jnp.zeros_like(db_out)

    eye = (iota((size, size), 0) == iota((size, size), 1)).astype(BF)
    for s in range(n):
        rows = slice(s * size, (s + 1) * size)
        x_o[rows, :] = x_ref[s, 0]
        turned = dot_t(eye, x_ref[s, 0, size - 16 :, :size])
        gate = jnp.sum(jnp.where(iota(turned.shape, 1) >= 14, turned, 0.0), axis=1, keepdims=True)
        sg_o[rows, :] = (gate * c_ref[s, 0].astype(F32)).astype(BF)
    x = x_o[...]
    slot_grad = sg_o[...]
    db_out[0:1, :] += col_sum(slot_grad.astype(F32))

    @pl.when(step == 0)
    def _():
        for q in range(parts):
            for c in copies(q):
                c.wait()

    for q in range(parts):
        cols = slice(q * piece, (q + 1) * piece)
        pre = dot(x, win[:, cols]) + b_in[q, 0:1, :]
        square = pre * pre
        turn = jnp.tanh(pre * (GELU_A + GELU_A * GELU_B * square))
        half_turn = 0.5 * turn + 0.5
        act_o[:, cols] = (pre * half_turn).astype(BF)
        slope = half_turn + (0.5 * pre) * (1.0 - turn * turn) * (GELU_A + 3 * GELU_A * GELU_B * square)
        pre_grad = dot_t(slot_grad, wout[cols, :]) * slope
        pre_o[:, cols] = pre_grad.astype(BF)
        db_in[q, 0:1, :] += col_sum(pre_grad)
    out = (dot(act_o[...], wout[...]) + b_out[0:1, :]).astype(BF)
    back = dot_t(pre_o[...], win[...])
    ones = jnp.ones((16, width), BF)
    for s in range(n):
        rows = slice(s * size, (s + 1) * size)
        r_o[s, 0] = out[rows]
        d_o[s] = back[rows].astype(BF)
        prod = c_ref[s, 0].astype(F32) * out[rows].astype(F32)
        high = prod.astype(BF)
        low = (prod - high.astype(F32)).astype(BF)
        gate_grad = dot_t(ones, high) + dot_t(ones, low)
        grad_high = gate_grad.astype(BF).astype(F32)
        row = iota(gate_grad.shape, 0)
        tail = back[(s + 1) * size - 16 : (s + 1) * size, :size]
        both = jnp.where(row == 14, grad_high, gate_grad - grad_high)
        d_o[s, size - 16 :, :size] = jnp.where(row < 14, tail, both).astype(BF)


def expert_call(x, c, arrays, places, b_in, b_out, half, halves, before):
    experts, _, size, width = x.shape
    parts, _, piece = b_in.shape
    n = max(1, 256 // size)
    steps = experts // n
    rows, hidden = n * size, parts * piece
    before = list(before)
    tall = lambda cols: pl.BlockSpec((rows, cols), lambda i: (half * steps + i, 0))
    of_half = pl.BlockSpec((n, 1, size, width), lambda i: (i, half, 0, 0))
    total = halves * experts * size
    return pl.pallas_call(
        functools.partial(expert_kernel, places, len(arrays), len(before)),
        grid=(steps,),
        in_specs=[
            pl.BlockSpec((n, 1, size, width), lambda i: (i, 0, 0, 0)),
            of_half,
            whole((parts, 8, piece)),
            whole((8, width)),
        ]
        + [ANY] * (len(arrays) + len(before)),
        out_specs=[
            tall(hidden),
            tall(hidden),
            tall(width),
            tall(width),
            of_half,
            pl.BlockSpec((n, size, width), lambda i: (i, 0, 0)),
            whole((parts, 8, piece)),
            whole((8, width)),
        ],
        out_shape=[
            jax.ShapeDtypeStruct((total, hidden), BF),
            jax.ShapeDtypeStruct((total, hidden), BF),
            jax.ShapeDtypeStruct((total, width), BF),
            jax.ShapeDtypeStruct((total, width), BF),
            jax.ShapeDtypeStruct((experts, halves, size, width), BF),
            jax.ShapeDtypeStruct((experts, size, width), BF),
            jax.ShapeDtypeStruct((parts, 8, piece), F32),
            jax.ShapeDtypeStruct((8, width), F32),
        ],
        scratch_shapes=[
            pltpu.VMEM((width, hidden), BF),
            pltpu.VMEM((hidden, width), BF),
            pltpu.SemaphoreType.DMA((2 * parts,)),
        ],
        input_output_aliases={4 + len(arrays) + i: i for i in range(len(before))},
        compiler_params=params(44),
        cost_estimate=SMALL,
        name="expert_" + "ab"[half],
    )(x, c, b_in, b_out, *arrays, *before)


def weight_kernel(piece, q_in, q_out, x, pre, act, grad, bias, in_o, out_o, xs, ps, acts, gs, sems):
    width = x.shape[1]
    copies = [
        pltpu.make_async_copy(x, xs, sems.at[0]),
        pltpu.make_async_copy(pre.at[:, pl.ds(q_in * piece, piece)], ps, sems.at[1]),
        pltpu.make_async_copy(act.at[:, pl.ds(q_out * piece, piece)], acts, sems.at[2]),
        pltpu.make_async_copy(grad, gs, sems.at[3]),
    ]
    for c in copies:
        c.start()
    in_o[width:, :] = bias[q_in].astype(in_o.dtype)
    copies[0].wait()
    copies[1].wait()
    in_o[:width, :] = t_dot(xs[...], ps[...]).astype(in_o.dtype)
    copies[2].wait()
    copies[3].wait()
    out_o[...] = t_dot(acts[...], gs[...]).astype(out_o.dtype)


def weight_grads(x, pre, act, grad, bias, piece, q_in, q_out, kind):
    total, width = x.shape
    vmem = pl.BlockSpec(memory_space=pltpu.VMEM)
    return pl.pallas_call(
        functools.partial(weight_kernel, piece, q_in, q_out),
        in_specs=[ANY] * 4 + [vmem],
        out_specs=[vmem] * 2,
        out_shape=[
            jax.ShapeDtypeStruct((width + 16, piece), kind),
            jax.ShapeDtypeStruct((piece, width), kind),
        ],
        scratch_shapes=[
            pltpu.VMEM((total, width), BF),
            pltpu.VMEM((total, piece), BF),
            pltpu.VMEM((total, piece), BF),
            pltpu.VMEM((total, width), BF),
            pltpu.SemaphoreType.DMA((4,)),
        ],
        compiler_params=params(60),
        cost_estimate=SMALL,
        name="weight_grads",
    )(x, pre, act, grad, bias)


def backward_kernel(experts, n, split, off, count, slots, cot, n1_far, qkv, att_far, aa, n2, probs_in, w_far, w_out, small, *refs):
    backs = refs[:n]
    ag_o, gp_o, dq_o = refs[n : n + 3]
    grads = refs[n + 3 : n + 3 + split]
    dw, ds, marks, ag_all, dq_all, n1, att, w, sems = refs[n + 3 + split :]
    img = pl.program_id(0)
    width = n1.shape[-1]
    late = [
        pltpu.make_async_copy(far, here, sems.at[k])
        for k, (far, here) in enumerate(((n1_far, n1), (att_far, att), (w_far, w)))
    ]
    size = backs[0].shape[1]
    total = experts * size

    @pl.when(img == 0)
    def _():
        for c in late:
            c.start()
        ds[...] = jnp.zeros_like(ds)
        line = iota((LANES, size), 0)
        for h in range(n):
            for e in range(experts):
                ends = backs[h][e, size - 16 :, :size].astype(F32)
                for k in range(2):
                    marks[2 * h + k, :, e * size : (e + 1) * size] = jnp.where(
                        line == e, ends[14 + k : 15 + k, :], 0.0
                    ).astype(BF)

    def vec(k):
        return small[experts + k : experts + k + 1, :]

    def add_vec(k, value):
        ds[experts + k : experts + k + 1, :] += value

    alive = (img < count[0]).astype(F32)
    up = cot[0].astype(F32)
    rows = up.shape[0]
    normed = n2[0]
    lane = iota((rows, LANES), 1)
    router = jnp.where(iota(small.shape, 0) < experts, small[...], 0.0).astype(BF)
    logits = jnp.where(lane < experts, dot_t(normed, router), NEG_FILL)
    exps = jnp.exp(logits - jnp.max(logits, axis=-1, keepdims=True))
    probs = exps / jnp.sum(exps, axis=-1, keepdims=True)
    gp_o[0] = probs
    first, second = slots[0, :, 0:1], slots[0, :, 1:2]
    normed_grad = jnp.zeros((rows, width), F32)
    placed = jnp.zeros((rows, LANES), F32)
    for h in range(n):
        place = iota((rows, total), 1) + h * total
        hot = ((place == first) | (place == second)).astype(BF)
        normed_grad = normed_grad + dot(hot, backs[h][...].reshape(total, width))
        placed = placed + dot_t(hot, marks[2 * h]) + dot_t(hot, marks[2 * h + 1])
    logit_grad = (
        probs * (placed - jnp.sum(probs * placed, axis=-1, keepdims=True))
    ).astype(BF)
    normed_grad = normed_grad + dot(logit_grad, router)
    ds[...] += jnp.where(iota(ds.shape, 0) < experts, t_dot(logit_grad, normed), 0.0)
    unit, inverse = norm_stats(aa[0])
    add_vec(3, col_sum(normed_grad * unit))
    add_vec(4, col_sum(normed_grad))
    after_grad = up + norm_back(unit, inverse, vec(3), normed_grad)
    attn_grad = (alive * after_grad).astype(BF)
    add_vec(2, col_sum(attn_grad.astype(F32)))
    ag_all[img] = attn_grad
    att_grad = dot_t(attn_grad, w_out[...]).astype(BF)
    low = lane < LANES // 2
    scale = (width // HEADS) ** -0.5
    for pair in range(HEADS // 2):
        c = pair * LANES
        q2 = qkv[0, :, c : c + LANES]
        k2 = qkv[0, :, width + c : width + c + LANES]
        v2 = qkv[0, :, 2 * width + c : 2 * width + c + LANES]
        o2 = att_grad[:, c : c + LANES]
        got = []
        for side, mask in enumerate((low, ~low)):
            prob = probs_in[0, 2 * pair + side]
            prob_grad = dot_t(v2, jnp.where(mask, o2, jnp.zeros_like(o2)))
            score_grad = (prob * (prob_grad - col_sum(prob * prob_grad))).astype(BF)
            got.append(
                (
                    t_dot(score_grad, k2) * scale,
                    dot(score_grad, q2) * scale,
                    dot(prob.astype(BF), o2),
                )
            )
        for k in range(3):
            dq_o[0, :, k * width + c : k * width + c + LANES] = jnp.where(
                low, got[0][k], got[1][k]
            ).astype(BF)
    grad = dq_o[0]
    dq_all[img] = grad
    for k in range(3):
        ds[experts + 5 + k : experts + 6 + k, :] += col_sum(grad[:, k * width : (k + 1) * width].astype(F32))
    ag_o[0] = after_grad

    @pl.when(img == pl.num_programs(0) - 1)
    def _():
        dw[:, 4 * width : 4 * width + LANES] = jnp.transpose(ds[...])
        for c in late:
            c.wait()
        left = n1[...].reshape(-1, width)
        for k in range(3):
            cols = slice(k * width, (k + 1) * width)
            dw[:, cols] = t_dot(left, dq_all[:, :, cols].reshape(-1, width))
        dw[:, 3 * width : 4 * width] = t_dot(
            att[...].reshape(-1, width), ag_all[...].reshape(-1, width)
        )
        with_weight = jnp.zeros((width, LANES), F32)
        with_sums = jnp.zeros((width, LANES), F32)
        for k in range(3 * width // LANES):
            cols = slice(k * LANES, (k + 1) * LANES)
            part, at = divmod(k * LANES, width)
            value = w[:, cols].astype(F32)
            sums = ds[experts + 5 + part : experts + 6 + part, at : at + LANES]
            with_weight = with_weight + value * dw[:, cols]
            with_sums = with_sums + value * sums
        sums = jnp.sum(with_sums, axis=1, keepdims=True)
        at = 4 * width
        sides = w[:, at : at + LANES].astype(F32)
        gain, shift = sides[:, experts : experts + 1], sides[:, experts + 1 : experts + 2]
        gains = (jnp.sum(with_weight, axis=1, keepdims=True) - shift * sums) / gain
        spot = iota((width, LANES), 1)
        cols = slice(at, at + LANES)
        dw[:, cols] = jnp.where(
            spot == experts, gains, jnp.where(spot == experts + 1, sums, dw[:, cols])
        )
        if split == 1:
            grads[0][...] = dw[...].astype(BF)
        else:
            cols = grads[0].shape[1]
            step = width // 16
            for h in range(2):
                col = pl.multiple_of(off[16 + h], LANES)
                for r in range(16):
                    row = pl.multiple_of(off[r], 16)
                    grads[h][r * step : (r + 1) * step, :] = dw[
                        pl.ds(row, step), pl.ds(col, cols)
                    ].astype(BF)


def backward(off, count, slots, cot, n1, qkv, att, aa, n2, prob, w, small, backs, experts, split):
    images, rows, width = cot.shape
    width_all = w.shape[1]
    n = len(backs)
    block = lambda cols: pl.BlockSpec((1, rows, cols), lambda i: (i, 0, 0))
    got = pl.pallas_call(
        functools.partial(backward_kernel, experts, n, split),
        grid=(images,),
        in_specs=[SMEM, SMEM, block(2), block(width), ANY, block(3 * width), ANY, block(width), block(width)]
        + [pl.BlockSpec((1, HEADS, rows, rows), lambda i: (i, 0, 0, 0))]
        + [ANY, pl.BlockSpec((width, width), lambda i: (0, 3), pipeline_mode=pl.Buffered(1)), whole(small.shape)]
        + [whole(backs[0].shape)] * n,
        out_specs=[block(width), block(LANES), block(3 * width)] + [whole((width, width_all // split))] * split,
        out_shape=[
            jax.ShapeDtypeStruct((images, rows, width), F32),
            jax.ShapeDtypeStruct((images, rows, LANES), F32),
            jax.ShapeDtypeStruct((images, rows, 3 * width), BF),
        ]
        + [jax.ShapeDtypeStruct((width, width_all // split), BF)] * split,
        scratch_shapes=[
            pltpu.VMEM((width, width_all), F32),
            pltpu.VMEM((LANES, width), F32),
            pltpu.VMEM((2 * n, LANES, backs[0].shape[0] * backs[0].shape[1]), BF),
            pltpu.VMEM((images, rows, width), BF),
            pltpu.VMEM((images, rows, 3 * width), BF),
            pltpu.VMEM((images, rows, width), BF),
            pltpu.VMEM((images, rows, width), BF),
            pltpu.VMEM(w.shape, BF),
            pltpu.SemaphoreType.DMA((3,)),
        ],
        compiler_params=params(),
        cost_estimate=SMALL,
        name="tokens_backward",
    )(off, count, slots, cot, n1, qkv, att, aa, n2, prob, w, w, small, *backs)
    return got[0], got[1], got[2], got[3:]


def place_rows(out, value):
    for k in range(out.shape[0] // SEQ):

        @pl.when(pl.program_id(0) == k)
        def _():
            out[k * SEQ : (k + 1) * SEQ, :] = value[:SEQ]


def finish_kernel(experts, after_grad, grad, tok, w, small, out):
    width = tok.shape[-1]
    normed_grad = dot_t(grad[0], w[...])
    unit, inverse = norm_stats(tok[0].astype(F32))
    value = after_grad[0] + norm_back(unit, inverse, small[experts : experts + 1, :], normed_grad)
    place_rows(out, value)


def finish(after_grad, grad, tok, w, small, experts):
    images, rows, width = tok.shape
    block = lambda cols: pl.BlockSpec((1, rows, cols), lambda i: (i, 0, 0))
    return pl.pallas_call(
        functools.partial(finish_kernel, experts),
        grid=(images,),
        in_specs=[block(width), block(3 * width), block(width), whole((width, 3 * width)), whole(small.shape)],
        out_specs=whole((images * SEQ, width)),
        out_shape=jax.ShapeDtypeStruct((images * SEQ, width), F32),
        compiler_params=params(34),
        cost_estimate=SMALL,
        name="tokens_finish",
    )(after_grad, grad, tok, w, small)


def output_kernel(count, slots, aa, probs, outs, out, total_f):
    rows = aa.shape[1]
    experts, n, size, width = outs.shape
    total = experts * size
    alive = (pl.program_id(0) < count[0]).astype(F32)
    first, second = slots[0, :, 0:1], slots[0, :, 1:2]
    gates = jnp.concatenate(
        [jnp.broadcast_to(probs[0, :, e : e + 1], (rows, size)) for e in range(experts)], axis=1
    )
    moe = jnp.zeros(aa.shape[1:], F32)
    for h in range(n):
        place = iota((rows, total), 1) + h * total
        gate = jnp.where((place == first) | (place == second), gates, 0.0)
        high = gate.astype(BF)
        low = (gate - high.astype(F32)).astype(BF)
        value = outs[:, h].reshape(total, width)
        moe = moe + dot(high, value) + dot(low, value)
    place_rows(total_f, aa[0] + alive * moe)

    @pl.when(pl.program_id(0) == pl.num_programs(0) - 1)
    def _():
        out[...] = total_f[...].astype(BF)


def block_output(count, slots, aa, probs, outs):
    images, rows, width = aa.shape
    block = lambda cols: pl.BlockSpec((1, rows, cols), lambda i: (i, 0, 0))
    return pl.pallas_call(
        output_kernel,
        grid=(images,),
        in_specs=[SMEM, block(2), block(width), block(LANES), whole(outs.shape)],
        out_specs=whole((images * SEQ, width)),
        out_shape=jax.ShapeDtypeStruct((images * SEQ, width), BF),
        scratch_shapes=[pltpu.VMEM((images * SEQ, width), F32)],
        compiler_params=params(34),
        cost_estimate=SMALL,
        name="block_output",
    )(count, slots, aa, probs, outs)


def local(sizes, *args):
    (tokens, image_count, routes, capacity, ln1_gain, ln1_bias, qkv_weight, qv_bias, out_weight, out_bias,
     ln2_gain, ln2_bias, router_weight, expert_in, expert_in_bias, expert_out, expert_out_bias, cotangent) = args
    dp, experts = sizes
    grouped = sizes == (4, 8)
    devices = dp * experts
    me_d = lax.axis_index("dp")
    me_e = lax.axis_index("expert")
    core = me_e % 2
    token_count, width = tokens.shape
    images = token_count // SEQ
    rows = up16(SEQ)
    cap = max(2, 5 * token_count // (2 * experts))
    halves = 2 if grouped else 1
    half_cap = -(-cap // halves)
    block_rows = up16(half_cap + 2)

    def hop(value, mask):
        return lax.ppermute(value, BOTH, [(i, i ^ mask) for i in range(devices)])

    def by_image(value):
        value = value.reshape(images, SEQ, value.shape[-1])
        fill = -1 if value.dtype == jnp.int32 else 0
        return jnp.pad(value, ((0, 0), (0, rows - SEQ), (0, 0)), constant_values=fill)

    def side_rows(values):
        return functools.reduce(
            lambda a, b: a + b,
            [jnp.pad(v.astype(F32)[None], ((k, 7 - k), (0, 0))) for k, v in enumerate(values)],
        )

    def slots_and_blocks(value):
        return first_dispatch(image_count, capacity, routes.T, value, half_cap, block_rows, halves)

    def slot_forms(slots):
        slots = slots.reshape(2, images, SEQ)
        slots = jnp.pad(slots, ((0, 0), (0, 0), (0, rows - SEQ)), constant_values=-1)
        return slots.transpose(1, 2, 0), slots.reshape(2, -1)

    def after(values, *done):
        return lax.optimization_barrier((values, done))[0]

    tok = by_image(tokens)

    vectors = [ln1_gain, ln1_bias, out_bias, ln2_gain, ln2_bias]
    width_all = 4 * width + 2 * LANES
    wide = expert_in.shape[2]
    spot = me_d * expert_out_bias.shape[1]
    if grouped:
        half = width_all // 2
        mine, other = pack_dense(
            core.reshape(1).astype(jnp.int32), qkv_weight, out_weight, router_weight.T, side_rows(vectors), qv_bias
        )
        got = hop(other, 1)
        chip = jnp.where(
            core == 0, jnp.concatenate([mine, got], axis=0), jnp.concatenate([got, mine], axis=0)
        )
        bias_out = lax.dynamic_update_slice(jnp.zeros((1, width), BF), expert_out_bias, (0, spot))
        bias = jnp.concatenate([expert_in_bias, bias_out, jnp.zeros((14, wide), BF)], axis=0)
        one = jnp.concatenate([expert_in[0], bias], axis=0)
        two = jnp.concatenate([expert_out[0], bias], axis=0)
        from_x, from_y = hop(expert_in[0], 8), hop(expert_out[0], 16)
        cot_blocks, slots = slots_and_blocks(after(cotangent, chip))
        slots_col, slots_row = slot_forms(slots)
        line = jnp.concatenate([chip] + [hop(chip, 2 * dz) for dz in (1, 2, 3)], axis=0)
        held, from_x, from_y = after((line, from_x, from_y))
        own = [line] + [hop(held, 8 * dxy) for dxy in (3, 1, 2)]
        own = [own[0], own[2], own[3], own[1]]
        step = width // 16
        at_rows = jnp.stack([((me_d ^ a) * 4 + ((me_e // 2) ^ b)) * step for a in range(4) for b in range(4)])
        at_cols = jnp.stack([core * half, (1 - core) * half])
        off_back = jnp.concatenate([at_rows, at_cols]).astype(jnp.int32)
        off = jnp.concatenate([at_rows, at_rows, jnp.repeat(at_cols, 4)]).astype(jnp.int32)
        own, tok, slots_row, off, one, two = after((own, tok, slots_row, off, one, two))
        pieces = own + [hop(piece, 1) for piece in own]
        subs = 4
        later_one, later_two, relay_x, relay_y = after((one, two, from_x, from_y), *own)
        near = hop(later_one, 16), hop(later_two, 8)
        relays = hop(relay_x, 16), hop(relay_y, 8), hop(near[0][width:], 8)
        arrays = [one, from_x, near[0], relays[0]]
        biases = [bias, near[1][width:], near[0][width:], relays[2]]
        b_in = jnp.stack([v[:8] for v in biases]).astype(F32)
        arrays += [two, near[1], from_y, relays[1]]
        places = tuple((q, 0) for q in range(8))
        b_out = jnp.broadcast_to(jnp.sum(b_in[:, 1], axis=0), (8, width))
        after_line = held
    else:
        fill = width_all - 4 * width - experts - 7
        pack = jnp.concatenate(
            [qkv_weight, out_weight, router_weight, jnp.stack(vectors, axis=1), qv_bias.T, jnp.zeros((ln1_gain.shape[0], fill), BF)], axis=1
        )
        pieces = [lax.all_gather(pack, BOTH, axis=0, tiled=True)]
        cot_blocks, slots = slots_and_blocks(cotangent)
        slots_col, slots_row = slot_forms(slots)
        off = jnp.zeros((2,), jnp.int32)
        off_back = off
        subs = 1
        after_line = pieces[0]
        w_in = lax.all_gather(expert_in[0], "dp", axis=0, tiled=False)
        w_out = lax.all_gather(expert_out[0], "dp", axis=0, tiled=False)
        arrays = [w[q] for w in (w_in, w_out) for q in range(dp)]
        places = tuple((q, 0) for q in range(2 * dp))
        b_in = lax.all_gather(jnp.broadcast_to(expert_in_bias, (8, wide)), "dp", axis=0, tiled=False).astype(F32)
        b_out = jnp.broadcast_to(
            lax.all_gather(expert_out_bias, "dp", axis=1, tiled=True).astype(F32), (8, width)
        )

    def exchange(blocks):
        return lax.all_to_all(blocks, "expert", 0, 0, tiled=True)

    cot_sent = exchange(after(cot_blocks, after_line))
    cot = by_image(cotangent)

    w, small, qkv, n1, att, aa, n2, prob = forward(off, subs, pieces, image_count, tok, experts, width_all)
    row_sent = []
    flat = n2.reshape(-1, width)
    for h in range(halves):
        sent = dispatch(slots_row, flat, small, experts, block_rows, h, 1, "ab"[h])
        waits = (near, relays)[h] if grouped else ()
        sent, cot_sent = after((sent, cot_sent), *row_sent, *waits)
        if h:
            sent, cot, slots_col = after((sent, cot, slots_col))
        row_sent.append(exchange(sent))

    back, grads_out, db_ins, db_outs, tall = [], [], [], [], ()
    for h in range(halves):
        *tall, d, db_in, db_out = expert_call(
            row_sent[h], cot_sent, arrays, places, b_in, b_out, h, halves, tall
        )
        grads_out.append(d)
        if h + 1 < halves:
            back.append(exchange(d))
        db_ins.append(db_in)
        db_outs.append(db_out)
    *tall, outs_back = tall
    db_in, db_out = sum(db_ins), sum(db_outs)

    both = [db_in[:, 0:1]]
    if grouped:
        both.append(jnp.broadcast_to(db_out[0:1], db_in[:, 0:1].shape))
    bias_sums = jnp.concatenate(
        [*both, jnp.zeros((dp, 16 - len(both), wide), F32)], axis=1
    )

    def weights_of(q_in, q_out, kind):
        act, pre, rows_in, slot_grad = tall
        return weight_grads(rows_in, pre, act, slot_grad, bias_sums, wide, q_in, q_out, kind)

    if grouped:
        far_in, far_out = weights_of(3, 3, BF)
        tall = after(tall, far_in, far_out, *back)
        back.append(exchange(after(grads_out[-1], far_in, far_out, *back)))
        far_in, far_out = hop(far_in, 8), hop(far_out, 16)
        near_in, near_out = weights_of(1, 2, BF)
        last_in, last_out = weights_of(2, 1, BF)
        last_in = (last_in.astype(F32) + far_in.astype(F32)).astype(BF)
        last_out = (last_out.astype(F32) + far_out.astype(F32)).astype(BF)
        ready = (near_in, near_out, last_in, last_out)
        near_in, near_out = hop(near_in, 8), hop(near_out, 16)
        last_in, last_out = hop(last_in, 16), hop(last_out, 8)
        arrived = (near_in, near_out, last_in, last_out)
    else:
        ready = arrived = ()
        scatter = lambda v: lax.psum_scatter(v, "dp", scatter_dimension=0, tiled=True).astype(F32)
        back.append(exchange(grads_out[-1]))
        every = [weights_of(q, q, BF) for q in range(dp)]
        g_in = scatter(jnp.stack([e[0][:width] for e in every]))
        g_out = scatter(jnp.stack([e[1] for e in every]))
        g_b_in = lax.psum_scatter(
            db_in[:, 0].reshape(1, -1).astype(BF), "dp", scatter_dimension=1, tiled=True
        ).astype(F32)
        g_b_out = lax.psum_scatter(db_out[0:1].astype(BF), "dp", scatter_dimension=1, tiled=True).astype(F32)

    r_sent = exchange(after(outs_back, *back))
    back = after(back, *ready)
    after_grad, probs, grad, grads = backward(
        off_back, image_count, slots_col, cot, n1, qkv, att, aa, n2, prob, w, small, back, experts,
        2 if grouped else 1,
    )
    grads = after(grads, *arrived)
    block_out = block_output(image_count, slots_col, aa, probs, r_sent)
    def add(*values):
        return functools.reduce(lambda a, b: a + b, [v.astype(F32) for v in values])

    if grouped:
        sibling = hop(grads[1], 1)
        quarter = width // 4
        ways = [slice(a * quarter, (a + 1) * quarter) for a in range(4)]
        ways = [add(grads[0][a], sibling[a]).astype(BF) for a in ways]
        tall, bias_sums = after((tall, bias_sums), *ways)
        own_in, own_out = weights_of(0, 0, F32)
        g_in = add(own_in[:width], near_in[:width], last_in[:width])[None]
        g_bias = add(own_in[width:], near_in[width:], last_in[width:])
        g_out = add(own_out, near_out, last_out)[None]
        g_b_in = g_bias[0:1]
        g_b_out = lax.dynamic_slice(g_bias[1:2], (0, spot), expert_out_bias.shape)
        after_grad, grad = after((after_grad, grad), own_in, own_out)
    tokens_grad = finish(after_grad, grad, tok, w, small, experts)

    if grouped:
        ways[0], tokens_grad, g_in, g_out = after((ways[0], tokens_grad, g_in, g_out))
        line = add(ways[0], *[hop(ways[a], 8 * a) for a in (1, 2, 3)]).astype(BF)
        line, r_sent = after((line, r_sent))
        step = width // 16
        cuts = [line[b * step : (b + 1) * step] for b in range(4)]
        chip = add(cuts[0], *[hop(cuts[b], 2 * b) for b in (1, 2, 3)])
        n_rows = step // 2
        keep = lax.dynamic_slice_in_dim(chip, core * n_rows, n_rows, 0)
        chip, block_out = after((chip, block_out))
        give = lax.dynamic_slice_in_dim(chip, (1 - core) * n_rows, n_rows, 0)
        got = hop(give.astype(BF), 1).astype(F32)
        dense = jnp.where(
            core == 0, jnp.concatenate([keep, got], axis=1), jnp.concatenate([got, keep], axis=1)
        )
    else:
        dense = lax.psum_scatter(grads[0], BOTH, scatter_dimension=0, tiled=True).astype(F32)
    side = dense[:, 4 * width :]
    vecs = [side[:, experts + k] for k in range(8)]
    return (
        block_out,
        tokens_grad,
        vecs[0],
        vecs[1],
        dense[:, : 3 * width],
        jnp.stack([vecs[5], vecs[7]], axis=0),
        dense[:, 3 * width : 4 * width],
        vecs[2],
        vecs[3],
        vecs[4],
        side[:, :experts],
        g_in,
        g_b_in,
        g_out,
        g_b_out,
    )


def solution(mesh):
    rows, line, cols = P(BOTH, None), P(BOTH), P(None, BOTH)
    experts = (P("expert", None, "dp"), P("expert", "dp"), P("expert", "dp", None), P("expert", "dp"))
    dense = (line, line, rows, cols, rows, line, line, line, rows)
    return jax.shard_map(
        functools.partial(local, (mesh.shape["dp"], mesh.shape["expert"])),
        mesh=mesh,
        in_specs=(rows, line, rows, P(), *dense, *experts, rows),
        out_specs=(rows, rows, *dense, *experts),
        check_vma=False,
    )
```

```python
import functools

import jax
import jax.numpy as jnp
from jax import lax
from jax.experimental import pallas as pl
from jax.experimental.pallas import tpu as pltpu
from jax.sharding import PartitionSpec as P

HEADS = 12
SEQ = 197
EPS_NORM = 1e-06
NEG_FILL = -1e30
BF = jnp.bfloat16
F32 = jnp.float32
LANES = 128
GELU_A = 0.7978845608028654
GELU_B = 0.044715
BOTH = ("dp", "expert")


def up16(n):
    return -(-n // 16) * 16


def dot(left, right):
    return jnp.dot(left, right, preferred_element_type=F32)


def dot_t(left, right):
    return lax.dot_general(left, right, (((1,), (1,)), ((), ())), preferred_element_type=F32)


def t_dot(left, right):
    return lax.dot_general(left, right, (((0,), (0,)), ((), ())), preferred_element_type=F32)


def iota(shape, dim):
    return lax.broadcasted_iota(jnp.int32, shape, dim)


def params(mib=60):
    return pltpu.CompilerParams(vmem_limit_bytes=mib << 20)


def whole(shape):
    zeros = (0,) * len(shape)
    return pl.BlockSpec(shape, lambda *_: zeros, pipeline_mode=pl.Buffered(1))


SMALL = pl.CostEstimate(flops=1 << 20, bytes_accessed=1 << 16, transcendentals=0)
LARGE = pl.CostEstimate(flops=1 << 34, bytes_accessed=1 << 16, transcendentals=0)
SMEM = pl.BlockSpec(memory_space=pltpu.SMEM)
ANY = pl.BlockSpec(memory_space=pl.ANY)


def norm_stats(values):
    centered = values - jnp.mean(values, axis=-1, keepdims=True)
    inverse = lax.rsqrt(jnp.mean(centered * centered, axis=-1, keepdims=True) + EPS_NORM)
    return centered * inverse, inverse


def norm_back(unit, inverse, gain, grad):
    scaled = grad * gain
    mean_one = jnp.mean(scaled, axis=-1, keepdims=True)
    mean_two = jnp.mean(scaled * unit, axis=-1, keepdims=True)
    return inverse * (scaled - mean_one - unit * mean_two)


def col_sum(values):
    return jnp.sum(values, axis=0, keepdims=True)


def pack_kernel(core, qkv, out, router, vectors, pair, mine, other):
    rows = qkv.shape[0]
    eye = (iota((rows, rows), 0) == iota((rows, rows), 1)).astype(BF)
    turned = [dot_t(eye, router[...]), dot_t(eye, vectors[...].astype(BF))[:, :5], dot_t(eye, pair[...])]
    used = sum(t.shape[1] for t in turned)
    turned = jnp.concatenate([*turned, jnp.zeros((rows, 2 * LANES - used), F32)], axis=1)
    value = jnp.concatenate([qkv[...], out[...], turned.astype(BF)], axis=1)
    half = value.shape[1] // 2

    @pl.when(core[0] == 0)
    def _():
        mine[...] = value[:, :half]
        other[...] = value[:, half:]

    @pl.when(core[0] != 0)
    def _():
        mine[...] = value[:, half:]
        other[...] = value[:, :half]


def pack_dense(core, qkv, out, router, vectors, pair):
    rows = qkv.shape[0]
    half = (qkv.shape[1] + out.shape[1] + 2 * LANES) // 2
    vmem = pl.BlockSpec(memory_space=pltpu.VMEM)
    return pl.pallas_call(
        pack_kernel,
        in_specs=[SMEM] + [vmem] * 5,
        out_specs=[vmem] * 2,
        out_shape=[jax.ShapeDtypeStruct((rows, half), BF)] * 2,
        compiler_params=params(60),
        cost_estimate=LARGE,
        name="pack_dense",
    )(core, qkv, out, router, vectors, pair)


def forward_kernel(experts, subs, off, count, tok, *refs):
    n_pieces = len(refs) - 10
    pieces = refs[:n_pieces]
    w_o, small, qkv_o, n1_o, att_o, aa_o, n2_o, prob_o, w, sems = refs[n_pieces:]
    img = pl.program_id(0)
    width = tok.shape[-1]

    @pl.when(img == 0)
    def _():
        copies = []
        for i, piece in enumerate(pieces):
            rows, cols = piece.shape[0] // subs, piece.shape[1]
            col = pl.multiple_of(off[n_pieces * subs + i], LANES)
            for j in range(subs):
                row = pl.multiple_of(off[i * subs + j], 16)
                copies.append(
                    pltpu.make_async_copy(
                        piece.at[pl.ds(j * rows, rows), :],
                        w.at[pl.ds(row, rows), pl.ds(col, cols)],
                        sems.at[i * subs + j],
                    )
                )
        for c in copies:
            c.start()
        for c in copies:
            c.wait()
        small[...] = jnp.transpose(w[:, 4 * width : 4 * width + LANES].astype(F32))
        pltpu.make_async_copy(w, w_o, sems.at[0]).start()

    def vec(k):
        return small[experts + k : experts + k + 1, :]

    x = tok[0].astype(F32)
    rows = x.shape[0]
    unit, _ = norm_stats(x)
    n1 = (unit * vec(0) + vec(1)).astype(BF)
    n1_o[0] = n1
    biases = (vec(5), None, vec(6))
    for part in range(3):
        cols = slice(part * width, (part + 1) * width)
        block = dot(n1, w[:, cols])
        if biases[part] is not None:
            block = block + biases[part]
        qkv_o[0, :, cols] = block.astype(BF)
    low = iota((rows, LANES), 1) < LANES // 2
    seen = iota((rows, rows), 0) < SEQ
    scale = (width // HEADS) ** -0.5
    for pair in range(HEADS // 2):
        c = pair * LANES
        q2 = qkv_o[0, :, c : c + LANES]
        k2 = qkv_o[0, :, width + c : width + c + LANES]
        v2 = qkv_o[0, :, 2 * width + c : 2 * width + c + LANES]
        got = []
        for side, mask in enumerate((low, ~low)):
            scores = dot_t(k2, jnp.where(mask, q2, jnp.zeros_like(q2))) * scale
            scores = jnp.where(seen, scores, NEG_FILL)
            exps = jnp.exp(scores - jnp.max(scores, axis=0, keepdims=True))
            prob = exps * (1.0 / col_sum(exps))
            prob_o[0, 2 * pair + side] = prob
            got.append(t_dot(prob.astype(BF), v2))
        att_o[0, :, c : c + LANES] = jnp.where(low, got[0], got[1]).astype(BF)
    alive = (img < count[0]).astype(F32)
    after = x + alive * (dot(att_o[0], w[:, 3 * width : 4 * width]) + vec(2))
    aa_o[0] = after
    unit, _ = norm_stats(after)
    n2_o[0] = (unit * vec(3) + vec(4)).astype(BF)

    @pl.when(img == pl.num_programs(0) - 1)
    def _():
        pltpu.make_async_copy(w, w_o, sems.at[0]).wait()


def forward(off, subs, pieces, count, tok, experts, width_all):
    images, rows, width = tok.shape
    block = lambda cols: pl.BlockSpec((1, rows, cols), lambda i: (i, 0, 0))
    shape = lambda cols, t: jax.ShapeDtypeStruct((images, rows, cols), t)
    return pl.pallas_call(
        functools.partial(forward_kernel, experts, subs),
        grid=(images,),
        in_specs=[SMEM, SMEM, block(width)] + [ANY] * len(pieces),
        out_specs=[
            ANY,
            whole((LANES, width)),
            block(3 * width),
            block(width),
            block(width),
            block(width),
            block(width),
            pl.BlockSpec((1, HEADS, rows, rows), lambda i: (i, 0, 0, 0)),
        ],
        out_shape=[
            jax.ShapeDtypeStruct((width, width_all), BF),
            jax.ShapeDtypeStruct((LANES, width), F32),
            shape(3 * width, BF),
            shape(width, BF),
            shape(width, BF),
            shape(width, F32),
            shape(width, BF),
            jax.ShapeDtypeStruct((images, HEADS, rows, rows), F32),
        ],
        scratch_shapes=[
            pltpu.VMEM((width, width_all), BF),
            pltpu.SemaphoreType.DMA((len(pieces) * subs,)),
        ],
        compiler_params=params(60),
        cost_estimate=SMALL,
        name="tokens_forward",
    )(off, count, tok, *pieces)


def dispatch_kernel(experts, half, gated, slots, x, *refs):
    out = refs[-1]
    value = x[...]
    halves, block_rows = out.shape[1:3]
    first, second = slots[0:1, :], slots[1:2, :]
    if gated:
        router = refs[0][...].astype(BF)
        logits = dot_t(router, value)
        logits = jnp.where(iota(logits.shape, 0) < experts, logits, NEG_FILL)
        exps = jnp.exp(logits - jnp.max(logits, axis=0, keepdims=True))
        probs = exps / jnp.sum(exps, axis=0, keepdims=True)
    total = experts * block_rows
    for h in range(halves):
        place = iota((total, value.shape[0]), 0) + (half + h) * total
        hot = ((place == first) | (place == second)).astype(BF)
        out[:, h] = dot(hot, value).astype(BF).reshape(experts, block_rows, value.shape[1])
        if gated:
            row = iota((16, value.shape[0]), 0)
            for e in range(experts):
                gate = probs[e : e + 1, :]
                high = gate.astype(BF).astype(F32)
                pair = jnp.where(row == 14, high, jnp.where(row == 15, gate - high, 0.0))
                placed = dot_t(pair.astype(BF), hot[e * block_rows : (e + 1) * block_rows])
                tail = out[e, h, block_rows - 16 :, :block_rows].astype(F32)
                out[e, h, block_rows - 16 :, :block_rows] = jnp.where(
                    iota(tail.shape, 0) < 14, tail, placed
                ).astype(BF)


def dispatch(slots, x, small, experts, block_rows, half, halves, tag):
    rows, width = x.shape
    gated = small is not None
    more = [small] if gated else []
    vmem = pl.BlockSpec(memory_space=pltpu.VMEM)
    return pl.pallas_call(
        functools.partial(dispatch_kernel, experts, half, gated),
        in_specs=[vmem] * (2 + len(more)),
        out_specs=vmem,
        out_shape=jax.ShapeDtypeStruct((experts, halves, block_rows, width), BF),
        compiler_params=params(24),
        cost_estimate=SMALL,
        name="dispatch_" + tag,
    )(slots, x, *more)


def first_kernel(experts, half_cap, count, capacity, routes, x, out, slots):
    rows = routes.shape[1]
    halves, block_rows = out.shape[1:3]
    alive = iota((1, rows), 1) < count[0] * SEQ
    name = iota((up16(experts), rows), 0)
    earlier = (iota((rows, rows), 0) < iota((rows, rows), 1)).astype(BF)
    limits = jnp.zeros((up16(experts), 1), F32)
    for e in range(experts):
        limits = jnp.where(name[:, 0:1] == e, capacity[e].astype(F32), limits)
    base = 0.0
    for k in range(2):
        hit = jnp.where((routes[k : k + 1, :] == name) & alive, 1.0, 0.0)
        place = col_sum(hit * (dot(hit.astype(BF), earlier) + base))
        keep = place < col_sum(hit * limits)
        base = jnp.sum(hit, axis=1, keepdims=True)
        place = place.astype(jnp.int32)
        half = (place >= half_cap).astype(jnp.int32)
        spot = (half * experts + routes[k : k + 1, :]) * block_rows + place - half * half_cap
        slots[k : k + 1, :] = jnp.where(keep, spot, -1)
    dispatch_kernel(experts, 0, False, slots, x, out)


def first_dispatch(count, capacity, routes, x, half_cap, block_rows, halves):
    rows, width = x.shape
    experts = capacity.shape[0]
    vmem = pl.BlockSpec(memory_space=pltpu.VMEM)
    return pl.pallas_call(
        functools.partial(first_kernel, experts, half_cap),
        in_specs=[SMEM, SMEM, vmem, vmem],
        out_specs=[vmem, vmem],
        out_shape=[
            jax.ShapeDtypeStruct((experts, halves, block_rows, width), BF),
            jax.ShapeDtypeStruct((2, rows), jnp.int32),
        ],
        compiler_params=params(24),
        cost_estimate=SMALL,
        name="dispatch_first",
    )(count, capacity, routes, x)


def expert_kernel(places, n_arrays, n_before, *refs):
    x_ref, c_ref, b_in, b_out = refs[:4]
    arrays, parts = refs[4 : 4 + n_arrays], len(places) // 2
    rest = refs[4 + n_arrays + n_before :]
    act_o, pre_o, x_o, sg_o, r_o, d_o, db_in, db_out, win, wout, sems = rest
    step = pl.program_id(0)
    n, _, size, width = x_ref.shape
    piece = win.shape[1] // parts

    def copies(q):
        cols = pl.ds(q * piece, piece)
        (one, at_one), (two, at_two) = places[q], places[parts + q]
        return (
            pltpu.make_async_copy(
                arrays[one].at[pl.ds(at_one, width), :], win.at[:, cols], sems.at[q]
            ),
            pltpu.make_async_copy(
                arrays[two].at[pl.ds(at_two, piece), :], wout.at[cols, :], sems.at[parts + q]
            ),
        )

    @pl.when(step == 0)
    def _():
        for q in range(parts):
            for c in copies(q):
                c.start()
        db_in[...] = jnp.zeros_like(db_in)
        db_out[...] = jnp.zeros_like(db_out)

    eye = (iota((size, size), 0) == iota((size, size), 1)).astype(BF)
    for s in range(n):
        rows = slice(s * size, (s + 1) * size)
        x_o[rows, :] = x_ref[s, 0]
        turned = dot_t(eye, x_ref[s, 0, size - 16 :, :size])
        gate = jnp.sum(jnp.where(iota(turned.shape, 1) >= 14, turned, 0.0), axis=1, keepdims=True)
        sg_o[rows, :] = (gate * c_ref[s, 0].astype(F32)).astype(BF)
    x = x_o[...]
    slot_grad = sg_o[...]
    db_out[0:1, :] += col_sum(slot_grad.astype(F32))

    @pl.when(step == 0)
    def _():
        for q in range(parts):
            for c in copies(q):
                c.wait()

    for q in range(parts):
        cols = slice(q * piece, (q + 1) * piece)
        pre = dot(x, win[:, cols]) + b_in[q, 0:1, :]
        square = pre * pre
        turn = jnp.tanh(pre * (GELU_A + GELU_A * GELU_B * square))
        half_turn = 0.5 * turn + 0.5
        act_o[:, cols] = (pre * half_turn).astype(BF)
        slope = half_turn + (0.5 * pre) * (1.0 - turn * turn) * (GELU_A + 3 * GELU_A * GELU_B * square)
        pre_grad = dot_t(slot_grad, wout[cols, :]) * slope
        pre_o[:, cols] = pre_grad.astype(BF)
        db_in[q, 0:1, :] += col_sum(pre_grad)
    out = (dot(act_o[...], wout[...]) + b_out[0:1, :]).astype(BF)
    back = dot_t(pre_o[...], win[...])
    ones = jnp.ones((16, width), BF)
    for s in range(n):
        rows = slice(s * size, (s + 1) * size)
        r_o[s, 0] = out[rows]
        d_o[s] = back[rows].astype(BF)
        prod = c_ref[s, 0].astype(F32) * out[rows].astype(F32)
        high = prod.astype(BF)
        low = (prod - high.astype(F32)).astype(BF)
        gate_grad = dot_t(ones, high) + dot_t(ones, low)
        grad_high = gate_grad.astype(BF).astype(F32)
        row = iota(gate_grad.shape, 0)
        tail = back[(s + 1) * size - 16 : (s + 1) * size, :size]
        both = jnp.where(row == 14, grad_high, gate_grad - grad_high)
        d_o[s, size - 16 :, :size] = jnp.where(row < 14, tail, both).astype(BF)


def expert_call(x, c, arrays, places, b_in, b_out, half, halves, before):
    experts, _, size, width = x.shape
    parts, _, piece = b_in.shape
    n = max(1, 256 // size)
    steps = experts // n
    rows, hidden = n * size, parts * piece
    before = list(before)
    tall = lambda cols: pl.BlockSpec((rows, cols), lambda i: (half * steps + i, 0))
    of_half = pl.BlockSpec((n, 1, size, width), lambda i: (i, half, 0, 0))
    total = halves * experts * size
    return pl.pallas_call(
        functools.partial(expert_kernel, places, len(arrays), len(before)),
        grid=(steps,),
        in_specs=[
            pl.BlockSpec((n, 1, size, width), lambda i: (i, 0, 0, 0)),
            of_half,
            whole((parts, 8, piece)),
            whole((8, width)),
        ]
        + [ANY] * (len(arrays) + len(before)),
        out_specs=[
            tall(hidden),
            tall(hidden),
            tall(width),
            tall(width),
            of_half,
            pl.BlockSpec((n, size, width), lambda i: (i, 0, 0)),
            whole((parts, 8, piece)),
            whole((8, width)),
        ],
        out_shape=[
            jax.ShapeDtypeStruct((total, hidden), BF),
            jax.ShapeDtypeStruct((total, hidden), BF),
            jax.ShapeDtypeStruct((total, width), BF),
            jax.ShapeDtypeStruct((total, width), BF),
            jax.ShapeDtypeStruct((experts, halves, size, width), BF),
            jax.ShapeDtypeStruct((experts, size, width), BF),
            jax.ShapeDtypeStruct((parts, 8, piece), F32),
            jax.ShapeDtypeStruct((8, width), F32),
        ],
        scratch_shapes=[
            pltpu.VMEM((width, hidden), BF),
            pltpu.VMEM((hidden, width), BF),
            pltpu.SemaphoreType.DMA((2 * parts,)),
        ],
        input_output_aliases={4 + len(arrays) + i: i for i in range(len(before))},
        compiler_params=params(44),
        cost_estimate=SMALL,
        name="expert_" + "ab"[half],
    )(x, c, b_in, b_out, *arrays, *before)


def weight_kernel(piece, q_in, q_out, n_more, x, pre, act, grad, bias, *refs):
    more, (in_o, out_o, bias_o, xs, ps, acts, gs, held, sems) = refs[:n_more], refs[n_more:]
    width = x.shape[1]
    copies = [
        pltpu.make_async_copy(x, xs, sems.at[0]),
        pltpu.make_async_copy(pre.at[:, pl.ds(q_in * piece, piece)], ps, sems.at[1]),
        pltpu.make_async_copy(act.at[:, pl.ds(q_out * piece, piece)], acts, sems.at[2]),
        pltpu.make_async_copy(grad, gs, sems.at[3]),
    ]
    extra = [
        pltpu.make_async_copy(far, held.at[k, pl.ds(0, far.shape[0]), :], sems.at[4 + k])
        for k, far in enumerate(more)
    ]
    copies[0].start()
    copies[1].start()
    copies[0].wait()
    copies[1].wait()
    for c in [copies[2], copies[3], *extra]:
        c.start()
    first = t_dot(xs[...], ps[...])
    sums = bias[q_in]
    for k in range(n_more // 2):
        extra[k].wait()
        first = first + held[k, :width, :].astype(F32)
        sums = sums + held[k, width:, :].astype(F32)
    in_o[:width, :] = first.astype(in_o.dtype)
    bias_o[...] = sums.astype(bias_o.dtype)
    if not n_more:
        in_o[width:, :] = sums.astype(in_o.dtype)
    copies[2].wait()
    copies[3].wait()
    second = t_dot(acts[...], gs[...])
    for k in range(n_more // 2, n_more):
        extra[k].wait()
        second = second + held[k, :piece, :].astype(F32)
    out_o[...] = second.astype(out_o.dtype)


def weight_grads(x, pre, act, grad, bias, piece, q_in, q_out, kind, more=()):
    total, width = x.shape
    vmem = pl.BlockSpec(memory_space=pltpu.VMEM)
    return pl.pallas_call(
        functools.partial(weight_kernel, piece, q_in, q_out, len(more)),
        in_specs=[ANY] * 4 + [vmem] + [ANY] * len(more),
        out_specs=[vmem] * 3,
        out_shape=[
            jax.ShapeDtypeStruct((width if more else width + 16, piece), kind),
            jax.ShapeDtypeStruct((piece, width), kind),
            jax.ShapeDtypeStruct((16, piece), kind),
        ],
        scratch_shapes=[
            pltpu.VMEM((total, width), BF),
            pltpu.VMEM((total, piece), BF),
            pltpu.VMEM((total, piece), BF),
            pltpu.VMEM((total, width), BF),
            pltpu.VMEM((max(1, len(more)), width + 16, width), BF),
            pltpu.SemaphoreType.DMA((4 + len(more),)),
        ],
        compiler_params=params(60),
        cost_estimate=SMALL,
        name="weight_grads",
    )(x, pre, act, grad, bias, *more)


def backward_kernel(experts, n, split, off, count, slots, cot, n1_far, qkv, att_far, aa, n2, probs_in, w_far, w_out, small, *refs):
    backs = refs[:n]
    ag_o, gp_o, dq_o = refs[n : n + 3]
    grads = refs[n + 3 : n + 3 + split]
    dw, ds, marks, ag_all, dq_all, n1, att, w, sems = refs[n + 3 + split :]
    img = pl.program_id(0)
    width = n1.shape[-1]
    late = [
        pltpu.make_async_copy(far, here, sems.at[k])
        for k, (far, here) in enumerate(((n1_far, n1), (att_far, att), (w_far, w)))
    ]
    size = backs[0].shape[1]
    total = experts * size

    @pl.when(img == 0)
    def _():
        for c in late:
            c.start()
        ds[...] = jnp.zeros_like(ds)
        line = iota((LANES, size), 0)
        for h in range(n):
            for e in range(experts):
                ends = backs[h][e, size - 16 :, :size].astype(F32)
                for k in range(2):
                    marks[2 * h + k, :, e * size : (e + 1) * size] = jnp.where(
                        line == e, ends[14 + k : 15 + k, :], 0.0
                    ).astype(BF)

    def vec(k):
        return small[experts + k : experts + k + 1, :]

    def add_vec(k, value):
        ds[experts + k : experts + k + 1, :] += value

    alive = (img < count[0]).astype(F32)
    up = cot[0].astype(F32)
    rows = up.shape[0]
    normed = n2[0]
    lane = iota((rows, LANES), 1)
    router = jnp.where(iota(small.shape, 0) < experts, small[...], 0.0).astype(BF)
    logits = jnp.where(lane < experts, dot_t(normed, router), NEG_FILL)
    exps = jnp.exp(logits - jnp.max(logits, axis=-1, keepdims=True))
    probs = exps / jnp.sum(exps, axis=-1, keepdims=True)
    gp_o[0] = probs
    first, second = slots[0, :, 0:1], slots[0, :, 1:2]
    normed_grad = jnp.zeros((rows, width), F32)
    placed = jnp.zeros((rows, LANES), F32)
    for h in range(n):
        place = iota((rows, total), 1) + h * total
        hot = ((place == first) | (place == second)).astype(BF)
        normed_grad = normed_grad + dot(hot, backs[h][...].reshape(total, width))
        placed = placed + dot_t(hot, marks[2 * h]) + dot_t(hot, marks[2 * h + 1])
    logit_grad = (
        probs * (placed - jnp.sum(probs * placed, axis=-1, keepdims=True))
    ).astype(BF)
    normed_grad = normed_grad + dot(logit_grad, router)
    ds[...] += jnp.where(iota(ds.shape, 0) < experts, t_dot(logit_grad, normed), 0.0)
    unit, inverse = norm_stats(aa[0])
    add_vec(3, col_sum(normed_grad * unit))
    add_vec(4, col_sum(normed_grad))
    after_grad = up + norm_back(unit, inverse, vec(3), normed_grad)
    attn_grad = (alive * after_grad).astype(BF)
    add_vec(2, col_sum(attn_grad.astype(F32)))
    ag_all[img] = attn_grad
    att_grad = dot_t(attn_grad, w_out[...]).astype(BF)
    low = lane < LANES // 2
    scale = (width // HEADS) ** -0.5
    for pair in range(HEADS // 2):
        c = pair * LANES
        q2 = qkv[0, :, c : c + LANES]
        k2 = qkv[0, :, width + c : width + c + LANES]
        v2 = qkv[0, :, 2 * width + c : 2 * width + c + LANES]
        o2 = att_grad[:, c : c + LANES]
        got = []
        for side, mask in enumerate((low, ~low)):
            prob = probs_in[0, 2 * pair + side]
            prob_grad = dot_t(v2, jnp.where(mask, o2, jnp.zeros_like(o2)))
            score_grad = (prob * (prob_grad - col_sum(prob * prob_grad))).astype(BF)
            got.append(
                (
                    t_dot(score_grad, k2) * scale,
                    dot(score_grad, q2) * scale,
                    dot(prob.astype(BF), o2),
                )
            )
        for k in range(3):
            dq_o[0, :, k * width + c : k * width + c + LANES] = jnp.where(
                low, got[0][k], got[1][k]
            ).astype(BF)
    grad = dq_o[0]
    dq_all[img] = grad
    for k in range(3):
        ds[experts + 5 + k : experts + 6 + k, :] += col_sum(grad[:, k * width : (k + 1) * width].astype(F32))
    ag_o[0] = after_grad

    @pl.when(img == pl.num_programs(0) - 1)
    def _():
        dw[:, 4 * width : 4 * width + LANES] = jnp.transpose(ds[...])
        for c in late:
            c.wait()
        left = n1[...].reshape(-1, width)
        for k in range(3):
            cols = slice(k * width, (k + 1) * width)
            dw[:, cols] = t_dot(left, dq_all[:, :, cols].reshape(-1, width))
        dw[:, 3 * width : 4 * width] = t_dot(
            att[...].reshape(-1, width), ag_all[...].reshape(-1, width)
        )
        with_weight = jnp.zeros((width, LANES), F32)
        with_sums = jnp.zeros((width, LANES), F32)
        for k in range(3 * width // LANES):
            cols = slice(k * LANES, (k + 1) * LANES)
            part, at = divmod(k * LANES, width)
            value = w[:, cols].astype(F32)
            sums = ds[experts + 5 + part : experts + 6 + part, at : at + LANES]
            with_weight = with_weight + value * dw[:, cols]
            with_sums = with_sums + value * sums
        sums = jnp.sum(with_sums, axis=1, keepdims=True)
        at = 4 * width
        sides = w[:, at : at + LANES].astype(F32)
        gain, shift = sides[:, experts : experts + 1], sides[:, experts + 1 : experts + 2]
        gains = (jnp.sum(with_weight, axis=1, keepdims=True) - shift * sums) / gain
        spot = iota((width, LANES), 1)
        cols = slice(at, at + LANES)
        dw[:, cols] = jnp.where(
            spot == experts, gains, jnp.where(spot == experts + 1, sums, dw[:, cols])
        )
        if split == 1:
            grads[0][...] = dw[...].astype(BF)
        else:
            cols = grads[0].shape[1]
            step = width // 16
            for h in range(2):
                col = pl.multiple_of(off[16 + h], LANES)
                for r in range(16):
                    row = pl.multiple_of(off[r], 16)
                    grads[h][r * step : (r + 1) * step, :] = dw[
                        pl.ds(row, step), pl.ds(col, cols)
                    ].astype(BF)


def backward(off, count, slots, cot, n1, qkv, att, aa, n2, prob, w, small, backs, experts, split):
    images, rows, width = cot.shape
    width_all = w.shape[1]
    n = len(backs)
    block = lambda cols: pl.BlockSpec((1, rows, cols), lambda i: (i, 0, 0))
    got = pl.pallas_call(
        functools.partial(backward_kernel, experts, n, split),
        grid=(images,),
        in_specs=[SMEM, SMEM, block(2), block(width), ANY, block(3 * width), ANY, block(width), block(width)]
        + [pl.BlockSpec((1, HEADS, rows, rows), lambda i: (i, 0, 0, 0))]
        + [ANY, pl.BlockSpec((width, width), lambda i: (0, 3), pipeline_mode=pl.Buffered(1)), whole(small.shape)]
        + [whole(backs[0].shape)] * n,
        out_specs=[block(width), block(LANES), block(3 * width)] + [whole((width, width_all // split))] * split,
        out_shape=[
            jax.ShapeDtypeStruct((images, rows, width), F32),
            jax.ShapeDtypeStruct((images, rows, LANES), F32),
            jax.ShapeDtypeStruct((images, rows, 3 * width), BF),
        ]
        + [jax.ShapeDtypeStruct((width, width_all // split), BF)] * split,
        scratch_shapes=[
            pltpu.VMEM((width, width_all), F32),
            pltpu.VMEM((LANES, width), F32),
            pltpu.VMEM((2 * n, LANES, backs[0].shape[0] * backs[0].shape[1]), BF),
            pltpu.VMEM((images, rows, width), BF),
            pltpu.VMEM((images, rows, 3 * width), BF),
            pltpu.VMEM((images, rows, width), BF),
            pltpu.VMEM((images, rows, width), BF),
            pltpu.VMEM(w.shape, BF),
            pltpu.SemaphoreType.DMA((3,)),
        ],
        compiler_params=params(),
        cost_estimate=SMALL,
        name="tokens_backward",
    )(off, count, slots, cot, n1, qkv, att, aa, n2, prob, w, w, small, *backs)
    return got[0], got[1], got[2], got[3:]


def place_rows(out, value):
    for k in range(out.shape[0] // SEQ):

        @pl.when(pl.program_id(0) == k)
        def _():
            out[k * SEQ : (k + 1) * SEQ, :] = value[:SEQ]


def finish_kernel(experts, after_grad, grad, tok, w, small, out):
    width = tok.shape[-1]
    normed_grad = dot_t(grad[0], w[...])
    unit, inverse = norm_stats(tok[0].astype(F32))
    value = after_grad[0] + norm_back(unit, inverse, small[experts : experts + 1, :], normed_grad)
    place_rows(out, value)


def finish(after_grad, grad, tok, w, small, experts):
    images, rows, width = tok.shape
    block = lambda cols: pl.BlockSpec((1, rows, cols), lambda i: (i, 0, 0))
    return pl.pallas_call(
        functools.partial(finish_kernel, experts),
        grid=(images,),
        in_specs=[block(width), block(3 * width), block(width), whole((width, 3 * width)), whole(small.shape)],
        out_specs=whole((images * SEQ, width)),
        out_shape=jax.ShapeDtypeStruct((images * SEQ, width), F32),
        compiler_params=params(60),
        cost_estimate=SMALL,
        name="tokens_finish",
    )(after_grad, grad, tok, w, small)


def output_kernel(count, slots, aa, probs, outs, out, total_f):
    rows = aa.shape[1]
    experts, n, size, width = outs.shape
    total = experts * size
    alive = (pl.program_id(0) < count[0]).astype(F32)
    first, second = slots[0, :, 0:1], slots[0, :, 1:2]
    gates = jnp.concatenate(
        [jnp.broadcast_to(probs[0, :, e : e + 1], (rows, size)) for e in range(experts)], axis=1
    )
    moe = jnp.zeros(aa.shape[1:], F32)
    for h in range(n):
        place = iota((rows, total), 1) + h * total
        gate = jnp.where((place == first) | (place == second), gates, 0.0)
        high = gate.astype(BF)
        low = (gate - high.astype(F32)).astype(BF)
        value = outs[:, h].reshape(total, width)
        moe = moe + dot(high, value) + dot(low, value)
    place_rows(total_f, aa[0] + alive * moe)

    @pl.when(pl.program_id(0) == pl.num_programs(0) - 1)
    def _():
        out[...] = total_f[...].astype(BF)


def block_output(count, slots, aa, probs, outs):
    images, rows, width = aa.shape
    block = lambda cols: pl.BlockSpec((1, rows, cols), lambda i: (i, 0, 0))
    return pl.pallas_call(
        output_kernel,
        grid=(images,),
        in_specs=[SMEM, block(2), block(width), block(LANES), whole(outs.shape)],
        out_specs=whole((images * SEQ, width)),
        out_shape=jax.ShapeDtypeStruct((images * SEQ, width), BF),
        scratch_shapes=[pltpu.VMEM((images * SEQ, width), F32)],
        compiler_params=params(60),
        cost_estimate=SMALL,
        name="block_output",
    )(count, slots, aa, probs, outs)


def local(sizes, *args):
    (tokens, image_count, routes, capacity, ln1_gain, ln1_bias, qkv_weight, qv_bias, out_weight, out_bias,
     ln2_gain, ln2_bias, router_weight, expert_in, expert_in_bias, expert_out, expert_out_bias, cotangent) = args
    dp, experts = sizes
    grouped = sizes == (4, 8)
    devices = dp * experts
    me_d = lax.axis_index("dp")
    me_e = lax.axis_index("expert")
    core = me_e % 2
    token_count, width = tokens.shape
    images = token_count // SEQ
    rows = up16(SEQ)
    cap = max(2, 5 * token_count // (2 * experts))
    halves = 2 if grouped else 1
    half_cap = -(-cap // halves)
    block_rows = up16(half_cap + 2)

    def hop(value, mask):
        return lax.ppermute(value, BOTH, [(i, i ^ mask) for i in range(devices)])

    def by_image(value):
        value = value.reshape(images, SEQ, value.shape[-1])
        fill = -1 if value.dtype == jnp.int32 else 0
        return jnp.pad(value, ((0, 0), (0, rows - SEQ), (0, 0)), constant_values=fill)

    def side_rows(values):
        return functools.reduce(
            lambda a, b: a + b,
            [jnp.pad(v.astype(F32)[None], ((k, 7 - k), (0, 0))) for k, v in enumerate(values)],
        )

    def slots_and_blocks(value):
        return first_dispatch(image_count, capacity, routes.T, value, half_cap, block_rows, halves)

    def slot_forms(slots):
        slots = slots.reshape(2, images, SEQ)
        slots = jnp.pad(slots, ((0, 0), (0, 0), (0, rows - SEQ)), constant_values=-1)
        return slots.transpose(1, 2, 0), slots.reshape(2, -1)

    def after(values, *done):
        return lax.optimization_barrier((values, done))[0]

    tok = by_image(tokens)

    vectors = [ln1_gain, ln1_bias, out_bias, ln2_gain, ln2_bias]
    width_all = 4 * width + 2 * LANES
    wide = expert_in.shape[2]
    spot = me_d * expert_out_bias.shape[1]
    if grouped:
        half = width_all // 2
        mine, other = pack_dense(
            core.reshape(1).astype(jnp.int32), qkv_weight, out_weight, router_weight.T, side_rows(vectors), qv_bias
        )
        got = hop(other, 1)
        chip = jnp.where(
            core == 0, jnp.concatenate([mine, got], axis=0), jnp.concatenate([got, mine], axis=0)
        )
        bias_out = lax.dynamic_update_slice(jnp.zeros((1, width), BF), expert_out_bias, (0, spot))
        bias = jnp.concatenate([expert_in_bias, bias_out, jnp.zeros((14, wide), BF)], axis=0)
        one = jnp.concatenate([expert_in[0], bias], axis=0)
        two = jnp.concatenate([expert_out[0], bias], axis=0)
        from_x, from_y = hop(expert_in[0], 8), hop(expert_out[0], 16)
        cot_blocks, slots = slots_and_blocks(after(cotangent, chip))
        slots_col, slots_row = slot_forms(slots)
        line = jnp.concatenate([chip] + [hop(chip, 2 * dz) for dz in (1, 2, 3)], axis=0)
        held, from_x, from_y = after((line, from_x, from_y))
        own = [line] + [hop(held, 8 * dxy) for dxy in (3, 1, 2)]
        own = [own[0], own[2], own[3], own[1]]
        step = width // 16
        at_rows = jnp.stack([((me_d ^ a) * 4 + ((me_e // 2) ^ b)) * step for a in range(4) for b in range(4)])
        at_cols = jnp.stack([core * half, (1 - core) * half])
        off_back = jnp.concatenate([at_rows, at_cols]).astype(jnp.int32)
        off = jnp.concatenate([at_rows, at_rows, jnp.repeat(at_cols, 4)]).astype(jnp.int32)
        own, tok, slots_row, off, one, two = after((own, tok, slots_row, off, one, two))
        pieces = own + [hop(piece, 1) for piece in own]
        subs = 4
        later_one, later_two, relay_x, relay_y = after((one, two, from_x, from_y), *own)
        near = hop(later_one, 16), hop(later_two, 8)
        relays = hop(relay_x, 16), hop(relay_y, 8), hop(near[0][width:], 8)
        arrays = [one, from_x, near[0], relays[0]]
        biases = [bias, near[1][width:], near[0][width:], relays[2]]
        b_in = jnp.stack([v[:8] for v in biases]).astype(F32)
        arrays += [two, near[1], from_y, relays[1]]
        places = tuple((q, 0) for q in range(8))
        b_out = jnp.broadcast_to(jnp.sum(b_in[:, 1], axis=0), (8, width))
        after_line = held
    else:
        fill = width_all - 4 * width - experts - 7
        pack = jnp.concatenate(
            [qkv_weight, out_weight, router_weight, jnp.stack(vectors, axis=1), qv_bias.T, jnp.zeros((ln1_gain.shape[0], fill), BF)], axis=1
        )
        pieces = [lax.all_gather(pack, BOTH, axis=0, tiled=True)]
        cot_blocks, slots = slots_and_blocks(cotangent)
        slots_col, slots_row = slot_forms(slots)
        off = jnp.zeros((2,), jnp.int32)
        off_back = off
        subs = 1
        after_line = pieces[0]
        w_in = lax.all_gather(expert_in[0], "dp", axis=0, tiled=False)
        w_out = lax.all_gather(expert_out[0], "dp", axis=0, tiled=False)
        arrays = [w[q] for w in (w_in, w_out) for q in range(dp)]
        places = tuple((q, 0) for q in range(2 * dp))
        b_in = lax.all_gather(jnp.broadcast_to(expert_in_bias, (8, wide)), "dp", axis=0, tiled=False).astype(F32)
        b_out = jnp.broadcast_to(
            lax.all_gather(expert_out_bias, "dp", axis=1, tiled=True).astype(F32), (8, width)
        )

    def exchange(blocks):
        return lax.all_to_all(blocks, "expert", 0, 0, tiled=True)

    cot_sent = exchange(after(cot_blocks, after_line))
    cot = by_image(cotangent)

    w, small, qkv, n1, att, aa, n2, prob = forward(off, subs, pieces, image_count, tok, experts, width_all)
    row_sent = []
    flat = n2.reshape(-1, width)
    for h in range(halves):
        sent = dispatch(slots_row, flat, small, experts, block_rows, h, 1, "ab"[h])
        waits = (near, relays)[h] if grouped else ()
        sent, cot_sent = after((sent, cot_sent), *row_sent, *waits)
        if h:
            sent, cot, slots_col = after((sent, cot, slots_col))
        row_sent.append(exchange(sent))

    back, grads_out, db_ins, db_outs, tall = [], [], [], [], ()
    for h in range(halves):
        *tall, d, db_in, db_out = expert_call(
            row_sent[h], cot_sent, arrays, places, b_in, b_out, h, halves, tall
        )
        grads_out.append(d)
        if h + 1 < halves:
            back.append(exchange(d))
        db_ins.append(db_in)
        db_outs.append(db_out)
    *tall, outs_back = tall
    db_in, db_out = sum(db_ins), sum(db_outs)

    both = [db_in[:, 0:1]]
    if grouped:
        both.append(jnp.broadcast_to(db_out[0:1], db_in[:, 0:1].shape))
    bias_sums = jnp.concatenate(
        [*both, jnp.zeros((dp, 16 - len(both), wide), F32)], axis=1
    )

    def weights_of(q_in, q_out, kind, more=()):
        act, pre, rows_in, slot_grad = tall
        return weight_grads(rows_in, pre, act, slot_grad, bias_sums, wide, q_in, q_out, kind, more)

    if grouped:
        far_in, far_out, _ = weights_of(3, 3, BF)
        tall = after(tall, far_in, far_out, *back)
        back.append(exchange(after(grads_out[-1], far_in, far_out, *back)))
        far_in, far_out = hop(far_in, 8), hop(far_out, 16)
        near_in, near_out, _ = weights_of(1, 2, BF)
        last_in, last_out, _ = weights_of(2, 1, BF)
        last_in = (last_in.astype(F32) + far_in.astype(F32)).astype(BF)
        last_out = (last_out.astype(F32) + far_out.astype(F32)).astype(BF)
        ready = (near_in, near_out, last_in, last_out)
        near_in, near_out = hop(near_in, 8), hop(near_out, 16)
        last_in, last_out = hop(last_in, 16), hop(last_out, 8)
        arrived = (near_in, near_out, last_in, last_out)
    else:
        ready = arrived = ()
        scatter = lambda v: lax.psum_scatter(v, "dp", scatter_dimension=0, tiled=True).astype(F32)
        back.append(exchange(grads_out[-1]))
        every = [weights_of(q, q, BF) for q in range(dp)]
        g_in = scatter(jnp.stack([e[0][:width] for e in every]))
        g_out = scatter(jnp.stack([e[1] for e in every]))
        g_b_in = lax.psum_scatter(
            db_in[:, 0].reshape(1, -1).astype(BF), "dp", scatter_dimension=1, tiled=True
        ).astype(F32)
        g_b_out = lax.psum_scatter(db_out[0:1].astype(BF), "dp", scatter_dimension=1, tiled=True).astype(F32)

    r_sent = exchange(after(outs_back, *back))
    back = after(back, *ready)
    after_grad, probs, grad, grads = backward(
        off_back, image_count, slots_col, cot, n1, qkv, att, aa, n2, prob, w, small, back, experts,
        2 if grouped else 1,
    )
    grads = after(grads, *arrived)
    block_out = block_output(image_count, slots_col, aa, probs, r_sent)
    def add(*values):
        return functools.reduce(lambda a, b: a + b, [v.astype(F32) for v in values])

    if grouped:
        sibling = hop(grads[1], 1)
        quarter = width // 4
        ways = [slice(a * quarter, (a + 1) * quarter) for a in range(4)]
        ways = [add(grads[0][a], sibling[a]).astype(BF) for a in ways]
        tall, bias_sums = after((tall, bias_sums), *ways)
        own_in, own_out, g_bias = weights_of(0, 0, F32, (near_in, last_in, near_out, last_out))
        g_in, g_out = own_in[None], own_out[None]
        g_b_in = g_bias[0:1]
        g_b_out = lax.dynamic_slice(g_bias[1:2], (0, spot), expert_out_bias.shape)
        after_grad, grad = after((after_grad, grad), own_in, own_out)
    tokens_grad = finish(after_grad, grad, tok, w, small, experts)

    if grouped:
        ways[0], tokens_grad, g_in, g_out = after((ways[0], tokens_grad, g_in, g_out))
        line = add(ways[0], *[hop(ways[a], 8 * a) for a in (1, 2, 3)]).astype(BF)
        line, r_sent = after((line, r_sent))
        step = width // 16
        cuts = [line[b * step : (b + 1) * step] for b in range(4)]
        chip = add(cuts[0], *[hop(cuts[b], 2 * b) for b in (1, 2, 3)])
        n_rows = step // 2
        keep = lax.dynamic_slice_in_dim(chip, core * n_rows, n_rows, 0)
        chip, block_out = after((chip, block_out))
        give = lax.dynamic_slice_in_dim(chip, (1 - core) * n_rows, n_rows, 0)
        got = hop(give.astype(BF), 1).astype(F32)
        dense = jnp.where(
            core == 0, jnp.concatenate([keep, got], axis=1), jnp.concatenate([got, keep], axis=1)
        )
    else:
        dense = lax.psum_scatter(grads[0], BOTH, scatter_dimension=0, tiled=True).astype(F32)
    side = dense[:, 4 * width :]
    vecs = [side[:, experts + k] for k in range(8)]
    return (
        block_out,
        tokens_grad,
        vecs[0],
        vecs[1],
        dense[:, : 3 * width],
        jnp.stack([vecs[5], vecs[7]], axis=0),
        dense[:, 3 * width : 4 * width],
        vecs[2],
        vecs[3],
        vecs[4],
        side[:, :experts],
        g_in,
        g_b_in,
        g_out,
        g_b_out,
    )


def solution(mesh):
    rows, line, cols = P(BOTH, None), P(BOTH), P(None, BOTH)
    experts = (P("expert", None, "dp"), P("expert", "dp"), P("expert", "dp", None), P("expert", "dp"))
    dense = (line, line, rows, cols, rows, line, line, line, rows)
    return jax.shard_map(
        functools.partial(local, (mesh.shape["dp"], mesh.shape["expert"])),
        mesh=mesh,
        in_specs=(rows, line, rows, P(), *dense, *experts, rows),
        out_specs=(rows, rows, *dense, *experts),
        check_vma=False,
    )
```

```python
import functools

import jax
import jax.numpy as jnp
from jax import lax
from jax.experimental import pallas as pl
from jax.experimental.pallas import tpu as pltpu
from jax.sharding import PartitionSpec as P

HEADS = 12
SEQ = 197
EPS_NORM = 1e-06
NEG_FILL = -1e30
BF = jnp.bfloat16
F32 = jnp.float32
LANES = 128
GELU_A = 0.7978845608028654
GELU_B = 0.044715
BOTH = ("dp", "expert")


def up16(n):
    return -(-n // 16) * 16


def dot(left, right):
    return jnp.dot(left, right, preferred_element_type=F32)


def dot_t(left, right):
    return lax.dot_general(left, right, (((1,), (1,)), ((), ())), preferred_element_type=F32)


def t_dot(left, right):
    return lax.dot_general(left, right, (((0,), (0,)), ((), ())), preferred_element_type=F32)


def iota(shape, dim):
    return lax.broadcasted_iota(jnp.int32, shape, dim)


def params(mib=60):
    return pltpu.CompilerParams(vmem_limit_bytes=mib << 20)


def whole(shape):
    zeros = (0,) * len(shape)
    return pl.BlockSpec(shape, lambda *_: zeros, pipeline_mode=pl.Buffered(1))


SMALL = pl.CostEstimate(flops=1 << 20, bytes_accessed=1 << 16, transcendentals=0)
LARGE = pl.CostEstimate(flops=1 << 34, bytes_accessed=1 << 16, transcendentals=0)
SMEM = pl.BlockSpec(memory_space=pltpu.SMEM)
ANY = pl.BlockSpec(memory_space=pl.ANY)


def norm_stats(values):
    centered = values - jnp.mean(values, axis=-1, keepdims=True)
    inverse = lax.rsqrt(jnp.mean(centered * centered, axis=-1, keepdims=True) + EPS_NORM)
    return centered * inverse, inverse


def norm_back(unit, inverse, gain, grad):
    scaled = grad * gain
    mean_one = jnp.mean(scaled, axis=-1, keepdims=True)
    mean_two = jnp.mean(scaled * unit, axis=-1, keepdims=True)
    return inverse * (scaled - mean_one - unit * mean_two)


def col_sum(values):
    return jnp.sum(values, axis=0, keepdims=True)


def pack_kernel(core, qkv, out, router, vectors, pair, mine, other):
    rows = qkv.shape[0]
    eye = (iota((rows, rows), 0) == iota((rows, rows), 1)).astype(BF)
    turned = [dot_t(eye, router[...]), dot_t(eye, vectors[...].astype(BF))[:, :5], dot_t(eye, pair[...])]
    used = sum(t.shape[1] for t in turned)
    turned = jnp.concatenate([*turned, jnp.zeros((rows, 2 * LANES - used), F32)], axis=1)
    value = jnp.concatenate([qkv[...], out[...], turned.astype(BF)], axis=1)
    half = value.shape[1] // 2

    @pl.when(core[0] == 0)
    def _():
        mine[...] = value[:, :half]
        other[...] = value[:, half:]

    @pl.when(core[0] != 0)
    def _():
        mine[...] = value[:, half:]
        other[...] = value[:, :half]


def pack_dense(core, qkv, out, router, vectors, pair):
    rows = qkv.shape[0]
    half = (qkv.shape[1] + out.shape[1] + 2 * LANES) // 2
    vmem = pl.BlockSpec(memory_space=pltpu.VMEM)
    return pl.pallas_call(
        pack_kernel,
        in_specs=[SMEM] + [vmem] * 5,
        out_specs=[vmem] * 2,
        out_shape=[jax.ShapeDtypeStruct((rows, half), BF)] * 2,
        compiler_params=params(60),
        cost_estimate=LARGE,
        name="pack_dense",
    )(core, qkv, out, router, vectors, pair)


def forward_kernel(experts, subs, off, count, tok, *refs):
    n_pieces = len(refs) - 10
    pieces = refs[:n_pieces]
    w_o, small, qkv_o, n1_o, att_o, aa_o, n2_o, prob_o, w, sems = refs[n_pieces:]
    img = pl.program_id(0)
    width = tok.shape[-1]

    @pl.when(img == 0)
    def _():
        copies = []
        for i, piece in enumerate(pieces):
            rows, cols = piece.shape[0] // subs, piece.shape[1]
            col = pl.multiple_of(off[n_pieces * subs + i], LANES)
            for j in range(subs):
                row = pl.multiple_of(off[i * subs + j], 16)
                copies.append(
                    pltpu.make_async_copy(
                        piece.at[pl.ds(j * rows, rows), :],
                        w.at[pl.ds(row, rows), pl.ds(col, cols)],
                        sems.at[i * subs + j],
                    )
                )
        for c in copies:
            c.start()
        for c in copies:
            c.wait()
        small[...] = jnp.transpose(w[:, 4 * width : 4 * width + LANES].astype(F32))
        pltpu.make_async_copy(w, w_o, sems.at[0]).start()

    def vec(k):
        return small[experts + k : experts + k + 1, :]

    x = tok[0].astype(F32)
    rows = x.shape[0]
    unit, _ = norm_stats(x)
    n1 = (unit * vec(0) + vec(1)).astype(BF)
    n1_o[0] = n1
    biases = (vec(5), None, vec(6))
    for part in range(3):
        cols = slice(part * width, (part + 1) * width)
        block = dot(n1, w[:, cols])
        if biases[part] is not None:
            block = block + biases[part]
        qkv_o[0, :, cols] = block.astype(BF)
    low = iota((rows, LANES), 1) < LANES // 2
    seen = iota((rows, rows), 0) < SEQ
    scale = (width // HEADS) ** -0.5
    for pair in range(HEADS // 2):
        c = pair * LANES
        q2 = qkv_o[0, :, c : c + LANES]
        k2 = qkv_o[0, :, width + c : width + c + LANES]
        v2 = qkv_o[0, :, 2 * width + c : 2 * width + c + LANES]
        got = []
        for side, mask in enumerate((low, ~low)):
            scores = dot_t(k2, jnp.where(mask, q2, jnp.zeros_like(q2))) * scale
            scores = jnp.where(seen, scores, NEG_FILL)
            exps = jnp.exp(scores - jnp.max(scores, axis=0, keepdims=True))
            prob = exps * (1.0 / col_sum(exps))
            prob_o[0, 2 * pair + side] = prob
            got.append(t_dot(prob.astype(BF), v2))
        att_o[0, :, c : c + LANES] = jnp.where(low, got[0], got[1]).astype(BF)
    alive = (img < count[0]).astype(F32)
    after = x + alive * (dot(att_o[0], w[:, 3 * width : 4 * width]) + vec(2))
    aa_o[0] = after
    unit, _ = norm_stats(after)
    n2_o[0] = (unit * vec(3) + vec(4)).astype(BF)

    @pl.when(img == pl.num_programs(0) - 1)
    def _():
        pltpu.make_async_copy(w, w_o, sems.at[0]).wait()


def forward(off, subs, pieces, count, tok, experts, width_all):
    images, rows, width = tok.shape
    block = lambda cols: pl.BlockSpec((1, rows, cols), lambda i: (i, 0, 0))
    shape = lambda cols, t: jax.ShapeDtypeStruct((images, rows, cols), t)
    return pl.pallas_call(
        functools.partial(forward_kernel, experts, subs),
        grid=(images,),
        in_specs=[SMEM, SMEM, block(width)] + [ANY] * len(pieces),
        out_specs=[
            ANY,
            whole((LANES, width)),
            block(3 * width),
            block(width),
            block(width),
            block(width),
            block(width),
            pl.BlockSpec((1, HEADS, rows, rows), lambda i: (i, 0, 0, 0)),
        ],
        out_shape=[
            jax.ShapeDtypeStruct((width, width_all), BF),
            jax.ShapeDtypeStruct((LANES, width), F32),
            shape(3 * width, BF),
            shape(width, BF),
            shape(width, BF),
            shape(width, F32),
            shape(width, BF),
            jax.ShapeDtypeStruct((images, HEADS, rows, rows), F32),
        ],
        scratch_shapes=[
            pltpu.VMEM((width, width_all), BF),
            pltpu.SemaphoreType.DMA((len(pieces) * subs,)),
        ],
        compiler_params=params(60),
        cost_estimate=SMALL,
        name="tokens_forward",
    )(off, count, tok, *pieces)


def dispatch_kernel(experts, half, gated, slots, x, *refs):
    out = refs[-1]
    value = x[...]
    halves, block_rows = out.shape[1:3]
    first, second = slots[0:1, :], slots[1:2, :]
    if gated:
        router = refs[0][...].astype(BF)
        logits = dot_t(router, value)
        logits = jnp.where(iota(logits.shape, 0) < experts, logits, NEG_FILL)
        exps = jnp.exp(logits - jnp.max(logits, axis=0, keepdims=True))
        probs = exps / jnp.sum(exps, axis=0, keepdims=True)
    total = experts * block_rows
    for h in range(halves):
        place = iota((total, value.shape[0]), 0) + (half + h) * total
        hot = ((place == first) | (place == second)).astype(BF)
        out[:, h] = dot(hot, value).astype(BF).reshape(experts, block_rows, value.shape[1])
        if gated:
            row = iota((16, value.shape[0]), 0)
            for e in range(experts):
                gate = probs[e : e + 1, :]
                high = gate.astype(BF).astype(F32)
                pair = jnp.where(row == 14, high, jnp.where(row == 15, gate - high, 0.0))
                placed = dot_t(pair.astype(BF), hot[e * block_rows : (e + 1) * block_rows])
                tail = out[e, h, block_rows - 16 :, :block_rows].astype(F32)
                out[e, h, block_rows - 16 :, :block_rows] = jnp.where(
                    iota(tail.shape, 0) < 14, tail, placed
                ).astype(BF)


def dispatch(slots, x, small, experts, block_rows, half, halves, tag):
    rows, width = x.shape
    gated = small is not None
    more = [small] if gated else []
    vmem = pl.BlockSpec(memory_space=pltpu.VMEM)
    return pl.pallas_call(
        functools.partial(dispatch_kernel, experts, half, gated),
        in_specs=[vmem] * (2 + len(more)),
        out_specs=vmem,
        out_shape=jax.ShapeDtypeStruct((experts, halves, block_rows, width), BF),
        compiler_params=params(24),
        cost_estimate=SMALL,
        name="dispatch_" + tag,
    )(slots, x, *more)


def first_kernel(experts, half_cap, count, capacity, routes, x, out, slots):
    rows = routes.shape[1]
    halves, block_rows = out.shape[1:3]
    alive = iota((1, rows), 1) < count[0] * SEQ
    name = iota((up16(experts), rows), 0)
    earlier = (iota((rows, rows), 0) < iota((rows, rows), 1)).astype(BF)
    limits = jnp.zeros((up16(experts), 1), F32)
    for e in range(experts):
        limits = jnp.where(name[:, 0:1] == e, capacity[e].astype(F32), limits)
    base = 0.0
    for k in range(2):
        hit = jnp.where((routes[k : k + 1, :] == name) & alive, 1.0, 0.0)
        place = col_sum(hit * (dot(hit.astype(BF), earlier) + base))
        keep = place < col_sum(hit * limits)
        base = jnp.sum(hit, axis=1, keepdims=True)
        place = place.astype(jnp.int32)
        half = (place >= half_cap).astype(jnp.int32)
        spot = (half * experts + routes[k : k + 1, :]) * block_rows + place - half * half_cap
        slots[k : k + 1, :] = jnp.where(keep, spot, -1)
    dispatch_kernel(experts, 0, False, slots, x, out)


def first_dispatch(count, capacity, routes, x, half_cap, block_rows, halves):
    rows, width = x.shape
    experts = capacity.shape[0]
    vmem = pl.BlockSpec(memory_space=pltpu.VMEM)
    return pl.pallas_call(
        functools.partial(first_kernel, experts, half_cap),
        in_specs=[SMEM, SMEM, vmem, vmem],
        out_specs=[vmem, vmem],
        out_shape=[
            jax.ShapeDtypeStruct((experts, halves, block_rows, width), BF),
            jax.ShapeDtypeStruct((2, rows), jnp.int32),
        ],
        compiler_params=params(24),
        cost_estimate=SMALL,
        name="dispatch_first",
    )(count, capacity, routes, x)


def expert_kernel(places, n_arrays, n_before, *refs):
    x_ref, c_ref, b_in, b_out = refs[:4]
    arrays, parts = refs[4 : 4 + n_arrays], len(places) // 2
    rest = refs[4 + n_arrays + n_before :]
    act_o, pre_o, x_o, sg_o, r_o, d_o, db_in, db_out, win, wout, sems = rest
    step = pl.program_id(0)
    n, _, size, width = x_ref.shape
    piece = win.shape[1] // parts

    def copies(q):
        cols = pl.ds(q * piece, piece)
        (one, at_one), (two, at_two) = places[q], places[parts + q]
        return (
            pltpu.make_async_copy(
                arrays[one].at[pl.ds(at_one, width), :], win.at[:, cols], sems.at[q]
            ),
            pltpu.make_async_copy(
                arrays[two].at[pl.ds(at_two, piece), :], wout.at[cols, :], sems.at[parts + q]
            ),
        )

    @pl.when(step == 0)
    def _():
        for q in range(parts):
            for c in copies(q):
                c.start()
        db_in[...] = jnp.zeros_like(db_in)
        db_out[...] = jnp.zeros_like(db_out)

    eye = (iota((size, size), 0) == iota((size, size), 1)).astype(BF)
    for s in range(n):
        rows = slice(s * size, (s + 1) * size)
        x_o[rows, :] = x_ref[s, 0]
        turned = dot_t(eye, x_ref[s, 0, size - 16 :, :size])
        gate = jnp.sum(jnp.where(iota(turned.shape, 1) >= 14, turned, 0.0), axis=1, keepdims=True)
        sg_o[rows, :] = (gate * c_ref[s, 0].astype(F32)).astype(BF)
    x = x_o[...]
    slot_grad = sg_o[...]
    db_out[0:1, :] += col_sum(slot_grad.astype(F32))

    @pl.when(step == 0)
    def _():
        for q in range(parts):
            for c in copies(q):
                c.wait()

    for q in range(parts):
        cols = slice(q * piece, (q + 1) * piece)
        pre = dot(x, win[:, cols]) + b_in[q, 0:1, :]
        square = pre * pre
        turn = jnp.tanh(pre * (GELU_A + GELU_A * GELU_B * square))
        half_turn = 0.5 * turn + 0.5
        act_o[:, cols] = (pre * half_turn).astype(BF)
        slope = half_turn + (0.5 * pre) * (1.0 - turn * turn) * (GELU_A + 3 * GELU_A * GELU_B * square)
        pre_grad = dot_t(slot_grad, wout[cols, :]) * slope
        pre_o[:, cols] = pre_grad.astype(BF)
        db_in[q, 0:1, :] += col_sum(pre_grad)
    out = (dot(act_o[...], wout[...]) + b_out[0:1, :]).astype(BF)
    back = dot_t(pre_o[...], win[...])
    ones = jnp.ones((16, width), BF)
    for s in range(n):
        rows = slice(s * size, (s + 1) * size)
        r_o[s, 0] = out[rows]
        d_o[s] = back[rows].astype(BF)
        prod = c_ref[s, 0].astype(F32) * out[rows].astype(F32)
        high = prod.astype(BF)
        low = (prod - high.astype(F32)).astype(BF)
        gate_grad = dot_t(ones, high) + dot_t(ones, low)
        grad_high = gate_grad.astype(BF).astype(F32)
        row = iota(gate_grad.shape, 0)
        tail = back[(s + 1) * size - 16 : (s + 1) * size, :size]
        both = jnp.where(row == 14, grad_high, gate_grad - grad_high)
        d_o[s, size - 16 :, :size] = jnp.where(row < 14, tail, both).astype(BF)


def expert_call(x, c, arrays, places, b_in, b_out, half, halves, before):
    experts, _, size, width = x.shape
    parts, _, piece = b_in.shape
    n = max(1, 256 // size)
    steps = experts // n
    rows, hidden = n * size, parts * piece
    before = list(before)
    tall = lambda cols: pl.BlockSpec((rows, cols), lambda i: (half * steps + i, 0))
    of_half = pl.BlockSpec((n, 1, size, width), lambda i: (i, half, 0, 0))
    total = halves * experts * size
    return pl.pallas_call(
        functools.partial(expert_kernel, places, len(arrays), len(before)),
        grid=(steps,),
        in_specs=[
            pl.BlockSpec((n, 1, size, width), lambda i: (i, 0, 0, 0)),
            of_half,
            whole((parts, 8, piece)),
            whole((8, width)),
        ]
        + [ANY] * (len(arrays) + len(before)),
        out_specs=[
            tall(hidden),
            tall(hidden),
            tall(width),
            tall(width),
            of_half,
            pl.BlockSpec((n, size, width), lambda i: (i, 0, 0)),
            whole((parts, 8, piece)),
            whole((8, width)),
        ],
        out_shape=[
            jax.ShapeDtypeStruct((total, hidden), BF),
            jax.ShapeDtypeStruct((total, hidden), BF),
            jax.ShapeDtypeStruct((total, width), BF),
            jax.ShapeDtypeStruct((total, width), BF),
            jax.ShapeDtypeStruct((experts, halves, size, width), BF),
            jax.ShapeDtypeStruct((experts, size, width), BF),
            jax.ShapeDtypeStruct((parts, 8, piece), F32),
            jax.ShapeDtypeStruct((8, width), F32),
        ],
        scratch_shapes=[
            pltpu.VMEM((width, hidden), BF),
            pltpu.VMEM((hidden, width), BF),
            pltpu.SemaphoreType.DMA((2 * parts,)),
        ],
        input_output_aliases={4 + len(arrays) + i: i for i in range(len(before))},
        compiler_params=params(44),
        cost_estimate=SMALL,
        name="expert_" + "ab"[half],
    )(x, c, b_in, b_out, *arrays, *before)


def weight_kernel(piece, q_in, q_out, n_more, x, pre, act, grad, bias, *refs):
    more, (in_o, out_o, bias_o, xs, ps, acts, gs, held, sems) = refs[:n_more], refs[n_more:]
    width = x.shape[1]
    copies = [
        pltpu.make_async_copy(x, xs, sems.at[0]),
        pltpu.make_async_copy(pre.at[:, pl.ds(q_in * piece, piece)], ps, sems.at[1]),
        pltpu.make_async_copy(act.at[:, pl.ds(q_out * piece, piece)], acts, sems.at[2]),
        pltpu.make_async_copy(grad, gs, sems.at[3]),
    ]
    extra = [
        pltpu.make_async_copy(far, held.at[k, pl.ds(0, far.shape[0]), :], sems.at[4 + k])
        for k, far in enumerate(more)
    ]
    copies[0].start()
    copies[1].start()
    copies[0].wait()
    copies[1].wait()
    for c in [copies[2], copies[3], *extra]:
        c.start()
    first = t_dot(xs[...], ps[...])
    sums = bias[q_in]
    for k in range(n_more // 2):
        extra[k].wait()
        first = first + held[k, :width, :].astype(F32)
        sums = sums + held[k, width:, :].astype(F32)
    in_o[:width, :] = first.astype(in_o.dtype)
    bias_o[...] = sums.astype(bias_o.dtype)
    if not n_more:
        in_o[width:, :] = sums.astype(in_o.dtype)
    copies[2].wait()
    copies[3].wait()
    second = t_dot(acts[...], gs[...])
    for k in range(n_more // 2, n_more):
        extra[k].wait()
        second = second + held[k, :piece, :].astype(F32)
    out_o[...] = second.astype(out_o.dtype)


def weight_grads(x, pre, act, grad, bias, piece, q_in, q_out, kind, more=()):
    total, width = x.shape
    vmem = pl.BlockSpec(memory_space=pltpu.VMEM)
    return pl.pallas_call(
        functools.partial(weight_kernel, piece, q_in, q_out, len(more)),
        in_specs=[ANY] * 4 + [vmem] + [ANY] * len(more),
        out_specs=[vmem] * 3,
        out_shape=[
            jax.ShapeDtypeStruct((width if more else width + 16, piece), kind),
            jax.ShapeDtypeStruct((piece, width), kind),
            jax.ShapeDtypeStruct((16, piece), kind),
        ],
        scratch_shapes=[
            pltpu.VMEM((total, width), BF),
            pltpu.VMEM((total, piece), BF),
            pltpu.VMEM((total, piece), BF),
            pltpu.VMEM((total, width), BF),
            pltpu.VMEM((max(1, len(more)), width + 16, width), BF),
            pltpu.SemaphoreType.DMA((4 + len(more),)),
        ],
        compiler_params=params(60),
        cost_estimate=SMALL,
        name="weight_grads",
    )(x, pre, act, grad, bias, *more)


def backward_kernel(experts, n, split, off, count, slots, cot, n1_far, qkv, att_far, aa, n2, probs_in, w_far, w_out, small, *refs):
    backs = refs[:n]
    ag_o, gp_o, dq_o = refs[n : n + 3]
    grads = refs[n + 3 : n + 3 + split]
    dw, ds, marks, ag_all, dq_all, n1, att, w, sems = refs[n + 3 + split :]
    img = pl.program_id(0)
    width = n1.shape[-1]
    late = [
        pltpu.make_async_copy(far, here, sems.at[k])
        for k, (far, here) in enumerate(((n1_far, n1), (att_far, att), (w_far, w)))
    ]
    size = backs[0].shape[1]
    total = experts * size

    @pl.when(img == 0)
    def _():
        for c in late:
            c.start()
        ds[...] = jnp.zeros_like(ds)
        line = iota((LANES, size), 0)
        for h in range(n):
            for e in range(experts):
                ends = backs[h][e, size - 16 :, :size].astype(F32)
                for k in range(2):
                    marks[2 * h + k, :, e * size : (e + 1) * size] = jnp.where(
                        line == e, ends[14 + k : 15 + k, :], 0.0
                    ).astype(BF)

    def vec(k):
        return small[experts + k : experts + k + 1, :]

    def add_vec(k, value):
        ds[experts + k : experts + k + 1, :] += value

    alive = (img < count[0]).astype(F32)
    up = cot[0].astype(F32)
    rows = up.shape[0]
    normed = n2[0]
    lane = iota((rows, LANES), 1)
    router = jnp.where(iota(small.shape, 0) < experts, small[...], 0.0).astype(BF)
    logits = jnp.where(lane < experts, dot_t(normed, router), NEG_FILL)
    exps = jnp.exp(logits - jnp.max(logits, axis=-1, keepdims=True))
    probs = exps / jnp.sum(exps, axis=-1, keepdims=True)
    gp_o[0] = probs
    first, second = slots[0, :, 0:1], slots[0, :, 1:2]
    normed_grad = jnp.zeros((rows, width), F32)
    placed = jnp.zeros((rows, LANES), F32)
    for h in range(n):
        place = iota((rows, total), 1) + h * total
        hot = ((place == first) | (place == second)).astype(BF)
        normed_grad = normed_grad + dot(hot, backs[h][...].reshape(total, width))
        placed = placed + dot_t(hot, marks[2 * h]) + dot_t(hot, marks[2 * h + 1])
    logit_grad = (
        probs * (placed - jnp.sum(probs * placed, axis=-1, keepdims=True))
    ).astype(BF)
    normed_grad = normed_grad + dot(logit_grad, router)
    ds[...] += jnp.where(iota(ds.shape, 0) < experts, t_dot(logit_grad, normed), 0.0)
    unit, inverse = norm_stats(aa[0])
    add_vec(3, col_sum(normed_grad * unit))
    add_vec(4, col_sum(normed_grad))
    after_grad = up + norm_back(unit, inverse, vec(3), normed_grad)
    attn_grad = (alive * after_grad).astype(BF)
    add_vec(2, col_sum(attn_grad.astype(F32)))
    ag_all[img] = attn_grad
    att_grad = dot_t(attn_grad, w_out[...]).astype(BF)
    low = lane < LANES // 2
    scale = (width // HEADS) ** -0.5
    for pair in range(HEADS // 2):
        c = pair * LANES
        q2 = qkv[0, :, c : c + LANES]
        k2 = qkv[0, :, width + c : width + c + LANES]
        v2 = qkv[0, :, 2 * width + c : 2 * width + c + LANES]
        o2 = att_grad[:, c : c + LANES]
        got = []
        for side, mask in enumerate((low, ~low)):
            prob = probs_in[0, 2 * pair + side]
            prob_grad = dot_t(v2, jnp.where(mask, o2, jnp.zeros_like(o2)))
            score_grad = (prob * (prob_grad - col_sum(prob * prob_grad))).astype(BF)
            got.append(
                (
                    t_dot(score_grad, k2) * scale,
                    dot(score_grad, q2) * scale,
                    dot(prob.astype(BF), o2),
                )
            )
        for k in range(3):
            dq_o[0, :, k * width + c : k * width + c + LANES] = jnp.where(
                low, got[0][k], got[1][k]
            ).astype(BF)
    grad = dq_o[0]
    dq_all[img] = grad
    for k in range(3):
        ds[experts + 5 + k : experts + 6 + k, :] += col_sum(grad[:, k * width : (k + 1) * width].astype(F32))
    ag_o[0] = after_grad

    @pl.when(img == pl.num_programs(0) - 1)
    def _():
        dw[:, 4 * width : 4 * width + LANES] = jnp.transpose(ds[...])
        for c in late:
            c.wait()
        left = n1[...].reshape(-1, width)
        for k in range(3):
            cols = slice(k * width, (k + 1) * width)
            dw[:, cols] = t_dot(left, dq_all[:, :, cols].reshape(-1, width))
        dw[:, 3 * width : 4 * width] = t_dot(
            att[...].reshape(-1, width), ag_all[...].reshape(-1, width)
        )
        with_weight = jnp.zeros((width, LANES), F32)
        with_sums = jnp.zeros((width, LANES), F32)
        for k in range(3 * width // LANES):
            cols = slice(k * LANES, (k + 1) * LANES)
            part, at = divmod(k * LANES, width)
            value = w[:, cols].astype(F32)
            sums = ds[experts + 5 + part : experts + 6 + part, at : at + LANES]
            with_weight = with_weight + value * dw[:, cols]
            with_sums = with_sums + value * sums
        sums = jnp.sum(with_sums, axis=1, keepdims=True)
        at = 4 * width
        sides = w[:, at : at + LANES].astype(F32)
        gain, shift = sides[:, experts : experts + 1], sides[:, experts + 1 : experts + 2]
        gains = (jnp.sum(with_weight, axis=1, keepdims=True) - shift * sums) / gain
        spot = iota((width, LANES), 1)
        cols = slice(at, at + LANES)
        dw[:, cols] = jnp.where(
            spot == experts, gains, jnp.where(spot == experts + 1, sums, dw[:, cols])
        )
        if split == 1:
            grads[0][...] = dw[...].astype(BF)
        else:
            cols = grads[0].shape[1]
            step = width // 16
            for k in range(8):
                col = pl.multiple_of(off[16 + k // 4], LANES)
                for j in range(4):
                    row = pl.multiple_of(off[4 * (k % 4) + j], 16)
                    grads[k][j * step : (j + 1) * step, :] = dw[
                        pl.ds(row, step), pl.ds(col, cols)
                    ].astype(BF)


def backward(off, count, slots, cot, n1, qkv, att, aa, n2, prob, w, small, backs, experts, split):
    images, rows, width = cot.shape
    width_all = w.shape[1]
    n = len(backs)
    cut = (width, width_all) if split == 1 else (width // 4, width_all // 2)
    block = lambda cols: pl.BlockSpec((1, rows, cols), lambda i: (i, 0, 0))
    got = pl.pallas_call(
        functools.partial(backward_kernel, experts, n, split),
        grid=(images,),
        in_specs=[SMEM, SMEM, block(2), block(width), ANY, block(3 * width), ANY, block(width), block(width)]
        + [pl.BlockSpec((1, HEADS, rows, rows), lambda i: (i, 0, 0, 0))]
        + [ANY, pl.BlockSpec((width, width), lambda i: (0, 3), pipeline_mode=pl.Buffered(1)), whole(small.shape)]
        + [whole(backs[0].shape)] * n,
        out_specs=[block(width), block(LANES), block(3 * width)] + [whole(cut)] * split,
        out_shape=[
            jax.ShapeDtypeStruct((images, rows, width), F32),
            jax.ShapeDtypeStruct((images, rows, LANES), F32),
            jax.ShapeDtypeStruct((images, rows, 3 * width), BF),
        ]
        + [jax.ShapeDtypeStruct(cut, BF)] * split,
        scratch_shapes=[
            pltpu.VMEM((width, width_all), F32),
            pltpu.VMEM((LANES, width), F32),
            pltpu.VMEM((2 * n, LANES, backs[0].shape[0] * backs[0].shape[1]), BF),
            pltpu.VMEM((images, rows, width), BF),
            pltpu.VMEM((images, rows, 3 * width), BF),
            pltpu.VMEM((images, rows, width), BF),
            pltpu.VMEM((images, rows, width), BF),
            pltpu.VMEM(w.shape, BF),
            pltpu.SemaphoreType.DMA((3,)),
        ],
        compiler_params=params(),
        cost_estimate=SMALL,
        name="tokens_backward",
    )(off, count, slots, cot, n1, qkv, att, aa, n2, prob, w, w, small, *backs)
    return got[0], got[1], got[2], got[3:]


def place_rows(out, value):
    for k in range(out.shape[0] // SEQ):

        @pl.when(pl.program_id(0) == k)
        def _():
            out[k * SEQ : (k + 1) * SEQ, :] = value[:SEQ]


def finish_kernel(experts, after_grad, grad, tok, w, small, out):
    width = tok.shape[-1]
    normed_grad = dot_t(grad[0], w[...])
    unit, inverse = norm_stats(tok[0].astype(F32))
    value = after_grad[0] + norm_back(unit, inverse, small[experts : experts + 1, :], normed_grad)
    place_rows(out, value)


def finish(after_grad, grad, tok, w, small, experts):
    images, rows, width = tok.shape
    block = lambda cols: pl.BlockSpec((1, rows, cols), lambda i: (i, 0, 0))
    return pl.pallas_call(
        functools.partial(finish_kernel, experts),
        grid=(images,),
        in_specs=[block(width), block(3 * width), block(width), whole((width, 3 * width)), whole(small.shape)],
        out_specs=whole((images * SEQ, width)),
        out_shape=jax.ShapeDtypeStruct((images * SEQ, width), F32),
        compiler_params=params(60),
        cost_estimate=SMALL,
        name="tokens_finish",
    )(after_grad, grad, tok, w, small)


def output_kernel(count, slots, aa, probs, outs, out, total_f):
    rows = aa.shape[1]
    experts, n, size, width = outs.shape
    total = experts * size
    alive = (pl.program_id(0) < count[0]).astype(F32)
    first, second = slots[0, :, 0:1], slots[0, :, 1:2]
    gates = jnp.concatenate(
        [jnp.broadcast_to(probs[0, :, e : e + 1], (rows, size)) for e in range(experts)], axis=1
    )
    moe = jnp.zeros(aa.shape[1:], F32)
    for h in range(n):
        place = iota((rows, total), 1) + h * total
        gate = jnp.where((place == first) | (place == second), gates, 0.0)
        high = gate.astype(BF)
        low = (gate - high.astype(F32)).astype(BF)
        value = outs[:, h].reshape(total, width)
        moe = moe + dot(high, value) + dot(low, value)
    place_rows(total_f, aa[0] + alive * moe)

    @pl.when(pl.program_id(0) == pl.num_programs(0) - 1)
    def _():
        out[...] = total_f[...].astype(BF)


def block_output(count, slots, aa, probs, outs):
    images, rows, width = aa.shape
    block = lambda cols: pl.BlockSpec((1, rows, cols), lambda i: (i, 0, 0))
    return pl.pallas_call(
        output_kernel,
        grid=(images,),
        in_specs=[SMEM, block(2), block(width), block(LANES), whole(outs.shape)],
        out_specs=whole((images * SEQ, width)),
        out_shape=jax.ShapeDtypeStruct((images * SEQ, width), BF),
        scratch_shapes=[pltpu.VMEM((images * SEQ, width), F32)],
        compiler_params=params(60),
        cost_estimate=SMALL,
        name="block_output",
    )(count, slots, aa, probs, outs)


def local(sizes, *args):
    (tokens, image_count, routes, capacity, ln1_gain, ln1_bias, qkv_weight, qv_bias, out_weight, out_bias,
     ln2_gain, ln2_bias, router_weight, expert_in, expert_in_bias, expert_out, expert_out_bias, cotangent) = args
    dp, experts = sizes
    grouped = sizes == (4, 8)
    devices = dp * experts
    me_d = lax.axis_index("dp")
    me_e = lax.axis_index("expert")
    core = me_e % 2
    token_count, width = tokens.shape
    images = token_count // SEQ
    rows = up16(SEQ)
    cap = max(2, 5 * token_count // (2 * experts))
    halves = 2 if grouped else 1
    half_cap = -(-cap // halves)
    block_rows = up16(half_cap + 2)

    def hop(value, mask):
        return lax.ppermute(value, BOTH, [(i, i ^ mask) for i in range(devices)])

    def by_image(value):
        value = value.reshape(images, SEQ, value.shape[-1])
        fill = -1 if value.dtype == jnp.int32 else 0
        return jnp.pad(value, ((0, 0), (0, rows - SEQ), (0, 0)), constant_values=fill)

    def side_rows(values):
        return functools.reduce(
            lambda a, b: a + b,
            [jnp.pad(v.astype(F32)[None], ((k, 7 - k), (0, 0))) for k, v in enumerate(values)],
        )

    def slots_and_blocks(value):
        return first_dispatch(image_count, capacity, routes.T, value, half_cap, block_rows, halves)

    def slot_forms(slots):
        slots = slots.reshape(2, images, SEQ)
        slots = jnp.pad(slots, ((0, 0), (0, 0), (0, rows - SEQ)), constant_values=-1)
        return slots.transpose(1, 2, 0), slots.reshape(2, -1)

    def after(values, *done):
        return lax.optimization_barrier((values, done))[0]

    tok = by_image(tokens)

    vectors = [ln1_gain, ln1_bias, out_bias, ln2_gain, ln2_bias]
    width_all = 4 * width + 2 * LANES
    wide = expert_in.shape[2]
    spot = me_d * expert_out_bias.shape[1]
    if grouped:
        half = width_all // 2
        mine, other = pack_dense(
            core.reshape(1).astype(jnp.int32), qkv_weight, out_weight, router_weight.T, side_rows(vectors), qv_bias
        )
        got = hop(other, 1)
        chip = jnp.where(
            core == 0, jnp.concatenate([mine, got], axis=0), jnp.concatenate([got, mine], axis=0)
        )
        bias_out = lax.dynamic_update_slice(jnp.zeros((1, width), BF), expert_out_bias, (0, spot))
        bias = jnp.concatenate([expert_in_bias, bias_out, jnp.zeros((14, wide), BF)], axis=0)
        one = jnp.concatenate([expert_in[0], bias], axis=0)
        two = jnp.concatenate([expert_out[0], bias], axis=0)
        from_x, from_y = hop(expert_in[0], 8), hop(expert_out[0], 16)
        cot_blocks, slots = slots_and_blocks(after(cotangent, chip))
        slots_col, slots_row = slot_forms(slots)
        line = jnp.concatenate([chip] + [hop(chip, 2 * dz) for dz in (1, 2, 3)], axis=0)
        held, from_x, from_y = after((line, from_x, from_y))
        own = [line] + [hop(held, 8 * dxy) for dxy in (3, 1, 2)]
        own = [own[0], own[2], own[3], own[1]]
        step = width // 16
        at_rows = jnp.stack([((me_d ^ a) * 4 + ((me_e // 2) ^ b)) * step for a in range(4) for b in range(4)])
        at_cols = jnp.stack([core * half, (1 - core) * half])
        off_back = jnp.concatenate([at_rows, at_cols]).astype(jnp.int32)
        off = jnp.concatenate([at_rows, at_rows, jnp.repeat(at_cols, 4)]).astype(jnp.int32)
        own, tok, slots_row, off, one, two = after((own, tok, slots_row, off, one, two))
        pieces = own + [hop(piece, 1) for piece in own]
        subs = 4
        later_one, later_two, relay_x, relay_y = after((one, two, from_x, from_y), *own)
        near = hop(later_one, 16), hop(later_two, 8)
        relays = hop(relay_x, 16), hop(relay_y, 8), hop(near[0][width:], 8)
        arrays = [one, from_x, near[0], relays[0]]
        biases = [bias, near[1][width:], near[0][width:], relays[2]]
        b_in = jnp.stack([v[:8] for v in biases]).astype(F32)
        arrays += [two, near[1], from_y, relays[1]]
        places = tuple((q, 0) for q in range(8))
        b_out = jnp.broadcast_to(jnp.sum(b_in[:, 1], axis=0), (8, width))
        after_line = held
    else:
        fill = width_all - 4 * width - experts - 7
        pack = jnp.concatenate(
            [qkv_weight, out_weight, router_weight, jnp.stack(vectors, axis=1), qv_bias.T, jnp.zeros((ln1_gain.shape[0], fill), BF)], axis=1
        )
        pieces = [lax.all_gather(pack, BOTH, axis=0, tiled=True)]
        cot_blocks, slots = slots_and_blocks(cotangent)
        slots_col, slots_row = slot_forms(slots)
        off = jnp.zeros((2,), jnp.int32)
        off_back = off
        subs = 1
        after_line = pieces[0]
        w_in = lax.all_gather(expert_in[0], "dp", axis=0, tiled=False)
        w_out = lax.all_gather(expert_out[0], "dp", axis=0, tiled=False)
        arrays = [w[q] for w in (w_in, w_out) for q in range(dp)]
        places = tuple((q, 0) for q in range(2 * dp))
        b_in = lax.all_gather(jnp.broadcast_to(expert_in_bias, (8, wide)), "dp", axis=0, tiled=False).astype(F32)
        b_out = jnp.broadcast_to(
            lax.all_gather(expert_out_bias, "dp", axis=1, tiled=True).astype(F32), (8, width)
        )

    def exchange(blocks):
        return lax.all_to_all(blocks, "expert", 0, 0, tiled=True)

    cot_sent = exchange(after(cot_blocks, after_line))
    cot = by_image(cotangent)

    w, small, qkv, n1, att, aa, n2, prob = forward(off, subs, pieces, image_count, tok, experts, width_all)
    row_sent = []
    flat = n2.reshape(-1, width)
    for h in range(halves):
        sent = dispatch(slots_row, flat, small, experts, block_rows, h, 1, "ab"[h])
        waits = (near, relays)[h] if grouped else ()
        sent, cot_sent = after((sent, cot_sent), *row_sent, *waits)
        if h:
            sent, cot, slots_col = after((sent, cot, slots_col))
        row_sent.append(exchange(sent))

    back, grads_out, db_ins, db_outs, tall = [], [], [], [], ()
    for h in range(halves):
        *tall, d, db_in, db_out = expert_call(
            row_sent[h], cot_sent, arrays, places, b_in, b_out, h, halves, tall
        )
        grads_out.append(d)
        if h + 1 < halves:
            back.append(exchange(d))
        db_ins.append(db_in)
        db_outs.append(db_out)
    *tall, outs_back = tall
    db_in, db_out = sum(db_ins), sum(db_outs)

    both = [db_in[:, 0:1]]
    if grouped:
        both.append(jnp.broadcast_to(db_out[0:1], db_in[:, 0:1].shape))
    bias_sums = jnp.concatenate(
        [*both, jnp.zeros((dp, 16 - len(both), wide), F32)], axis=1
    )

    def weights_of(q_in, q_out, kind, more=()):
        act, pre, rows_in, slot_grad = tall
        return weight_grads(rows_in, pre, act, slot_grad, bias_sums, wide, q_in, q_out, kind, more)

    if grouped:
        far_in, far_out, _ = weights_of(3, 3, BF)
        tall = after(tall, far_in, far_out, *back)
        back.append(exchange(after(grads_out[-1], far_in, far_out, *back)))
        far_in, far_out = hop(far_in, 8), hop(far_out, 16)
        near_in, near_out, _ = weights_of(1, 2, BF)
        last_in, last_out, _ = weights_of(2, 1, BF)
        last_in = (last_in.astype(F32) + far_in.astype(F32)).astype(BF)
        last_out = (last_out.astype(F32) + far_out.astype(F32)).astype(BF)
        ready = (near_in, near_out, last_in, last_out)
        near_in, near_out = hop(near_in, 8), hop(near_out, 16)
        last_in, last_out = hop(last_in, 16), hop(last_out, 8)
        arrived = (near_in, near_out, last_in, last_out)
    else:
        ready = arrived = ()
        scatter = lambda v: lax.psum_scatter(v, "dp", scatter_dimension=0, tiled=True).astype(F32)
        back.append(exchange(grads_out[-1]))
        every = [weights_of(q, q, BF) for q in range(dp)]
        g_in = scatter(jnp.stack([e[0][:width] for e in every]))
        g_out = scatter(jnp.stack([e[1] for e in every]))
        g_b_in = lax.psum_scatter(
            db_in[:, 0].reshape(1, -1).astype(BF), "dp", scatter_dimension=1, tiled=True
        ).astype(F32)
        g_b_out = lax.psum_scatter(db_out[0:1].astype(BF), "dp", scatter_dimension=1, tiled=True).astype(F32)

    r_sent = exchange(after(outs_back, *back))
    back = after(back, *ready)
    after_grad, probs, grad, grads = backward(
        off_back, image_count, slots_col, cot, n1, qkv, att, aa, n2, prob, w, small, back, experts,
        8 if grouped else 1,
    )
    grads = after(grads, *arrived)
    block_out = block_output(image_count, slots_col, aa, probs, r_sent)
    def add(*values):
        return functools.reduce(lambda a, b: a + b, [v.astype(F32) for v in values])

    if grouped:
        sibling = {a: hop(grads[4 + a], 1) for a in (3, 1, 2, 0)}
        ways = [add(grads[a], sibling[a]).astype(BF) for a in range(4)]
        tall, bias_sums = after((tall, bias_sums), *ways)
        own_in, own_out, g_bias = weights_of(0, 0, F32, (near_in, last_in, near_out, last_out))
        g_in, g_out = own_in[None], own_out[None]
        g_b_in = g_bias[0:1]
        g_b_out = lax.dynamic_slice(g_bias[1:2], (0, spot), expert_out_bias.shape)
        after_grad, grad = after((after_grad, grad), own_in, own_out)
    tokens_grad = finish(after_grad, grad, tok, w, small, experts)

    if grouped:
        ways[0], tokens_grad, g_in, g_out = after((ways[0], tokens_grad, g_in, g_out))
        ways = [ways[0], *[hop(ways[a], 8 * a) for a in (3, 1, 2)]]
        step = width // 16
        cuts = [add(*[way[b * step : (b + 1) * step] for way in ways]) for b in range(4)]
        cuts = [cuts[0], *[c.astype(BF) for c in cuts[1:]]]
        cuts, r_sent = after((cuts, r_sent))
        chip = add(cuts[0], *[hop(cuts[b], 2 * b) for b in (1, 2, 3)])
        n_rows = step // 2
        keep = lax.dynamic_slice_in_dim(chip, core * n_rows, n_rows, 0)
        chip, block_out = after((chip, block_out))
        give = lax.dynamic_slice_in_dim(chip, (1 - core) * n_rows, n_rows, 0)
        got = hop(give.astype(BF), 1).astype(F32)
        dense = jnp.where(
            core == 0, jnp.concatenate([keep, got], axis=1), jnp.concatenate([got, keep], axis=1)
        )
    else:
        dense = lax.psum_scatter(grads[0], BOTH, scatter_dimension=0, tiled=True).astype(F32)
    side = dense[:, 4 * width :]
    vecs = [side[:, experts + k] for k in range(8)]
    return (
        block_out,
        tokens_grad,
        vecs[0],
        vecs[1],
        dense[:, : 3 * width],
        jnp.stack([vecs[5], vecs[7]], axis=0),
        dense[:, 3 * width : 4 * width],
        vecs[2],
        vecs[3],
        vecs[4],
        side[:, :experts],
        g_in,
        g_b_in,
        g_out,
        g_b_out,
    )


def solution(mesh):
    rows, line, cols = P(BOTH, None), P(BOTH), P(None, BOTH)
    experts = (P("expert", None, "dp"), P("expert", "dp"), P("expert", "dp", None), P("expert", "dp"))
    dense = (line, line, rows, cols, rows, line, line, line, rows)
    return jax.shard_map(
        functools.partial(local, (mesh.shape["dp"], mesh.shape["expert"])),
        mesh=mesh,
        in_specs=(rows, line, rows, P(), *dense, *experts, rows),
        out_specs=(rows, rows, *dense, *experts),
        check_vma=False,
    )
```

```python
import functools

import jax
import jax.numpy as jnp
from jax import lax
from jax.experimental import pallas as pl
from jax.experimental.pallas import tpu as pltpu
from jax.sharding import PartitionSpec as P

HEADS = 12
SEQ = 197
EPS_NORM = 1e-06
NEG_FILL = -1e30
BF = jnp.bfloat16
F32 = jnp.float32
LANES = 128
GELU_A = 0.7978845608028654
GELU_B = 0.044715
BOTH = ("dp", "expert")


def up16(n):
    return -(-n // 16) * 16


def dot(left, right):
    return jnp.dot(left, right, preferred_element_type=F32)


def dot_t(left, right):
    return lax.dot_general(left, right, (((1,), (1,)), ((), ())), preferred_element_type=F32)


def t_dot(left, right):
    return lax.dot_general(left, right, (((0,), (0,)), ((), ())), preferred_element_type=F32)


def iota(shape, dim):
    return lax.broadcasted_iota(jnp.int32, shape, dim)


def params(mib=60):
    return pltpu.CompilerParams(vmem_limit_bytes=mib << 20)


def whole(shape):
    zeros = (0,) * len(shape)
    return pl.BlockSpec(shape, lambda *_: zeros, pipeline_mode=pl.Buffered(1))


SMALL = pl.CostEstimate(flops=1 << 20, bytes_accessed=1 << 16, transcendentals=0)
LARGE = pl.CostEstimate(flops=1 << 34, bytes_accessed=1 << 16, transcendentals=0)
SMEM = pl.BlockSpec(memory_space=pltpu.SMEM)
ANY = pl.BlockSpec(memory_space=pl.ANY)


def norm_stats(values):
    centered = values - jnp.mean(values, axis=-1, keepdims=True)
    inverse = lax.rsqrt(jnp.mean(centered * centered, axis=-1, keepdims=True) + EPS_NORM)
    return centered * inverse, inverse


def norm_back(unit, inverse, gain, grad):
    scaled = grad * gain
    mean_one = jnp.mean(scaled, axis=-1, keepdims=True)
    mean_two = jnp.mean(scaled * unit, axis=-1, keepdims=True)
    return inverse * (scaled - mean_one - unit * mean_two)


def col_sum(values):
    return jnp.sum(values, axis=0, keepdims=True)


def pack_kernel(core, qkv, out, router, vectors, pair, mine, other):
    rows = qkv.shape[0]
    eye = (iota((rows, rows), 0) == iota((rows, rows), 1)).astype(BF)
    turned = [dot_t(eye, router[...]), dot_t(eye, vectors[...].astype(BF))[:, :5], dot_t(eye, pair[...])]
    used = sum(t.shape[1] for t in turned)
    turned = jnp.concatenate([*turned, jnp.zeros((rows, 2 * LANES - used), F32)], axis=1)
    value = jnp.concatenate([qkv[...], out[...], turned.astype(BF)], axis=1)
    half = value.shape[1] // 2

    @pl.when(core[0] == 0)
    def _():
        mine[...] = value[:, :half]
        other[...] = value[:, half:]

    @pl.when(core[0] != 0)
    def _():
        mine[...] = value[:, half:]
        other[...] = value[:, :half]


def pack_dense(core, qkv, out, router, vectors, pair):
    rows = qkv.shape[0]
    half = (qkv.shape[1] + out.shape[1] + 2 * LANES) // 2
    vmem = pl.BlockSpec(memory_space=pltpu.VMEM)
    return pl.pallas_call(
        pack_kernel,
        in_specs=[SMEM] + [vmem] * 5,
        out_specs=[vmem] * 2,
        out_shape=[jax.ShapeDtypeStruct((rows, half), BF)] * 2,
        compiler_params=params(60),
        cost_estimate=LARGE,
        name="pack_dense",
    )(core, qkv, out, router, vectors, pair)


def forward_kernel(experts, subs, off, count, tok, *refs):
    n_pieces = len(refs) - 10
    pieces = refs[:n_pieces]
    w_o, small, qkv_o, n1_o, att_o, aa_o, n2_o, prob_o, w, sems = refs[n_pieces:]
    img = pl.program_id(0)
    width = tok.shape[-1]

    @pl.when(img == 0)
    def _():
        copies = []
        for i, piece in enumerate(pieces):
            rows, cols = piece.shape[0] // subs, piece.shape[1]
            col = pl.multiple_of(off[n_pieces * subs + i], LANES)
            for j in range(subs):
                row = pl.multiple_of(off[i * subs + j], 16)
                copies.append(
                    pltpu.make_async_copy(
                        piece.at[pl.ds(j * rows, rows), :],
                        w.at[pl.ds(row, rows), pl.ds(col, cols)],
                        sems.at[i * subs + j],
                    )
                )
        for c in copies:
            c.start()
        for c in copies:
            c.wait()
        small[...] = jnp.transpose(w[:, 4 * width : 4 * width + LANES].astype(F32))
        pltpu.make_async_copy(w, w_o, sems.at[0]).start()

    def vec(k):
        return small[experts + k : experts + k + 1, :]

    x = tok[0].astype(F32)
    rows = x.shape[0]
    unit, _ = norm_stats(x)
    n1 = (unit * vec(0) + vec(1)).astype(BF)
    n1_o[0] = n1
    biases = (vec(5), None, vec(6))
    for part in range(3):
        cols = slice(part * width, (part + 1) * width)
        block = dot(n1, w[:, cols])
        if biases[part] is not None:
            block = block + biases[part]
        qkv_o[0, :, cols] = block.astype(BF)
    low = iota((rows, LANES), 1) < LANES // 2
    seen = iota((rows, rows), 0) < SEQ
    scale = (width // HEADS) ** -0.5
    for pair in range(HEADS // 2):
        c = pair * LANES
        q2 = qkv_o[0, :, c : c + LANES]
        k2 = qkv_o[0, :, width + c : width + c + LANES]
        v2 = qkv_o[0, :, 2 * width + c : 2 * width + c + LANES]
        got = []
        for side, mask in enumerate((low, ~low)):
            scores = dot_t(k2, jnp.where(mask, q2, jnp.zeros_like(q2))) * scale
            scores = jnp.where(seen, scores, NEG_FILL)
            exps = jnp.exp(scores - jnp.max(scores, axis=0, keepdims=True))
            prob = exps * (1.0 / col_sum(exps))
            prob_o[0, 2 * pair + side] = prob
            got.append(t_dot(prob.astype(BF), v2))
        att_o[0, :, c : c + LANES] = jnp.where(low, got[0], got[1]).astype(BF)
    alive = (img < count[0]).astype(F32)
    after = x + alive * (dot(att_o[0], w[:, 3 * width : 4 * width]) + vec(2))
    aa_o[0] = after
    unit, _ = norm_stats(after)
    n2_o[0] = (unit * vec(3) + vec(4)).astype(BF)

    @pl.when(img == pl.num_programs(0) - 1)
    def _():
        pltpu.make_async_copy(w, w_o, sems.at[0]).wait()


def forward(off, subs, pieces, count, tok, experts, width_all):
    images, rows, width = tok.shape
    block = lambda cols: pl.BlockSpec((1, rows, cols), lambda i: (i, 0, 0))
    shape = lambda cols, t: jax.ShapeDtypeStruct((images, rows, cols), t)
    return pl.pallas_call(
        functools.partial(forward_kernel, experts, subs),
        grid=(images,),
        in_specs=[SMEM, SMEM, block(width)] + [ANY] * len(pieces),
        out_specs=[
            ANY,
            whole((LANES, width)),
            block(3 * width),
            block(width),
            block(width),
            block(width),
            block(width),
            pl.BlockSpec((1, HEADS, rows, rows), lambda i: (i, 0, 0, 0)),
        ],
        out_shape=[
            jax.ShapeDtypeStruct((width, width_all), BF),
            jax.ShapeDtypeStruct((LANES, width), F32),
            shape(3 * width, BF),
            shape(width, BF),
            shape(width, BF),
            shape(width, F32),
            shape(width, BF),
            jax.ShapeDtypeStruct((images, HEADS, rows, rows), F32),
        ],
        scratch_shapes=[
            pltpu.VMEM((width, width_all), BF),
            pltpu.SemaphoreType.DMA((len(pieces) * subs,)),
        ],
        compiler_params=params(60),
        cost_estimate=SMALL,
        name="tokens_forward",
    )(off, count, tok, *pieces)


def dispatch_kernel(experts, half, gated, slots, x, *refs):
    out = refs[-1]
    value = x[...]
    halves, block_rows = out.shape[1:3]
    first, second = slots[0:1, :], slots[1:2, :]
    if gated:
        router = refs[0][...].astype(BF)
        logits = dot_t(router, value)
        logits = jnp.where(iota(logits.shape, 0) < experts, logits, NEG_FILL)
        exps = jnp.exp(logits - jnp.max(logits, axis=0, keepdims=True))
        probs = exps / jnp.sum(exps, axis=0, keepdims=True)
    total = experts * block_rows
    for h in range(halves):
        place = iota((total, value.shape[0]), 0) + (half + h) * total
        hot = ((place == first) | (place == second)).astype(BF)
        out[:, h] = dot(hot, value).astype(BF).reshape(experts, block_rows, value.shape[1])
        if gated:
            row = iota((16, value.shape[0]), 0)
            for e in range(experts):
                gate = probs[e : e + 1, :]
                high = gate.astype(BF).astype(F32)
                pair = jnp.where(row == 14, high, jnp.where(row == 15, gate - high, 0.0))
                placed = dot_t(pair.astype(BF), hot[e * block_rows : (e + 1) * block_rows])
                tail = out[e, h, block_rows - 16 :, :block_rows].astype(F32)
                out[e, h, block_rows - 16 :, :block_rows] = jnp.where(
                    iota(tail.shape, 0) < 14, tail, placed
                ).astype(BF)


def dispatch(slots, x, small, experts, block_rows, half, halves, tag):
    rows, width = x.shape
    gated = small is not None
    more = [small] if gated else []
    vmem = pl.BlockSpec(memory_space=pltpu.VMEM)
    return pl.pallas_call(
        functools.partial(dispatch_kernel, experts, half, gated),
        in_specs=[vmem] * (2 + len(more)),
        out_specs=vmem,
        out_shape=jax.ShapeDtypeStruct((experts, halves, block_rows, width), BF),
        compiler_params=params(24),
        cost_estimate=SMALL,
        name="dispatch_" + tag,
    )(slots, x, *more)


def first_kernel(experts, half_cap, count, capacity, routes, x, out, slots):
    rows = routes.shape[1]
    halves, block_rows = out.shape[1:3]
    alive = iota((1, rows), 1) < count[0] * SEQ
    name = iota((up16(experts), rows), 0)
    earlier = (iota((rows, rows), 0) < iota((rows, rows), 1)).astype(BF)
    limits = jnp.zeros((up16(experts), 1), F32)
    for e in range(experts):
        limits = jnp.where(name[:, 0:1] == e, capacity[e].astype(F32), limits)
    base = 0.0
    for k in range(2):
        hit = jnp.where((routes[k : k + 1, :] == name) & alive, 1.0, 0.0)
        place = col_sum(hit * (dot(hit.astype(BF), earlier) + base))
        keep = place < col_sum(hit * limits)
        base = jnp.sum(hit, axis=1, keepdims=True)
        place = place.astype(jnp.int32)
        half = (place >= half_cap).astype(jnp.int32)
        spot = (half * experts + routes[k : k + 1, :]) * block_rows + place - half * half_cap
        slots[k : k + 1, :] = jnp.where(keep, spot, -1)
    dispatch_kernel(experts, 0, False, slots, x, out)


def first_dispatch(count, capacity, routes, x, half_cap, block_rows, halves):
    rows, width = x.shape
    experts = capacity.shape[0]
    vmem = pl.BlockSpec(memory_space=pltpu.VMEM)
    return pl.pallas_call(
        functools.partial(first_kernel, experts, half_cap),
        in_specs=[SMEM, SMEM, vmem, vmem],
        out_specs=[vmem, vmem],
        out_shape=[
            jax.ShapeDtypeStruct((experts, halves, block_rows, width), BF),
            jax.ShapeDtypeStruct((2, rows), jnp.int32),
        ],
        compiler_params=params(24),
        cost_estimate=SMALL,
        name="dispatch_first",
    )(count, capacity, routes, x)


def expert_kernel(places, n_arrays, n_before, *refs):
    x_ref, c_ref, b_in, b_out = refs[:4]
    arrays, parts = refs[4 : 4 + n_arrays], len(places) // 2
    rest = refs[4 + n_arrays + n_before :]
    act_o, pre_o, x_o, sg_o, r_o, d_o, db_in, db_out, win, wout, sems = rest
    step = pl.program_id(0)
    n, _, size, width = x_ref.shape
    piece = win.shape[1] // parts

    def copies(q):
        cols = pl.ds(q * piece, piece)
        (one, at_one), (two, at_two) = places[q], places[parts + q]
        return (
            pltpu.make_async_copy(
                arrays[one].at[pl.ds(at_one, width), :], win.at[:, cols], sems.at[q]
            ),
            pltpu.make_async_copy(
                arrays[two].at[pl.ds(at_two, piece), :], wout.at[cols, :], sems.at[parts + q]
            ),
        )

    @pl.when(step == 0)
    def _():
        for q in range(parts):
            for c in copies(q):
                c.start()
        db_in[...] = jnp.zeros_like(db_in)
        db_out[...] = jnp.zeros_like(db_out)

    eye = (iota((size, size), 0) == iota((size, size), 1)).astype(BF)
    for s in range(n):
        rows = slice(s * size, (s + 1) * size)
        x_o[rows, :] = x_ref[s, 0]
        turned = dot_t(eye, x_ref[s, 0, size - 16 :, :size])
        gate = jnp.sum(jnp.where(iota(turned.shape, 1) >= 14, turned, 0.0), axis=1, keepdims=True)
        sg_o[rows, :] = (gate * c_ref[s, 0].astype(F32)).astype(BF)
    x = x_o[...]
    slot_grad = sg_o[...]
    db_out[0:1, :] += col_sum(slot_grad.astype(F32))

    @pl.when(step == 0)
    def _():
        for q in range(parts):
            for c in copies(q):
                c.wait()

    for q in range(parts):
        cols = slice(q * piece, (q + 1) * piece)
        pre = dot(x, win[:, cols]) + b_in[q, 0:1, :]
        square = pre * pre
        turn = jnp.tanh(pre * (GELU_A + GELU_A * GELU_B * square))
        half_turn = 0.5 * turn + 0.5
        act_o[:, cols] = (pre * half_turn).astype(BF)
        slope = half_turn + (0.5 * pre) * (1.0 - turn * turn) * (GELU_A + 3 * GELU_A * GELU_B * square)
        pre_grad = dot_t(slot_grad, wout[cols, :]) * slope
        pre_o[:, cols] = pre_grad.astype(BF)
        db_in[q, 0:1, :] += col_sum(pre_grad)
    out = (dot(act_o[...], wout[...]) + b_out[0:1, :]).astype(BF)
    back = dot_t(pre_o[...], win[...])
    ones = jnp.ones((16, width), BF)
    for s in range(n):
        rows = slice(s * size, (s + 1) * size)
        r_o[s, 0] = out[rows]
        d_o[s] = back[rows].astype(BF)
        prod = c_ref[s, 0].astype(F32) * out[rows].astype(F32)
        high = prod.astype(BF)
        low = (prod - high.astype(F32)).astype(BF)
        gate_grad = dot_t(ones, high) + dot_t(ones, low)
        grad_high = gate_grad.astype(BF).astype(F32)
        row = iota(gate_grad.shape, 0)
        tail = back[(s + 1) * size - 16 : (s + 1) * size, :size]
        both = jnp.where(row == 14, grad_high, gate_grad - grad_high)
        d_o[s, size - 16 :, :size] = jnp.where(row < 14, tail, both).astype(BF)


def expert_call(x, c, arrays, places, b_in, b_out, half, halves, before):
    experts, _, size, width = x.shape
    parts, _, piece = b_in.shape
    n = max(1, 256 // size)
    steps = experts // n
    rows, hidden = n * size, parts * piece
    before = list(before)
    tall = lambda cols: pl.BlockSpec((rows, cols), lambda i: (half * steps + i, 0))
    of_half = pl.BlockSpec((n, 1, size, width), lambda i: (i, half, 0, 0))
    total = halves * experts * size
    return pl.pallas_call(
        functools.partial(expert_kernel, places, len(arrays), len(before)),
        grid=(steps,),
        in_specs=[
            pl.BlockSpec((n, 1, size, width), lambda i: (i, 0, 0, 0)),
            of_half,
            whole((parts, 8, piece)),
            whole((8, width)),
        ]
        + [ANY] * (len(arrays) + len(before)),
        out_specs=[
            tall(hidden),
            tall(hidden),
            tall(width),
            tall(width),
            of_half,
            pl.BlockSpec((n, size, width), lambda i: (i, 0, 0)),
            whole((parts, 8, piece)),
            whole((8, width)),
        ],
        out_shape=[
            jax.ShapeDtypeStruct((total, hidden), BF),
            jax.ShapeDtypeStruct((total, hidden), BF),
            jax.ShapeDtypeStruct((total, width), BF),
            jax.ShapeDtypeStruct((total, width), BF),
            jax.ShapeDtypeStruct((experts, halves, size, width), BF),
            jax.ShapeDtypeStruct((experts, size, width), BF),
            jax.ShapeDtypeStruct((parts, 8, piece), F32),
            jax.ShapeDtypeStruct((8, width), F32),
        ],
        scratch_shapes=[
            pltpu.VMEM((width, hidden), BF),
            pltpu.VMEM((hidden, width), BF),
            pltpu.SemaphoreType.DMA((2 * parts,)),
        ],
        input_output_aliases={4 + len(arrays) + i: i for i in range(len(before))},
        compiler_params=params(44),
        cost_estimate=SMALL,
        name="expert_" + "ab"[half],
    )(x, c, b_in, b_out, *arrays, *before)


def weight_kernel(piece, q_in, q_out, n_more, x, pre, act, grad, bias, *refs):
    more, (in_o, out_o, bias_o, xs, ps, acts, gs, held, sems) = refs[:n_more], refs[n_more:]
    width = x.shape[1]
    copies = [
        pltpu.make_async_copy(x, xs, sems.at[0]),
        pltpu.make_async_copy(pre.at[:, pl.ds(q_in * piece, piece)], ps, sems.at[1]),
        pltpu.make_async_copy(act.at[:, pl.ds(q_out * piece, piece)], acts, sems.at[2]),
        pltpu.make_async_copy(grad, gs, sems.at[3]),
    ]
    extra = [
        pltpu.make_async_copy(far, held.at[k, pl.ds(0, far.shape[0]), :], sems.at[4 + k])
        for k, far in enumerate(more)
    ]
    copies[0].start()
    copies[1].start()
    copies[0].wait()
    copies[1].wait()
    for c in [copies[2], copies[3], *extra]:
        c.start()
    first = t_dot(xs[...], ps[...])
    sums = bias[q_in]
    for k in range(n_more // 2):
        extra[k].wait()
        first = first + held[k, :width, :].astype(F32)
        sums = sums + held[k, width:, :].astype(F32)
    in_o[:width, :] = first.astype(in_o.dtype)
    bias_o[...] = sums.astype(bias_o.dtype)
    if not n_more:
        in_o[width:, :] = sums.astype(in_o.dtype)
    copies[2].wait()
    copies[3].wait()
    second = t_dot(acts[...], gs[...])
    for k in range(n_more // 2, n_more):
        extra[k].wait()
        second = second + held[k, :piece, :].astype(F32)
    out_o[...] = second.astype(out_o.dtype)


def weight_grads(x, pre, act, grad, bias, piece, q_in, q_out, kind, more=()):
    total, width = x.shape
    vmem = pl.BlockSpec(memory_space=pltpu.VMEM)
    return pl.pallas_call(
        functools.partial(weight_kernel, piece, q_in, q_out, len(more)),
        in_specs=[ANY] * 4 + [vmem] + [ANY] * len(more),
        out_specs=[vmem] * 3,
        out_shape=[
            jax.ShapeDtypeStruct((width if more else width + 16, piece), kind),
            jax.ShapeDtypeStruct((piece, width), kind),
            jax.ShapeDtypeStruct((16, piece), kind),
        ],
        scratch_shapes=[
            pltpu.VMEM((total, width), BF),
            pltpu.VMEM((total, piece), BF),
            pltpu.VMEM((total, piece), BF),
            pltpu.VMEM((total, width), BF),
            pltpu.VMEM((max(1, len(more)), width + 16, width), BF),
            pltpu.SemaphoreType.DMA((4 + len(more),)),
        ],
        compiler_params=params(60),
        cost_estimate=SMALL,
        name="weight_grads",
    )(x, pre, act, grad, bias, *more)


def backward_kernel(experts, n, split, off, count, slots, cot, n1_far, qkv, att_far, aa, n2, probs_in, w_far, w_out, small, *refs):
    backs = refs[:n]
    ag_o, gp_o, dq_o = refs[n : n + 3]
    grads = refs[n + 3 : n + 3 + split]
    dw, ds, marks, ag_all, dq_all, n1, att, w, sems = refs[n + 3 + split :]
    img = pl.program_id(0)
    width = n1.shape[-1]
    late = [
        pltpu.make_async_copy(far, here, sems.at[k])
        for k, (far, here) in enumerate(((n1_far, n1), (att_far, att), (w_far, w)))
    ]
    size = backs[0].shape[1]
    total = experts * size

    @pl.when(img == 0)
    def _():
        for c in late:
            c.start()
        ds[...] = jnp.zeros_like(ds)
        line = iota((LANES, size), 0)
        for h in range(n):
            for e in range(experts):
                ends = backs[h][e, size - 16 :, :size].astype(F32)
                for k in range(2):
                    marks[2 * h + k, :, e * size : (e + 1) * size] = jnp.where(
                        line == e, ends[14 + k : 15 + k, :], 0.0
                    ).astype(BF)

    def vec(k):
        return small[experts + k : experts + k + 1, :]

    def add_vec(k, value):
        ds[experts + k : experts + k + 1, :] += value

    alive = (img < count[0]).astype(F32)
    up = cot[0].astype(F32)
    rows = up.shape[0]
    normed = n2[0]
    lane = iota((rows, LANES), 1)
    router = jnp.where(iota(small.shape, 0) < experts, small[...], 0.0).astype(BF)
    logits = jnp.where(lane < experts, dot_t(normed, router), NEG_FILL)
    exps = jnp.exp(logits - jnp.max(logits, axis=-1, keepdims=True))
    probs = exps / jnp.sum(exps, axis=-1, keepdims=True)
    gp_o[0] = probs
    first, second = slots[0, :, 0:1], slots[0, :, 1:2]
    normed_grad = jnp.zeros((rows, width), F32)
    placed = jnp.zeros((rows, LANES), F32)
    for h in range(n):
        place = iota((rows, total), 1) + h * total
        hot = ((place == first) | (place == second)).astype(BF)
        normed_grad = normed_grad + dot(hot, backs[h][...].reshape(total, width))
        placed = placed + dot_t(hot, marks[2 * h]) + dot_t(hot, marks[2 * h + 1])
    logit_grad = (
        probs * (placed - jnp.sum(probs * placed, axis=-1, keepdims=True))
    ).astype(BF)
    normed_grad = normed_grad + dot(logit_grad, router)
    ds[...] += jnp.where(iota(ds.shape, 0) < experts, t_dot(logit_grad, normed), 0.0)
    unit, inverse = norm_stats(aa[0])
    add_vec(3, col_sum(normed_grad * unit))
    add_vec(4, col_sum(normed_grad))
    after_grad = up + norm_back(unit, inverse, vec(3), normed_grad)
    attn_grad = (alive * after_grad).astype(BF)
    add_vec(2, col_sum(attn_grad.astype(F32)))
    ag_all[img] = attn_grad
    att_grad = dot_t(attn_grad, w_out[...]).astype(BF)
    low = lane < LANES // 2
    scale = (width // HEADS) ** -0.5
    for pair in range(HEADS // 2):
        c = pair * LANES
        q2 = qkv[0, :, c : c + LANES]
        k2 = qkv[0, :, width + c : width + c + LANES]
        v2 = qkv[0, :, 2 * width + c : 2 * width + c + LANES]
        o2 = att_grad[:, c : c + LANES]
        got = []
        for side, mask in enumerate((low, ~low)):
            prob = probs_in[0, 2 * pair + side]
            prob_grad = dot_t(v2, jnp.where(mask, o2, jnp.zeros_like(o2)))
            score_grad = (prob * (prob_grad - col_sum(prob * prob_grad))).astype(BF)
            got.append(
                (
                    t_dot(score_grad, k2) * scale,
                    dot(score_grad, q2) * scale,
                    dot(prob.astype(BF), o2),
                )
            )
        for k in range(3):
            dq_o[0, :, k * width + c : k * width + c + LANES] = jnp.where(
                low, got[0][k], got[1][k]
            ).astype(BF)
    grad = dq_o[0]
    dq_all[img] = grad
    for k in range(3):
        ds[experts + 5 + k : experts + 6 + k, :] += col_sum(grad[:, k * width : (k + 1) * width].astype(F32))
    ag_o[0] = after_grad

    @pl.when(img == pl.num_programs(0) - 1)
    def _():
        dw[:, 4 * width : 4 * width + LANES] = jnp.transpose(ds[...])
        for c in late:
            c.wait()
        left = n1[...].reshape(-1, width)
        for k in range(3):
            cols = slice(k * width, (k + 1) * width)
            dw[:, cols] = t_dot(left, dq_all[:, :, cols].reshape(-1, width))
        dw[:, 3 * width : 4 * width] = t_dot(
            att[...].reshape(-1, width), ag_all[...].reshape(-1, width)
        )
        with_weight = jnp.zeros((width, LANES), F32)
        with_sums = jnp.zeros((width, LANES), F32)
        for k in range(3 * width // LANES):
            cols = slice(k * LANES, (k + 1) * LANES)
            part, at = divmod(k * LANES, width)
            value = w[:, cols].astype(F32)
            sums = ds[experts + 5 + part : experts + 6 + part, at : at + LANES]
            with_weight = with_weight + value * dw[:, cols]
            with_sums = with_sums + value * sums
        sums = jnp.sum(with_sums, axis=1, keepdims=True)
        at = 4 * width
        sides = w[:, at : at + LANES].astype(F32)
        gain, shift = sides[:, experts : experts + 1], sides[:, experts + 1 : experts + 2]
        gains = (jnp.sum(with_weight, axis=1, keepdims=True) - shift * sums) / gain
        spot = iota((width, LANES), 1)
        cols = slice(at, at + LANES)
        dw[:, cols] = jnp.where(
            spot == experts, gains, jnp.where(spot == experts + 1, sums, dw[:, cols])
        )
        if split == 1:
            grads[0][...] = dw[...].astype(BF)
        else:
            cols = grads[0].shape[1]
            step = width // 16
            for h in range(2):
                col = pl.multiple_of(off[16 + h], LANES)
                for r in range(16):
                    row = pl.multiple_of(off[r], 16)
                    grads[h][r * step : (r + 1) * step, :] = dw[
                        pl.ds(row, step), pl.ds(col, cols)
                    ].astype(BF)


def backward(off, count, slots, cot, n1, qkv, att, aa, n2, prob, w, small, backs, experts, split):
    images, rows, width = cot.shape
    width_all = w.shape[1]
    n = len(backs)
    block = lambda cols: pl.BlockSpec((1, rows, cols), lambda i: (i, 0, 0))
    got = pl.pallas_call(
        functools.partial(backward_kernel, experts, n, split),
        grid=(images,),
        in_specs=[SMEM, SMEM, block(2), block(width), ANY, block(3 * width), ANY, block(width), block(width)]
        + [pl.BlockSpec((1, HEADS, rows, rows), lambda i: (i, 0, 0, 0))]
        + [ANY, pl.BlockSpec((width, width), lambda i: (0, 3), pipeline_mode=pl.Buffered(1)), whole(small.shape)]
        + [whole(backs[0].shape)] * n,
        out_specs=[block(width), block(LANES), block(3 * width)] + [whole((width, width_all // split))] * split,
        out_shape=[
            jax.ShapeDtypeStruct((images, rows, width), F32),
            jax.ShapeDtypeStruct((images, rows, LANES), F32),
            jax.ShapeDtypeStruct((images, rows, 3 * width), BF),
        ]
        + [jax.ShapeDtypeStruct((width, width_all // split), BF)] * split,
        scratch_shapes=[
            pltpu.VMEM((width, width_all), F32),
            pltpu.VMEM((LANES, width), F32),
            pltpu.VMEM((2 * n, LANES, backs[0].shape[0] * backs[0].shape[1]), BF),
            pltpu.VMEM((images, rows, width), BF),
            pltpu.VMEM((images, rows, 3 * width), BF),
            pltpu.VMEM((images, rows, width), BF),
            pltpu.VMEM((images, rows, width), BF),
            pltpu.VMEM(w.shape, BF),
            pltpu.SemaphoreType.DMA((3,)),
        ],
        compiler_params=params(),
        cost_estimate=SMALL,
        name="tokens_backward",
    )(off, count, slots, cot, n1, qkv, att, aa, n2, prob, w, w, small, *backs)
    return got[0], got[1], got[2], got[3:]


def place_rows(out, value):
    for k in range(out.shape[0] // SEQ):

        @pl.when(pl.program_id(0) == k)
        def _():
            out[k * SEQ : (k + 1) * SEQ, :] = value[:SEQ]


def finish_kernel(experts, after_grad, grad, tok, w, small, out):
    width = tok.shape[-1]
    normed_grad = dot_t(grad[0], w[...])
    unit, inverse = norm_stats(tok[0].astype(F32))
    value = after_grad[0] + norm_back(unit, inverse, small[experts : experts + 1, :], normed_grad)
    place_rows(out, value)


def finish(after_grad, grad, tok, w, small, experts):
    images, rows, width = tok.shape
    block = lambda cols: pl.BlockSpec((1, rows, cols), lambda i: (i, 0, 0))
    return pl.pallas_call(
        functools.partial(finish_kernel, experts),
        grid=(images,),
        in_specs=[block(width), block(3 * width), block(width), whole((width, 3 * width)), whole(small.shape)],
        out_specs=whole((images * SEQ, width)),
        out_shape=jax.ShapeDtypeStruct((images * SEQ, width), F32),
        compiler_params=params(60),
        cost_estimate=SMALL,
        name="tokens_finish",
    )(after_grad, grad, tok, w, small)


def output_kernel(count, slots, aa, probs, outs, out, total_f):
    rows = aa.shape[1]
    experts, n, size, width = outs.shape
    total = experts * size
    alive = (pl.program_id(0) < count[0]).astype(F32)
    first, second = slots[0, :, 0:1], slots[0, :, 1:2]
    gates = jnp.concatenate(
        [jnp.broadcast_to(probs[0, :, e : e + 1], (rows, size)) for e in range(experts)], axis=1
    )
    moe = jnp.zeros(aa.shape[1:], F32)
    for h in range(n):
        place = iota((rows, total), 1) + h * total
        gate = jnp.where((place == first) | (place == second), gates, 0.0)
        high = gate.astype(BF)
        low = (gate - high.astype(F32)).astype(BF)
        value = outs[:, h].reshape(total, width)
        moe = moe + dot(high, value) + dot(low, value)
    place_rows(total_f, aa[0] + alive * moe)

    @pl.when(pl.program_id(0) == pl.num_programs(0) - 1)
    def _():
        out[...] = total_f[...].astype(BF)


def block_output(count, slots, aa, probs, outs):
    images, rows, width = aa.shape
    block = lambda cols: pl.BlockSpec((1, rows, cols), lambda i: (i, 0, 0))
    return pl.pallas_call(
        output_kernel,
        grid=(images,),
        in_specs=[SMEM, block(2), block(width), block(LANES), whole(outs.shape)],
        out_specs=whole((images * SEQ, width)),
        out_shape=jax.ShapeDtypeStruct((images * SEQ, width), BF),
        scratch_shapes=[pltpu.VMEM((images * SEQ, width), F32)],
        compiler_params=params(60),
        cost_estimate=SMALL,
        name="block_output",
    )(count, slots, aa, probs, outs)


def local(sizes, *args):
    (tokens, image_count, routes, capacity, ln1_gain, ln1_bias, qkv_weight, qv_bias, out_weight, out_bias,
     ln2_gain, ln2_bias, router_weight, expert_in, expert_in_bias, expert_out, expert_out_bias, cotangent) = args
    dp, experts = sizes
    grouped = sizes == (4, 8)
    devices = dp * experts
    me_d = lax.axis_index("dp")
    me_e = lax.axis_index("expert")
    core = me_e % 2
    token_count, width = tokens.shape
    images = token_count // SEQ
    rows = up16(SEQ)
    cap = max(2, 5 * token_count // (2 * experts))
    halves = 2 if grouped else 1
    half_cap = -(-cap // halves)
    block_rows = up16(half_cap + 2)

    def hop(value, mask):
        return lax.ppermute(value, BOTH, [(i, i ^ mask) for i in range(devices)])

    def by_image(value):
        value = value.reshape(images, SEQ, value.shape[-1])
        fill = -1 if value.dtype == jnp.int32 else 0
        return jnp.pad(value, ((0, 0), (0, rows - SEQ), (0, 0)), constant_values=fill)

    def side_rows(values):
        return functools.reduce(
            lambda a, b: a + b,
            [jnp.pad(v.astype(F32)[None], ((k, 7 - k), (0, 0))) for k, v in enumerate(values)],
        )

    def slots_and_blocks(value):
        return first_dispatch(image_count, capacity, routes.T, value, half_cap, block_rows, halves)

    def slot_forms(slots):
        slots = slots.reshape(2, images, SEQ)
        slots = jnp.pad(slots, ((0, 0), (0, 0), (0, rows - SEQ)), constant_values=-1)
        return slots.transpose(1, 2, 0), slots.reshape(2, -1)

    def after(values, *done):
        return lax.optimization_barrier((values, done))[0]

    tok = by_image(tokens)

    vectors = [ln1_gain, ln1_bias, out_bias, ln2_gain, ln2_bias]
    width_all = 4 * width + 2 * LANES
    wide = expert_in.shape[2]
    spot = me_d * expert_out_bias.shape[1]
    if grouped:
        half = width_all // 2
        mine, other = pack_dense(
            core.reshape(1).astype(jnp.int32), qkv_weight, out_weight, router_weight.T, side_rows(vectors), qv_bias
        )
        got = hop(other, 1)
        chip = jnp.where(
            core == 0, jnp.concatenate([mine, got], axis=0), jnp.concatenate([got, mine], axis=0)
        )
        bias_out = lax.dynamic_update_slice(jnp.zeros((1, width), BF), expert_out_bias, (0, spot))
        bias = jnp.concatenate([expert_in_bias, bias_out, jnp.zeros((14, wide), BF)], axis=0)
        one = jnp.concatenate([expert_in[0], bias], axis=0)
        two = jnp.concatenate([expert_out[0], bias], axis=0)
        from_x, from_y = hop(expert_in[0], 8), hop(expert_out[0], 16)
        cot_blocks, slots = slots_and_blocks(after(cotangent, chip))
        slots_col, slots_row = slot_forms(slots)
        line = jnp.concatenate([chip] + [hop(chip, 2 * dz) for dz in (1, 2, 3)], axis=0)
        held, from_x, from_y = after((line, from_x, from_y))
        own = [line] + [hop(held, 8 * dxy) for dxy in (3, 1, 2)]
        own = [own[0], own[2], own[3], own[1]]
        step = width // 16
        at_rows = jnp.stack([((me_d ^ a) * 4 + ((me_e // 2) ^ b)) * step for a in range(4) for b in range(4)])
        at_cols = jnp.stack([core * half, (1 - core) * half])
        off_back = jnp.concatenate([at_rows, at_cols]).astype(jnp.int32)
        off = jnp.concatenate([at_rows, at_rows, jnp.repeat(at_cols, 4)]).astype(jnp.int32)
        own, tok, slots_row, off, one, two = after((own, tok, slots_row, off, one, two))
        pieces = own + [hop(piece, 1) for piece in own]
        subs = 4
        later_one, later_two, relay_x, relay_y = after((one, two, from_x, from_y), *own)
        near = hop(later_one, 16), hop(later_two, 8)
        relays = hop(relay_x, 16), hop(relay_y, 8), hop(near[0][width:], 8)
        arrays = [one, from_x, near[0], relays[0]]
        biases = [bias, near[1][width:], near[0][width:], relays[2]]
        b_in = jnp.stack([v[:8] for v in biases]).astype(F32)
        arrays += [two, near[1], from_y, relays[1]]
        places = tuple((q, 0) for q in range(8))
        b_out = jnp.broadcast_to(jnp.sum(b_in[:, 1], axis=0), (8, width))
        after_line = held
    else:
        fill = width_all - 4 * width - experts - 7
        pack = jnp.concatenate(
            [qkv_weight, out_weight, router_weight, jnp.stack(vectors, axis=1), qv_bias.T, jnp.zeros((ln1_gain.shape[0], fill), BF)], axis=1
        )
        pieces = [lax.all_gather(pack, BOTH, axis=0, tiled=True)]
        cot_blocks, slots = slots_and_blocks(cotangent)
        slots_col, slots_row = slot_forms(slots)
        off = jnp.zeros((2,), jnp.int32)
        off_back = off
        subs = 1
        after_line = pieces[0]
        w_in = lax.all_gather(expert_in[0], "dp", axis=0, tiled=False)
        w_out = lax.all_gather(expert_out[0], "dp", axis=0, tiled=False)
        arrays = [w[q] for w in (w_in, w_out) for q in range(dp)]
        places = tuple((q, 0) for q in range(2 * dp))
        b_in = lax.all_gather(jnp.broadcast_to(expert_in_bias, (8, wide)), "dp", axis=0, tiled=False).astype(F32)
        b_out = jnp.broadcast_to(
            lax.all_gather(expert_out_bias, "dp", axis=1, tiled=True).astype(F32), (8, width)
        )

    def exchange(blocks):
        return lax.all_to_all(blocks, "expert", 0, 0, tiled=True)

    cot_sent = exchange(after(cot_blocks, after_line))
    cot = by_image(cotangent)

    w, small, qkv, n1, att, aa, n2, prob = forward(off, subs, pieces, image_count, tok, experts, width_all)
    row_sent = []
    flat = n2.reshape(-1, width)
    for h in range(halves):
        sent = dispatch(slots_row, flat, small, experts, block_rows, h, 1, "ab"[h])
        waits = (near, relays)[h] if grouped else ()
        sent, cot_sent = after((sent, cot_sent), *row_sent, *waits)
        if h:
            sent, cot, slots_col = after((sent, cot, slots_col))
        row_sent.append(exchange(sent))

    back, grads_out, db_ins, db_outs, tall = [], [], [], [], ()
    for h in range(halves):
        *tall, d, db_in, db_out = expert_call(
            row_sent[h], cot_sent, arrays, places, b_in, b_out, h, halves, tall
        )
        grads_out.append(d)
        if h + 1 < halves:
            back.append(exchange(d))
        db_ins.append(db_in)
        db_outs.append(db_out)
    *tall, outs_back = tall
    db_in, db_out = sum(db_ins), sum(db_outs)

    both = [db_in[:, 0:1]]
    if grouped:
        both.append(jnp.broadcast_to(db_out[0:1], db_in[:, 0:1].shape))
    bias_sums = jnp.concatenate(
        [*both, jnp.zeros((dp, 16 - len(both), wide), F32)], axis=1
    )

    def weights_of(q_in, q_out, kind, more=()):
        act, pre, rows_in, slot_grad = tall
        return weight_grads(rows_in, pre, act, slot_grad, bias_sums, wide, q_in, q_out, kind, more)

    if grouped:
        far_in, far_out, _ = weights_of(3, 3, BF)
        tall = after(tall, far_in, far_out, *back)
        back.append(exchange(after(grads_out[-1], far_in, far_out, *back)))
        far_in, far_out = hop(far_in, 8), hop(far_out, 16)
        near_in, near_out, _ = weights_of(1, 2, BF)
        last_in, last_out, _ = weights_of(2, 1, BF)
        last_in = (last_in.astype(F32) + far_in.astype(F32)).astype(BF)
        last_out = (last_out.astype(F32) + far_out.astype(F32)).astype(BF)
        ready = (near_in, near_out, last_in, last_out)
        near_in, near_out = hop(near_in, 8), hop(near_out, 16)
        last_in, last_out = hop(last_in, 16), hop(last_out, 8)
        arrived = (near_in, near_out, last_in, last_out)
    else:
        ready = arrived = ()
        scatter = lambda v: lax.psum_scatter(v, "dp", scatter_dimension=0, tiled=True).astype(F32)
        back.append(exchange(grads_out[-1]))
        every = [weights_of(q, q, BF) for q in range(dp)]
        g_in = scatter(jnp.stack([e[0][:width] for e in every]))
        g_out = scatter(jnp.stack([e[1] for e in every]))
        g_b_in = lax.psum_scatter(
            db_in[:, 0].reshape(1, -1).astype(BF), "dp", scatter_dimension=1, tiled=True
        ).astype(F32)
        g_b_out = lax.psum_scatter(db_out[0:1].astype(BF), "dp", scatter_dimension=1, tiled=True).astype(F32)

    r_sent = exchange(after(outs_back, *back))
    back = after(back, *ready)
    after_grad, probs, grad, grads = backward(
        off_back, image_count, slots_col, cot, n1, qkv, att, aa, n2, prob, w, small, back, experts,
        2 if grouped else 1,
    )
    grads = after(grads, *arrived)
    block_out = block_output(image_count, slots_col, aa, probs, r_sent)
    def add(*values):
        return functools.reduce(lambda a, b: a + b, [v.astype(F32) for v in values])

    if grouped:
        sibling = hop(grads[1], 1)
        quarter = width // 4
        ways = [slice(a * quarter, (a + 1) * quarter) for a in range(4)]
        ways = [add(grads[0][a], sibling[a]).astype(BF) for a in ways]
        tall, bias_sums = after((tall, bias_sums), *ways)
        own_in, own_out, g_bias = weights_of(0, 0, F32, (near_in, last_in, near_out, last_out))
        g_in, g_out = own_in[None], own_out[None]
        g_b_in = g_bias[0:1]
        g_b_out = lax.dynamic_slice(g_bias[1:2], (0, spot), expert_out_bias.shape)
        after_grad, grad = after((after_grad, grad), own_in, own_out)
    tokens_grad = finish(after_grad, grad, tok, w, small, experts)

    if grouped:
        ways[0], tokens_grad, g_in, g_out = after((ways[0], tokens_grad, g_in, g_out))
        ways = [ways[0], *[hop(ways[a], 8 * a) for a in (1, 2, 3)]]
        step = width // 16
        cuts = [add(*[way[b * step : (b + 1) * step] for way in ways]) for b in range(4)]
        cuts = [cuts[0], *[c.astype(BF) for c in cuts[1:]]]
        cuts, r_sent = after((cuts, r_sent))
        chip = add(cuts[0], *[hop(cuts[b], 2 * b) for b in (1, 2, 3)])
        n_rows = step // 2
        keep = lax.dynamic_slice_in_dim(chip, core * n_rows, n_rows, 0)
        chip, block_out = after((chip, block_out))
        give = lax.dynamic_slice_in_dim(chip, (1 - core) * n_rows, n_rows, 0)
        got = hop(give.astype(BF), 1).astype(F32)
        dense = jnp.where(
            core == 0, jnp.concatenate([keep, got], axis=1), jnp.concatenate([got, keep], axis=1)
        )
    else:
        dense = lax.psum_scatter(grads[0], BOTH, scatter_dimension=0, tiled=True).astype(F32)
    side = dense[:, 4 * width :]
    vecs = [side[:, experts + k] for k in range(8)]
    return (
        block_out,
        tokens_grad,
        vecs[0],
        vecs[1],
        dense[:, : 3 * width],
        jnp.stack([vecs[5], vecs[7]], axis=0),
        dense[:, 3 * width : 4 * width],
        vecs[2],
        vecs[3],
        vecs[4],
        side[:, :experts],
        g_in,
        g_b_in,
        g_out,
        g_b_out,
    )


def solution(mesh):
    rows, line, cols = P(BOTH, None), P(BOTH), P(None, BOTH)
    experts = (P("expert", None, "dp"), P("expert", "dp"), P("expert", "dp", None), P("expert", "dp"))
    dense = (line, line, rows, cols, rows, line, line, line, rows)
    return jax.shard_map(
        functools.partial(local, (mesh.shape["dp"], mesh.shape["expert"])),
        mesh=mesh,
        in_specs=(rows, line, rows, P(), *dense, *experts, rows),
        out_specs=(rows, rows, *dense, *experts),
        check_vma=False,
    )
```

```python
import functools

import jax
import jax.numpy as jnp
from jax import lax
from jax.experimental import pallas as pl
from jax.experimental.pallas import tpu as pltpu
from jax.sharding import PartitionSpec as P

HEADS = 12
SEQ = 197
EPS_NORM = 1e-06
NEG_FILL = -1e30
BF = jnp.bfloat16
F32 = jnp.float32
LANES = 128
GELU_A = 0.7978845608028654
GELU_B = 0.044715
BOTH = ("dp", "expert")


def up16(n):
    return -(-n // 16) * 16


def dot(left, right):
    return jnp.dot(left, right, preferred_element_type=F32)


def dot_t(left, right):
    return lax.dot_general(left, right, (((1,), (1,)), ((), ())), preferred_element_type=F32)


def t_dot(left, right):
    return lax.dot_general(left, right, (((0,), (0,)), ((), ())), preferred_element_type=F32)


def iota(shape, dim):
    return lax.broadcasted_iota(jnp.int32, shape, dim)


def params(mib=60):
    return pltpu.CompilerParams(vmem_limit_bytes=mib << 20)


def whole(shape):
    zeros = (0,) * len(shape)
    return pl.BlockSpec(shape, lambda *_: zeros, pipeline_mode=pl.Buffered(1))


SMALL = pl.CostEstimate(flops=1 << 20, bytes_accessed=1 << 16, transcendentals=0)
LARGE = pl.CostEstimate(flops=1 << 34, bytes_accessed=1 << 16, transcendentals=0)
SMEM = pl.BlockSpec(memory_space=pltpu.SMEM)
ANY = pl.BlockSpec(memory_space=pl.ANY)


def norm_stats(values):
    centered = values - jnp.mean(values, axis=-1, keepdims=True)
    inverse = lax.rsqrt(jnp.mean(centered * centered, axis=-1, keepdims=True) + EPS_NORM)
    return centered * inverse, inverse


def norm_back(unit, inverse, gain, grad):
    scaled = grad * gain
    mean_one = jnp.mean(scaled, axis=-1, keepdims=True)
    mean_two = jnp.mean(scaled * unit, axis=-1, keepdims=True)
    return inverse * (scaled - mean_one - unit * mean_two)


def col_sum(values):
    return jnp.sum(values, axis=0, keepdims=True)


def pack_kernel(core, qkv, out, router, vectors, pair, mine, other):
    rows = qkv.shape[0]
    eye = (iota((rows, rows), 0) == iota((rows, rows), 1)).astype(BF)
    turned = [dot_t(eye, router[...]), dot_t(eye, vectors[...].astype(BF))[:, :5], dot_t(eye, pair[...])]
    used = sum(t.shape[1] for t in turned)
    turned = jnp.concatenate([*turned, jnp.zeros((rows, 2 * LANES - used), F32)], axis=1)
    value = jnp.concatenate([qkv[...], out[...], turned.astype(BF)], axis=1)
    half = value.shape[1] // 2

    @pl.when(core[0] == 0)
    def _():
        mine[...] = value[:, :half]
        other[...] = value[:, half:]

    @pl.when(core[0] != 0)
    def _():
        mine[...] = value[:, half:]
        other[...] = value[:, :half]


def pack_dense(core, qkv, out, router, vectors, pair):
    rows = qkv.shape[0]
    half = (qkv.shape[1] + out.shape[1] + 2 * LANES) // 2
    vmem = pl.BlockSpec(memory_space=pltpu.VMEM)
    return pl.pallas_call(
        pack_kernel,
        in_specs=[SMEM] + [vmem] * 5,
        out_specs=[vmem] * 2,
        out_shape=[jax.ShapeDtypeStruct((rows, half), BF)] * 2,
        compiler_params=params(60),
        cost_estimate=LARGE,
        name="pack_dense",
    )(core, qkv, out, router, vectors, pair)


def forward_kernel(experts, subs, off, count, tok, *refs):
    n_pieces = len(refs) - 10
    pieces = refs[:n_pieces]
    w_o, small, qkv_o, n1_o, att_o, aa_o, n2_o, prob_o, w, sems = refs[n_pieces:]
    img = pl.program_id(0)
    width = tok.shape[-1]

    @pl.when(img == 0)
    def _():
        copies = []
        for i, piece in enumerate(pieces):
            rows, cols = piece.shape[0] // subs, piece.shape[1]
            col = pl.multiple_of(off[n_pieces * subs + i], LANES)
            for j in range(subs):
                row = pl.multiple_of(off[i * subs + j], 16)
                copies.append(
                    pltpu.make_async_copy(
                        piece.at[pl.ds(j * rows, rows), :],
                        w.at[pl.ds(row, rows), pl.ds(col, cols)],
                        sems.at[i * subs + j],
                    )
                )
        for c in copies:
            c.start()
        for c in copies:
            c.wait()
        small[...] = jnp.transpose(w[:, 4 * width : 4 * width + LANES].astype(F32))
        pltpu.make_async_copy(w, w_o, sems.at[0]).start()

    def vec(k):
        return small[experts + k : experts + k + 1, :]

    x = tok[0].astype(F32)
    rows = x.shape[0]
    unit, _ = norm_stats(x)
    n1 = (unit * vec(0) + vec(1)).astype(BF)
    n1_o[0] = n1
    biases = (vec(5), None, vec(6))
    for part in range(3):
        cols = slice(part * width, (part + 1) * width)
        block = dot(n1, w[:, cols])
        if biases[part] is not None:
            block = block + biases[part]
        qkv_o[0, :, cols] = block.astype(BF)
    low = iota((rows, LANES), 1) < LANES // 2
    seen = iota((rows, rows), 0) < SEQ
    scale = (width // HEADS) ** -0.5
    for pair in range(HEADS // 2):
        c = pair * LANES
        q2 = qkv_o[0, :, c : c + LANES]
        k2 = qkv_o[0, :, width + c : width + c + LANES]
        v2 = qkv_o[0, :, 2 * width + c : 2 * width + c + LANES]
        got = []
        for side, mask in enumerate((low, ~low)):
            scores = dot_t(k2, jnp.where(mask, q2, jnp.zeros_like(q2))) * scale
            scores = jnp.where(seen, scores, NEG_FILL)
            exps = jnp.exp(scores - jnp.max(scores, axis=0, keepdims=True))
            prob = exps * (1.0 / col_sum(exps))
            prob_o[0, 2 * pair + side] = prob
            got.append(t_dot(prob.astype(BF), v2))
        att_o[0, :, c : c + LANES] = jnp.where(low, got[0], got[1]).astype(BF)
    alive = (img < count[0]).astype(F32)
    after = x + alive * (dot(att_o[0], w[:, 3 * width : 4 * width]) + vec(2))
    aa_o[0] = after
    unit, _ = norm_stats(after)
    n2_o[0] = (unit * vec(3) + vec(4)).astype(BF)

    @pl.when(img == pl.num_programs(0) - 1)
    def _():
        pltpu.make_async_copy(w, w_o, sems.at[0]).wait()


def forward(off, subs, pieces, count, tok, experts, width_all):
    images, rows, width = tok.shape
    block = lambda cols: pl.BlockSpec((1, rows, cols), lambda i: (i, 0, 0))
    shape = lambda cols, t: jax.ShapeDtypeStruct((images, rows, cols), t)
    return pl.pallas_call(
        functools.partial(forward_kernel, experts, subs),
        grid=(images,),
        in_specs=[SMEM, SMEM, block(width)] + [ANY] * len(pieces),
        out_specs=[
            ANY,
            whole((LANES, width)),
            block(3 * width),
            block(width),
            block(width),
            block(width),
            block(width),
            pl.BlockSpec((1, HEADS, rows, rows), lambda i: (i, 0, 0, 0)),
        ],
        out_shape=[
            jax.ShapeDtypeStruct((width, width_all), BF),
            jax.ShapeDtypeStruct((LANES, width), F32),
            shape(3 * width, BF),
            shape(width, BF),
            shape(width, BF),
            shape(width, F32),
            shape(width, BF),
            jax.ShapeDtypeStruct((images, HEADS, rows, rows), F32),
        ],
        scratch_shapes=[
            pltpu.VMEM((width, width_all), BF),
            pltpu.SemaphoreType.DMA((len(pieces) * subs,)),
        ],
        compiler_params=params(60),
        cost_estimate=SMALL,
        name="tokens_forward",
    )(off, count, tok, *pieces)


def dispatch_kernel(experts, half, gated, slots, x, *refs):
    out = refs[-1]
    value = x[...]
    halves, block_rows = out.shape[1:3]
    first, second = slots[0:1, :], slots[1:2, :]
    if gated:
        router = refs[0][...].astype(BF)
        logits = dot_t(router, value)
        logits = jnp.where(iota(logits.shape, 0) < experts, logits, NEG_FILL)
        exps = jnp.exp(logits - jnp.max(logits, axis=0, keepdims=True))
        probs = exps / jnp.sum(exps, axis=0, keepdims=True)
    total = experts * block_rows
    for h in range(halves):
        place = iota((total, value.shape[0]), 0) + (half + h) * total
        hot = ((place == first) | (place == second)).astype(BF)
        out[:, h] = dot(hot, value).astype(BF).reshape(experts, block_rows, value.shape[1])
        if gated:
            row = iota((16, value.shape[0]), 0)
            for e in range(experts):
                gate = probs[e : e + 1, :]
                high = gate.astype(BF).astype(F32)
                pair = jnp.where(row == 14, high, jnp.where(row == 15, gate - high, 0.0))
                placed = dot_t(pair.astype(BF), hot[e * block_rows : (e + 1) * block_rows])
                tail = out[e, h, block_rows - 16 :, :block_rows].astype(F32)
                out[e, h, block_rows - 16 :, :block_rows] = jnp.where(
                    iota(tail.shape, 0) < 14, tail, placed
                ).astype(BF)


def dispatch(slots, x, small, experts, block_rows, half, halves, tag):
    rows, width = x.shape
    gated = small is not None
    more = [small] if gated else []
    vmem = pl.BlockSpec(memory_space=pltpu.VMEM)
    return pl.pallas_call(
        functools.partial(dispatch_kernel, experts, half, gated),
        in_specs=[vmem] * (2 + len(more)),
        out_specs=vmem,
        out_shape=jax.ShapeDtypeStruct((experts, halves, block_rows, width), BF),
        compiler_params=params(24),
        cost_estimate=SMALL,
        name="dispatch_" + tag,
    )(slots, x, *more)


def first_kernel(experts, half_cap, count, capacity, routes, x, out, slots):
    rows = routes.shape[1]
    halves, block_rows = out.shape[1:3]
    alive = iota((1, rows), 1) < count[0] * SEQ
    name = iota((up16(experts), rows), 0)
    earlier = (iota((rows, rows), 0) < iota((rows, rows), 1)).astype(BF)
    limits = jnp.zeros((up16(experts), 1), F32)
    for e in range(experts):
        limits = jnp.where(name[:, 0:1] == e, capacity[e].astype(F32), limits)
    base = 0.0
    for k in range(2):
        hit = jnp.where((routes[k : k + 1, :] == name) & alive, 1.0, 0.0)
        place = col_sum(hit * (dot(hit.astype(BF), earlier) + base))
        keep = place < col_sum(hit * limits)
        base = jnp.sum(hit, axis=1, keepdims=True)
        place = place.astype(jnp.int32)
        half = (place >= half_cap).astype(jnp.int32)
        spot = (half * experts + routes[k : k + 1, :]) * block_rows + place - half * half_cap
        slots[k : k + 1, :] = jnp.where(keep, spot, -1)
    dispatch_kernel(experts, 0, False, slots, x, out)


def first_dispatch(count, capacity, routes, x, half_cap, block_rows, halves):
    rows, width = x.shape
    experts = capacity.shape[0]
    vmem = pl.BlockSpec(memory_space=pltpu.VMEM)
    return pl.pallas_call(
        functools.partial(first_kernel, experts, half_cap),
        in_specs=[SMEM, SMEM, vmem, vmem],
        out_specs=[vmem, vmem],
        out_shape=[
            jax.ShapeDtypeStruct((experts, halves, block_rows, width), BF),
            jax.ShapeDtypeStruct((2, rows), jnp.int32),
        ],
        compiler_params=params(24),
        cost_estimate=SMALL,
        name="dispatch_first",
    )(count, capacity, routes, x)


def expert_kernel(places, n_arrays, n_before, *refs):
    x_ref, c_ref, b_in, b_out = refs[:4]
    arrays, parts = refs[4 : 4 + n_arrays], len(places) // 2
    rest = refs[4 + n_arrays + n_before :]
    act_o, pre_o, x_o, sg_o, r_o, d_o, db_in, db_out, win, wout, sems = rest
    step = pl.program_id(0)
    n, _, size, width = x_ref.shape
    piece = win.shape[1] // parts

    def copies(q):
        cols = pl.ds(q * piece, piece)
        (one, at_one), (two, at_two) = places[q], places[parts + q]
        return (
            pltpu.make_async_copy(
                arrays[one].at[pl.ds(at_one, width), :], win.at[:, cols], sems.at[q]
            ),
            pltpu.make_async_copy(
                arrays[two].at[pl.ds(at_two, piece), :], wout.at[cols, :], sems.at[parts + q]
            ),
        )

    @pl.when(step == 0)
    def _():
        for q in range(parts):
            for c in copies(q):
                c.start()
        db_in[...] = jnp.zeros_like(db_in)
        db_out[...] = jnp.zeros_like(db_out)

    eye = (iota((size, size), 0) == iota((size, size), 1)).astype(BF)
    for s in range(n):
        rows = slice(s * size, (s + 1) * size)
        x_o[rows, :] = x_ref[s, 0]
        turned = dot_t(eye, x_ref[s, 0, size - 16 :, :size])
        gate = jnp.sum(jnp.where(iota(turned.shape, 1) >= 14, turned, 0.0), axis=1, keepdims=True)
        sg_o[rows, :] = (gate * c_ref[s, 0].astype(F32)).astype(BF)
    x = x_o[...]
    slot_grad = sg_o[...]
    db_out[0:1, :] += col_sum(slot_grad.astype(F32))

    @pl.when(step == 0)
    def _():
        for q in range(parts):
            for c in copies(q):
                c.wait()

    for q in range(parts):
        cols = slice(q * piece, (q + 1) * piece)
        pre = dot(x, win[:, cols]) + b_in[q, 0:1, :]
        square = pre * pre
        turn = jnp.tanh(pre * (GELU_A + GELU_A * GELU_B * square))
        half_turn = 0.5 * turn + 0.5
        act_o[:, cols] = (pre * half_turn).astype(BF)
        slope = half_turn + (0.5 * pre) * (1.0 - turn * turn) * (GELU_A + 3 * GELU_A * GELU_B * square)
        pre_grad = dot_t(slot_grad, wout[cols, :]) * slope
        pre_o[:, cols] = pre_grad.astype(BF)
        db_in[q, 0:1, :] += col_sum(pre_grad)
    out = (dot(act_o[...], wout[...]) + b_out[0:1, :]).astype(BF)
    back = dot_t(pre_o[...], win[...])
    ones = jnp.ones((16, width), BF)
    for s in range(n):
        rows = slice(s * size, (s + 1) * size)
        r_o[s, 0] = out[rows]
        d_o[s] = back[rows].astype(BF)
        prod = c_ref[s, 0].astype(F32) * out[rows].astype(F32)
        high = prod.astype(BF)
        low = (prod - high.astype(F32)).astype(BF)
        gate_grad = dot_t(ones, high) + dot_t(ones, low)
        grad_high = gate_grad.astype(BF).astype(F32)
        row = iota(gate_grad.shape, 0)
        tail = back[(s + 1) * size - 16 : (s + 1) * size, :size]
        both = jnp.where(row == 14, grad_high, gate_grad - grad_high)
        d_o[s, size - 16 :, :size] = jnp.where(row < 14, tail, both).astype(BF)


def expert_call(x, c, arrays, places, b_in, b_out, half, halves, before):
    experts, _, size, width = x.shape
    parts, _, piece = b_in.shape
    n = max(1, 256 // size)
    steps = experts // n
    rows, hidden = n * size, parts * piece
    before = list(before)
    tall = lambda cols: pl.BlockSpec((rows, cols), lambda i: (half * steps + i, 0))
    of_half = pl.BlockSpec((n, 1, size, width), lambda i: (i, half, 0, 0))
    total = halves * experts * size
    return pl.pallas_call(
        functools.partial(expert_kernel, places, len(arrays), len(before)),
        grid=(steps,),
        in_specs=[
            pl.BlockSpec((n, 1, size, width), lambda i: (i, 0, 0, 0)),
            of_half,
            whole((parts, 8, piece)),
            whole((8, width)),
        ]
        + [ANY] * (len(arrays) + len(before)),
        out_specs=[
            tall(hidden),
            tall(hidden),
            tall(width),
            tall(width),
            of_half,
            pl.BlockSpec((n, size, width), lambda i: (i, 0, 0)),
            whole((parts, 8, piece)),
            whole((8, width)),
        ],
        out_shape=[
            jax.ShapeDtypeStruct((total, hidden), BF),
            jax.ShapeDtypeStruct((total, hidden), BF),
            jax.ShapeDtypeStruct((total, width), BF),
            jax.ShapeDtypeStruct((total, width), BF),
            jax.ShapeDtypeStruct((experts, halves, size, width), BF),
            jax.ShapeDtypeStruct((experts, size, width), BF),
            jax.ShapeDtypeStruct((parts, 8, piece), F32),
            jax.ShapeDtypeStruct((8, width), F32),
        ],
        scratch_shapes=[
            pltpu.VMEM((width, hidden), BF),
            pltpu.VMEM((hidden, width), BF),
            pltpu.SemaphoreType.DMA((2 * parts,)),
        ],
        input_output_aliases={4 + len(arrays) + i: i for i in range(len(before))},
        compiler_params=params(44),
        cost_estimate=SMALL,
        name="expert_" + "ab"[half],
    )(x, c, b_in, b_out, *arrays, *before)


def weight_kernel(piece, q_in, q_out, n_more, x, pre, act, grad, bias, *refs):
    more, (in_o, out_o, bias_o, xs, ps, acts, gs, held, sems) = refs[:n_more], refs[n_more:]
    width = x.shape[1]
    copies = [
        pltpu.make_async_copy(x, xs, sems.at[0]),
        pltpu.make_async_copy(pre.at[:, pl.ds(q_in * piece, piece)], ps, sems.at[1]),
        pltpu.make_async_copy(act.at[:, pl.ds(q_out * piece, piece)], acts, sems.at[2]),
        pltpu.make_async_copy(grad, gs, sems.at[3]),
    ]
    extra = [
        pltpu.make_async_copy(far, held.at[k, pl.ds(0, far.shape[0]), :], sems.at[4 + k])
        for k, far in enumerate(more)
    ]
    copies[0].start()
    copies[1].start()
    copies[0].wait()
    copies[1].wait()
    for c in [copies[2], copies[3], *extra]:
        c.start()
    first = t_dot(xs[...], ps[...])
    sums = bias[q_in]
    for k in range(n_more // 2):
        extra[k].wait()
        first = first + held[k, :width, :].astype(F32)
        sums = sums + held[k, width:, :].astype(F32)
    in_o[:width, :] = first.astype(in_o.dtype)
    bias_o[...] = sums.astype(bias_o.dtype)
    if not n_more:
        in_o[width:, :] = sums.astype(in_o.dtype)
    copies[2].wait()
    copies[3].wait()
    second = t_dot(acts[...], gs[...])
    for k in range(n_more // 2, n_more):
        extra[k].wait()
        second = second + held[k, :piece, :].astype(F32)
    out_o[...] = second.astype(out_o.dtype)


def weight_grads(x, pre, act, grad, bias, piece, q_in, q_out, kind, more=()):
    total, width = x.shape
    vmem = pl.BlockSpec(memory_space=pltpu.VMEM)
    return pl.pallas_call(
        functools.partial(weight_kernel, piece, q_in, q_out, len(more)),
        in_specs=[ANY] * 4 + [vmem] + [ANY] * len(more),
        out_specs=[vmem] * 3,
        out_shape=[
            jax.ShapeDtypeStruct((width if more else width + 16, piece), kind),
            jax.ShapeDtypeStruct((piece, width), kind),
            jax.ShapeDtypeStruct((16, piece), kind),
        ],
        scratch_shapes=[
            pltpu.VMEM((total, width), BF),
            pltpu.VMEM((total, piece), BF),
            pltpu.VMEM((total, piece), BF),
            pltpu.VMEM((total, width), BF),
            pltpu.VMEM((max(1, len(more)), width + 16, width), BF),
            pltpu.SemaphoreType.DMA((4 + len(more),)),
        ],
        compiler_params=params(60),
        cost_estimate=SMALL,
        name="weight_grads",
    )(x, pre, act, grad, bias, *more)


def backward_kernel(experts, n, split, off, count, slots, cot, n1_far, qkv, att_far, aa, n2, probs_in, w_far, w_out, small, *refs):
    backs = refs[:n]
    ag_o, gp_o, dq_o = refs[n : n + 3]
    grads = refs[n + 3 : n + 3 + split]
    dw, ds, marks, ag_all, dq_all, n1, att, w, sems = refs[n + 3 + split :]
    img = pl.program_id(0)
    width = n1.shape[-1]
    late = [
        pltpu.make_async_copy(far, here, sems.at[k])
        for k, (far, here) in enumerate(((n1_far, n1), (att_far, att), (w_far, w)))
    ]
    size = backs[0].shape[1]
    total = experts * size

    @pl.when(img == 0)
    def _():
        for c in late:
            c.start()
        ds[...] = jnp.zeros_like(ds)
        line = iota((LANES, size), 0)
        for h in range(n):
            for e in range(experts):
                ends = backs[h][e, size - 16 :, :size].astype(F32)
                for k in range(2):
                    marks[2 * h + k, :, e * size : (e + 1) * size] = jnp.where(
                        line == e, ends[14 + k : 15 + k, :], 0.0
                    ).astype(BF)

    def vec(k):
        return small[experts + k : experts + k + 1, :]

    def add_vec(k, value):
        ds[experts + k : experts + k + 1, :] += value

    alive = (img < count[0]).astype(F32)
    up = cot[0].astype(F32)
    rows = up.shape[0]
    normed = n2[0]
    lane = iota((rows, LANES), 1)
    router = jnp.where(iota(small.shape, 0) < experts, small[...], 0.0).astype(BF)
    logits = jnp.where(lane < experts, dot_t(normed, router), NEG_FILL)
    exps = jnp.exp(logits - jnp.max(logits, axis=-1, keepdims=True))
    probs = exps / jnp.sum(exps, axis=-1, keepdims=True)
    gp_o[0] = probs
    first, second = slots[0, :, 0:1], slots[0, :, 1:2]
    normed_grad = jnp.zeros((rows, width), F32)
    placed = jnp.zeros((rows, LANES), F32)
    for h in range(n):
        place = iota((rows, total), 1) + h * total
        hot = ((place == first) | (place == second)).astype(BF)
        normed_grad = normed_grad + dot(hot, backs[h][...].reshape(total, width))
        placed = placed + dot_t(hot, marks[2 * h]) + dot_t(hot, marks[2 * h + 1])
    logit_grad = (
        probs * (placed - jnp.sum(probs * placed, axis=-1, keepdims=True))
    ).astype(BF)
    normed_grad = normed_grad + dot(logit_grad, router)
    ds[...] += jnp.where(iota(ds.shape, 0) < experts, t_dot(logit_grad, normed), 0.0)
    unit, inverse = norm_stats(aa[0])
    add_vec(3, col_sum(normed_grad * unit))
    add_vec(4, col_sum(normed_grad))
    after_grad = up + norm_back(unit, inverse, vec(3), normed_grad)
    attn_grad = (alive * after_grad).astype(BF)
    add_vec(2, col_sum(attn_grad.astype(F32)))
    ag_all[img] = attn_grad
    att_grad = dot_t(attn_grad, w_out[...]).astype(BF)
    low = lane < LANES // 2
    scale = (width // HEADS) ** -0.5
    for pair in range(HEADS // 2):
        c = pair * LANES
        q2 = qkv[0, :, c : c + LANES]
        k2 = qkv[0, :, width + c : width + c + LANES]
        v2 = qkv[0, :, 2 * width + c : 2 * width + c + LANES]
        o2 = att_grad[:, c : c + LANES]
        got = []
        for side, mask in enumerate((low, ~low)):
            prob = probs_in[0, 2 * pair + side]
            prob_grad = dot_t(v2, jnp.where(mask, o2, jnp.zeros_like(o2)))
            score_grad = (prob * (prob_grad - col_sum(prob * prob_grad))).astype(BF)
            got.append(
                (
                    t_dot(score_grad, k2) * scale,
                    dot(score_grad, q2) * scale,
                    dot(prob.astype(BF), o2),
                )
            )
        for k in range(3):
            dq_o[0, :, k * width + c : k * width + c + LANES] = jnp.where(
                low, got[0][k], got[1][k]
            ).astype(BF)
    grad = dq_o[0]
    dq_all[img] = grad
    for k in range(3):
        ds[experts + 5 + k : experts + 6 + k, :] += col_sum(grad[:, k * width : (k + 1) * width].astype(F32))
    ag_o[0] = after_grad

    @pl.when(img == pl.num_programs(0) - 1)
    def _():
        dw[:, 4 * width : 4 * width + LANES] = jnp.transpose(ds[...])
        for c in late:
            c.wait()
        left = n1[...].reshape(-1, width)
        for k in range(3):
            cols = slice(k * width, (k + 1) * width)
            dw[:, cols] = t_dot(left, dq_all[:, :, cols].reshape(-1, width))
        dw[:, 3 * width : 4 * width] = t_dot(
            att[...].reshape(-1, width), ag_all[...].reshape(-1, width)
        )
        with_weight = jnp.zeros((width, LANES), F32)
        with_sums = jnp.zeros((width, LANES), F32)
        for k in range(3 * width // LANES):
            cols = slice(k * LANES, (k + 1) * LANES)
            part, at = divmod(k * LANES, width)
            value = w[:, cols].astype(F32)
            sums = ds[experts + 5 + part : experts + 6 + part, at : at + LANES]
            with_weight = with_weight + value * dw[:, cols]
            with_sums = with_sums + value * sums
        sums = jnp.sum(with_sums, axis=1, keepdims=True)
        at = 4 * width
        sides = w[:, at : at + LANES].astype(F32)
        gain, shift = sides[:, experts : experts + 1], sides[:, experts + 1 : experts + 2]
        gains = (jnp.sum(with_weight, axis=1, keepdims=True) - shift * sums) / gain
        spot = iota((width, LANES), 1)
        cols = slice(at, at + LANES)
        dw[:, cols] = jnp.where(
            spot == experts, gains, jnp.where(spot == experts + 1, sums, dw[:, cols])
        )
        if split == 1:
            grads[0][...] = dw[...].astype(BF)
        else:
            cols = grads[0].shape[1]
            step = width // 16
            for h in range(2):
                col = pl.multiple_of(off[16 + h], LANES)
                for r in range(16):
                    row = pl.multiple_of(off[r], 16)
                    grads[h][r * step : (r + 1) * step, :] = dw[
                        pl.ds(row, step), pl.ds(col, cols)
                    ].astype(BF)


def backward(off, count, slots, cot, n1, qkv, att, aa, n2, prob, w, small, backs, experts, split):
    images, rows, width = cot.shape
    width_all = w.shape[1]
    n = len(backs)
    block = lambda cols: pl.BlockSpec((1, rows, cols), lambda i: (i, 0, 0))
    got = pl.pallas_call(
        functools.partial(backward_kernel, experts, n, split),
        grid=(images,),
        in_specs=[SMEM, SMEM, block(2), block(width), ANY, block(3 * width), ANY, block(width), block(width)]
        + [pl.BlockSpec((1, HEADS, rows, rows), lambda i: (i, 0, 0, 0))]
        + [ANY, pl.BlockSpec((width, width), lambda i: (0, 3), pipeline_mode=pl.Buffered(1)), whole(small.shape)]
        + [whole(backs[0].shape)] * n,
        out_specs=[block(width), block(LANES), block(3 * width)] + [whole((width, width_all // split))] * split,
        out_shape=[
            jax.ShapeDtypeStruct((images, rows, width), F32),
            jax.ShapeDtypeStruct((images, rows, LANES), F32),
            jax.ShapeDtypeStruct((images, rows, 3 * width), BF),
        ]
        + [jax.ShapeDtypeStruct((width, width_all // split), BF)] * split,
        scratch_shapes=[
            pltpu.VMEM((width, width_all), F32),
            pltpu.VMEM((LANES, width), F32),
            pltpu.VMEM((2 * n, LANES, backs[0].shape[0] * backs[0].shape[1]), BF),
            pltpu.VMEM((images, rows, width), BF),
            pltpu.VMEM((images, rows, 3 * width), BF),
            pltpu.VMEM((images, rows, width), BF),
            pltpu.VMEM((images, rows, width), BF),
            pltpu.VMEM(w.shape, BF),
            pltpu.SemaphoreType.DMA((3,)),
        ],
        compiler_params=params(),
        cost_estimate=SMALL,
        name="tokens_backward",
    )(off, count, slots, cot, n1, qkv, att, aa, n2, prob, w, w, small, *backs)
    return got[0], got[1], got[2], got[3:]


def place_rows(out, value):
    for k in range(out.shape[0] // SEQ):

        @pl.when(pl.program_id(0) == k)
        def _():
            out[k * SEQ : (k + 1) * SEQ, :] = value[:SEQ]


def finish_kernel(experts, after_grad, grad, tok, w, small, out):
    width = tok.shape[-1]
    normed_grad = dot_t(grad[0], w[...])
    unit, inverse = norm_stats(tok[0].astype(F32))
    value = after_grad[0] + norm_back(unit, inverse, small[experts : experts + 1, :], normed_grad)
    place_rows(out, value)


def finish(after_grad, grad, tok, w, small, experts):
    images, rows, width = tok.shape
    block = lambda cols: pl.BlockSpec((1, rows, cols), lambda i: (i, 0, 0))
    return pl.pallas_call(
        functools.partial(finish_kernel, experts),
        grid=(images,),
        in_specs=[block(width), block(3 * width), block(width), whole((width, 3 * width)), whole(small.shape)],
        out_specs=whole((images * SEQ, width)),
        out_shape=jax.ShapeDtypeStruct((images * SEQ, width), F32),
        compiler_params=params(60),
        cost_estimate=SMALL,
        name="tokens_finish",
    )(after_grad, grad, tok, w, small)


def output_kernel(count, slots, aa, probs, outs, out, total_f):
    rows = aa.shape[1]
    experts, n, size, width = outs.shape
    total = experts * size
    alive = (pl.program_id(0) < count[0]).astype(F32)
    first, second = slots[0, :, 0:1], slots[0, :, 1:2]
    gates = jnp.concatenate(
        [jnp.broadcast_to(probs[0, :, e : e + 1], (rows, size)) for e in range(experts)], axis=1
    )
    moe = jnp.zeros(aa.shape[1:], F32)
    for h in range(n):
        place = iota((rows, total), 1) + h * total
        gate = jnp.where((place == first) | (place == second), gates, 0.0)
        high = gate.astype(BF)
        low = (gate - high.astype(F32)).astype(BF)
        value = outs[:, h].reshape(total, width)
        moe = moe + dot(high, value) + dot(low, value)
    place_rows(total_f, aa[0] + alive * moe)

    @pl.when(pl.program_id(0) == pl.num_programs(0) - 1)
    def _():
        out[...] = total_f[...].astype(BF)


def block_output(count, slots, aa, probs, outs):
    images, rows, width = aa.shape
    block = lambda cols: pl.BlockSpec((1, rows, cols), lambda i: (i, 0, 0))
    return pl.pallas_call(
        output_kernel,
        grid=(images,),
        in_specs=[SMEM, block(2), block(width), block(LANES), whole(outs.shape)],
        out_specs=whole((images * SEQ, width)),
        out_shape=jax.ShapeDtypeStruct((images * SEQ, width), BF),
        scratch_shapes=[pltpu.VMEM((images * SEQ, width), F32)],
        compiler_params=params(60),
        cost_estimate=SMALL,
        name="block_output",
    )(count, slots, aa, probs, outs)


def local(sizes, *args):
    (tokens, image_count, routes, capacity, ln1_gain, ln1_bias, qkv_weight, qv_bias, out_weight, out_bias,
     ln2_gain, ln2_bias, router_weight, expert_in, expert_in_bias, expert_out, expert_out_bias, cotangent) = args
    dp, experts = sizes
    grouped = sizes == (4, 8)
    devices = dp * experts
    me_d = lax.axis_index("dp")
    me_e = lax.axis_index("expert")
    core = me_e % 2
    token_count, width = tokens.shape
    images = token_count // SEQ
    rows = up16(SEQ)
    cap = max(2, 5 * token_count // (2 * experts))
    halves = 2 if grouped else 1
    half_cap = -(-cap // halves)
    block_rows = up16(half_cap + 2)

    def hop(value, mask):
        return lax.ppermute(value, BOTH, [(i, i ^ mask) for i in range(devices)])

    def by_image(value):
        value = value.reshape(images, SEQ, value.shape[-1])
        fill = -1 if value.dtype == jnp.int32 else 0
        return jnp.pad(value, ((0, 0), (0, rows - SEQ), (0, 0)), constant_values=fill)

    def side_rows(values):
        return functools.reduce(
            lambda a, b: a + b,
            [jnp.pad(v.astype(F32)[None], ((k, 7 - k), (0, 0))) for k, v in enumerate(values)],
        )

    def slots_and_blocks(value):
        return first_dispatch(image_count, capacity, routes.T, value, half_cap, block_rows, halves)

    def slot_forms(slots):
        slots = slots.reshape(2, images, SEQ)
        slots = jnp.pad(slots, ((0, 0), (0, 0), (0, rows - SEQ)), constant_values=-1)
        return slots.transpose(1, 2, 0), slots.reshape(2, -1)

    def after(values, *done):
        return lax.optimization_barrier((values, done))[0]

    tok = by_image(tokens)

    vectors = [ln1_gain, ln1_bias, out_bias, ln2_gain, ln2_bias]
    width_all = 4 * width + 2 * LANES
    wide = expert_in.shape[2]
    spot = me_d * expert_out_bias.shape[1]
    if grouped:
        half = width_all // 2
        mine, other = pack_dense(
            core.reshape(1).astype(jnp.int32), qkv_weight, out_weight, router_weight.T, side_rows(vectors), qv_bias
        )
        got = hop(other, 1)
        chip = jnp.where(
            core == 0, jnp.concatenate([mine, got], axis=0), jnp.concatenate([got, mine], axis=0)
        )
        bias_out = lax.dynamic_update_slice(jnp.zeros((1, width), BF), expert_out_bias, (0, spot))
        bias = jnp.concatenate([expert_in_bias, bias_out, jnp.zeros((14, wide), BF)], axis=0)
        one = jnp.concatenate([expert_in[0], bias], axis=0)
        two = jnp.concatenate([expert_out[0], bias], axis=0)
        from_x, from_y = hop(expert_in[0], 8), hop(expert_out[0], 16)
        cot_blocks, slots = slots_and_blocks(after(cotangent, chip))
        slots_col, slots_row = slot_forms(slots)
        line = jnp.concatenate([chip] + [hop(chip, 2 * dz) for dz in (1, 2, 3)], axis=0)
        held, from_x, from_y = after((line, from_x, from_y))
        own = [line] + [hop(held, 8 * dxy) for dxy in (3, 1, 2)]
        own = [own[0], own[2], own[3], own[1]]
        step = width // 16
        at_rows = jnp.stack([((me_d ^ a) * 4 + ((me_e // 2) ^ b)) * step for a in range(4) for b in range(4)])
        at_cols = jnp.stack([core * half, (1 - core) * half])
        off_back = jnp.concatenate([at_rows, at_cols]).astype(jnp.int32)
        off = jnp.concatenate([at_rows, at_rows, jnp.repeat(at_cols, 4)]).astype(jnp.int32)
        own, tok, slots_row, off, one, two = after((own, tok, slots_row, off, one, two))
        pieces = own + [hop(piece, 1) for piece in own]
        subs = 4
        later_one, later_two, relay_x, relay_y = after((one, two, from_x, from_y), *own)
        near = hop(later_one, 16), hop(later_two, 8)
        relays = hop(relay_x, 16), hop(relay_y, 8), hop(near[0][width:], 8)
        arrays = [one, from_x, near[0], relays[0]]
        biases = [bias, near[1][width:], near[0][width:], relays[2]]
        b_in = jnp.stack([v[:8] for v in biases]).astype(F32)
        arrays += [two, near[1], from_y, relays[1]]
        places = tuple((q, 0) for q in range(8))
        b_out = jnp.broadcast_to(jnp.sum(b_in[:, 1], axis=0), (8, width))
        after_line = held
    else:
        fill = width_all - 4 * width - experts - 7
        pack = jnp.concatenate(
            [qkv_weight, out_weight, router_weight, jnp.stack(vectors, axis=1), qv_bias.T, jnp.zeros((ln1_gain.shape[0], fill), BF)], axis=1
        )
        pieces = [lax.all_gather(pack, BOTH, axis=0, tiled=True)]
        cot_blocks, slots = slots_and_blocks(cotangent)
        slots_col, slots_row = slot_forms(slots)
        off = jnp.zeros((2,), jnp.int32)
        off_back = off
        subs = 1
        after_line = pieces[0]
        w_in = lax.all_gather(expert_in[0], "dp", axis=0, tiled=False)
        w_out = lax.all_gather(expert_out[0], "dp", axis=0, tiled=False)
        arrays = [w[q] for w in (w_in, w_out) for q in range(dp)]
        places = tuple((q, 0) for q in range(2 * dp))
        b_in = lax.all_gather(jnp.broadcast_to(expert_in_bias, (8, wide)), "dp", axis=0, tiled=False).astype(F32)
        b_out = jnp.broadcast_to(
            lax.all_gather(expert_out_bias, "dp", axis=1, tiled=True).astype(F32), (8, width)
        )

    def exchange(blocks):
        return lax.all_to_all(blocks, "expert", 0, 0, tiled=True)

    cot_sent = exchange(after(cot_blocks, after_line))
    cot = by_image(cotangent)

    w, small, qkv, n1, att, aa, n2, prob = forward(off, subs, pieces, image_count, tok, experts, width_all)
    row_sent = []
    flat = n2.reshape(-1, width)
    for h in range(halves):
        sent = dispatch(slots_row, flat, small, experts, block_rows, h, 1, "ab"[h])
        waits = (near, relays)[h] if grouped else ()
        sent, cot_sent = after((sent, cot_sent), *row_sent, *waits)
        if h:
            sent, cot, slots_col = after((sent, cot, slots_col))
        row_sent.append(exchange(sent))

    back, grads_out, db_ins, db_outs, tall = [], [], [], [], ()
    for h in range(halves):
        *tall, d, db_in, db_out = expert_call(
            row_sent[h], cot_sent, arrays, places, b_in, b_out, h, halves, tall
        )
        grads_out.append(d)
        if h + 1 < halves:
            back.append(exchange(d))
        db_ins.append(db_in)
        db_outs.append(db_out)
    *tall, outs_back = tall
    db_in, db_out = sum(db_ins), sum(db_outs)

    both = [db_in[:, 0:1]]
    if grouped:
        both.append(jnp.broadcast_to(db_out[0:1], db_in[:, 0:1].shape))
    bias_sums = jnp.concatenate(
        [*both, jnp.zeros((dp, 16 - len(both), wide), F32)], axis=1
    )

    def weights_of(q_in, q_out, kind, more=()):
        act, pre, rows_in, slot_grad = tall
        return weight_grads(rows_in, pre, act, slot_grad, bias_sums, wide, q_in, q_out, kind, more)

    if grouped:
        far_in, far_out, _ = weights_of(3, 3, BF)
        tall = after(tall, far_in, far_out, *back)
        back.append(exchange(after(grads_out[-1], far_in, far_out, *back)))
        far_in, far_out = hop(far_in, 8), hop(far_out, 16)
        near_in, near_out, _ = weights_of(1, 2, BF)
        last_in, last_out, _ = weights_of(2, 1, BF)
        last_in = (last_in.astype(F32) + far_in.astype(F32)).astype(BF)
        last_out = (last_out.astype(F32) + far_out.astype(F32)).astype(BF)
        ready = (near_in, near_out, last_in, last_out)
        near_in, near_out = hop(near_in, 8), hop(near_out, 16)
        last_in, last_out = hop(last_in, 16), hop(last_out, 8)
        arrived = (near_in, near_out, last_in, last_out)
    else:
        ready = arrived = ()
        scatter = lambda v: lax.psum_scatter(v, "dp", scatter_dimension=0, tiled=True).astype(F32)
        back.append(exchange(grads_out[-1]))
        every = [weights_of(q, q, BF) for q in range(dp)]
        g_in = scatter(jnp.stack([e[0][:width] for e in every]))
        g_out = scatter(jnp.stack([e[1] for e in every]))
        g_b_in = lax.psum_scatter(
            db_in[:, 0].reshape(1, -1).astype(BF), "dp", scatter_dimension=1, tiled=True
        ).astype(F32)
        g_b_out = lax.psum_scatter(db_out[0:1].astype(BF), "dp", scatter_dimension=1, tiled=True).astype(F32)

    r_sent = exchange(after(outs_back, *back))
    back = after(back, *ready)
    after_grad, probs, grad, grads = backward(
        off_back, image_count, slots_col, cot, n1, qkv, att, aa, n2, prob, w, small, back, experts,
        2 if grouped else 1,
    )
    grads = after(grads, *arrived)
    block_out = block_output(image_count, slots_col, aa, probs, r_sent)
    def add(*values):
        return functools.reduce(lambda a, b: a + b, [v.astype(F32) for v in values])

    if grouped:
        sibling = hop(grads[1], 1)
        quarter = width // 4
        ways = [slice(a * quarter, (a + 1) * quarter) for a in range(4)]
        ways = [add(grads[0][a], sibling[a]).astype(BF) for a in ways]
        tall, bias_sums = after((tall, bias_sums), *ways)
        own_in, own_out, g_bias = weights_of(0, 0, F32, (near_in, last_in, near_out, last_out))
        g_in, g_out = own_in[None], own_out[None]
        g_b_in = g_bias[0:1]
        g_b_out = lax.dynamic_slice(g_bias[1:2], (0, spot), expert_out_bias.shape)
        after_grad, grad = after((after_grad, grad), own_in, own_out)
    tokens_grad = finish(after_grad, grad, tok, w, small, experts)

    if grouped:
        ways[0], tokens_grad, g_in, g_out = after((ways[0], tokens_grad, g_in, g_out))
        ways = [ways[0], *[hop(ways[a], 8 * a) for a in (1, 2, 3)]]
        step = width // 16
        cuts = [add(*[way[b * step : (b + 1) * step] for way in ways]) for b in range(4)]
        cuts = [cuts[0], *[c.astype(BF) for c in cuts[1:]]]
        cuts[0], block_out = after((cuts[0], block_out))
        chip = add(cuts[0], *[hop(cuts[b], 2 * b) for b in (1, 2, 3)])
        n_rows = step // 2
        keep = lax.dynamic_slice_in_dim(chip, core * n_rows, n_rows, 0)
        give = lax.dynamic_slice_in_dim(chip, (1 - core) * n_rows, n_rows, 0)
        got = hop(give.astype(BF), 1).astype(F32)
        dense = jnp.where(
            core == 0, jnp.concatenate([keep, got], axis=1), jnp.concatenate([got, keep], axis=1)
        )
    else:
        dense = lax.psum_scatter(grads[0], BOTH, scatter_dimension=0, tiled=True).astype(F32)
    side = dense[:, 4 * width :]
    vecs = [side[:, experts + k] for k in range(8)]
    return (
        block_out,
        tokens_grad,
        vecs[0],
        vecs[1],
        dense[:, : 3 * width],
        jnp.stack([vecs[5], vecs[7]], axis=0),
        dense[:, 3 * width : 4 * width],
        vecs[2],
        vecs[3],
        vecs[4],
        side[:, :experts],
        g_in,
        g_b_in,
        g_out,
        g_b_out,
    )


def solution(mesh):
    rows, line, cols = P(BOTH, None), P(BOTH), P(None, BOTH)
    experts = (P("expert", None, "dp"), P("expert", "dp"), P("expert", "dp", None), P("expert", "dp"))
    dense = (line, line, rows, cols, rows, line, line, line, rows)
    return jax.shard_map(
        functools.partial(local, (mesh.shape["dp"], mesh.shape["expert"])),
        mesh=mesh,
        in_specs=(rows, line, rows, P(), *dense, *experts, rows),
        out_specs=(rows, rows, *dense, *experts),
        check_vma=False,
    )
```

```python
import functools

import jax
import jax.numpy as jnp
from jax import lax
from jax.experimental import pallas as pl
from jax.experimental.pallas import tpu as pltpu
from jax.sharding import PartitionSpec as P

HEADS = 12
SEQ = 197
EPS_NORM = 1e-06
NEG_FILL = -1e30
BF = jnp.bfloat16
F32 = jnp.float32
LANES = 128
GELU_A = 0.7978845608028654
GELU_B = 0.044715
BOTH = ("dp", "expert")


def up16(n):
    return -(-n // 16) * 16


def dot(left, right):
    return jnp.dot(left, right, preferred_element_type=F32)


def dot_t(left, right):
    return lax.dot_general(left, right, (((1,), (1,)), ((), ())), preferred_element_type=F32)


def t_dot(left, right):
    return lax.dot_general(left, right, (((0,), (0,)), ((), ())), preferred_element_type=F32)


def iota(shape, dim):
    return lax.broadcasted_iota(jnp.int32, shape, dim)


def params(mib=60):
    return pltpu.CompilerParams(vmem_limit_bytes=mib << 20)


def whole(shape):
    zeros = (0,) * len(shape)
    return pl.BlockSpec(shape, lambda *_: zeros, pipeline_mode=pl.Buffered(1))


SMALL = pl.CostEstimate(flops=1 << 20, bytes_accessed=1 << 16, transcendentals=0)
LARGE = pl.CostEstimate(flops=1 << 34, bytes_accessed=1 << 16, transcendentals=0)
SMEM = pl.BlockSpec(memory_space=pltpu.SMEM)
ANY = pl.BlockSpec(memory_space=pl.ANY)


def norm_stats(values):
    centered = values - jnp.mean(values, axis=-1, keepdims=True)
    inverse = lax.rsqrt(jnp.mean(centered * centered, axis=-1, keepdims=True) + EPS_NORM)
    return centered * inverse, inverse


def norm_back(unit, inverse, gain, grad):
    scaled = grad * gain
    mean_one = jnp.mean(scaled, axis=-1, keepdims=True)
    mean_two = jnp.mean(scaled * unit, axis=-1, keepdims=True)
    return inverse * (scaled - mean_one - unit * mean_two)


def col_sum(values):
    return jnp.sum(values, axis=0, keepdims=True)


def pack_kernel(core, qkv, out, router, vectors, pair, mine, other):
    rows = qkv.shape[0]
    eye = (iota((rows, rows), 0) == iota((rows, rows), 1)).astype(BF)
    turned = [dot_t(eye, router[...]), dot_t(eye, vectors[...].astype(BF))[:, :5], dot_t(eye, pair[...])]
    used = sum(t.shape[1] for t in turned)
    turned = jnp.concatenate([*turned, jnp.zeros((rows, 2 * LANES - used), F32)], axis=1)
    value = jnp.concatenate([qkv[...], out[...], turned.astype(BF)], axis=1)
    half = value.shape[1] // 2

    @pl.when(core[0] == 0)
    def _():
        mine[...] = value[:, :half]
        other[...] = value[:, half:]

    @pl.when(core[0] != 0)
    def _():
        mine[...] = value[:, half:]
        other[...] = value[:, :half]


def pack_dense(core, qkv, out, router, vectors, pair):
    rows = qkv.shape[0]
    half = (qkv.shape[1] + out.shape[1] + 2 * LANES) // 2
    vmem = pl.BlockSpec(memory_space=pltpu.VMEM)
    return pl.pallas_call(
        pack_kernel,
        in_specs=[SMEM] + [vmem] * 5,
        out_specs=[vmem] * 2,
        out_shape=[jax.ShapeDtypeStruct((rows, half), BF)] * 2,
        compiler_params=params(60),
        cost_estimate=LARGE,
        name="pack_dense",
    )(core, qkv, out, router, vectors, pair)


def forward_kernel(experts, subs, off, count, tok, *refs):
    n_pieces = len(refs) - 10
    pieces = refs[:n_pieces]
    w_o, small, qkv_o, n1_o, att_o, aa_o, n2_o, prob_o, w, sems = refs[n_pieces:]
    img = pl.program_id(0)
    width = tok.shape[-1]

    @pl.when(img == 0)
    def _():
        copies = []
        for i, piece in enumerate(pieces):
            rows, cols = piece.shape[0] // subs, piece.shape[1]
            col = pl.multiple_of(off[n_pieces * subs + i], LANES)
            for j in range(subs):
                row = pl.multiple_of(off[i * subs + j], 16)
                copies.append(
                    pltpu.make_async_copy(
                        piece.at[pl.ds(j * rows, rows), :],
                        w.at[pl.ds(row, rows), pl.ds(col, cols)],
                        sems.at[i * subs + j],
                    )
                )
        for c in copies:
            c.start()
        for c in copies:
            c.wait()
        small[...] = jnp.transpose(w[:, 4 * width : 4 * width + LANES].astype(F32))
        pltpu.make_async_copy(w, w_o, sems.at[0]).start()

    def vec(k):
        return small[experts + k : experts + k + 1, :]

    x = tok[0].astype(F32)
    rows = x.shape[0]
    unit, _ = norm_stats(x)
    n1 = (unit * vec(0) + vec(1)).astype(BF)
    n1_o[0] = n1
    biases = (vec(5), None, vec(6))
    for part in range(3):
        cols = slice(part * width, (part + 1) * width)
        block = dot(n1, w[:, cols])
        if biases[part] is not None:
            block = block + biases[part]
        qkv_o[0, :, cols] = block.astype(BF)
    low = iota((rows, LANES), 1) < LANES // 2
    seen = iota((rows, rows), 0) < SEQ
    scale = (width // HEADS) ** -0.5
    for pair in range(HEADS // 2):
        c = pair * LANES
        q2 = qkv_o[0, :, c : c + LANES]
        k2 = qkv_o[0, :, width + c : width + c + LANES]
        v2 = qkv_o[0, :, 2 * width + c : 2 * width + c + LANES]
        got = []
        for side, mask in enumerate((low, ~low)):
            scores = dot_t(k2, jnp.where(mask, q2, jnp.zeros_like(q2))) * scale
            scores = jnp.where(seen, scores, NEG_FILL)
            exps = jnp.exp(scores - jnp.max(scores, axis=0, keepdims=True))
            prob = exps * (1.0 / col_sum(exps))
            prob_o[0, 2 * pair + side] = prob
            got.append(t_dot(prob.astype(BF), v2))
        att_o[0, :, c : c + LANES] = jnp.where(low, got[0], got[1]).astype(BF)
    alive = (img < count[0]).astype(F32)
    after = x + alive * (dot(att_o[0], w[:, 3 * width : 4 * width]) + vec(2))
    aa_o[0] = after
    unit, _ = norm_stats(after)
    n2_o[0] = (unit * vec(3) + vec(4)).astype(BF)

    @pl.when(img == pl.num_programs(0) - 1)
    def _():
        pltpu.make_async_copy(w, w_o, sems.at[0]).wait()


def forward(off, subs, pieces, count, tok, experts, width_all):
    images, rows, width = tok.shape
    block = lambda cols: pl.BlockSpec((1, rows, cols), lambda i: (i, 0, 0))
    shape = lambda cols, t: jax.ShapeDtypeStruct((images, rows, cols), t)
    return pl.pallas_call(
        functools.partial(forward_kernel, experts, subs),
        grid=(images,),
        in_specs=[SMEM, SMEM, block(width)] + [ANY] * len(pieces),
        out_specs=[
            ANY,
            whole((LANES, width)),
            block(3 * width),
            block(width),
            block(width),
            block(width),
            block(width),
            pl.BlockSpec((1, HEADS, rows, rows), lambda i: (i, 0, 0, 0)),
        ],
        out_shape=[
            jax.ShapeDtypeStruct((width, width_all), BF),
            jax.ShapeDtypeStruct((LANES, width), F32),
            shape(3 * width, BF),
            shape(width, BF),
            shape(width, BF),
            shape(width, F32),
            shape(width, BF),
            jax.ShapeDtypeStruct((images, HEADS, rows, rows), F32),
        ],
        scratch_shapes=[
            pltpu.VMEM((width, width_all), BF),
            pltpu.SemaphoreType.DMA((len(pieces) * subs,)),
        ],
        compiler_params=params(60),
        cost_estimate=SMALL,
        name="tokens_forward",
    )(off, count, tok, *pieces)


def dispatch_kernel(experts, half, gated, slots, x, *refs):
    out = refs[-1]
    value = x[...]
    halves, block_rows = out.shape[1:3]
    first, second = slots[0:1, :], slots[1:2, :]
    if gated:
        router = refs[0][...].astype(BF)
        logits = dot_t(router, value)
        logits = jnp.where(iota(logits.shape, 0) < experts, logits, NEG_FILL)
        exps = jnp.exp(logits - jnp.max(logits, axis=0, keepdims=True))
        probs = exps / jnp.sum(exps, axis=0, keepdims=True)
    total = experts * block_rows
    for h in range(halves):
        place = iota((total, value.shape[0]), 0) + (half + h) * total
        hot = ((place == first) | (place == second)).astype(BF)
        out[:, h] = dot(hot, value).astype(BF).reshape(experts, block_rows, value.shape[1])
        if gated:
            row = iota((16, value.shape[0]), 0)
            for e in range(experts):
                gate = probs[e : e + 1, :]
                high = gate.astype(BF).astype(F32)
                pair = jnp.where(row == 14, high, jnp.where(row == 15, gate - high, 0.0))
                placed = dot_t(pair.astype(BF), hot[e * block_rows : (e + 1) * block_rows])
                tail = out[e, h, block_rows - 16 :, :block_rows].astype(F32)
                out[e, h, block_rows - 16 :, :block_rows] = jnp.where(
                    iota(tail.shape, 0) < 14, tail, placed
                ).astype(BF)


def dispatch(slots, x, small, experts, block_rows, half, halves, tag):
    rows, width = x.shape
    gated = small is not None
    more = [small] if gated else []
    vmem = pl.BlockSpec(memory_space=pltpu.VMEM)
    return pl.pallas_call(
        functools.partial(dispatch_kernel, experts, half, gated),
        in_specs=[vmem] * (2 + len(more)),
        out_specs=vmem,
        out_shape=jax.ShapeDtypeStruct((experts, halves, block_rows, width), BF),
        compiler_params=params(24),
        cost_estimate=SMALL,
        name="dispatch_" + tag,
    )(slots, x, *more)


def first_kernel(experts, half_cap, count, capacity, routes, x, out, slots):
    rows = routes.shape[1]
    halves, block_rows = out.shape[1:3]
    alive = iota((1, rows), 1) < count[0] * SEQ
    name = iota((up16(experts), rows), 0)
    earlier = (iota((rows, rows), 0) < iota((rows, rows), 1)).astype(BF)
    limits = jnp.zeros((up16(experts), 1), F32)
    for e in range(experts):
        limits = jnp.where(name[:, 0:1] == e, capacity[e].astype(F32), limits)
    base = 0.0
    for k in range(2):
        hit = jnp.where((routes[k : k + 1, :] == name) & alive, 1.0, 0.0)
        place = col_sum(hit * (dot(hit.astype(BF), earlier) + base))
        keep = place < col_sum(hit * limits)
        base = jnp.sum(hit, axis=1, keepdims=True)
        place = place.astype(jnp.int32)
        half = (place >= half_cap).astype(jnp.int32)
        spot = (half * experts + routes[k : k + 1, :]) * block_rows + place - half * half_cap
        slots[k : k + 1, :] = jnp.where(keep, spot, -1)
    dispatch_kernel(experts, 0, False, slots, x, out)


def first_dispatch(count, capacity, routes, x, half_cap, block_rows, halves):
    rows, width = x.shape
    experts = capacity.shape[0]
    vmem = pl.BlockSpec(memory_space=pltpu.VMEM)
    return pl.pallas_call(
        functools.partial(first_kernel, experts, half_cap),
        in_specs=[SMEM, SMEM, vmem, vmem],
        out_specs=[vmem, vmem],
        out_shape=[
            jax.ShapeDtypeStruct((experts, halves, block_rows, width), BF),
            jax.ShapeDtypeStruct((2, rows), jnp.int32),
        ],
        compiler_params=params(24),
        cost_estimate=SMALL,
        name="dispatch_first",
    )(count, capacity, routes, x)


def expert_kernel(places, n_arrays, n_before, *refs):
    x_ref, c_ref, b_in, b_out = refs[:4]
    arrays, parts = refs[4 : 4 + n_arrays], len(places) // 2
    rest = refs[4 + n_arrays + n_before :]
    act_o, pre_o, x_o, sg_o, r_o, d_o, db_in, db_out, win, wout, sems = rest
    step = pl.program_id(0)
    n, _, size, width = x_ref.shape
    piece = win.shape[1] // parts

    def copies(q):
        cols = pl.ds(q * piece, piece)
        (one, at_one), (two, at_two) = places[q], places[parts + q]
        return (
            pltpu.make_async_copy(
                arrays[one].at[pl.ds(at_one, width), :], win.at[:, cols], sems.at[q]
            ),
            pltpu.make_async_copy(
                arrays[two].at[pl.ds(at_two, piece), :], wout.at[cols, :], sems.at[parts + q]
            ),
        )

    @pl.when(step == 0)
    def _():
        for q in range(parts):
            for c in copies(q):
                c.start()
        db_in[...] = jnp.zeros_like(db_in)
        db_out[...] = jnp.zeros_like(db_out)

    eye = (iota((size, size), 0) == iota((size, size), 1)).astype(BF)
    for s in range(n):
        rows = slice(s * size, (s + 1) * size)
        x_o[rows, :] = x_ref[s, 0]
        turned = dot_t(eye, x_ref[s, 0, size - 16 :, :size])
        gate = jnp.sum(jnp.where(iota(turned.shape, 1) >= 14, turned, 0.0), axis=1, keepdims=True)
        sg_o[rows, :] = (gate * c_ref[s, 0].astype(F32)).astype(BF)
    x = x_o[...]
    slot_grad = sg_o[...]
    db_out[0:1, :] += col_sum(slot_grad.astype(F32))

    @pl.when(step == 0)
    def _():
        for q in range(parts):
            for c in copies(q):
                c.wait()

    for q in range(parts):
        cols = slice(q * piece, (q + 1) * piece)
        pre = dot(x, win[:, cols]) + b_in[q, 0:1, :]
        square = pre * pre
        turn = jnp.tanh(pre * (GELU_A + GELU_A * GELU_B * square))
        half_turn = 0.5 * turn + 0.5
        act_o[:, cols] = (pre * half_turn).astype(BF)
        slope = half_turn + (0.5 * pre) * (1.0 - turn * turn) * (GELU_A + 3 * GELU_A * GELU_B * square)
        pre_grad = dot_t(slot_grad, wout[cols, :]) * slope
        pre_o[:, cols] = pre_grad.astype(BF)
        db_in[q, 0:1, :] += col_sum(pre_grad)
    out = (dot(act_o[...], wout[...]) + b_out[0:1, :]).astype(BF)
    back = dot_t(pre_o[...], win[...])
    ones = jnp.ones((16, width), BF)
    for s in range(n):
        rows = slice(s * size, (s + 1) * size)
        r_o[s, 0] = out[rows]
        d_o[s] = back[rows].astype(BF)
        prod = c_ref[s, 0].astype(F32) * out[rows].astype(F32)
        high = prod.astype(BF)
        low = (prod - high.astype(F32)).astype(BF)
        gate_grad = dot_t(ones, high) + dot_t(ones, low)
        grad_high = gate_grad.astype(BF).astype(F32)
        row = iota(gate_grad.shape, 0)
        tail = back[(s + 1) * size - 16 : (s + 1) * size, :size]
        both = jnp.where(row == 14, grad_high, gate_grad - grad_high)
        d_o[s, size - 16 :, :size] = jnp.where(row < 14, tail, both).astype(BF)


def expert_call(x, c, arrays, places, b_in, b_out, half, halves, before):
    experts, _, size, width = x.shape
    parts, _, piece = b_in.shape
    n = max(1, 256 // size)
    steps = experts // n
    rows, hidden = n * size, parts * piece
    before = list(before)
    tall = lambda cols: pl.BlockSpec((rows, cols), lambda i: (half * steps + i, 0))
    of_half = pl.BlockSpec((n, 1, size, width), lambda i: (i, half, 0, 0))
    total = halves * experts * size
    return pl.pallas_call(
        functools.partial(expert_kernel, places, len(arrays), len(before)),
        grid=(steps,),
        in_specs=[
            pl.BlockSpec((n, 1, size, width), lambda i: (i, 0, 0, 0)),
            of_half,
            whole((parts, 8, piece)),
            whole((8, width)),
        ]
        + [ANY] * (len(arrays) + len(before)),
        out_specs=[
            tall(hidden),
            tall(hidden),
            tall(width),
            tall(width),
            of_half,
            pl.BlockSpec((n, size, width), lambda i: (i, 0, 0)),
            whole((parts, 8, piece)),
            whole((8, width)),
        ],
        out_shape=[
            jax.ShapeDtypeStruct((total, hidden), BF),
            jax.ShapeDtypeStruct((total, hidden), BF),
            jax.ShapeDtypeStruct((total, width), BF),
            jax.ShapeDtypeStruct((total, width), BF),
            jax.ShapeDtypeStruct((experts, halves, size, width), BF),
            jax.ShapeDtypeStruct((experts, size, width), BF),
            jax.ShapeDtypeStruct((parts, 8, piece), F32),
            jax.ShapeDtypeStruct((8, width), F32),
        ],
        scratch_shapes=[
            pltpu.VMEM((width, hidden), BF),
            pltpu.VMEM((hidden, width), BF),
            pltpu.SemaphoreType.DMA((2 * parts,)),
        ],
        input_output_aliases={4 + len(arrays) + i: i for i in range(len(before))},
        compiler_params=params(44),
        cost_estimate=SMALL,
        name="expert_" + "ab"[half],
    )(x, c, b_in, b_out, *arrays, *before)


def weight_kernel(piece, q_in, q_out, n_more, x, pre, act, grad, bias, *refs):
    more, (in_o, out_o, bias_o, xs, ps, acts, gs, held, sems) = refs[:n_more], refs[n_more:]
    width = x.shape[1]
    step = x.shape[0] // 4
    pairs = (
        (x, 0, xs),
        (pre, q_in * piece, ps),
        (act, q_out * piece, acts),
        (grad, 0, gs),
    )
    copies = [
        [
            pltpu.make_async_copy(
                far.at[pl.ds(c * step, step), pl.ds(col, here.shape[1])],
                here.at[pl.ds(c * step, step), :],
                sems.at[4 * k + c],
            )
            for c in range(4)
        ]
        for k, (far, col, here) in enumerate(pairs)
    ]
    extra = [
        pltpu.make_async_copy(far, held.at[k, pl.ds(0, far.shape[0]), :], sems.at[16 + k])
        for k, far in enumerate(more)
    ]
    for c in [*copies[0], *copies[1]]:
        c.start()
    for c in [*copies[0], *copies[1]]:
        c.wait()
    for c in [*copies[2], *copies[3], *extra]:
        c.start()
    first = t_dot(xs[...], ps[...])
    sums = bias[q_in]
    for k in range(n_more // 2):
        extra[k].wait()
        first = first + held[k, :width, :].astype(F32)
        sums = sums + held[k, width:, :].astype(F32)
    in_o[:width, :] = first.astype(in_o.dtype)
    bias_o[...] = sums.astype(bias_o.dtype)
    if not n_more:
        in_o[width:, :] = sums.astype(in_o.dtype)
    for c in [*copies[2], *copies[3]]:
        c.wait()
    second = t_dot(acts[...], gs[...])
    for k in range(n_more // 2, n_more):
        extra[k].wait()
        second = second + held[k, :piece, :].astype(F32)
    out_o[...] = second.astype(out_o.dtype)


def weight_grads(x, pre, act, grad, bias, piece, q_in, q_out, kind, more=()):
    total, width = x.shape
    vmem = pl.BlockSpec(memory_space=pltpu.VMEM)
    return pl.pallas_call(
        functools.partial(weight_kernel, piece, q_in, q_out, len(more)),
        in_specs=[ANY] * 4 + [vmem] + [ANY] * len(more),
        out_specs=[vmem] * 3,
        out_shape=[
            jax.ShapeDtypeStruct((width if more else width + 16, piece), kind),
            jax.ShapeDtypeStruct((piece, width), kind),
            jax.ShapeDtypeStruct((16, piece), kind),
        ],
        scratch_shapes=[
            pltpu.VMEM((total, width), BF),
            pltpu.VMEM((total, piece), BF),
            pltpu.VMEM((total, piece), BF),
            pltpu.VMEM((total, width), BF),
            pltpu.VMEM((max(1, len(more)), width + 16, width), BF),
            pltpu.SemaphoreType.DMA((16 + len(more),)),
        ],
        compiler_params=params(60),
        cost_estimate=SMALL,
        name="weight_grads",
    )(x, pre, act, grad, bias, *more)


def backward_kernel(experts, n, split, off, count, slots, cot, n1_far, qkv, att_far, aa, n2, probs_in, w_far, w_out, small, *refs):
    backs = refs[:n]
    ag_o, gp_o, dq_o = refs[n : n + 3]
    grads = refs[n + 3 : n + 3 + split]
    dw, ds, marks, ag_all, dq_all, n1, att, w, sems = refs[n + 3 + split :]
    img = pl.program_id(0)
    width = n1.shape[-1]
    late = [
        pltpu.make_async_copy(far, here, sems.at[k])
        for k, (far, here) in enumerate(((n1_far, n1), (att_far, att), (w_far, w)))
    ]
    size = backs[0].shape[1]
    total = experts * size

    @pl.when(img == 0)
    def _():
        for c in late:
            c.start()
        ds[...] = jnp.zeros_like(ds)
        line = iota((LANES, size), 0)
        for h in range(n):
            for e in range(experts):
                ends = backs[h][e, size - 16 :, :size].astype(F32)
                for k in range(2):
                    marks[2 * h + k, :, e * size : (e + 1) * size] = jnp.where(
                        line == e, ends[14 + k : 15 + k, :], 0.0
                    ).astype(BF)

    def vec(k):
        return small[experts + k : experts + k + 1, :]

    def add_vec(k, value):
        ds[experts + k : experts + k + 1, :] += value

    alive = (img < count[0]).astype(F32)
    up = cot[0].astype(F32)
    rows = up.shape[0]
    normed = n2[0]
    lane = iota((rows, LANES), 1)
    router = jnp.where(iota(small.shape, 0) < experts, small[...], 0.0).astype(BF)
    logits = jnp.where(lane < experts, dot_t(normed, router), NEG_FILL)
    exps = jnp.exp(logits - jnp.max(logits, axis=-1, keepdims=True))
    probs = exps / jnp.sum(exps, axis=-1, keepdims=True)
    gp_o[0] = probs
    first, second = slots[0, :, 0:1], slots[0, :, 1:2]
    normed_grad = jnp.zeros((rows, width), F32)
    placed = jnp.zeros((rows, LANES), F32)
    for h in range(n):
        place = iota((rows, total), 1) + h * total
        hot = ((place == first) | (place == second)).astype(BF)
        normed_grad = normed_grad + dot(hot, backs[h][...].reshape(total, width))
        placed = placed + dot_t(hot, marks[2 * h]) + dot_t(hot, marks[2 * h + 1])
    logit_grad = (
        probs * (placed - jnp.sum(probs * placed, axis=-1, keepdims=True))
    ).astype(BF)
    normed_grad = normed_grad + dot(logit_grad, router)
    ds[...] += jnp.where(iota(ds.shape, 0) < experts, t_dot(logit_grad, normed), 0.0)
    unit, inverse = norm_stats(aa[0])
    add_vec(3, col_sum(normed_grad * unit))
    add_vec(4, col_sum(normed_grad))
    after_grad = up + norm_back(unit, inverse, vec(3), normed_grad)
    attn_grad = (alive * after_grad).astype(BF)
    add_vec(2, col_sum(attn_grad.astype(F32)))
    ag_all[img] = attn_grad
    att_grad = dot_t(attn_grad, w_out[...]).astype(BF)
    low = lane < LANES // 2
    scale = (width // HEADS) ** -0.5
    for pair in range(HEADS // 2):
        c = pair * LANES
        q2 = qkv[0, :, c : c + LANES]
        k2 = qkv[0, :, width + c : width + c + LANES]
        v2 = qkv[0, :, 2 * width + c : 2 * width + c + LANES]
        o2 = att_grad[:, c : c + LANES]
        got = []
        for side, mask in enumerate((low, ~low)):
            prob = probs_in[0, 2 * pair + side]
            prob_grad = dot_t(v2, jnp.where(mask, o2, jnp.zeros_like(o2)))
            score_grad = (prob * (prob_grad - col_sum(prob * prob_grad))).astype(BF)
            got.append(
                (
                    t_dot(score_grad, k2) * scale,
                    dot(score_grad, q2) * scale,
                    dot(prob.astype(BF), o2),
                )
            )
        for k in range(3):
            dq_o[0, :, k * width + c : k * width + c + LANES] = jnp.where(
                low, got[0][k], got[1][k]
            ).astype(BF)
    grad = dq_o[0]
    dq_all[img] = grad
    for k in range(3):
        ds[experts + 5 + k : experts + 6 + k, :] += col_sum(grad[:, k * width : (k + 1) * width].astype(F32))
    ag_o[0] = after_grad

    @pl.when(img == pl.num_programs(0) - 1)
    def _():
        dw[:, 4 * width : 4 * width + LANES] = jnp.transpose(ds[...])
        for c in late:
            c.wait()
        left = n1[...].reshape(-1, width)
        for k in range(3):
            cols = slice(k * width, (k + 1) * width)
            dw[:, cols] = t_dot(left, dq_all[:, :, cols].reshape(-1, width))
        dw[:, 3 * width : 4 * width] = t_dot(
            att[...].reshape(-1, width), ag_all[...].reshape(-1, width)
        )
        with_weight = jnp.zeros((width, LANES), F32)
        with_sums = jnp.zeros((width, LANES), F32)
        for k in range(3 * width // LANES):
            cols = slice(k * LANES, (k + 1) * LANES)
            part, at = divmod(k * LANES, width)
            value = w[:, cols].astype(F32)
            sums = ds[experts + 5 + part : experts + 6 + part, at : at + LANES]
            with_weight = with_weight + value * dw[:, cols]
            with_sums = with_sums + value * sums
        sums = jnp.sum(with_sums, axis=1, keepdims=True)
        at = 4 * width
        sides = w[:, at : at + LANES].astype(F32)
        gain, shift = sides[:, experts : experts + 1], sides[:, experts + 1 : experts + 2]
        gains = (jnp.sum(with_weight, axis=1, keepdims=True) - shift * sums) / gain
        spot = iota((width, LANES), 1)
        cols = slice(at, at + LANES)
        dw[:, cols] = jnp.where(
            spot == experts, gains, jnp.where(spot == experts + 1, sums, dw[:, cols])
        )
        if split == 1:
            grads[0][...] = dw[...].astype(BF)
        else:
            cols = grads[0].shape[1]
            step = width // 16
            for h in range(2):
                col = pl.multiple_of(off[16 + h], LANES)
                for r in range(16):
                    row = pl.multiple_of(off[r], 16)
                    grads[h][r * step : (r + 1) * step, :] = dw[
                        pl.ds(row, step), pl.ds(col, cols)
                    ].astype(BF)


def backward(off, count, slots, cot, n1, qkv, att, aa, n2, prob, w, small, backs, experts, split):
    images, rows, width = cot.shape
    width_all = w.shape[1]
    n = len(backs)
    block = lambda cols: pl.BlockSpec((1, rows, cols), lambda i: (i, 0, 0))
    got = pl.pallas_call(
        functools.partial(backward_kernel, experts, n, split),
        grid=(images,),
        in_specs=[SMEM, SMEM, block(2), block(width), ANY, block(3 * width), ANY, block(width), block(width)]
        + [pl.BlockSpec((1, HEADS, rows, rows), lambda i: (i, 0, 0, 0))]
        + [ANY, pl.BlockSpec((width, width), lambda i: (0, 3), pipeline_mode=pl.Buffered(1)), whole(small.shape)]
        + [whole(backs[0].shape)] * n,
        out_specs=[block(width), block(LANES), block(3 * width)] + [whole((width, width_all // split))] * split,
        out_shape=[
            jax.ShapeDtypeStruct((images, rows, width), F32),
            jax.ShapeDtypeStruct((images, rows, LANES), F32),
            jax.ShapeDtypeStruct((images, rows, 3 * width), BF),
        ]
        + [jax.ShapeDtypeStruct((width, width_all // split), BF)] * split,
        scratch_shapes=[
            pltpu.VMEM((width, width_all), F32),
            pltpu.VMEM((LANES, width), F32),
            pltpu.VMEM((2 * n, LANES, backs[0].shape[0] * backs[0].shape[1]), BF),
            pltpu.VMEM((images, rows, width), BF),
            pltpu.VMEM((images, rows, 3 * width), BF),
            pltpu.VMEM((images, rows, width), BF),
            pltpu.VMEM((images, rows, width), BF),
            pltpu.VMEM(w.shape, BF),
            pltpu.SemaphoreType.DMA((3,)),
        ],
        compiler_params=params(),
        cost_estimate=SMALL,
        name="tokens_backward",
    )(off, count, slots, cot, n1, qkv, att, aa, n2, prob, w, w, small, *backs)
    return got[0], got[1], got[2], got[3:]


def place_rows(out, value):
    for k in range(out.shape[0] // SEQ):

        @pl.when(pl.program_id(0) == k)
        def _():
            out[k * SEQ : (k + 1) * SEQ, :] = value[:SEQ]


def finish_kernel(experts, after_grad, grad, tok, w, small, out):
    width = tok.shape[-1]
    normed_grad = dot_t(grad[0], w[...])
    unit, inverse = norm_stats(tok[0].astype(F32))
    value = after_grad[0] + norm_back(unit, inverse, small[experts : experts + 1, :], normed_grad)
    place_rows(out, value)


def finish(after_grad, grad, tok, w, small, experts):
    images, rows, width = tok.shape
    block = lambda cols: pl.BlockSpec((1, rows, cols), lambda i: (i, 0, 0))
    return pl.pallas_call(
        functools.partial(finish_kernel, experts),
        grid=(images,),
        in_specs=[block(width), block(3 * width), block(width), whole((width, 3 * width)), whole(small.shape)],
        out_specs=whole((images * SEQ, width)),
        out_shape=jax.ShapeDtypeStruct((images * SEQ, width), F32),
        compiler_params=params(60),
        cost_estimate=SMALL,
        name="tokens_finish",
    )(after_grad, grad, tok, w, small)


def output_kernel(count, slots, aa, probs, outs, out, total_f):
    rows = aa.shape[1]
    experts, n, size, width = outs.shape
    total = experts * size
    alive = (pl.program_id(0) < count[0]).astype(F32)
    first, second = slots[0, :, 0:1], slots[0, :, 1:2]
    gates = jnp.concatenate(
        [jnp.broadcast_to(probs[0, :, e : e + 1], (rows, size)) for e in range(experts)], axis=1
    )
    moe = jnp.zeros(aa.shape[1:], F32)
    for h in range(n):
        place = iota((rows, total), 1) + h * total
        gate = jnp.where((place == first) | (place == second), gates, 0.0)
        high = gate.astype(BF)
        low = (gate - high.astype(F32)).astype(BF)
        value = outs[:, h].reshape(total, width)
        moe = moe + dot(high, value) + dot(low, value)
    place_rows(total_f, aa[0] + alive * moe)

    @pl.when(pl.program_id(0) == pl.num_programs(0) - 1)
    def _():
        out[...] = total_f[...].astype(BF)


def block_output(count, slots, aa, probs, outs):
    images, rows, width = aa.shape
    block = lambda cols: pl.BlockSpec((1, rows, cols), lambda i: (i, 0, 0))
    return pl.pallas_call(
        output_kernel,
        grid=(images,),
        in_specs=[SMEM, block(2), block(width), block(LANES), whole(outs.shape)],
        out_specs=whole((images * SEQ, width)),
        out_shape=jax.ShapeDtypeStruct((images * SEQ, width), BF),
        scratch_shapes=[pltpu.VMEM((images * SEQ, width), F32)],
        compiler_params=params(60),
        cost_estimate=SMALL,
        name="block_output",
    )(count, slots, aa, probs, outs)


def local(sizes, *args):
    (tokens, image_count, routes, capacity, ln1_gain, ln1_bias, qkv_weight, qv_bias, out_weight, out_bias,
     ln2_gain, ln2_bias, router_weight, expert_in, expert_in_bias, expert_out, expert_out_bias, cotangent) = args
    dp, experts = sizes
    grouped = sizes == (4, 8)
    devices = dp * experts
    me_d = lax.axis_index("dp")
    me_e = lax.axis_index("expert")
    core = me_e % 2
    token_count, width = tokens.shape
    images = token_count // SEQ
    rows = up16(SEQ)
    cap = max(2, 5 * token_count // (2 * experts))
    halves = 2 if grouped else 1
    half_cap = -(-cap // halves)
    block_rows = up16(half_cap + 2)

    def hop(value, mask):
        return lax.ppermute(value, BOTH, [(i, i ^ mask) for i in range(devices)])

    def by_image(value):
        value = value.reshape(images, SEQ, value.shape[-1])
        fill = -1 if value.dtype == jnp.int32 else 0
        return jnp.pad(value, ((0, 0), (0, rows - SEQ), (0, 0)), constant_values=fill)

    def side_rows(values):
        return functools.reduce(
            lambda a, b: a + b,
            [jnp.pad(v.astype(F32)[None], ((k, 7 - k), (0, 0))) for k, v in enumerate(values)],
        )

    def slots_and_blocks(value):
        return first_dispatch(image_count, capacity, routes.T, value, half_cap, block_rows, halves)

    def slot_forms(slots):
        slots = slots.reshape(2, images, SEQ)
        slots = jnp.pad(slots, ((0, 0), (0, 0), (0, rows - SEQ)), constant_values=-1)
        return slots.transpose(1, 2, 0), slots.reshape(2, -1)

    def after(values, *done):
        return lax.optimization_barrier((values, done))[0]

    tok = by_image(tokens)

    vectors = [ln1_gain, ln1_bias, out_bias, ln2_gain, ln2_bias]
    width_all = 4 * width + 2 * LANES
    wide = expert_in.shape[2]
    spot = me_d * expert_out_bias.shape[1]
    if grouped:
        half = width_all // 2
        mine, other = pack_dense(
            core.reshape(1).astype(jnp.int32), qkv_weight, out_weight, router_weight.T, side_rows(vectors), qv_bias
        )
        got = hop(other, 1)
        chip = jnp.where(
            core == 0, jnp.concatenate([mine, got], axis=0), jnp.concatenate([got, mine], axis=0)
        )
        bias_out = lax.dynamic_update_slice(jnp.zeros((1, width), BF), expert_out_bias, (0, spot))
        bias = jnp.concatenate([expert_in_bias, bias_out, jnp.zeros((14, wide), BF)], axis=0)
        one = jnp.concatenate([expert_in[0], bias], axis=0)
        two = jnp.concatenate([expert_out[0], bias], axis=0)
        from_x, from_y = hop(expert_in[0], 8), hop(expert_out[0], 16)
        cot_blocks, slots = slots_and_blocks(after(cotangent, chip))
        slots_col, slots_row = slot_forms(slots)
        line = jnp.concatenate([chip] + [hop(chip, 2 * dz) for dz in (1, 2, 3)], axis=0)
        held, from_x, from_y = after((line, from_x, from_y))
        own = [line] + [hop(held, 8 * dxy) for dxy in (3, 1, 2)]
        own = [own[0], own[2], own[3], own[1]]
        step = width // 16
        at_rows = jnp.stack([((me_d ^ a) * 4 + ((me_e // 2) ^ b)) * step for a in range(4) for b in range(4)])
        at_cols = jnp.stack([core * half, (1 - core) * half])
        off_back = jnp.concatenate([at_rows, at_cols]).astype(jnp.int32)
        off = jnp.concatenate([at_rows, at_rows, jnp.repeat(at_cols, 4)]).astype(jnp.int32)
        own, tok, slots_row, off, one, two = after((own, tok, slots_row, off, one, two))
        pieces = own + [hop(piece, 1) for piece in own]
        subs = 4
        later_one, later_two, relay_x, relay_y = after((one, two, from_x, from_y), *own)
        near = hop(later_one, 16), hop(later_two, 8)
        relays = hop(relay_x, 16), hop(relay_y, 8), hop(near[0][width:], 8)
        arrays = [one, from_x, near[0], relays[0]]
        biases = [bias, near[1][width:], near[0][width:], relays[2]]
        b_in = jnp.stack([v[:8] for v in biases]).astype(F32)
        arrays += [two, near[1], from_y, relays[1]]
        places = tuple((q, 0) for q in range(8))
        b_out = jnp.broadcast_to(jnp.sum(b_in[:, 1], axis=0), (8, width))
        after_line = held
    else:
        fill = width_all - 4 * width - experts - 7
        pack = jnp.concatenate(
            [qkv_weight, out_weight, router_weight, jnp.stack(vectors, axis=1), qv_bias.T, jnp.zeros((ln1_gain.shape[0], fill), BF)], axis=1
        )
        pieces = [lax.all_gather(pack, BOTH, axis=0, tiled=True)]
        cot_blocks, slots = slots_and_blocks(cotangent)
        slots_col, slots_row = slot_forms(slots)
        off = jnp.zeros((2,), jnp.int32)
        off_back = off
        subs = 1
        after_line = pieces[0]
        w_in = lax.all_gather(expert_in[0], "dp", axis=0, tiled=False)
        w_out = lax.all_gather(expert_out[0], "dp", axis=0, tiled=False)
        arrays = [w[q] for w in (w_in, w_out) for q in range(dp)]
        places = tuple((q, 0) for q in range(2 * dp))
        b_in = lax.all_gather(jnp.broadcast_to(expert_in_bias, (8, wide)), "dp", axis=0, tiled=False).astype(F32)
        b_out = jnp.broadcast_to(
            lax.all_gather(expert_out_bias, "dp", axis=1, tiled=True).astype(F32), (8, width)
        )

    def exchange(blocks):
        return lax.all_to_all(blocks, "expert", 0, 0, tiled=True)

    cot_sent = exchange(after(cot_blocks, after_line))
    cot = by_image(cotangent)

    w, small, qkv, n1, att, aa, n2, prob = forward(off, subs, pieces, image_count, tok, experts, width_all)
    row_sent = []
    flat = n2.reshape(-1, width)
    for h in range(halves):
        sent = dispatch(slots_row, flat, small, experts, block_rows, h, 1, "ab"[h])
        waits = (near, relays)[h] if grouped else ()
        sent, cot_sent = after((sent, cot_sent), *row_sent, *waits)
        if h:
            sent, cot, slots_col = after((sent, cot, slots_col))
        row_sent.append(exchange(sent))

    back, grads_out, db_ins, db_outs, tall = [], [], [], [], ()
    for h in range(halves):
        *tall, d, db_in, db_out = expert_call(
            row_sent[h], cot_sent, arrays, places, b_in, b_out, h, halves, tall
        )
        grads_out.append(d)
        if h + 1 < halves:
            back.append(exchange(d))
        db_ins.append(db_in)
        db_outs.append(db_out)
    *tall, outs_back = tall
    db_in, db_out = sum(db_ins), sum(db_outs)

    both = [db_in[:, 0:1]]
    if grouped:
        both.append(jnp.broadcast_to(db_out[0:1], db_in[:, 0:1].shape))
    bias_sums = jnp.concatenate(
        [*both, jnp.zeros((dp, 16 - len(both), wide), F32)], axis=1
    )

    def weights_of(q_in, q_out, kind, more=()):
        act, pre, rows_in, slot_grad = tall
        return weight_grads(rows_in, pre, act, slot_grad, bias_sums, wide, q_in, q_out, kind, more)

    if grouped:
        far_in, far_out, _ = weights_of(3, 3, BF)
        tall = after(tall, far_in, far_out, *back)
        back.append(exchange(after(grads_out[-1], far_in, far_out, *back)))
        far_in, far_out = hop(far_in, 8), hop(far_out, 16)
        near_in, near_out, _ = weights_of(1, 2, BF)
        last_in, last_out, _ = weights_of(2, 1, BF)
        last_in = (last_in.astype(F32) + far_in.astype(F32)).astype(BF)
        last_out = (last_out.astype(F32) + far_out.astype(F32)).astype(BF)
        ready = (near_in, near_out, last_in, last_out)
        near_in, near_out = hop(near_in, 8), hop(near_out, 16)
        last_in, last_out = hop(last_in, 16), hop(last_out, 8)
        arrived = (near_in, near_out, last_in, last_out)
    else:
        ready = arrived = ()
        scatter = lambda v: lax.psum_scatter(v, "dp", scatter_dimension=0, tiled=True).astype(F32)
        back.append(exchange(grads_out[-1]))
        every = [weights_of(q, q, BF) for q in range(dp)]
        g_in = scatter(jnp.stack([e[0][:width] for e in every]))
        g_out = scatter(jnp.stack([e[1] for e in every]))
        g_b_in = lax.psum_scatter(
            db_in[:, 0].reshape(1, -1).astype(BF), "dp", scatter_dimension=1, tiled=True
        ).astype(F32)
        g_b_out = lax.psum_scatter(db_out[0:1].astype(BF), "dp", scatter_dimension=1, tiled=True).astype(F32)

    r_sent = exchange(after(outs_back, *back))
    back = after(back, *ready)
    after_grad, probs, grad, grads = backward(
        off_back, image_count, slots_col, cot, n1, qkv, att, aa, n2, prob, w, small, back, experts,
        2 if grouped else 1,
    )
    grads = after(grads, *arrived)
    block_out = block_output(image_count, slots_col, aa, probs, r_sent)
    def add(*values):
        return functools.reduce(lambda a, b: a + b, [v.astype(F32) for v in values])

    if grouped:
        sibling = hop(grads[1], 1)
        quarter = width // 4
        ways = [slice(a * quarter, (a + 1) * quarter) for a in range(4)]
        ways = [add(grads[0][a], sibling[a]).astype(BF) for a in ways]
        tall, bias_sums = after((tall, bias_sums), *ways)
        own_in, own_out, g_bias = weights_of(0, 0, F32, (near_in, last_in, near_out, last_out))
        g_in, g_out = own_in[None], own_out[None]
        g_b_in = g_bias[0:1]
        g_b_out = lax.dynamic_slice(g_bias[1:2], (0, spot), expert_out_bias.shape)
        after_grad, grad = after((after_grad, grad), own_in, own_out)
    tokens_grad = finish(after_grad, grad, tok, w, small, experts)

    if grouped:
        ways[0], tokens_grad, g_in, g_out = after((ways[0], tokens_grad, g_in, g_out))
        ways = [ways[0], *[hop(ways[a], 8 * a) for a in (1, 2, 3)]]
        step = width // 16
        cuts = [add(*[way[b * step : (b + 1) * step] for way in ways]) for b in range(4)]
        cuts = [cuts[0], *[c.astype(BF) for c in cuts[1:]]]
        cuts[0], block_out = after((cuts[0], block_out))
        chip = add(cuts[0], *[hop(cuts[b], 2 * b) for b in (1, 2, 3)])
        n_rows = step // 2
        keep = lax.dynamic_slice_in_dim(chip, core * n_rows, n_rows, 0)
        give = lax.dynamic_slice_in_dim(chip, (1 - core) * n_rows, n_rows, 0)
        got = hop(give.astype(BF), 1).astype(F32)
        dense = jnp.where(
            core == 0, jnp.concatenate([keep, got], axis=1), jnp.concatenate([got, keep], axis=1)
        )
    else:
        dense = lax.psum_scatter(grads[0], BOTH, scatter_dimension=0, tiled=True).astype(F32)
    side = dense[:, 4 * width :]
    vecs = [side[:, experts + k] for k in range(8)]
    return (
        block_out,
        tokens_grad,
        vecs[0],
        vecs[1],
        dense[:, : 3 * width],
        jnp.stack([vecs[5], vecs[7]], axis=0),
        dense[:, 3 * width : 4 * width],
        vecs[2],
        vecs[3],
        vecs[4],
        side[:, :experts],
        g_in,
        g_b_in,
        g_out,
        g_b_out,
    )


def solution(mesh):
    rows, line, cols = P(BOTH, None), P(BOTH), P(None, BOTH)
    experts = (P("expert", None, "dp"), P("expert", "dp"), P("expert", "dp", None), P("expert", "dp"))
    dense = (line, line, rows, cols, rows, line, line, line, rows)
    return jax.shard_map(
        functools.partial(local, (mesh.shape["dp"], mesh.shape["expert"])),
        mesh=mesh,
        in_specs=(rows, line, rows, P(), *dense, *experts, rows),
        out_specs=(rows, rows, *dense, *experts),
        check_vma=False,
    )
```

```python
import functools

import jax
import jax.numpy as jnp
from jax import lax
from jax.experimental import pallas as pl
from jax.experimental.pallas import tpu as pltpu
from jax.sharding import PartitionSpec as P

HEADS = 12
SEQ = 197
EPS_NORM = 1e-06
NEG_FILL = -1e30
BF = jnp.bfloat16
F32 = jnp.float32
LANES = 128
GELU_A = 0.7978845608028654
GELU_B = 0.044715
BOTH = ("dp", "expert")


def up16(n):
    return -(-n // 16) * 16


def dot(left, right):
    return jnp.dot(left, right, preferred_element_type=F32)


def dot_t(left, right):
    return lax.dot_general(left, right, (((1,), (1,)), ((), ())), preferred_element_type=F32)


def t_dot(left, right):
    return lax.dot_general(left, right, (((0,), (0,)), ((), ())), preferred_element_type=F32)


def iota(shape, dim):
    return lax.broadcasted_iota(jnp.int32, shape, dim)


def params(mib=60):
    return pltpu.CompilerParams(vmem_limit_bytes=mib << 20)


def whole(shape):
    zeros = (0,) * len(shape)
    return pl.BlockSpec(shape, lambda *_: zeros, pipeline_mode=pl.Buffered(1))


SMALL = pl.CostEstimate(flops=1 << 20, bytes_accessed=1 << 16, transcendentals=0)
LARGE = pl.CostEstimate(flops=1 << 34, bytes_accessed=1 << 16, transcendentals=0)
SMEM = pl.BlockSpec(memory_space=pltpu.SMEM)
ANY = pl.BlockSpec(memory_space=pl.ANY)


def norm_stats(values):
    centered = values - jnp.mean(values, axis=-1, keepdims=True)
    inverse = lax.rsqrt(jnp.mean(centered * centered, axis=-1, keepdims=True) + EPS_NORM)
    return centered * inverse, inverse


def norm_back(unit, inverse, gain, grad):
    scaled = grad * gain
    mean_one = jnp.mean(scaled, axis=-1, keepdims=True)
    mean_two = jnp.mean(scaled * unit, axis=-1, keepdims=True)
    return inverse * (scaled - mean_one - unit * mean_two)


def col_sum(values):
    return jnp.sum(values, axis=0, keepdims=True)


def pack_kernel(core, qkv, out, router, vectors, pair, mine, other):
    rows = qkv.shape[0]
    eye = (iota((rows, rows), 0) == iota((rows, rows), 1)).astype(BF)
    turned = [dot_t(eye, router[...]), dot_t(eye, vectors[...].astype(BF))[:, :5], dot_t(eye, pair[...])]
    used = sum(t.shape[1] for t in turned)
    turned = jnp.concatenate([*turned, jnp.zeros((rows, 2 * LANES - used), F32)], axis=1)
    value = jnp.concatenate([qkv[...], out[...], turned.astype(BF)], axis=1)
    half = value.shape[1] // 2

    @pl.when(core[0] == 0)
    def _():
        mine[...] = value[:, :half]
        other[...] = value[:, half:]

    @pl.when(core[0] != 0)
    def _():
        mine[...] = value[:, half:]
        other[...] = value[:, :half]


def pack_dense(core, qkv, out, router, vectors, pair):
    rows = qkv.shape[0]
    half = (qkv.shape[1] + out.shape[1] + 2 * LANES) // 2
    vmem = pl.BlockSpec(memory_space=pltpu.VMEM)
    return pl.pallas_call(
        pack_kernel,
        in_specs=[SMEM] + [vmem] * 5,
        out_specs=[vmem] * 2,
        out_shape=[jax.ShapeDtypeStruct((rows, half), BF)] * 2,
        compiler_params=params(60),
        cost_estimate=LARGE,
        name="pack_dense",
    )(core, qkv, out, router, vectors, pair)


def forward_kernel(experts, subs, off, count, tok, *refs):
    n_pieces = len(refs) - 10
    pieces = refs[:n_pieces]
    w_o, small, qkv_o, n1_o, att_o, aa_o, n2_o, prob_o, w, sems = refs[n_pieces:]
    img = pl.program_id(0)
    width = tok.shape[-1]

    @pl.when(img == 0)
    def _():
        copies = []
        for i, piece in enumerate(pieces):
            rows, cols = piece.shape[0] // subs, piece.shape[1]
            col = pl.multiple_of(off[n_pieces * subs + i], LANES)
            for j in range(subs):
                row = pl.multiple_of(off[i * subs + j], 16)
                copies.append(
                    pltpu.make_async_copy(
                        piece.at[pl.ds(j * rows, rows), :],
                        w.at[pl.ds(row, rows), pl.ds(col, cols)],
                        sems.at[i * subs + j],
                    )
                )
        for c in copies:
            c.start()
        for c in copies:
            c.wait()
        small[...] = jnp.transpose(w[:, 4 * width : 4 * width + LANES].astype(F32))
        pltpu.make_async_copy(w, w_o, sems.at[0]).start()

    def vec(k):
        return small[experts + k : experts + k + 1, :]

    x = tok[0].astype(F32)
    rows = x.shape[0]
    unit, _ = norm_stats(x)
    n1 = (unit * vec(0) + vec(1)).astype(BF)
    n1_o[0] = n1
    biases = (vec(5), None, vec(6))
    for part in range(3):
        cols = slice(part * width, (part + 1) * width)
        block = dot(n1, w[:, cols])
        if biases[part] is not None:
            block = block + biases[part]
        qkv_o[0, :, cols] = block.astype(BF)
    low = iota((rows, LANES), 1) < LANES // 2
    seen = iota((rows, rows), 0) < SEQ
    scale = (width // HEADS) ** -0.5
    for pair in range(HEADS // 2):
        c = pair * LANES
        q2 = qkv_o[0, :, c : c + LANES]
        k2 = qkv_o[0, :, width + c : width + c + LANES]
        v2 = qkv_o[0, :, 2 * width + c : 2 * width + c + LANES]
        got = []
        for side, mask in enumerate((low, ~low)):
            scores = dot_t(k2, jnp.where(mask, q2, jnp.zeros_like(q2))) * scale
            scores = jnp.where(seen, scores, NEG_FILL)
            exps = jnp.exp(scores - jnp.max(scores, axis=0, keepdims=True))
            prob = exps * (1.0 / col_sum(exps))
            prob = prob.astype(BF)
            prob_o[0, 2 * pair + side] = prob
            got.append(t_dot(prob, v2))
        att_o[0, :, c : c + LANES] = jnp.where(low, got[0], got[1]).astype(BF)
    alive = (img < count[0]).astype(F32)
    after = x + alive * (dot(att_o[0], w[:, 3 * width : 4 * width]) + vec(2))
    aa_o[0] = after
    unit, _ = norm_stats(after)
    n2_o[0] = (unit * vec(3) + vec(4)).astype(BF)

    @pl.when(img == pl.num_programs(0) - 1)
    def _():
        pltpu.make_async_copy(w, w_o, sems.at[0]).wait()


def forward(off, subs, pieces, count, tok, experts, width_all):
    images, rows, width = tok.shape
    block = lambda cols: pl.BlockSpec((1, rows, cols), lambda i: (i, 0, 0))
    shape = lambda cols, t: jax.ShapeDtypeStruct((images, rows, cols), t)
    return pl.pallas_call(
        functools.partial(forward_kernel, experts, subs),
        grid=(images,),
        in_specs=[SMEM, SMEM, block(width)] + [ANY] * len(pieces),
        out_specs=[
            ANY,
            whole((LANES, width)),
            block(3 * width),
            block(width),
            block(width),
            block(width),
            block(width),
            pl.BlockSpec((1, HEADS, rows, rows), lambda i: (i, 0, 0, 0)),
        ],
        out_shape=[
            jax.ShapeDtypeStruct((width, width_all), BF),
            jax.ShapeDtypeStruct((LANES, width), F32),
            shape(3 * width, BF),
            shape(width, BF),
            shape(width, BF),
            shape(width, F32),
            shape(width, BF),
            jax.ShapeDtypeStruct((images, HEADS, rows, rows), BF),
        ],
        scratch_shapes=[
            pltpu.VMEM((width, width_all), BF),
            pltpu.SemaphoreType.DMA((len(pieces) * subs,)),
        ],
        compiler_params=params(60),
        cost_estimate=SMALL,
        name="tokens_forward",
    )(off, count, tok, *pieces)


def dispatch_kernel(experts, half, gated, slots, x, *refs):
    out = refs[-1]
    value = x[...]
    halves, block_rows = out.shape[1:3]
    first, second = slots[0:1, :], slots[1:2, :]
    if gated:
        router = refs[0][...].astype(BF)
        logits = dot_t(router, value)
        logits = jnp.where(iota(logits.shape, 0) < experts, logits, NEG_FILL)
        exps = jnp.exp(logits - jnp.max(logits, axis=0, keepdims=True))
        probs = exps / jnp.sum(exps, axis=0, keepdims=True)
    total = experts * block_rows
    for h in range(halves):
        place = iota((total, value.shape[0]), 0) + (half + h) * total
        hot = ((place == first) | (place == second)).astype(BF)
        out[:, h] = dot(hot, value).astype(BF).reshape(experts, block_rows, value.shape[1])
        if gated:
            row = iota((16, value.shape[0]), 0)
            for e in range(experts):
                gate = probs[e : e + 1, :]
                high = gate.astype(BF).astype(F32)
                pair = jnp.where(row == 14, high, jnp.where(row == 15, gate - high, 0.0))
                placed = dot_t(pair.astype(BF), hot[e * block_rows : (e + 1) * block_rows])
                tail = out[e, h, block_rows - 16 :, :block_rows].astype(F32)
                out[e, h, block_rows - 16 :, :block_rows] = jnp.where(
                    iota(tail.shape, 0) < 14, tail, placed
                ).astype(BF)


def dispatch(slots, x, small, experts, block_rows, half, halves, tag):
    rows, width = x.shape
    gated = small is not None
    more = [small] if gated else []
    vmem = pl.BlockSpec(memory_space=pltpu.VMEM)
    return pl.pallas_call(
        functools.partial(dispatch_kernel, experts, half, gated),
        in_specs=[vmem] * (2 + len(more)),
        out_specs=vmem,
        out_shape=jax.ShapeDtypeStruct((experts, halves, block_rows, width), BF),
        compiler_params=params(24),
        cost_estimate=SMALL,
        name="dispatch_" + tag,
    )(slots, x, *more)


def first_kernel(experts, half_cap, count, capacity, routes, x, out, slots):
    rows = routes.shape[1]
    halves, block_rows = out.shape[1:3]
    alive = iota((1, rows), 1) < count[0] * SEQ
    name = iota((up16(experts), rows), 0)
    earlier = (iota((rows, rows), 0) < iota((rows, rows), 1)).astype(BF)
    limits = jnp.zeros((up16(experts), 1), F32)
    for e in range(experts):
        limits = jnp.where(name[:, 0:1] == e, capacity[e].astype(F32), limits)
    base = 0.0
    for k in range(2):
        hit = jnp.where((routes[k : k + 1, :] == name) & alive, 1.0, 0.0)
        place = col_sum(hit * (dot(hit.astype(BF), earlier) + base))
        keep = place < col_sum(hit * limits)
        base = jnp.sum(hit, axis=1, keepdims=True)
        place = place.astype(jnp.int32)
        half = (place >= half_cap).astype(jnp.int32)
        spot = (half * experts + routes[k : k + 1, :]) * block_rows + place - half * half_cap
        slots[k : k + 1, :] = jnp.where(keep, spot, -1)
    dispatch_kernel(experts, 0, False, slots, x, out)


def first_dispatch(count, capacity, routes, x, half_cap, block_rows, halves):
    rows, width = x.shape
    experts = capacity.shape[0]
    vmem = pl.BlockSpec(memory_space=pltpu.VMEM)
    return pl.pallas_call(
        functools.partial(first_kernel, experts, half_cap),
        in_specs=[SMEM, SMEM, vmem, vmem],
        out_specs=[vmem, vmem],
        out_shape=[
            jax.ShapeDtypeStruct((experts, halves, block_rows, width), BF),
            jax.ShapeDtypeStruct((2, rows), jnp.int32),
        ],
        compiler_params=params(24),
        cost_estimate=SMALL,
        name="dispatch_first",
    )(count, capacity, routes, x)


def expert_kernel(places, n_arrays, n_before, *refs):
    x_ref, c_ref, b_in, b_out = refs[:4]
    arrays, parts = refs[4 : 4 + n_arrays], len(places) // 2
    rest = refs[4 + n_arrays + n_before :]
    act_o, pre_o, x_o, sg_o, r_o, d_o, db_in, db_out, win, wout, sems = rest
    step = pl.program_id(0)
    n, _, size, width = x_ref.shape
    piece = win.shape[1] // parts

    def copies(q):
        cols = pl.ds(q * piece, piece)
        (one, at_one), (two, at_two) = places[q], places[parts + q]
        return (
            pltpu.make_async_copy(
                arrays[one].at[pl.ds(at_one, width), :], win.at[:, cols], sems.at[q]
            ),
            pltpu.make_async_copy(
                arrays[two].at[pl.ds(at_two, piece), :], wout.at[cols, :], sems.at[parts + q]
            ),
        )

    @pl.when(step == 0)
    def _():
        for q in range(parts):
            for c in copies(q):
                c.start()
        db_in[...] = jnp.zeros_like(db_in)
        db_out[...] = jnp.zeros_like(db_out)

    eye = (iota((size, size), 0) == iota((size, size), 1)).astype(BF)
    for s in range(n):
        rows = slice(s * size, (s + 1) * size)
        x_o[rows, :] = x_ref[s, 0]
        turned = dot_t(eye, x_ref[s, 0, size - 16 :, :size])
        gate = jnp.sum(jnp.where(iota(turned.shape, 1) >= 14, turned, 0.0), axis=1, keepdims=True)
        sg_o[rows, :] = (gate * c_ref[s, 0].astype(F32)).astype(BF)
    x = x_o[...]
    slot_grad = sg_o[...]
    db_out[0:1, :] += col_sum(slot_grad.astype(F32))

    @pl.when(step == 0)
    def _():
        for q in range(parts):
            for c in copies(q):
                c.wait()

    for q in range(parts):
        cols = slice(q * piece, (q + 1) * piece)
        pre = dot(x, win[:, cols]) + b_in[q, 0:1, :]
        square = pre * pre
        turn = jnp.tanh(pre * (GELU_A + GELU_A * GELU_B * square))
        half_turn = 0.5 * turn + 0.5
        act_o[:, cols] = (pre * half_turn).astype(BF)
        slope = half_turn + (0.5 * pre) * (1.0 - turn * turn) * (GELU_A + 3 * GELU_A * GELU_B * square)
        pre_grad = dot_t(slot_grad, wout[cols, :]) * slope
        pre_o[:, cols] = pre_grad.astype(BF)
        db_in[q, 0:1, :] += col_sum(pre_grad)
    out = (dot(act_o[...], wout[...]) + b_out[0:1, :]).astype(BF)
    back = dot_t(pre_o[...], win[...])
    ones = jnp.ones((16, width), BF)
    for s in range(n):
        rows = slice(s * size, (s + 1) * size)
        r_o[s, 0] = out[rows]
        d_o[s] = back[rows].astype(BF)
        prod = c_ref[s, 0].astype(F32) * out[rows].astype(F32)
        high = prod.astype(BF)
        low = (prod - high.astype(F32)).astype(BF)
        gate_grad = dot_t(ones, high) + dot_t(ones, low)
        grad_high = gate_grad.astype(BF).astype(F32)
        row = iota(gate_grad.shape, 0)
        tail = back[(s + 1) * size - 16 : (s + 1) * size, :size]
        both = jnp.where(row == 14, grad_high, gate_grad - grad_high)
        d_o[s, size - 16 :, :size] = jnp.where(row < 14, tail, both).astype(BF)


def expert_call(x, c, arrays, places, b_in, b_out, half, halves, before):
    experts, _, size, width = x.shape
    parts, _, piece = b_in.shape
    n = max(1, 256 // size)
    steps = experts // n
    rows, hidden = n * size, parts * piece
    before = list(before)
    tall = lambda cols: pl.BlockSpec((rows, cols), lambda i: (half * steps + i, 0))
    of_half = pl.BlockSpec((n, 1, size, width), lambda i: (i, half, 0, 0))
    total = halves * experts * size
    return pl.pallas_call(
        functools.partial(expert_kernel, places, len(arrays), len(before)),
        grid=(steps,),
        in_specs=[
            pl.BlockSpec((n, 1, size, width), lambda i: (i, 0, 0, 0)),
            of_half,
            whole((parts, 8, piece)),
            whole((8, width)),
        ]
        + [ANY] * (len(arrays) + len(before)),
        out_specs=[
            tall(hidden),
            tall(hidden),
            tall(width),
            tall(width),
            of_half,
            pl.BlockSpec((n, size, width), lambda i: (i, 0, 0)),
            whole((parts, 8, piece)),
            whole((8, width)),
        ],
        out_shape=[
            jax.ShapeDtypeStruct((total, hidden), BF),
            jax.ShapeDtypeStruct((total, hidden), BF),
            jax.ShapeDtypeStruct((total, width), BF),
            jax.ShapeDtypeStruct((total, width), BF),
            jax.ShapeDtypeStruct((experts, halves, size, width), BF),
            jax.ShapeDtypeStruct((experts, size, width), BF),
            jax.ShapeDtypeStruct((parts, 8, piece), F32),
            jax.ShapeDtypeStruct((8, width), F32),
        ],
        scratch_shapes=[
            pltpu.VMEM((width, hidden), BF),
            pltpu.VMEM((hidden, width), BF),
            pltpu.SemaphoreType.DMA((2 * parts,)),
        ],
        input_output_aliases={4 + len(arrays) + i: i for i in range(len(before))},
        compiler_params=params(44),
        cost_estimate=SMALL,
        name="expert_" + "ab"[half],
    )(x, c, b_in, b_out, *arrays, *before)


def weight_kernel(piece, q_in, q_out, n_more, x, pre, act, grad, bias, *refs):
    more, (in_o, out_o, bias_o, xs, ps, acts, gs, held, sems) = refs[:n_more], refs[n_more:]
    width = x.shape[1]
    copies = [
        pltpu.make_async_copy(x, xs, sems.at[0]),
        pltpu.make_async_copy(pre.at[:, pl.ds(q_in * piece, piece)], ps, sems.at[1]),
        pltpu.make_async_copy(act.at[:, pl.ds(q_out * piece, piece)], acts, sems.at[2]),
        pltpu.make_async_copy(grad, gs, sems.at[3]),
    ]
    extra = [
        pltpu.make_async_copy(far, held.at[k, pl.ds(0, far.shape[0]), :], sems.at[4 + k])
        for k, far in enumerate(more)
    ]
    copies[0].start()
    copies[1].start()
    copies[0].wait()
    copies[1].wait()
    for c in [copies[2], copies[3], *extra]:
        c.start()
    first = t_dot(xs[...], ps[...])
    sums = bias[q_in]
    for k in range(n_more // 2):
        extra[k].wait()
        first = first + held[k, :width, :].astype(F32)
        sums = sums + held[k, width:, :].astype(F32)
    in_o[:width, :] = first.astype(in_o.dtype)
    bias_o[...] = sums.astype(bias_o.dtype)
    if not n_more:
        in_o[width:, :] = sums.astype(in_o.dtype)
    copies[2].wait()
    copies[3].wait()
    second = t_dot(acts[...], gs[...])
    for k in range(n_more // 2, n_more):
        extra[k].wait()
        second = second + held[k, :piece, :].astype(F32)
    out_o[...] = second.astype(out_o.dtype)


def weight_grads(x, pre, act, grad, bias, piece, q_in, q_out, kind, more=()):
    total, width = x.shape
    vmem = pl.BlockSpec(memory_space=pltpu.VMEM)
    return pl.pallas_call(
        functools.partial(weight_kernel, piece, q_in, q_out, len(more)),
        in_specs=[ANY] * 4 + [vmem] + [ANY] * len(more),
        out_specs=[vmem] * 3,
        out_shape=[
            jax.ShapeDtypeStruct((width if more else width + 16, piece), kind),
            jax.ShapeDtypeStruct((piece, width), kind),
            jax.ShapeDtypeStruct((16, piece), kind),
        ],
        scratch_shapes=[
            pltpu.VMEM((total, width), BF),
            pltpu.VMEM((total, piece), BF),
            pltpu.VMEM((total, piece), BF),
            pltpu.VMEM((total, width), BF),
            pltpu.VMEM((max(1, len(more)), width + 16, width), BF),
            pltpu.SemaphoreType.DMA((4 + len(more),)),
        ],
        compiler_params=params(60),
        cost_estimate=SMALL,
        name="weight_grads",
    )(x, pre, act, grad, bias, *more)


def backward_kernel(experts, n, split, off, count, slots, cot, n1_far, qkv, att_far, aa, n2, probs_in, w_far, w_out, small, *refs):
    backs = refs[:n]
    ag_o, gp_o, dq_o = refs[n : n + 3]
    grads = refs[n + 3 : n + 3 + split]
    dw, ds, marks, ag_all, dq_all, n1, att, w, sems = refs[n + 3 + split :]
    img = pl.program_id(0)
    width = n1.shape[-1]
    late = [
        pltpu.make_async_copy(far, here, sems.at[k])
        for k, (far, here) in enumerate(((n1_far, n1), (att_far, att), (w_far, w)))
    ]
    size = backs[0].shape[1]
    total = experts * size

    @pl.when(img == 0)
    def _():
        for c in late:
            c.start()
        ds[...] = jnp.zeros_like(ds)
        line = iota((LANES, size), 0)
        for h in range(n):
            for e in range(experts):
                ends = backs[h][e, size - 16 :, :size].astype(F32)
                for k in range(2):
                    marks[2 * h + k, :, e * size : (e + 1) * size] = jnp.where(
                        line == e, ends[14 + k : 15 + k, :], 0.0
                    ).astype(BF)

    def vec(k):
        return small[experts + k : experts + k + 1, :]

    def add_vec(k, value):
        ds[experts + k : experts + k + 1, :] += value

    alive = (img < count[0]).astype(F32)
    up = cot[0].astype(F32)
    rows = up.shape[0]
    normed = n2[0]
    lane = iota((rows, LANES), 1)
    router = jnp.where(iota(small.shape, 0) < experts, small[...], 0.0).astype(BF)
    logits = jnp.where(lane < experts, dot_t(normed, router), NEG_FILL)
    exps = jnp.exp(logits - jnp.max(logits, axis=-1, keepdims=True))
    probs = exps / jnp.sum(exps, axis=-1, keepdims=True)
    gp_o[0] = probs
    first, second = slots[0, :, 0:1], slots[0, :, 1:2]
    normed_grad = jnp.zeros((rows, width), F32)
    placed = jnp.zeros((rows, LANES), F32)
    for h in range(n):
        place = iota((rows, total), 1) + h * total
        hot = ((place == first) | (place == second)).astype(BF)
        normed_grad = normed_grad + dot(hot, backs[h][...].reshape(total, width))
        placed = placed + dot_t(hot, marks[2 * h]) + dot_t(hot, marks[2 * h + 1])
    logit_grad = (
        probs * (placed - jnp.sum(probs * placed, axis=-1, keepdims=True))
    ).astype(BF)
    normed_grad = normed_grad + dot(logit_grad, router)
    ds[...] += jnp.where(iota(ds.shape, 0) < experts, t_dot(logit_grad, normed), 0.0)
    unit, inverse = norm_stats(aa[0])
    add_vec(3, col_sum(normed_grad * unit))
    add_vec(4, col_sum(normed_grad))
    after_grad = up + norm_back(unit, inverse, vec(3), normed_grad)
    attn_grad = (alive * after_grad).astype(BF)
    add_vec(2, col_sum(attn_grad.astype(F32)))
    ag_all[img] = attn_grad
    att_grad = dot_t(attn_grad, w_out[...]).astype(BF)
    low = lane < LANES // 2
    scale = (width // HEADS) ** -0.5
    for pair in range(HEADS // 2):
        c = pair * LANES
        q2 = qkv[0, :, c : c + LANES]
        k2 = qkv[0, :, width + c : width + c + LANES]
        v2 = qkv[0, :, 2 * width + c : 2 * width + c + LANES]
        o2 = att_grad[:, c : c + LANES]
        got = []
        for side, mask in enumerate((low, ~low)):
            rounded = probs_in[0, 2 * pair + side]
            prob = rounded.astype(F32)
            prob_grad = dot_t(v2, jnp.where(mask, o2, jnp.zeros_like(o2)))
            score_grad = (prob * (prob_grad - col_sum(prob * prob_grad))).astype(BF)
            got.append(
                (
                    t_dot(score_grad, k2) * scale,
                    dot(score_grad, q2) * scale,
                    dot(rounded, o2),
                )
            )
        for k in range(3):
            dq_o[0, :, k * width + c : k * width + c + LANES] = jnp.where(
                low, got[0][k], got[1][k]
            ).astype(BF)
    grad = dq_o[0]
    dq_all[img] = grad
    for k in range(3):
        ds[experts + 5 + k : experts + 6 + k, :] += col_sum(grad[:, k * width : (k + 1) * width].astype(F32))
    ag_o[0] = after_grad

    @pl.when(img == pl.num_programs(0) - 1)
    def _():
        dw[:, 4 * width : 4 * width + LANES] = jnp.transpose(ds[...])
        for c in late:
            c.wait()
        left = n1[...].reshape(-1, width)
        for k in range(3):
            cols = slice(k * width, (k + 1) * width)
            dw[:, cols] = t_dot(left, dq_all[:, :, cols].reshape(-1, width))
        dw[:, 3 * width : 4 * width] = t_dot(
            att[...].reshape(-1, width), ag_all[...].reshape(-1, width)
        )
        with_weight = jnp.zeros((width, LANES), F32)
        with_sums = jnp.zeros((width, LANES), F32)
        for k in range(3 * width // LANES):
            cols = slice(k * LANES, (k + 1) * LANES)
            part, at = divmod(k * LANES, width)
            value = w[:, cols].astype(F32)
            sums = ds[experts + 5 + part : experts + 6 + part, at : at + LANES]
            with_weight = with_weight + value * dw[:, cols]
            with_sums = with_sums + value * sums
        sums = jnp.sum(with_sums, axis=1, keepdims=True)
        at = 4 * width
        sides = w[:, at : at + LANES].astype(F32)
        gain, shift = sides[:, experts : experts + 1], sides[:, experts + 1 : experts + 2]
        gains = (jnp.sum(with_weight, axis=1, keepdims=True) - shift * sums) / gain
        spot = iota((width, LANES), 1)
        cols = slice(at, at + LANES)
        dw[:, cols] = jnp.where(
            spot == experts, gains, jnp.where(spot == experts + 1, sums, dw[:, cols])
        )
        if split == 1:
            grads[0][...] = dw[...].astype(BF)
        else:
            cols = grads[0].shape[1]
            step = width // 16
            for h in range(2):
                col = pl.multiple_of(off[16 + h], LANES)
                for r in range(16):
                    row = pl.multiple_of(off[r], 16)
                    grads[h][r * step : (r + 1) * step, :] = dw[
                        pl.ds(row, step), pl.ds(col, cols)
                    ].astype(BF)


def backward(off, count, slots, cot, n1, qkv, att, aa, n2, prob, w, small, backs, experts, split):
    images, rows, width = cot.shape
    width_all = w.shape[1]
    n = len(backs)
    block = lambda cols: pl.BlockSpec((1, rows, cols), lambda i: (i, 0, 0))
    got = pl.pallas_call(
        functools.partial(backward_kernel, experts, n, split),
        grid=(images,),
        in_specs=[SMEM, SMEM, block(2), block(width), ANY, block(3 * width), ANY, block(width), block(width)]
        + [pl.BlockSpec((1, HEADS, rows, rows), lambda i: (i, 0, 0, 0))]
        + [ANY, pl.BlockSpec((width, width), lambda i: (0, 3), pipeline_mode=pl.Buffered(1)), whole(small.shape)]
        + [whole(backs[0].shape)] * n,
        out_specs=[block(width), block(LANES), block(3 * width)] + [whole((width, width_all // split))] * split,
        out_shape=[
            jax.ShapeDtypeStruct((images, rows, width), F32),
            jax.ShapeDtypeStruct((images, rows, LANES), F32),
            jax.ShapeDtypeStruct((images, rows, 3 * width), BF),
        ]
        + [jax.ShapeDtypeStruct((width, width_all // split), BF)] * split,
        scratch_shapes=[
            pltpu.VMEM((width, width_all), F32),
            pltpu.VMEM((LANES, width), F32),
            pltpu.VMEM((2 * n, LANES, backs[0].shape[0] * backs[0].shape[1]), BF),
            pltpu.VMEM((images, rows, width), BF),
            pltpu.VMEM((images, rows, 3 * width), BF),
            pltpu.VMEM((images, rows, width), BF),
            pltpu.VMEM((images, rows, width), BF),
            pltpu.VMEM(w.shape, BF),
            pltpu.SemaphoreType.DMA((3,)),
        ],
        compiler_params=params(),
        cost_estimate=SMALL,
        name="tokens_backward",
    )(off, count, slots, cot, n1, qkv, att, aa, n2, prob, w, w, small, *backs)
    return got[0], got[1], got[2], got[3:]


def place_rows(out, value):
    for k in range(out.shape[0] // SEQ):

        @pl.when(pl.program_id(0) == k)
        def _():
            out[k * SEQ : (k + 1) * SEQ, :] = value[:SEQ]


def finish_kernel(experts, after_grad, grad, tok, w, small, out):
    width = tok.shape[-1]
    normed_grad = dot_t(grad[0], w[...])
    unit, inverse = norm_stats(tok[0].astype(F32))
    value = after_grad[0] + norm_back(unit, inverse, small[experts : experts + 1, :], normed_grad)
    place_rows(out, value)


def finish(after_grad, grad, tok, w, small, experts):
    images, rows, width = tok.shape
    block = lambda cols: pl.BlockSpec((1, rows, cols), lambda i: (i, 0, 0))
    return pl.pallas_call(
        functools.partial(finish_kernel, experts),
        grid=(images,),
        in_specs=[block(width), block(3 * width), block(width), whole((width, 3 * width)), whole(small.shape)],
        out_specs=whole((images * SEQ, width)),
        out_shape=jax.ShapeDtypeStruct((images * SEQ, width), F32),
        compiler_params=params(60),
        cost_estimate=SMALL,
        name="tokens_finish",
    )(after_grad, grad, tok, w, small)


def output_kernel(count, slots, aa, probs, outs, out, total_f):
    rows = aa.shape[1]
    experts, n, size, width = outs.shape
    total = experts * size
    alive = (pl.program_id(0) < count[0]).astype(F32)
    first, second = slots[0, :, 0:1], slots[0, :, 1:2]
    gates = jnp.concatenate(
        [jnp.broadcast_to(probs[0, :, e : e + 1], (rows, size)) for e in range(experts)], axis=1
    )
    moe = jnp.zeros(aa.shape[1:], F32)
    for h in range(n):
        place = iota((rows, total), 1) + h * total
        gate = jnp.where((place == first) | (place == second), gates, 0.0)
        high = gate.astype(BF)
        low = (gate - high.astype(F32)).astype(BF)
        value = outs[:, h].reshape(total, width)
        moe = moe + dot(high, value) + dot(low, value)
    place_rows(total_f, aa[0] + alive * moe)

    @pl.when(pl.program_id(0) == pl.num_programs(0) - 1)
    def _():
        out[...] = total_f[...].astype(BF)


def block_output(count, slots, aa, probs, outs):
    images, rows, width = aa.shape
    block = lambda cols: pl.BlockSpec((1, rows, cols), lambda i: (i, 0, 0))
    return pl.pallas_call(
        output_kernel,
        grid=(images,),
        in_specs=[SMEM, block(2), block(width), block(LANES), whole(outs.shape)],
        out_specs=whole((images * SEQ, width)),
        out_shape=jax.ShapeDtypeStruct((images * SEQ, width), BF),
        scratch_shapes=[pltpu.VMEM((images * SEQ, width), F32)],
        compiler_params=params(60),
        cost_estimate=SMALL,
        name="block_output",
    )(count, slots, aa, probs, outs)


def local(sizes, *args):
    (tokens, image_count, routes, capacity, ln1_gain, ln1_bias, qkv_weight, qv_bias, out_weight, out_bias,
     ln2_gain, ln2_bias, router_weight, expert_in, expert_in_bias, expert_out, expert_out_bias, cotangent) = args
    dp, experts = sizes
    grouped = sizes == (4, 8)
    devices = dp * experts
    me_d = lax.axis_index("dp")
    me_e = lax.axis_index("expert")
    core = me_e % 2
    token_count, width = tokens.shape
    images = token_count // SEQ
    rows = up16(SEQ)
    cap = max(2, 5 * token_count // (2 * experts))
    halves = 2 if grouped else 1
    half_cap = -(-cap // halves)
    block_rows = up16(half_cap + 2)

    def hop(value, mask):
        return lax.ppermute(value, BOTH, [(i, i ^ mask) for i in range(devices)])

    def by_image(value):
        value = value.reshape(images, SEQ, value.shape[-1])
        fill = -1 if value.dtype == jnp.int32 else 0
        return jnp.pad(value, ((0, 0), (0, rows - SEQ), (0, 0)), constant_values=fill)

    def side_rows(values):
        return functools.reduce(
            lambda a, b: a + b,
            [jnp.pad(v.astype(F32)[None], ((k, 7 - k), (0, 0))) for k, v in enumerate(values)],
        )

    def slots_and_blocks(value):
        return first_dispatch(image_count, capacity, routes.T, value, half_cap, block_rows, halves)

    def slot_forms(slots):
        slots = slots.reshape(2, images, SEQ)
        slots = jnp.pad(slots, ((0, 0), (0, 0), (0, rows - SEQ)), constant_values=-1)
        return slots.transpose(1, 2, 0), slots.reshape(2, -1)

    def after(values, *done):
        return lax.optimization_barrier((values, done))[0]

    tok = by_image(tokens)

    vectors = [ln1_gain, ln1_bias, out_bias, ln2_gain, ln2_bias]
    width_all = 4 * width + 2 * LANES
    wide = expert_in.shape[2]
    spot = me_d * expert_out_bias.shape[1]
    if grouped:
        half = width_all // 2
        mine, other = pack_dense(
            core.reshape(1).astype(jnp.int32), qkv_weight, out_weight, router_weight.T, side_rows(vectors), qv_bias
        )
        got = hop(other, 1)
        chip = jnp.where(
            core == 0, jnp.concatenate([mine, got], axis=0), jnp.concatenate([got, mine], axis=0)
        )
        bias_out = lax.dynamic_update_slice(jnp.zeros((1, width), BF), expert_out_bias, (0, spot))
        bias = jnp.concatenate([expert_in_bias, bias_out, jnp.zeros((14, wide), BF)], axis=0)
        one = jnp.concatenate([expert_in[0], bias], axis=0)
        two = jnp.concatenate([expert_out[0], bias], axis=0)
        from_x, from_y = hop(expert_in[0], 8), hop(expert_out[0], 16)
        cot_blocks, slots = slots_and_blocks(after(cotangent, chip))
        slots_col, slots_row = slot_forms(slots)
        line = jnp.concatenate([chip] + [hop(chip, 2 * dz) for dz in (1, 2, 3)], axis=0)
        held, from_x, from_y = after((line, from_x, from_y))
        own = [line] + [hop(held, 8 * dxy) for dxy in (3, 1, 2)]
        own = [own[0], own[2], own[3], own[1]]
        step = width // 16
        at_rows = jnp.stack([((me_d ^ a) * 4 + ((me_e // 2) ^ b)) * step for a in range(4) for b in range(4)])
        at_cols = jnp.stack([core * half, (1 - core) * half])
        off_back = jnp.concatenate([at_rows, at_cols]).astype(jnp.int32)
        off = jnp.concatenate([at_rows, at_rows, jnp.repeat(at_cols, 4)]).astype(jnp.int32)
        own, tok, slots_row, off, one, two = after((own, tok, slots_row, off, one, two))
        pieces = own + [hop(piece, 1) for piece in own]
        subs = 4
        later_one, later_two, relay_x, relay_y = after((one, two, from_x, from_y), *own)
        near = hop(later_one, 16), hop(later_two, 8)
        relays = hop(relay_x, 16), hop(relay_y, 8), hop(near[0][width:], 8)
        arrays = [one, from_x, near[0], relays[0]]
        biases = [bias, near[1][width:], near[0][width:], relays[2]]
        b_in = jnp.stack([v[:8] for v in biases]).astype(F32)
        arrays += [two, near[1], from_y, relays[1]]
        places = tuple((q, 0) for q in range(8))
        b_out = jnp.broadcast_to(jnp.sum(b_in[:, 1], axis=0), (8, width))
        after_line = held
    else:
        fill = width_all - 4 * width - experts - 7
        pack = jnp.concatenate(
            [qkv_weight, out_weight, router_weight, jnp.stack(vectors, axis=1), qv_bias.T, jnp.zeros((ln1_gain.shape[0], fill), BF)], axis=1
        )
        pieces = [lax.all_gather(pack, BOTH, axis=0, tiled=True)]
        cot_blocks, slots = slots_and_blocks(cotangent)
        slots_col, slots_row = slot_forms(slots)
        off = jnp.zeros((2,), jnp.int32)
        off_back = off
        subs = 1
        after_line = pieces[0]
        w_in = lax.all_gather(expert_in[0], "dp", axis=0, tiled=False)
        w_out = lax.all_gather(expert_out[0], "dp", axis=0, tiled=False)
        arrays = [w[q] for w in (w_in, w_out) for q in range(dp)]
        places = tuple((q, 0) for q in range(2 * dp))
        b_in = lax.all_gather(jnp.broadcast_to(expert_in_bias, (8, wide)), "dp", axis=0, tiled=False).astype(F32)
        b_out = jnp.broadcast_to(
            lax.all_gather(expert_out_bias, "dp", axis=1, tiled=True).astype(F32), (8, width)
        )

    def exchange(blocks):
        return lax.all_to_all(blocks, "expert", 0, 0, tiled=True)

    cot_sent = exchange(after(cot_blocks, after_line))
    cot = by_image(cotangent)

    w, small, qkv, n1, att, aa, n2, prob = forward(off, subs, pieces, image_count, tok, experts, width_all)
    row_sent = []
    flat = n2.reshape(-1, width)
    for h in range(halves):
        sent = dispatch(slots_row, flat, small, experts, block_rows, h, 1, "ab"[h])
        waits = (near, relays)[h] if grouped else ()
        sent, cot_sent = after((sent, cot_sent), *row_sent, *waits)
        if h:
            sent, cot, slots_col = after((sent, cot, slots_col))
        row_sent.append(exchange(sent))

    back, grads_out, db_ins, db_outs, tall = [], [], [], [], ()
    for h in range(halves):
        *tall, d, db_in, db_out = expert_call(
            row_sent[h], cot_sent, arrays, places, b_in, b_out, h, halves, tall
        )
        grads_out.append(d)
        if h + 1 < halves:
            back.append(exchange(d))
        db_ins.append(db_in)
        db_outs.append(db_out)
    *tall, outs_back = tall
    db_in, db_out = sum(db_ins), sum(db_outs)

    both = [db_in[:, 0:1]]
    if grouped:
        both.append(jnp.broadcast_to(db_out[0:1], db_in[:, 0:1].shape))
    bias_sums = jnp.concatenate(
        [*both, jnp.zeros((dp, 16 - len(both), wide), F32)], axis=1
    )

    def weights_of(q_in, q_out, kind, more=()):
        act, pre, rows_in, slot_grad = tall
        return weight_grads(rows_in, pre, act, slot_grad, bias_sums, wide, q_in, q_out, kind, more)

    if grouped:
        far_in, far_out, _ = weights_of(3, 3, BF)
        tall = after(tall, far_in, far_out, *back)
        back.append(exchange(after(grads_out[-1], far_in, far_out, *back)))
        far_in, far_out = hop(far_in, 8), hop(far_out, 16)
        near_in, near_out, _ = weights_of(1, 2, BF)
        last_in, last_out, _ = weights_of(2, 1, BF)
        last_in = (last_in.astype(F32) + far_in.astype(F32)).astype(BF)
        last_out = (last_out.astype(F32) + far_out.astype(F32)).astype(BF)
        ready = (near_in, near_out, last_in, last_out)
        near_in, near_out = hop(near_in, 8), hop(near_out, 16)
        last_in, last_out = hop(last_in, 16), hop(last_out, 8)
        arrived = (near_in, near_out, last_in, last_out)
    else:
        ready = arrived = ()
        scatter = lambda v: lax.psum_scatter(v, "dp", scatter_dimension=0, tiled=True).astype(F32)
        back.append(exchange(grads_out[-1]))
        every = [weights_of(q, q, BF) for q in range(dp)]
        g_in = scatter(jnp.stack([e[0][:width] for e in every]))
        g_out = scatter(jnp.stack([e[1] for e in every]))
        g_b_in = lax.psum_scatter(
            db_in[:, 0].reshape(1, -1).astype(BF), "dp", scatter_dimension=1, tiled=True
        ).astype(F32)
        g_b_out = lax.psum_scatter(db_out[0:1].astype(BF), "dp", scatter_dimension=1, tiled=True).astype(F32)

    r_sent = exchange(after(outs_back, *back))
    back = after(back, *ready)
    after_grad, probs, grad, grads = backward(
        off_back, image_count, slots_col, cot, n1, qkv, att, aa, n2, prob, w, small, back, experts,
        2 if grouped else 1,
    )
    grads = after(grads, *arrived)
    block_out = block_output(image_count, slots_col, aa, probs, r_sent)
    def add(*values):
        return functools.reduce(lambda a, b: a + b, [v.astype(F32) for v in values])

    if grouped:
        sibling = hop(grads[1], 1)
        quarter = width // 4
        ways = [slice(a * quarter, (a + 1) * quarter) for a in range(4)]
        ways = [add(grads[0][a], sibling[a]).astype(BF) for a in ways]
        tall, bias_sums = after((tall, bias_sums), *ways)
        own_in, own_out, g_bias = weights_of(0, 0, F32, (near_in, last_in, near_out, last_out))
        g_in, g_out = own_in[None], own_out[None]
        g_b_in = g_bias[0:1]
        g_b_out = lax.dynamic_slice(g_bias[1:2], (0, spot), expert_out_bias.shape)
        after_grad, grad = after((after_grad, grad), own_in, own_out)
    tokens_grad = finish(after_grad, grad, tok, w, small, experts)

    if grouped:
        ways[0], tokens_grad, g_in, g_out = after((ways[0], tokens_grad, g_in, g_out))
        ways = [ways[0], *[hop(ways[a], 8 * a) for a in (1, 2, 3)]]
        step = width // 16
        cuts = [add(*[way[b * step : (b + 1) * step] for way in ways]) for b in range(4)]
        cuts = [cuts[0], *[c.astype(BF) for c in cuts[1:]]]
        cuts[0], block_out = after((cuts[0], block_out))
        chip = add(cuts[0], *[hop(cuts[b], 2 * b) for b in (1, 2, 3)])
        n_rows = step // 2
        keep = lax.dynamic_slice_in_dim(chip, core * n_rows, n_rows, 0)
        give = lax.dynamic_slice_in_dim(chip, (1 - core) * n_rows, n_rows, 0)
        got = hop(give.astype(BF), 1).astype(F32)
        dense = jnp.where(
            core == 0, jnp.concatenate([keep, got], axis=1), jnp.concatenate([got, keep], axis=1)
        )
    else:
        dense = lax.psum_scatter(grads[0], BOTH, scatter_dimension=0, tiled=True).astype(F32)
    side = dense[:, 4 * width :]
    vecs = [side[:, experts + k] for k in range(8)]
    return (
        block_out,
        tokens_grad,
        vecs[0],
        vecs[1],
        dense[:, : 3 * width],
        jnp.stack([vecs[5], vecs[7]], axis=0),
        dense[:, 3 * width : 4 * width],
        vecs[2],
        vecs[3],
        vecs[4],
        side[:, :experts],
        g_in,
        g_b_in,
        g_out,
        g_b_out,
    )


def solution(mesh):
    rows, line, cols = P(BOTH, None), P(BOTH), P(None, BOTH)
    experts = (P("expert", None, "dp"), P("expert", "dp"), P("expert", "dp", None), P("expert", "dp"))
    dense = (line, line, rows, cols, rows, line, line, line, rows)
    return jax.shard_map(
        functools.partial(local, (mesh.shape["dp"], mesh.shape["expert"])),
        mesh=mesh,
        in_specs=(rows, line, rows, P(), *dense, *experts, rows),
        out_specs=(rows, rows, *dense, *experts),
        check_vma=False,
    )
```
